32 devices in a mesh: parts: 2 (over y), pre: 4 (over z), tp: 4 (over x, core).
Axes of the slice: x: 2, y: 2, z: 4, core: 2. Of those that a mesh axis runs over, the one named last changes fastest.
Arguments:
- queries: bfloat16 [4096, 4096], P(('parts', 'pre'), 'tp'), parts along dimension 0, may hold values from -4.5 to 4.5
- new_keys: bfloat16 [4096, 1024], P(('parts', 'pre'), 'tp'), parts along dimension 0, may hold values from -4.5 to 4.5
- new_values: bfloat16 [4096, 1024], P(('parts', 'pre'), 'tp'), parts along dimension 0, may hold values from -4 to 4
- lengths: int32 [8], P('parts'), parts along dimension 0, may hold values from 1 to 1024, 2048 in all
- block_slot: int32 [256], P('parts'), parts along dimension 0, may hold values from 0 to 127, as said below
Outputs:
- attended: bfloat16 [4096, 4096], P(('parts', 'pre'), 'tp'), parts along dimension 0
- kv_cache: bfloat16 [256, 16, 2048], P(('parts', 'pre'), None, 'tp'), parts along dimension 0
The draws below stay inside these ranges and needn't reach their ends.
There are 2 independent parts, one for each index of `parts`. The reference program is written for one: setup_inputs(seed, part) draws one part's arguments, and reference() takes and returns one part's arrays. A program takes and returns all parts, laid end to end along the dimension named above; each array names one. Nothing has to cross between parts.
Inputs may be any that keep to these rules, and one draw needn't show every extreme that they name: `block_slot`: A permutation of the 128 slots. The 32 blocks held by one index of pre (blocks of its own rows) take exactly 8 slots of every decode owner.
All inputs are finite; a program needn't handle non-finite values.
Results may differ from the reference program's by a relative error of at most 0.0036.
Values may be sent and summed in bfloat16 or wider, within the bound.
No kernel may reach another device: no remote copies, remote signals or barrier semaphores. Data moves between devices by JAX's collectives and lax.ppermute only.
A program may use at most 64 MiB of HBM per device.

```python
import math
import jax
import jax.numpy as jnp
import numpy as np
from jax import lax

HEADS = 32
KVH = 8
HD = 128
REQS = 4
BLK = 16
GROUP = 4
SEQ = 2048
NBLK = 128
BPD = 32
SENDS = 8


def draw_queries(key, part):
    own_key = jax.random.fold_in(key, 3)
    values = jnp.clip(jax.random.normal(own_key, (SEQ, HEADS * HD), jnp.float32), -4.5, 4.5)
    return values.astype(jnp.bfloat16)


def draw_new_keys(key, part):
    own_key = jax.random.fold_in(key, 5)
    values = jnp.clip(jax.random.normal(own_key, (SEQ, KVH * HD), jnp.float32), -4.5, 4.5)
    return values.astype(jnp.bfloat16)


def draw_block_slot(key, part):
    key = jax.random.fold_in(key, 7)
    owners = NBLK // BPD
    send_keys = jax.random.split(jax.random.fold_in(key, 1), owners)
    take_keys = jax.random.split(jax.random.fold_in(key, 2), owners)
    local_order = jax.vmap(lambda seed_key: jax.random.permutation(seed_key, BPD))(send_keys).astype(jnp.int32)
    arrival = jax.vmap(lambda seed_key: jax.random.permutation(seed_key, BPD))(take_keys).astype(jnp.int32)
    column = jnp.arange(BPD, dtype=jnp.int32)
    target = column // SENDS
    within = column % SENDS
    sender = jnp.arange(owners, dtype=jnp.int32)
    slot_value = target[None, :] * BPD + arrival[target[None, :], sender[:, None] * SENDS + within[None, :]]
    slot_table = jnp.zeros((owners, BPD), jnp.int32).at[sender[:, None], local_order].set(slot_value.astype(jnp.int32))
    return slot_table.reshape(NBLK)


def block_levels(stream_key, dims, cuts, smallest, top_value):
    gain = 1.0
    for dim, shards_of in cuts:
        steps = jax.random.uniform(jax.random.fold_in(jax.random.fold_in(stream_key, 6), dim), (shards_of,), jnp.float32, smallest / len(cuts), top_value / len(cuts))
        gain = gain * jnp.repeat(jnp.exp(steps), dims[dim] // shards_of).reshape((-1,) + (1,) * (len(dims) - 1 - dim))
    return gain


def split_up(amount, total, limit, lean):
    portions = [(1 << 20) // math.isqrt(rank ** lean) + 1 for rank in range(2, amount + 1)]
    spare, counts = total - limit - (amount - 1), [1] * (amount - 1)
    while spare > 0:
        candidates = [i for i in range(amount - 1) if counts[i] < limit]
        mass, budget = sum([portions[i] for i in candidates]), spare
        for i in candidates:
            addition = min(limit - counts[i], max(1, budget * portions[i] // mass), spare)
            counts[i] = counts[i] + addition
            spare = spare - addition
    return np.array([limit] + counts)


def ragged(rng, count, total, bound, lean):
    if count == 2:
        one = jax.random.randint(rng, (), max(1, total - bound), min(bound, total - 1) + 1)
        return jnp.stack([one, total - one])
    sizes = jnp.asarray(split_up(count, total, bound, lean), jnp.int32)
    twos = (count - 1) // 2
    giver, receiver = sizes[1:1 + 2 * twos:2], sizes[2:2 + 2 * twos:2]
    slack = jnp.minimum(giver - 1, bound - receiver)
    moved = jax.random.randint(jax.random.fold_in(rng, 1), (twos,), 0, 1 << 20) % (slack + 1)
    sizes = sizes.at[1:1 + 2 * twos:2].set(giver - moved).at[2:2 + 2 * twos:2].set(receiver + moved)
    return sizes[jax.random.permutation(jax.random.fold_in(rng, 2), count)]


def noise(key, shape, width, reach, cuts=(), held_as=jnp.bfloat16):
    result = jax.random.normal(key, shape, jnp.float32) * width
    if len(cuts) > 0:
        result = block_levels(key, shape, cuts, -0.22, 0.18) * result
    return jnp.clip(result, min=-reach, max=reach).astype(held_as)


def setup_inputs(seed: int = 0, part: int = 0) -> dict:
    streams_of = jax.random.split(jax.random.key(seed), 6)
    part_splits = jax.random.split(jax.random.fold_in(streams_of[5], part), 6)
    return {
        "queries": draw_queries(jax.random.fold_in(jax.random.fold_in(streams_of[5], part), 71), part),
        "new_keys": draw_new_keys(jax.random.fold_in(jax.random.fold_in(streams_of[5], part), 71), part),
        "new_values": noise(part_splits[2], (SEQ, KVH * HD), 1.0, 4.0, ((0, 4), (1, 4))),
        "lengths": ragged(part_splits[3], REQS, SEQ, SEQ // 2, 2).astype(jnp.int32),
        "block_slot": draw_block_slot(jax.random.fold_in(jax.random.fold_in(streams_of[5], part), 71), part),
    }


def request_starts(lengths, positions):
    request_ends = jnp.cumsum(lengths).astype(jnp.int32)
    before = request_ends[None, :] <= positions[:, None]
    return jnp.sum(jnp.where(before, lengths[None, :], 0), axis=1).astype(jnp.int32)


def reference(queries, new_keys, new_values, lengths, block_slot):
    positions = jnp.arange(SEQ, dtype=jnp.int32)
    starts = request_starts(lengths, positions)
    allowed = (positions[None, :] <= positions[:, None]) & (positions[None, :] >= starts[:, None])
    query_heads = jnp.transpose(queries.reshape(SEQ, HEADS, HD), (1, 0, 2))
    key_heads = jnp.transpose(new_keys.reshape(SEQ, KVH, HD), (1, 0, 2))
    value_heads = jnp.transpose(new_values.reshape(SEQ, KVH, HD), (1, 0, 2))

    def one_head(head_index):
        group_index = head_index // GROUP
        scores = jnp.dot(query_heads[head_index], key_heads[group_index].T, preferred_element_type=jnp.float32) * (HD ** -0.5)
        scores = jnp.where(allowed, scores, -jnp.inf)
        largest = jnp.max(scores, axis=1, keepdims=True)
        probs = jnp.where(allowed, jnp.exp(scores - largest), 0.0)
        denominator = jnp.sum(probs, axis=1, keepdims=True)
        mixed = jnp.dot(probs.astype(jnp.bfloat16), value_heads[group_index], preferred_element_type=jnp.float32)
        return (mixed / denominator).astype(jnp.bfloat16)

    per_head = lax.map(one_head, jnp.arange(HEADS, dtype=jnp.int32))
    attended = jnp.transpose(per_head, (1, 0, 2)).reshape(SEQ, HEADS * HD)
    joined = jnp.concatenate([new_keys.reshape(SEQ, KVH, 1, HD), new_values.reshape(SEQ, KVH, 1, HD)], axis=2)
    joined = joined.reshape(NBLK, BLK, 2 * KVH * HD)
    kv_cache = jnp.zeros_like(joined).at[block_slot].set(joined)
    return attended, kv_cache
```

```python
import functools
import math

import jax
import jax.numpy as jnp
from jax import lax
from jax.experimental import pallas as pl
from jax.experimental.pallas import tpu as pltpu
from jax.sharding import PartitionSpec as P

HD = 128
BLK = 16
GROUP = 4
ROW_TILE = 128
KEY_TILE = 256
MASKED = -1e30
EXP_SCALE = math.log2(math.e) * HD ** (-0.5)

VMEM = pl.BlockSpec(memory_space=pltpu.VMEM)
SMEM = pl.BlockSpec(memory_space=pltpu.SMEM)


def start_of(lengths_ref, position):
    end = jnp.int32(0)
    start = jnp.int32(0)
    for r in range(lengths_ref.shape[0]):
        end = end + lengths_ref[r]
        start = jnp.where(end <= position, end, start)
    return start


def end_of(lengths_ref, position):
    end = jnp.int32(0)
    found = jnp.int32(0)
    for r in reversed(range(lengths_ref.shape[0])):
        total = jnp.int32(0)
        for s in range(r + 1):
            total = total + lengths_ref[s]
        found = jnp.where(total > position, total, found)
    return found


def row_starts(lengths_ref, positions):
    end = jnp.int32(0)
    starts = jnp.zeros_like(positions)
    for r in range(lengths_ref.shape[0]):
        end = end + lengths_ref[r]
        starts = jnp.where(positions >= end, end, starts)
    return starts


def stack_heads(q_ref, row, g):
    cols = [
        q_ref[pl.ds(row, ROW_TILE), (g * GROUP + j) * HD : (g * GROUP + j + 1) * HD]
        for j in range(GROUP)
    ]
    return jnp.concatenate(cols, axis=0)


def scores_of(queries, keys, allowed):
    scores = lax.dot_general(
        queries, keys, (((1,), (1,)), ((), ())), preferred_element_type=jnp.float32
    )
    shaped = scores.reshape(GROUP, ROW_TILE, keys.shape[0])
    shaped = jnp.where(allowed[None], shaped, MASKED)
    return shaped.reshape(GROUP * ROW_TILE, keys.shape[0])


def with_ones(values):
    return jnp.concatenate([values, jnp.ones_like(values)], axis=1)


def near_kernel(
    lengths_ref, q_ref, k_ref, v_ref, pk_ref, pv_ref,
    out_ref, acc_ref, stat_ref,
    kbuf, vbuf, top, summed,
):
    rows = q_ref.shape[0]
    kv_count = k_ref.shape[1] // HD
    first = lax.axis_index("pre") * rows
    for g in range(kv_count):
        span = slice(g * HD, (g + 1) * HD)
        kbuf[g, :rows] = pk_ref[:, span]
        kbuf[g, rows:] = k_ref[:, span]
        vbuf[g, :rows] = with_ones(pv_ref[:, span])
        vbuf[g, rows:] = with_ones(v_ref[:, span])
    lane = lax.broadcasted_iota(jnp.int32, (ROW_TILE, HD), 1)

    def row_step(i, _):
        row = pl.multiple_of(i * ROW_TILE, ROW_TILE)
        t0 = first + row
        low = jnp.maximum(start_of(lengths_ref, t0) - (first - rows), 0)
        positions = t0 + lax.broadcasted_iota(jnp.int32, (ROW_TILE, KEY_TILE), 0)
        starts = row_starts(lengths_ref, positions)
        column = lax.broadcasted_iota(jnp.int32, (ROW_TILE, KEY_TILE), 1)
        top[...] = jnp.full_like(top, MASKED)
        summed[...] = jnp.zeros_like(summed)
        last_tile = (rows + row) // KEY_TILE
        tiles = last_tile - low // KEY_TILE + 1

        def key_step(n, _):
            key = pl.multiple_of((last_tile - n) * KEY_TILE, KEY_TILE)
            at = first - rows + key + column
            allowed = (at <= positions) & (at >= starts)
            for g in range(kv_count):
                scores = scores_of(
                    stack_heads(q_ref, row, g), kbuf[g, pl.ds(key, KEY_TILE)], allowed
                )
                old = top[g]
                new = jnp.maximum(old, jnp.max(scores, axis=1, keepdims=True))
                factor = jnp.exp2((old - new) * EXP_SCALE)
                weights = jnp.exp2((scores - new[:, :1]) * EXP_SCALE).astype(jnp.bfloat16)
                part = jnp.dot(
                    weights, vbuf[g, pl.ds(key, KEY_TILE)], preferred_element_type=jnp.float32
                )
                summed[g, :, :HD] = summed[g, :, :HD] * factor + part[:, :HD]
                summed[g, :, HD:] = summed[g, :, HD:] * factor + part[:, HD:]
                top[g] = new
            return 0

        lax.fori_loop(0, tiles, key_step, 0)
        stat = jnp.zeros((ROW_TILE, HD), jnp.float32)
        for g in range(kv_count):
            for j in range(GROUP):
                head = g * GROUP + j
                part = slice(j * ROW_TILE, (j + 1) * ROW_TILE)
                value = summed[g, part, :HD]
                total = summed[g, part, HD:]
                span = slice(head * HD, (head + 1) * HD)
                acc_ref[pl.ds(row, ROW_TILE), span] = value
                out_ref[pl.ds(row, ROW_TILE), span] = (value / total).astype(out_ref.dtype)
                stat = jnp.where(lane == head, top[g, part], stat)
                stat = jnp.where(lane == HD // 2 + head, total, stat)
        stat_ref[pl.ds(row, ROW_TILE)] = stat
        return 0

    lax.fori_loop(0, rows // ROW_TILE, row_step, 0)


def place(dst_ref, slot, k_ref, v_ref, row):
    for g in range(k_ref.shape[1] // HD):
        span = slice(g * HD, (g + 1) * HD)
        dst_ref[slot, :, 2 * g * HD : (2 * g + 1) * HD] = k_ref[pl.ds(row, BLK), span]
        dst_ref[slot, :, (2 * g + 1) * HD : (2 * g + 2) * HD] = v_ref[pl.ds(row, BLK), span]


def far_kernel(
    hop, pre,
    lengths_ref, slot_ref, q_ref, k_ref, v_ref, acc_in, stat_in, out_in, cache_in,
    out_ref, acc_ref, stat_ref, cache_ref,
):
    rows = q_ref.shape[0]
    kv_count = k_ref.shape[1] // HD
    blocks = rows // BLK
    me = lax.axis_index("pre")
    first = me * rows
    key_first = first - hop * rows
    out_ref[...] = out_in[...]
    acc_ref[...] = acc_in[...]
    stat_ref[...] = stat_in[...]
    cache_ref[...] = cache_in[...]
    lane = lax.broadcasted_iota(jnp.int32, (ROW_TILE, HD), 1)
    start = start_of(lengths_ref, first)
    low = jnp.maximum(start - key_first, 0)
    reach = jnp.minimum(end_of(lengths_ref, first) - first, rows)
    wanted = (key_first >= 0) & (low < rows)
    row_tiles = jnp.where(wanted, (reach + ROW_TILE - 1) // ROW_TILE, 0)
    tiles = rows // KEY_TILE - low // KEY_TILE

    def row_step(i, _):
        row = pl.multiple_of(i * ROW_TILE, ROW_TILE)
        positions = first + row + lax.broadcasted_iota(jnp.int32, (ROW_TILE, KEY_TILE), 0)
        starts = row_starts(lengths_ref, positions)
        column = lax.broadcasted_iota(jnp.int32, (ROW_TILE, KEY_TILE), 1)

        def key_step(n, _):
            key = pl.multiple_of(rows - (n + 1) * KEY_TILE, KEY_TILE)
            allowed = (key_first + key + column) >= starts
            stat = stat_ref[pl.ds(row, ROW_TILE)]
            fresh = stat
            for g in range(kv_count):
                scores = scores_of(
                    stack_heads(q_ref, row, g),
                    k_ref[pl.ds(key, KEY_TILE), g * HD : (g + 1) * HD],
                    allowed,
                )
                highest = jnp.max(scores, axis=1, keepdims=True)
                values = with_ones(v_ref[pl.ds(key, KEY_TILE), g * HD : (g + 1) * HD])
                for j in range(GROUP):
                    head = g * GROUP + j
                    part = slice(j * ROW_TILE, (j + 1) * ROW_TILE)
                    span = slice(head * HD, (head + 1) * HD)
                    old = stat[:, head : head + 1]
                    total = stat[:, HD // 2 + head : HD // 2 + head + 1]
                    new = jnp.maximum(old, highest[part])
                    factor = jnp.exp2((old - new) * EXP_SCALE)
                    weights = jnp.exp2((scores[part] - new) * EXP_SCALE).astype(jnp.bfloat16)
                    added = jnp.dot(weights, values, preferred_element_type=jnp.float32)
                    total = total * factor + added[:, HD:]
                    value = acc_ref[pl.ds(row, ROW_TILE), span] * factor + added[:, :HD]
                    acc_ref[pl.ds(row, ROW_TILE), span] = value
                    out_ref[pl.ds(row, ROW_TILE), span] = (value / total).astype(out_ref.dtype)
                    fresh = jnp.where(lane == head, new, fresh)
                    fresh = jnp.where(lane == HD // 2 + head, total, fresh)
            stat_ref[pl.ds(row, ROW_TILE)] = fresh
            return 0

        lax.fori_loop(0, tiles, key_step, 0)
        return 0

    lax.fori_loop(0, row_tiles, row_step, 0)

    def cache_step(b, _):
        slot = slot_ref[(me - hop) * blocks + b]

        @pl.when(slot // blocks == me)
        def _():
            place(cache_ref, slot - me * blocks, k_ref, v_ref, b * BLK)

        return 0

    lax.fori_loop(0, jnp.where(me >= hop, blocks, 0), cache_step, 0)


def pack_kernel(pre, slot_ref, k_ref, v_ref, sent_ref, counts):
    blocks = k_ref.shape[0] // BLK
    per_peer = blocks // pre
    me = lax.axis_index("pre")
    for owner in range(pre):
        counts[owner] = 0

    def step(b, _):
        slot = slot_ref[me * blocks + b]
        owner = slot // blocks
        n = counts[owner]
        counts[owner] = n + 1
        distance = lax.rem(owner - me + pre, pre)

        @pl.when(distance > 0)
        def _():
            place(sent_ref, (distance - 1) * per_peer + n, k_ref, v_ref, b * BLK)

        return 0

    lax.fori_loop(0, blocks, step, 0)


def place_kernel(pre, near_hops, hops, slot_ref, got_ref, *refs):
    near, cache_ref = refs[:-1], refs[-1]
    blocks = near[0].shape[0] // BLK
    per_peer = blocks // pre
    me = lax.axis_index("pre")
    for back in range(near_hops):
        k_ref, v_ref = near[2 * back], near[2 * back + 1]

        def near_step(b, _):
            slot = slot_ref[(me - back) * blocks + b]

            @pl.when(slot // blocks == me)
            def _():
                place(cache_ref, slot - me * blocks, k_ref, v_ref, b * BLK)

            return 0

        lax.fori_loop(0, jnp.where(me >= back, blocks, 0), near_step, 0)
    for distance in range(1, pre):
        source = lax.rem(me - distance + pre, pre)

        def far_step(b, n):
            slot = slot_ref[source * blocks + b]
            mine = slot // blocks == me

            @pl.when(mine)
            def _():
                cache_ref[slot - me * blocks] = got_ref[(distance - 1) * per_peer + n]

            return n + jnp.where(mine, 1, 0)

        beyond = jnp.logical_or(source > me, distance > hops)
        lax.fori_loop(0, jnp.where(beyond, blocks, 0), far_step, jnp.int32(0))


def on_device(queries, new_keys, new_values, lengths, block_slot):
    rows = queries.shape[0]
    kv_count = new_keys.shape[1] // HD
    width = new_keys.shape[1] * 2
    blocks = rows // BLK
    pre = lax.axis_size("pre")
    per_peer = blocks // pre
    hops = pre // 2
    bf16, f32 = jnp.bfloat16, jnp.float32
    shape = jax.ShapeDtypeStruct
    big = pltpu.CompilerParams(vmem_limit_bytes=40 * 2**20)

    forward = [(i, i + 1) for i in range(pre - 1)]
    pk = lax.ppermute(new_keys, "pre", forward)
    pv = lax.ppermute(new_values, "pre", forward)

    sent = pl.pallas_call(
        functools.partial(pack_kernel, pre),
        out_shape=shape(((pre - 1) * per_peer, BLK, width), bf16),
        in_specs=[SMEM, VMEM, VMEM],
        out_specs=VMEM,
        scratch_shapes=[pltpu.SMEM((pre,), jnp.int32)],
        cost_estimate=pl.CostEstimate(flops=0, bytes_accessed=2**20, transcendentals=0),
        name="pack_blocks",
    )(block_slot, new_keys, new_values)
    got = []
    for distance in range(1, pre):
        pairs = [
            (i, (i + distance) % pre)
            for i in range(pre)
            if i + distance >= pre or distance > hops
        ]
        got.append(
            lax.ppermute(sent[(distance - 1) * per_peer : distance * per_peer], "pre", pairs)
        )
    got = jnp.concatenate(got, axis=0)

    attended, acc, stat = pl.pallas_call(
        near_kernel,
        out_shape=(
            shape(queries.shape, bf16),
            shape(queries.shape, f32),
            shape((rows, HD), f32),
        ),
        in_specs=[SMEM] + [VMEM] * 5,
        out_specs=(VMEM, VMEM, VMEM),
        scratch_shapes=[
            pltpu.VMEM((kv_count, 2 * rows, HD), bf16),
            pltpu.VMEM((kv_count, 2 * rows, 2 * HD), bf16),
            pltpu.VMEM((kv_count, GROUP * ROW_TILE, HD), f32),
            pltpu.VMEM((kv_count, GROUP * ROW_TILE, 2 * HD), f32),
        ],
        cost_estimate=pl.CostEstimate(
            flops=4 * rows * rows * 2 * queries.shape[1],
            bytes_accessed=6 * 2**20,
            transcendentals=rows * rows * 2 * kv_count * GROUP,
        ),
        compiler_params=big,
        name="near_attention",
    )(lengths, queries, new_keys, new_values, pk, pv)

    chain = [(new_keys, new_values), (pk, pv)]
    for hop in range(2, hops + 1):
        pairs = [(i, i + 1) for i in range(hop - 1, pre - 1)]
        chain.append(tuple(lax.ppermute(piece, "pre", pairs) for piece in chain[-1]))
    flat = [piece for pair in chain[:2] for piece in pair]
    cache = pl.pallas_call(
        functools.partial(place_kernel, pre, 2, hops),
        out_shape=shape((blocks, BLK, width), bf16),
        in_specs=[SMEM] + [VMEM] * (1 + len(flat)),
        out_specs=VMEM,
        cost_estimate=pl.CostEstimate(flops=0, bytes_accessed=2**21, transcendentals=0),
        name="place_blocks",
    )(block_slot, got, *flat)
    for hop in range(2, hops + 1):
        attended, acc, stat, cache = pl.pallas_call(
            functools.partial(far_kernel, hop, pre),
            out_shape=(
                shape(attended.shape, bf16),
                shape(acc.shape, f32),
                shape(stat.shape, f32),
                shape(cache.shape, bf16),
            ),
            in_specs=[SMEM, SMEM] + [VMEM] * 7,
            out_specs=(VMEM,) * 4,
            input_output_aliases={5: 1, 6: 2, 7: 0, 8: 3},
            cost_estimate=pl.CostEstimate(
                flops=rows * rows * queries.shape[1],
                bytes_accessed=6 * 2**20,
                transcendentals=rows * rows * kv_count,
            ),
            compiler_params=big,
            name="far_attention",
        )(lengths, block_slot, queries, *chain[hop], acc, stat, attended, cache)
    return (attended, cache)


def solution(mesh):
    placed = (
        P(("parts", "pre"), "tp"),
        P(("parts", "pre"), "tp"),
        P(("parts", "pre"), "tp"),
        P("parts"),
        P("parts"),
    )
    return jax.shard_map(
        on_device,
        mesh=mesh,
        in_specs=placed,
        out_specs=(P(("parts", "pre"), "tp"), P(("parts", "pre"), None, "tp")),
        check_vma=False,
    )
```

```python
import functools
import math

import jax
import jax.numpy as jnp
from jax import lax
from jax.experimental import pallas as pl
from jax.experimental.pallas import tpu as pltpu
from jax.sharding import PartitionSpec as P

HD = 128
BLK = 16
GROUP = 4
TILE = 256
ONES = 16
MASKED = -1e30
EXP_SCALE = math.log2(math.e) * HD ** (-0.5)

VMEM = pl.BlockSpec(memory_space=pltpu.VMEM)
SMEM = pl.BlockSpec(memory_space=pltpu.SMEM)
ANY = pl.BlockSpec(memory_space=pl.ANY)


def start_of(lengths_ref, position):
    end = jnp.int32(0)
    start = jnp.int32(0)
    for r in range(lengths_ref.shape[0]):
        end = end + lengths_ref[r]
        start = jnp.where(end <= position, end, start)
    return start


def row_starts(lengths_ref, positions):
    end = jnp.int32(0)
    starts = jnp.zeros_like(positions)
    for r in range(lengths_ref.shape[0]):
        end = end + lengths_ref[r]
        starts = jnp.where(positions >= end, end, starts)
    return starts


def fill_bias(bias_ref, lengths_ref, row_first, key_first, low, high, causal):
    shape = (high - low, TILE)
    positions = row_first + lax.broadcasted_iota(jnp.int32, (8, TILE), 1)
    starts = row_starts(lengths_ref, positions)
    keys = key_first + low + lax.broadcasted_iota(jnp.int32, shape, 0)
    keys = keys.reshape((high - low) // 8, 8, TILE)
    allowed = keys >= starts[None]
    if causal:
        allowed = allowed & (keys <= positions[None])
    bias_ref[low:high] = jnp.where(allowed, 0.0, MASKED).reshape(shape)


def turn_values(v_ref, turned):
    for g in range(turned.shape[0]):
        turned[g, :HD] = v_ref[:, g * HD : (g + 1) * HD].T
        turned[g, HD:] = jnp.ones((ONES, turned.shape[2]), turned.dtype)


def absorb(q_ref, k_ref, turned, bias_ref, state, tile, low, high, fresh):
    acc_ref, top_ref, sum_ref = state
    for g in range(turned.shape[0]):
        keys = k_ref[low:high, g * HD : (g + 1) * HD]
        values = turned[g, :, low:high]
        for j in range(GROUP):
            head = g * GROUP + j
            at = slice((tile * GROUP + j) * TILE, (tile * GROUP + j + 1) * TILE)
            queries = q_ref[tile * TILE : (tile + 1) * TILE, head * HD : (head + 1) * HD]
            scores = lax.dot_general(
                keys, queries, (((1,), (1,)), ((), ())), preferred_element_type=jnp.float32
            )
            scores = (scores + bias_ref[low:high]).reshape((high - low) // 8, 8, TILE)
            highest = jnp.max(jnp.max(scores, axis=0), axis=0, keepdims=True)
            new = jnp.broadcast_to(highest, (8, TILE))
            if not fresh:
                old = top_ref[g, :, at]
                new = jnp.maximum(old, new)
                factor = jnp.exp2((old - new) * EXP_SCALE)
            weights = jnp.exp2((scores - new[None]) * EXP_SCALE)
            weights = weights.reshape(high - low, TILE).astype(jnp.bfloat16)
            added = jnp.dot(values, weights, preferred_element_type=jnp.float32)
            value, total = added[:HD], added[HD : HD + 8]
            if not fresh:
                total = total + sum_ref[g, :, at] * factor
                kept = acc_ref[g, :, at].reshape(HD // 8, 8, TILE) * factor[None]
                value = value + kept.reshape(HD, TILE)
            acc_ref[g, :, at] = value
            sum_ref[g, :, at] = total
            top_ref[g, :, at] = new


def finish(state, tile, out_ref, row):
    acc_ref, _, sum_ref = state
    for g in range(acc_ref.shape[0]):
        for j in range(GROUP):
            head = g * GROUP + j
            at = slice((tile * GROUP + j) * TILE, (tile * GROUP + j + 1) * TILE)
            inverse = 1.0 / sum_ref[g, :, at]
            value = acc_ref[g, :, at].reshape(HD // 8, 8, TILE) * inverse[None]
            value = value.reshape(HD, TILE).astype(out_ref.dtype).T
            out_ref[row : row + TILE, head * HD : (head + 1) * HD] = value


def own_kernel(lengths_ref, q_ref, k_ref, v_ref, acc_ref, top_ref, sum_ref, turned, bias):
    rows = q_ref.shape[0]
    first = lax.axis_index("pre") * rows
    state = (acc_ref, top_ref, sum_ref)
    turn_values(v_ref, turned)
    for tile in range(rows // TILE):
        high = (tile + 1) * TILE
        fill_bias(bias, lengths_ref, first + tile * TILE, first, 0, high, True)
        absorb(q_ref, k_ref, turned, bias, state, tile, 0, high, True)


def absorb_far(lengths_ref, hop, q_ref, k_ref, turned, bias, state, then):
    rows = q_ref.shape[0]
    first = lax.axis_index("pre") * rows
    key_first = first - hop * rows
    for tile in range(rows // TILE):
        row_first = first + tile * TILE
        low = jnp.maximum(start_of(lengths_ref, row_first) - key_first, 0)
        low = jnp.where(key_first >= 0, low, rows)
        for cut in range(rows // TILE):
            at = cut * TILE

            @pl.when((low >= at) & (low < at + TILE))
            def _():
                fill_bias(bias, lengths_ref, row_first, key_first, at, rows, False)
                absorb(q_ref, k_ref, turned, bias, state, tile, at, rows, False)

        then(tile, low < rows)


def prev_kernel(
    lengths_ref, q_ref, k_ref, v_ref, acc_in, top_in, sum_in,
    out_ref, acc_ref, top_ref, sum_ref, turned, bias,
):
    state = (acc_ref, top_ref, sum_ref)
    for old, new in zip((acc_in, top_in, sum_in), state):
        new[...] = old[...]
    turn_values(v_ref, turned)

    def then(tile, changed):
        finish(state, tile, out_ref, tile * TILE)

    absorb_far(lengths_ref, 1, q_ref, k_ref, turned, bias, state, then)


def place(dst_ref, slot, k_ref, v_ref, row):
    for g in range(k_ref.shape[1] // HD):
        span = slice(g * HD, (g + 1) * HD)
        dst_ref[slot, :, 2 * g * HD : (2 * g + 1) * HD] = k_ref[pl.ds(row, BLK), span]
        dst_ref[slot, :, (2 * g + 1) * HD : (2 * g + 2) * HD] = v_ref[pl.ds(row, BLK), span]


def far_kernel(
    hop, pre, last,
    lengths_ref, slot_ref, q_ref, k_ref, v_ref, acc_in, top_in, sum_in, out_in, cache_in,
    out_ref, acc_ref, top_ref, sum_ref, cache_ref,
    turned, bias, out_tile, out_sem, blocks_buf, block_sems,
):
    rows = q_ref.shape[0]
    blocks = rows // BLK
    me = lax.axis_index("pre")
    state = (acc_ref, top_ref, sum_ref)
    if last:
        source = lax.rem(me - hop + pre, pre)

        def cache_step(b, n):
            slot = slot_ref[source * blocks + b]
            mine = slot // blocks == me

            @pl.when(mine)
            def _():
                place(blocks_buf, n, k_ref, v_ref, b * BLK)
                pltpu.make_async_copy(
                    blocks_buf.at[n], cache_ref.at[slot - me * blocks], block_sems.at[n]
                ).start()

            return n + jnp.where(mine, 1, 0)

        lax.fori_loop(0, blocks, cache_step, jnp.int32(0))

    first = me * rows
    wanted = (first >= hop * rows) & (start_of(lengths_ref, first) < first - (hop - 1) * rows)

    @pl.when(wanted)
    def _():
        for old, new in zip((acc_in, top_in, sum_in), state):
            new[...] = old[...]
        turn_values(v_ref, turned)

        def then(tile, changed):
            @pl.when(changed)
            def _():
                finish(state, tile, out_tile, 0)
                copy = pltpu.make_async_copy(
                    out_tile, out_ref.at[tile * TILE : (tile + 1) * TILE], out_sem
                )
                copy.start()
                copy.wait()

        absorb_far(lengths_ref, hop, q_ref, k_ref, turned, bias, state, then)

    if last:
        for n in range(blocks // pre):
            pltpu.make_async_copy(blocks_buf.at[n], cache_ref.at[0], block_sems.at[n]).wait()
    else:
        @pl.when(jnp.logical_not(wanted))
        def _():
            for old, new in zip((acc_in, top_in, sum_in), state):
                new[...] = old[...]


def pack_kernel(pre, hops, slot_ref, k_ref, v_ref, sent_ref, counts):
    blocks = k_ref.shape[0] // BLK
    per_peer = blocks // pre
    me = lax.axis_index("pre")
    for owner in range(pre):
        counts[owner] = 0

    def step(b, _):
        slot = slot_ref[me * blocks + b]
        owner = slot // blocks
        n = counts[owner]
        counts[owner] = n + 1
        distance = lax.rem(owner - me + pre, pre)

        @pl.when(distance > hops)
        def _():
            place(sent_ref, (distance - hops - 1) * per_peer + n, k_ref, v_ref, b * BLK)

        return 0

    lax.fori_loop(0, blocks, step, 0)


def place_kernel(pre, hops, slot_ref, got_ref, *refs):
    near, cache_ref = refs[:-1], refs[-1]
    blocks = near[0].shape[0] // BLK
    per_peer = blocks // pre
    me = lax.axis_index("pre")
    for back in range(hops):
        k_ref, v_ref = near[2 * back], near[2 * back + 1]
        source = lax.rem(me - back + pre, pre)

        def near_step(b, _):
            slot = slot_ref[source * blocks + b]

            @pl.when(slot // blocks == me)
            def _():
                place(cache_ref, slot - me * blocks, k_ref, v_ref, b * BLK)

            return 0

        lax.fori_loop(0, blocks, near_step, 0)
    for distance in range(hops + 1, pre):
        source = lax.rem(me - distance + pre, pre)

        def far_step(b, n):
            slot = slot_ref[source * blocks + b]
            mine = slot // blocks == me

            @pl.when(mine)
            def _():
                cache_ref[slot - me * blocks] = got_ref[(distance - hops - 1) * per_peer + n]

            return n + jnp.where(mine, 1, 0)

        lax.fori_loop(0, blocks, far_step, jnp.int32(0))


def on_device(queries, new_keys, new_values, lengths, block_slot):
    rows, q_width = queries.shape
    kv_count = new_keys.shape[1] // HD
    width = new_keys.shape[1] * 2
    blocks = rows // BLK
    pre = lax.axis_size("pre")
    per_peer = blocks // pre
    hops = pre // 2
    bf16, f32 = jnp.bfloat16, jnp.float32
    shape = jax.ShapeDtypeStruct
    params = pltpu.CompilerParams(vmem_limit_bytes=32 * 2**20)
    ring = [(i, (i + 1) % pre) for i in range(pre)]
    state = (
        shape((kv_count, HD, GROUP * rows), f32),
        shape((kv_count, 8, GROUP * rows), f32),
        shape((kv_count, 8, GROUP * rows), f32),
    )
    scratch = [
        pltpu.VMEM((kv_count, HD + ONES, rows), bf16),
        pltpu.VMEM((rows, TILE), f32),
    ]

    def cost(share, moved):
        pairs = int(rows * rows * share)
        return pl.CostEstimate(
            flops=4 * pairs * q_width,
            bytes_accessed=moved * 2**20,
            transcendentals=pairs * kv_count * GROUP,
        )

    pk = lax.ppermute(new_keys, "pre", ring)
    pv = lax.ppermute(new_values, "pre", ring)

    sent = pl.pallas_call(
        functools.partial(pack_kernel, pre, hops),
        out_shape=shape(((pre - 1 - hops) * per_peer, BLK, width), bf16),
        in_specs=[SMEM, VMEM, VMEM],
        out_specs=VMEM,
        scratch_shapes=[pltpu.SMEM((pre,), jnp.int32)],
        cost_estimate=cost(0, 1),
        name="pack_blocks",
    )(block_slot, new_keys, new_values)
    got = []
    for distance in range(hops + 1, pre):
        at = (distance - hops - 1) * per_peer
        pairs = [(i, (i + distance) % pre) for i in range(pre)]
        got.append(lax.ppermute(sent[at : at + per_peer], "pre", pairs))
    got = jnp.concatenate(got, axis=0)

    running = pl.pallas_call(
        own_kernel,
        out_shape=state,
        in_specs=[SMEM, VMEM, VMEM, VMEM],
        out_specs=(VMEM,) * 3,
        scratch_shapes=scratch,
        cost_estimate=cost(1, 4),
        compiler_params=params,
        name="own_attention",
    )(lengths, queries, new_keys, new_values)

    chain = [(new_keys, new_values), (pk, pv)]
    for hop in range(2, hops + 1):
        chain.append(tuple(lax.ppermute(piece, "pre", ring) for piece in chain[-1]))

    attended, *running = pl.pallas_call(
        prev_kernel,
        out_shape=(shape(queries.shape, bf16),) + state,
        in_specs=[SMEM] + [VMEM] * 6,
        out_specs=(VMEM,) * 4,
        scratch_shapes=scratch,
        input_output_aliases={4: 1, 5: 2, 6: 3},
        cost_estimate=cost(1, 5),
        compiler_params=params,
        name="prev_attention",
    )(lengths, queries, pk, pv, *running)

    flat = [piece for pair in chain[:-1] for piece in pair]
    cache = pl.pallas_call(
        functools.partial(place_kernel, pre, hops),
        out_shape=shape((blocks, BLK, width), bf16),
        in_specs=[SMEM] + [VMEM] * (1 + len(flat)),
        out_specs=VMEM,
        cost_estimate=cost(0, 2),
        name="place_blocks",
    )(block_slot, got, *flat)
    for hop in range(2, hops + 1):
        attended, *running, cache = pl.pallas_call(
            functools.partial(far_kernel, hop, pre, hop == hops),
            out_shape=(shape(attended.shape, bf16),) + state + (shape(cache.shape, bf16),),
            in_specs=[SMEM, SMEM] + [VMEM] * 6 + [ANY, ANY],
            out_specs=(ANY,) + (VMEM,) * 3 + (ANY,),
            scratch_shapes=scratch + [
                pltpu.VMEM((TILE, q_width), bf16),
                pltpu.SemaphoreType.DMA,
                pltpu.VMEM((per_peer, BLK, width), bf16),
                pltpu.SemaphoreType.DMA((per_peer,)),
            ],
            input_output_aliases={5: 1, 6: 2, 7: 3, 8: 0, 9: 4},
            cost_estimate=cost(0.25, 2),
            compiler_params=params,
            name="far_attention",
        )(lengths, block_slot, queries, *chain[hop], *running, attended, cache)
    return (attended, cache)


def solution(mesh):
    placed = (
        P(("parts", "pre"), "tp"),
        P(("parts", "pre"), "tp"),
        P(("parts", "pre"), "tp"),
        P("parts"),
        P("parts"),
    )
    return jax.shard_map(
        on_device,
        mesh=mesh,
        in_specs=placed,
        out_specs=(P(("parts", "pre"), "tp"), P(("parts", "pre"), None, "tp")),
        check_vma=False,
    )
```

```python
import functools
import math

import jax
import jax.numpy as jnp
from jax import lax
from jax.experimental import pallas as pl
from jax.experimental.pallas import tpu as pltpu
from jax.sharding import PartitionSpec as P

HD = 128
BLK = 16
GROUP = 4
TILE = 256
ONES = 16
MASKED = -1e30
EXP_SCALE = math.log2(math.e) * HD ** (-0.5)

VMEM = pl.BlockSpec(memory_space=pltpu.VMEM)
SMEM = pl.BlockSpec(memory_space=pltpu.SMEM)
HBM = pl.BlockSpec(memory_space=pltpu.HBM)


def start_of(lengths_ref, position):
    end = jnp.int32(0)
    start = jnp.int32(0)
    for r in range(lengths_ref.shape[0]):
        end = end + lengths_ref[r]
        start = jnp.where(end <= position, end, start)
    return start


def row_starts(lengths_ref, positions):
    end = jnp.int32(0)
    starts = jnp.zeros_like(positions)
    for r in range(lengths_ref.shape[0]):
        end = end + lengths_ref[r]
        starts = jnp.where(positions >= end, end, starts)
    return starts


def fill_bias(bias_ref, lengths_ref, row_first, key_first, low, high, causal):
    shape = (high - low, TILE)
    positions = row_first + lax.broadcasted_iota(jnp.int32, (8, TILE), 1)
    starts = row_starts(lengths_ref, positions)
    keys = key_first + low + lax.broadcasted_iota(jnp.int32, shape, 0)
    keys = keys.reshape((high - low) // 8, 8, TILE)
    allowed = keys >= starts[None]
    if causal:
        allowed = allowed & (keys <= positions[None])
    bias_ref[low:high] = jnp.where(allowed, 0.0, MASKED).reshape(shape)


def turn_values(v_ref, turned):
    for g in range(turned.shape[0]):
        turned[g, :HD] = v_ref[:, g * HD : (g + 1) * HD].T
        turned[g, HD:] = jnp.ones((ONES, turned.shape[2]), turned.dtype)


def lanes_of(tile, j):
    return slice((tile * GROUP + j) * TILE, (tile * GROUP + j + 1) * TILE)


def absorb(q_ref, k_ref, turned, bias_ref, old_state, tile, low, high, emit):
    for g in range(turned.shape[0]):
        keys = k_ref[low:high, g * HD : (g + 1) * HD]
        values = turned[g, :, low:high]
        heads = range(g * GROUP, (g + 1) * GROUP)
        queries = jnp.concatenate(
            [q_ref[tile * TILE : (tile + 1) * TILE, h * HD : (h + 1) * HD] for h in heads], axis=0
        )
        all_scores = lax.dot_general(
            keys, queries, (((1,), (1,)), ((), ())), preferred_element_type=jnp.float32
        )
        all_weights, tops, factors = [], [], []
        for j in range(GROUP):
            scores = all_scores[:, j * TILE : (j + 1) * TILE] + bias_ref[low:high]
            scores = scores.reshape((high - low) // 8, 8, TILE)
            highest = jnp.max(jnp.max(scores, axis=0), axis=0, keepdims=True)
            new = jnp.broadcast_to(highest, (8, TILE))
            if old_state is not None:
                old = old_state[1][g, :, lanes_of(tile, j)]
                new = jnp.maximum(old, new)
                factors.append(jnp.exp2((old - new) * EXP_SCALE))
            weights = jnp.exp2((scores - new[None]) * EXP_SCALE)
            all_weights.append(weights.reshape(high - low, TILE).astype(jnp.bfloat16))
            tops.append(new)
        all_added = jnp.dot(
            values, jnp.concatenate(all_weights, axis=1), preferred_element_type=jnp.float32
        )
        for j in range(GROUP):
            added = all_added[:, j * TILE : (j + 1) * TILE]
            value, total = added[:HD], added[HD : HD + 8]
            if old_state is not None:
                total = total + old_state[2][g, :, lanes_of(tile, j)] * factors[j]
                kept = old_state[0][g, :, lanes_of(tile, j)].reshape(HD // 8, 8, TILE)
                value = value + (kept * factors[j][None]).reshape(HD, TILE)
            emit(g, j, value, tops[j], total)


def keep(state, tile):
    def emit(g, j, value, top, total):
        for ref, array in zip(state, (value, top, total)):
            ref[g, :, lanes_of(tile, j)] = array

    return emit


def finish(out_ref, row):
    def emit(g, j, value, top, total):
        head = g * GROUP + j
        value = value.reshape(HD // 8, 8, TILE) * (1.0 / total)[None]
        value = value.reshape(HD, TILE).astype(out_ref.dtype).T
        out_ref[row : row + TILE, head * HD : (head + 1) * HD] = value

    return emit


def block_of(k_ref, v_ref, row):
    parts = []
    for g in range(k_ref.shape[1] // HD):
        span = slice(g * HD, (g + 1) * HD)
        parts += [k_ref[pl.ds(row, BLK), span], v_ref[pl.ds(row, BLK), span]]
    return jnp.concatenate(parts, axis=1)


def own_slot(slot, me, blocks):
    local = slot - me * blocks
    return jnp.where((local >= 0) & (local < blocks), local, blocks)


def own_kernel(
    pre, hops, lengths_ref, slot_ref, q_hbm, k_hbm, v_hbm,
    acc_ref, top_ref, sum_ref, sent_hbm,
    q_ref, k_ref, v_ref, turned, bias, sent, counts, sems,
):
    rows = q_ref.shape[0]
    blocks = rows // BLK
    per_peer = blocks // pre
    spare = sent.shape[0] - 1
    me = lax.axis_index("pre")
    first = me * rows
    loads = [
        pltpu.make_async_copy(src, dst, sems.at[n])
        for n, (src, dst) in enumerate(((k_hbm, k_ref), (v_hbm, v_ref), (q_hbm, q_ref)))
    ]
    for load in loads:
        load.start()
    for owner in range(pre):
        counts[owner] = 0
    loads[0].wait()
    loads[1].wait()

    def step(b, _):
        owner = slot_ref[me * blocks + b] // blocks
        n = counts[owner]
        counts[owner] = n + 1
        distance = lax.rem(owner - me + pre, pre)
        at = jnp.where(distance > hops, (distance - hops - 1) * per_peer + n, spare)
        sent[at] = block_of(k_ref, v_ref, pl.multiple_of(b * BLK, BLK))
        return 0

    lax.fori_loop(0, blocks, step, 0, unroll=4)
    store = pltpu.make_async_copy(sent.at[0:spare], sent_hbm, sems.at[3])
    store.start()
    turn_values(v_ref, turned)
    loads[2].wait()
    for tile in range(rows // TILE):
        high = (tile + 1) * TILE
        fill_bias(bias, lengths_ref, first + tile * TILE, first, 0, high, True)
        emit = keep((acc_ref, top_ref, sum_ref), tile)
        absorb(q_ref, k_ref, turned, bias, None, tile, 0, high, emit)
    store.wait()


def lowest_key(lengths_ref, hop, tile, rows):
    first = lax.axis_index("pre") * rows
    key_first = first - hop * rows
    low = jnp.maximum(start_of(lengths_ref, first + tile * TILE) - key_first, 0)
    return jnp.where(key_first >= 0, jnp.minimum(low, rows), rows)


def absorb_far(lengths_ref, hop, low, q_ref, k_ref, turned, bias, old_state, tile, emit):
    rows = q_ref.shape[0]
    first = lax.axis_index("pre") * rows
    for at in range(0, rows, TILE):

        @pl.when((low >= at) & (low < at + TILE))
        def _():
            fill_bias(
                bias, lengths_ref, first + tile * TILE, first - hop * rows, at, rows, False
            )
            absorb(q_ref, k_ref, turned, bias, old_state, tile, at, rows, emit)


def prev_kernel(
    lengths_ref, q_ref, k_ref, v_ref, acc_in, top_in, sum_in,
    out_hbm, acc_ref, top_ref, sum_ref, turned, bias, out_buf, sems,
):
    rows = q_ref.shape[0]
    old_state = (acc_in, top_in, sum_in)
    turn_values(v_ref, turned)
    stores = []
    for tile in range(rows // TILE):
        keep_it = keep((acc_ref, top_ref, sum_ref), tile)
        end_it = finish(out_buf, tile * TILE)

        def emit(*result):
            keep_it(*result)
            end_it(*result)

        low = lowest_key(lengths_ref, 1, tile, rows)
        absorb_far(lengths_ref, 1, low, q_ref, k_ref, turned, bias, old_state, tile, emit)

        @pl.when(low == rows)
        def _():
            for g in range(turned.shape[0]):
                for j in range(GROUP):
                    end_it(g, j, *(ref[g, :, lanes_of(tile, j)] for ref in old_state))

        at = slice(tile * TILE, (tile + 1) * TILE)
        stores.append(pltpu.make_async_copy(out_buf.at[at], out_hbm.at[at], sems.at[tile]))
        stores[-1].start()
    for store in stores:
        store.wait()


def far_kernel(
    hop, pre, last,
    lengths_ref, slot_ref, q_ref, k_ref, v_ref, acc_in, top_in, sum_in, cache_in, out_in,
    *refs,
):
    if last:
        out_hbm, cache_hbm, cache, turned, bias, out_buf, sems = refs
        state = None
    else:
        out_hbm, *state, turned, bias, out_buf, sems = refs
    rows = q_ref.shape[0]
    blocks = rows // BLK
    me = lax.axis_index("pre")
    old_state = (acc_in, top_in, sum_in)
    tiles = rows // TILE
    if last:
        source = lax.rem(me - hop + pre, pre)
        cache[...] = cache_in[...]

        def cache_step(b, _):
            at = own_slot(slot_ref[source * blocks + b], me, blocks)
            cache[at] = block_of(k_ref, v_ref, pl.multiple_of(b * BLK, BLK))
            return 0

        lax.fori_loop(0, blocks, cache_step, 0, unroll=4)
        cache_store = pltpu.make_async_copy(cache.at[0:blocks], cache_hbm, sems.at[tiles])
        cache_store.start()

    lows = [lowest_key(lengths_ref, hop, tile, rows) for tile in range(tiles)]
    stores = []

    @pl.when(lows[0] < rows)
    def _():
        turn_values(v_ref, turned)

    for tile, low in enumerate(lows):
        end_it = finish(out_buf, tile * TILE)

        def emit(*result):
            if not last:
                keep(state, tile)(*result)
            end_it(*result)

        at = slice(tile * TILE, (tile + 1) * TILE)
        stores.append(pltpu.make_async_copy(out_buf.at[at], out_hbm.at[at], sems.at[tile]))
        absorb_far(lengths_ref, hop, low, q_ref, k_ref, turned, bias, old_state, tile, emit)
        pl.when(low < rows)(stores[-1].start)
    for low, store in zip(lows, stores):
        pl.when(low < rows)(store.wait)
    if last:
        cache_store.wait()


def place_kernel(pre, hops, slot_ref, got_ref, *refs):
    near, cache_ref = refs[:-1], refs[-1]
    blocks = near[0].shape[0] // BLK
    per_peer = blocks // pre
    me = lax.axis_index("pre")
    for back in range(hops):
        k_ref, v_ref = near[2 * back], near[2 * back + 1]
        source = lax.rem(me - back + pre, pre)

        def near_step(b, _):
            at = own_slot(slot_ref[source * blocks + b], me, blocks)
            cache_ref[at] = block_of(k_ref, v_ref, pl.multiple_of(b * BLK, BLK))
            return 0

        lax.fori_loop(0, blocks, near_step, 0, unroll=4)
    for distance in range(hops + 1, pre):
        source = lax.rem(me - distance + pre, pre)

        def far_step(b, n):
            at = own_slot(slot_ref[source * blocks + b], me, blocks)
            cache_ref[at] = got_ref[(distance - hops - 1) * per_peer + jnp.minimum(n, per_peer - 1)]
            return n + jnp.where(at < blocks, 1, 0)

        lax.fori_loop(0, blocks, far_step, jnp.int32(0), unroll=4)


def on_device(queries, new_keys, new_values, lengths, block_slot):
    rows, q_width = queries.shape
    kv_width = new_keys.shape[1]
    kv_count = kv_width // HD
    blocks = rows // BLK
    pre = lax.axis_size("pre")
    per_peer = blocks // pre
    hops = pre // 2
    far = (pre - 1 - hops) * per_peer
    tiles = rows // TILE
    bf16, f32 = jnp.bfloat16, jnp.float32
    shape = jax.ShapeDtypeStruct
    params = pltpu.CompilerParams(vmem_limit_bytes=24 * 2**20)
    ring = [(i, (i + 1) % pre) for i in range(pre)]
    state = (
        shape((kv_count, HD, GROUP * rows), f32),
        shape((kv_count, 8, GROUP * rows), f32),
        shape((kv_count, 8, GROUP * rows), f32),
    )
    turned = pltpu.VMEM((kv_count, HD + ONES, rows), bf16)
    bias = pltpu.VMEM((rows, TILE), f32)
    out_buf = pltpu.VMEM((rows, q_width), bf16)
    attended_shape = shape(queries.shape, bf16)
    cache_shape = shape((blocks, BLK, 2 * kv_width), bf16)
    open_cache = (blocks + 1, BLK, 2 * kv_width)

    def cost(share, moved):
        pairs = int(rows * rows * share)
        return pl.CostEstimate(
            flops=4 * pairs * q_width,
            bytes_accessed=moved * 2**20,
            transcendentals=pairs * kv_count * GROUP,
        )

    pk = lax.ppermute(new_keys, "pre", ring)
    pv = lax.ppermute(new_values, "pre", ring)

    *running, sent = pl.pallas_call(
        functools.partial(own_kernel, pre, hops),
        out_shape=state + (shape((far, BLK, 2 * kv_width), bf16),),
        in_specs=[SMEM, SMEM, HBM, HBM, HBM],
        out_specs=(VMEM,) * 3 + (HBM,),
        scratch_shapes=[
            pltpu.VMEM((rows, q_width), bf16),
            pltpu.VMEM((rows, kv_width), bf16),
            pltpu.VMEM((rows, kv_width), bf16),
            turned,
            bias,
            pltpu.VMEM((far + 1, BLK, 2 * kv_width), bf16),
            pltpu.SMEM((pre,), jnp.int32),
            pltpu.SemaphoreType.DMA((4,)),
        ],
        cost_estimate=cost(1, 4),
        compiler_params=params,
        name="own_attention",
    )(lengths, block_slot, queries, new_keys, new_values)
    got = []
    for distance in range(hops + 1, pre):
        at = (distance - hops - 1) * per_peer
        pairs = [(i, (i + distance) % pre) for i in range(pre)]
        got.append(lax.ppermute(sent[at : at + per_peer], "pre", pairs))
    got = jnp.concatenate(got, axis=0)
    running[1], pk = lax.optimization_barrier((running[1], pk))
    running[2], pv = lax.optimization_barrier((running[2], pv))

    chain = [(new_keys, new_values), (pk, pv)]
    for hop in range(2, hops + 1):
        chain.append(tuple(lax.ppermute(piece, "pre", ring) for piece in chain[-1]))

    attended, *running = pl.pallas_call(
        prev_kernel,
        out_shape=(attended_shape,) + state,
        in_specs=[SMEM] + [VMEM] * 6,
        out_specs=(HBM,) + (VMEM,) * 3,
        scratch_shapes=[turned, bias, out_buf, pltpu.SemaphoreType.DMA((tiles,))],
        cost_estimate=cost(1, 5),
        compiler_params=params,
        name="prev_attention",
    )(lengths, queries, pk, pv, *running)

    flat = [piece for pair in chain[:-1] for piece in pair]
    cache = pl.pallas_call(
        functools.partial(place_kernel, pre, hops),
        out_shape=shape(open_cache, bf16),
        in_specs=[SMEM] + [VMEM] * (1 + len(flat)),
        out_specs=VMEM,
        cost_estimate=cost(0, 2),
        compiler_params=params,
        name="place_blocks",
    )(block_slot, got, *flat)
    for hop in range(2, hops + 1):
        last = hop == hops
        attended, *running = pl.pallas_call(
            functools.partial(far_kernel, hop, pre, last),
            out_shape=(attended_shape,) + ((cache_shape,) if last else state),
            in_specs=[SMEM, SMEM] + [VMEM] * 7 + [HBM],
            out_specs=(HBM,) + ((HBM,) if last else (VMEM,) * 3),
            scratch_shapes=([pltpu.VMEM(open_cache, bf16)] if last else [])
            + [turned, bias, out_buf, pltpu.SemaphoreType.DMA((tiles + 1,))],
            input_output_aliases={9: 0},
            cost_estimate=cost(0.25, 2),
            compiler_params=params,
            name="far_attention",
        )(lengths, block_slot, queries, *chain[hop], *running, cache, attended)
    return (attended, running[0])


def solution(mesh):
    placed = (
        P(("parts", "pre"), "tp"),
        P(("parts", "pre"), "tp"),
        P(("parts", "pre"), "tp"),
        P("parts"),
        P("parts"),
    )
    return jax.shard_map(
        on_device,
        mesh=mesh,
        in_specs=placed,
        out_specs=(P(("parts", "pre"), "tp"), P(("parts", "pre"), None, "tp")),
        check_vma=False,
    )
```

```python
import functools
import math

import jax
import jax.numpy as jnp
from jax import lax
from jax.experimental import pallas as pl
from jax.experimental.pallas import tpu as pltpu
from jax.sharding import PartitionSpec as P

HD = 128
BLK = 16
GROUP = 4
TILE = 256
ONES = 16
MASKED = -1e30
EXP_SCALE = math.log2(math.e) * HD ** (-0.5)

VMEM = pl.BlockSpec(memory_space=pltpu.VMEM)
SMEM = pl.BlockSpec(memory_space=pltpu.SMEM)
HBM = pl.BlockSpec(memory_space=pltpu.HBM)


def start_of(lengths_ref, position):
    end = jnp.int32(0)
    start = jnp.int32(0)
    for r in range(lengths_ref.shape[0]):
        end = end + lengths_ref[r]
        start = jnp.where(end <= position, end, start)
    return start


def row_starts(lengths_ref, positions):
    end = jnp.int32(0)
    starts = jnp.zeros_like(positions)
    for r in range(lengths_ref.shape[0]):
        end = end + lengths_ref[r]
        starts = jnp.where(positions >= end, end, starts)
    return starts


def fill_bias(bias_ref, lengths_ref, row_first, key_first, low, high, causal):
    shape = (high - low, TILE)
    positions = row_first + lax.broadcasted_iota(jnp.int32, (8, TILE), 1)
    starts = row_starts(lengths_ref, positions)
    keys = key_first + low + lax.broadcasted_iota(jnp.int32, shape, 0)
    keys = keys.reshape((high - low) // 8, 8, TILE)
    allowed = keys >= starts[None]
    if causal:
        allowed = allowed & (keys <= positions[None])
    bias_ref[low:high] = jnp.where(allowed, 0.0, MASKED).reshape(shape)


def turn_values(v_ref, turned):
    for g in range(turned.shape[0]):
        turned[g, :HD] = v_ref[:, g * HD : (g + 1) * HD].T
        turned[g, HD:] = jnp.ones((ONES, turned.shape[2]), turned.dtype)


def lanes_of(tile, j):
    return slice((tile * GROUP + j) * TILE, (tile * GROUP + j + 1) * TILE)


def weigh(q_ref, k_ref, bias_ref, old_top, tile, low, high, g, emit):
    keys = k_ref[low:high, g * HD : (g + 1) * HD]
    heads = range(g * GROUP, (g + 1) * GROUP)
    queries = jnp.concatenate(
        [q_ref[tile * TILE : (tile + 1) * TILE, h * HD : (h + 1) * HD] for h in heads], axis=0
    )
    all_scores = lax.dot_general(
        keys, queries, (((1,), (1,)), ((), ())), preferred_element_type=jnp.float32
    )
    for j in range(GROUP):
        scores = all_scores[:, j * TILE : (j + 1) * TILE] + bias_ref[low:high]
        scores = scores.reshape((high - low) // 8, 8, TILE)
        highest = jnp.max(jnp.max(scores, axis=0), axis=0, keepdims=True)
        top = jnp.broadcast_to(highest, (8, TILE))
        factor = None
        if old_top is not None:
            old = old_top[g, :, lanes_of(tile, j)]
            top = jnp.maximum(old, top)
            factor = jnp.exp2((old - top) * EXP_SCALE)
        weights = jnp.exp2((scores - top[None]) * EXP_SCALE)
        emit(j, weights.reshape(high - low, TILE).astype(jnp.bfloat16), top, factor)


def mix(values, weights, g, tile, old, emit):
    all_added = jnp.dot(values, weights, preferred_element_type=jnp.float32)
    for j in range(GROUP):
        at = lanes_of(tile, j)
        added = all_added[:, j * TILE : (j + 1) * TILE]
        value, total = added[:HD], added[HD : HD + 8]
        if old is not None:
            acc_ref, sum_ref, factor_ref = old
            factor = factor_ref[g, :, at]
            total = total + sum_ref[g, :, at] * factor
            kept = acc_ref[g, :, at].reshape(HD // 8, 8, TILE) * factor[None]
            value = value + kept.reshape(HD, TILE)
        emit(g, j, value, total)


def keep(state, tile):
    def emit(g, j, value, total):
        for ref, array in zip(state, (value, total)):
            ref[g, :, lanes_of(tile, j)] = array

    return emit


def finish(out_ref, row):
    def emit(g, j, value, total):
        head = g * GROUP + j
        value = value.reshape(HD // 8, 8, TILE) * (1.0 / total)[None]
        value = value.reshape(HD, TILE).astype(out_ref.dtype).T
        out_ref[row : row + TILE, head * HD : (head + 1) * HD] = value

    return emit


def block_of(k_ref, v_ref, row):
    parts = []
    for g in range(k_ref.shape[1] // HD):
        span = slice(g * HD, (g + 1) * HD)
        parts += [k_ref[pl.ds(row, BLK), span], v_ref[pl.ds(row, BLK), span]]
    return jnp.concatenate(parts, axis=1)


def own_slot(slot, me, blocks):
    local = slot - me * blocks
    return jnp.where((local >= 0) & (local < blocks), local, blocks)


def own_kernel(
    pre, hops, lengths_ref, slot_ref, q_hbm, k_hbm, v_hbm,
    acc_ref, sum_ref, top_ref, sent_hbm,
    q_ref, k_ref, v_ref, turned, bias, sent, counts, sems,
):
    rows = q_ref.shape[0]
    blocks = rows // BLK
    per_peer = blocks // pre
    spare = sent.shape[0] - 1
    me = lax.axis_index("pre")
    first = me * rows
    loads = [
        pltpu.make_async_copy(src, dst, sems.at[n])
        for n, (src, dst) in enumerate(((k_hbm, k_ref), (v_hbm, v_ref), (q_hbm, q_ref)))
    ]
    for load in loads:
        load.start()
    for owner in range(pre):
        counts[owner] = 0
    loads[0].wait()
    loads[1].wait()

    def step(b, _):
        owner = slot_ref[me * blocks + b] // blocks
        n = counts[owner]
        counts[owner] = n + 1
        distance = lax.rem(owner - me + pre, pre)
        at = jnp.where(distance > hops, (distance - hops - 1) * per_peer + n, spare)
        sent[at] = block_of(k_ref, v_ref, pl.multiple_of(b * BLK, BLK))
        return 0

    lax.fori_loop(0, blocks, step, 0, unroll=4)
    store = pltpu.make_async_copy(sent.at[0:spare], sent_hbm, sems.at[3])
    store.start()
    turn_values(v_ref, turned)
    loads[2].wait()
    for tile in range(rows // TILE):
        high = (tile + 1) * TILE
        fill_bias(bias, lengths_ref, first + tile * TILE, first, 0, high, True)
        for g in range(turned.shape[0]):
            all_weights = []

            def emit(j, weights, top, factor):
                all_weights.append(weights)
                top_ref[g, :, lanes_of(tile, j)] = top

            weigh(q_ref, k_ref, bias, None, tile, 0, high, g, emit)
            all_weights = jnp.concatenate(all_weights, axis=1)
            mix(turned[g, :, :high], all_weights, g, tile, None, keep((acc_ref, sum_ref), tile))
    store.wait()


def lowest_key(lengths_ref, hop, tile, rows):
    first = lax.axis_index("pre") * rows
    key_first = first - hop * rows
    low = jnp.maximum(start_of(lengths_ref, first + tile * TILE) - key_first, 0)
    return jnp.where(key_first >= 0, jnp.minimum(low, rows), rows)


def where_seen(low, rows, act):
    for at in range(0, rows, TILE):
        pl.when((low >= at) & (low < at + TILE))(functools.partial(act, at))


def scores_kernel(hop, lengths_ref, q_ref, k_ref, old_top, weights_ref, factor_ref, top_ref, bias):
    rows = q_ref.shape[0]
    first = lax.axis_index("pre") * rows
    for tile in range(rows // TILE):

        def act(at):
            fill_bias(
                bias, lengths_ref, first + tile * TILE, first - hop * rows, at, rows, False
            )
            for g in range(weights_ref.shape[1]):

                def emit(j, weights, top, factor):
                    weights_ref[tile, g, at:rows, j * TILE : (j + 1) * TILE] = weights
                    top_ref[g, :, lanes_of(tile, j)] = top
                    factor_ref[g, :, lanes_of(tile, j)] = factor

                weigh(q_ref, k_ref, bias, old_top, tile, at, rows, g, emit)

        where_seen(lowest_key(lengths_ref, hop, tile, rows), rows, act)


def values_kernel(
    hop, first_out, last, lengths_ref, v_ref, weights_ref, factor_ref, acc_in, sum_in, *refs
):
    refs = refs if first_out else refs[1:]
    out_hbm, *state, turned, out_buf, sems = refs
    rows = v_ref.shape[0]
    tiles = rows // TILE
    kv_count = turned.shape[0]
    lows = [lowest_key(lengths_ref, hop, tile, rows) for tile in range(tiles)]
    pl.when(lows[0] < rows)(functools.partial(turn_values, v_ref, turned))
    stores = []
    for tile, low in enumerate(lows):
        end_it = finish(out_buf, tile * TILE)

        def act(at):
            def emit(*result):
                if not last:
                    keep(state, tile)(*result)
                end_it(*result)

            for g in range(kv_count):
                weights = weights_ref[tile, g, at:rows]
                old = (acc_in, sum_in, factor_ref)
                mix(turned[g, :, at:rows], weights, g, tile, old, emit)

        where_seen(low, rows, act)
        span = slice(tile * TILE, (tile + 1) * TILE)
        store = pltpu.make_async_copy(out_buf.at[span], out_hbm.at[span], sems.at[tile])
        stores.append(store)
        if first_out:

            @pl.when(low == rows)
            def _():
                for g in range(kv_count):
                    for j in range(GROUP):
                        end_it(g, j, *(ref[g, :, lanes_of(tile, j)] for ref in (acc_in, sum_in)))

            store.start()
        else:
            pl.when(low < rows)(store.start)
    for low, store in zip(lows, stores):
        if first_out:
            store.wait()
        else:
            pl.when(low < rows)(store.wait)


def place_kernel(pre, hops, slot_ref, got_ref, *refs):
    near, cache_hbm, cache, sem = refs[:-3], *refs[-3:]
    blocks = near[0].shape[0] // BLK
    per_peer = blocks // pre
    me = lax.axis_index("pre")
    for back in range(hops + 1):
        k_ref, v_ref = near[2 * back], near[2 * back + 1]
        source = lax.rem(me - back + pre, pre)

        def near_step(b, _):
            at = own_slot(slot_ref[source * blocks + b], me, blocks)
            cache[at] = block_of(k_ref, v_ref, pl.multiple_of(b * BLK, BLK))
            return 0

        lax.fori_loop(0, blocks, near_step, 0, unroll=4)
    for distance in range(hops + 1, pre):
        source = lax.rem(me - distance + pre, pre)

        def far_step(b, n):
            at = own_slot(slot_ref[source * blocks + b], me, blocks)
            cache[at] = got_ref[(distance - hops - 1) * per_peer + jnp.minimum(n, per_peer - 1)]
            return n + jnp.where(at < blocks, 1, 0)

        lax.fori_loop(0, blocks, far_step, jnp.int32(0), unroll=4)
    store = pltpu.make_async_copy(cache.at[0:blocks], cache_hbm, sem)
    store.start()
    store.wait()


def on_device(queries, new_keys, new_values, lengths, block_slot):
    rows, q_width = queries.shape
    kv_width = new_keys.shape[1]
    kv_count = kv_width // HD
    blocks = rows // BLK
    pre = lax.axis_size("pre")
    per_peer = blocks // pre
    hops = pre // 2
    far = (pre - 1 - hops) * per_peer
    tiles = rows // TILE
    bf16, f32 = jnp.bfloat16, jnp.float32
    shape = jax.ShapeDtypeStruct
    params = pltpu.CompilerParams(vmem_limit_bytes=24 * 2**20)
    all_params = pltpu.CompilerParams(vmem_limit_bytes=56 * 2**20)
    ring = [(i, (i + 1) % pre) for i in range(pre)]
    acc_shape = shape((kv_count, HD, GROUP * rows), f32)
    stat_shape = shape((kv_count, 8, GROUP * rows), f32)
    weights_shape = shape((tiles, kv_count, rows, GROUP * TILE), bf16)
    attended_shape = shape(queries.shape, bf16)
    cache_shape = shape((blocks, BLK, 2 * kv_width), bf16)
    turned = pltpu.VMEM((kv_count, HD + ONES, rows), bf16)
    bias = pltpu.VMEM((rows, TILE), f32)

    def cost(share, moved):
        pairs = int(rows * rows * share)
        return pl.CostEstimate(
            flops=4 * pairs * q_width,
            bytes_accessed=moved * 2**20,
            transcendentals=pairs * kv_count * GROUP,
        )

    def after(array, *others):
        return lax.optimization_barrier((array, *others))[0]

    k, v = lax.ppermute(new_keys, "pre", ring), lax.ppermute(new_values, "pre", ring)

    acc, total, top, sent = pl.pallas_call(
        functools.partial(own_kernel, pre, hops),
        out_shape=(acc_shape, stat_shape, stat_shape, shape((far, BLK, 2 * kv_width), bf16)),
        in_specs=[SMEM, SMEM, HBM, HBM, HBM],
        out_specs=(VMEM,) * 3 + (HBM,),
        scratch_shapes=[
            pltpu.VMEM((rows, q_width), bf16),
            pltpu.VMEM((rows, kv_width), bf16),
            pltpu.VMEM((rows, kv_width), bf16),
            turned,
            bias,
            pltpu.VMEM((far + 1, BLK, 2 * kv_width), bf16),
            pltpu.SMEM((pre,), jnp.int32),
            pltpu.SemaphoreType.DMA((4,)),
        ],
        cost_estimate=cost(1, 4),
        compiler_params=all_params,
        name="own_attention",
    )(lengths, block_slot, queries, new_keys, new_values)

    k = after(k, top)
    chain = [new_keys, new_values]
    attended = None
    for hop in range(1, hops + 1):
        first_out, last = hop == 1, hop == hops
        next_k = None if last else lax.ppermute(k, "pre", ring)
        weights, factor, top = pl.pallas_call(
            functools.partial(scores_kernel, hop),
            out_shape=(weights_shape, stat_shape, stat_shape),
            in_specs=[SMEM] + [VMEM] * 3,
            out_specs=(VMEM,) * 3,
            scratch_shapes=[bias],
            cost_estimate=cost(0.5, 3),
            compiler_params=params,
            name="scores",
        )(lengths, queries, k, top)
        v = after(v, factor)
        chain += [k, v]
        next_v = None if last else lax.ppermute(v, "pre", ring)
        attended, *state = pl.pallas_call(
            functools.partial(values_kernel, hop, first_out, last),
            out_shape=(attended_shape,) + (() if last else (acc_shape, stat_shape)),
            in_specs=[SMEM] + [VMEM] * 5 + ([] if first_out else [HBM]),
            out_specs=(HBM,) + (() if last else (VMEM, VMEM)),
            scratch_shapes=[
                turned,
                pltpu.VMEM((rows, q_width), bf16),
                pltpu.SemaphoreType.DMA((tiles,)),
            ],
            input_output_aliases={} if first_out else {6: 0},
            cost_estimate=cost(0.5, 3),
            compiler_params=params,
            name="values",
        )(lengths, v, weights, factor, acc, total, *([] if first_out else [attended]))
        if first_out:
            sent = after(sent, state[1] if state else attended)
            got = []
            for distance in range(hops + 1, pre):
                at = (distance - hops - 1) * per_peer
                pairs = [(i, (i + distance) % pre) for i in range(pre)]
                got.append(lax.ppermute(sent[at : at + per_peer], "pre", pairs))
            got = jnp.concatenate(got, axis=0)
        if not last:
            acc, total = state
            k, v = after(next_k, total), next_v

    cache = pl.pallas_call(
        functools.partial(place_kernel, pre, hops),
        out_shape=cache_shape,
        in_specs=[SMEM] + [VMEM] * (1 + len(chain)),
        out_specs=HBM,
        scratch_shapes=[
            pltpu.VMEM((blocks + 1, BLK, 2 * kv_width), bf16),
            pltpu.SemaphoreType.DMA,
        ],
        cost_estimate=cost(0, 2),
        compiler_params=params,
        name="place_blocks",
    )(block_slot, got, *chain)
    return (attended, cache)


def solution(mesh):
    placed = (
        P(("parts", "pre"), "tp"),
        P(("parts", "pre"), "tp"),
        P(("parts", "pre"), "tp"),
        P("parts"),
        P("parts"),
    )
    return jax.shard_map(
        on_device,
        mesh=mesh,
        in_specs=placed,
        out_specs=(P(("parts", "pre"), "tp"), P(("parts", "pre"), None, "tp")),
        check_vma=False,
    )
```

```python
import functools
import math

import jax
import jax.numpy as jnp
from jax import lax
from jax.experimental import pallas as pl
from jax.experimental.pallas import tpu as pltpu
from jax.sharding import PartitionSpec as P

HD = 128
BLK = 16
GROUP = 4
TILE = 256
ONES = 16
MASKED = -1e30
EXP_SCALE = math.log2(math.e) * HD ** (-0.5)

VMEM = pl.BlockSpec(memory_space=pltpu.VMEM)
SMEM = pl.BlockSpec(memory_space=pltpu.SMEM)
HBM = pl.BlockSpec(memory_space=pltpu.HBM)


def start_of(lengths_ref, position):
    end = jnp.int32(0)
    start = jnp.int32(0)
    for r in range(lengths_ref.shape[0]):
        end = end + lengths_ref[r]
        start = jnp.where(end <= position, end, start)
    return start


def row_starts(lengths_ref, positions):
    end = jnp.int32(0)
    starts = jnp.zeros_like(positions)
    for r in range(lengths_ref.shape[0]):
        end = end + lengths_ref[r]
        starts = jnp.where(positions >= end, end, starts)
    return starts


def fill_bias(bias_ref, lengths_ref, row_first, key_first, low, high, causal):
    shape = (high - low, TILE)
    positions = row_first + lax.broadcasted_iota(jnp.int32, (8, TILE), 1)
    starts = row_starts(lengths_ref, positions)
    keys = key_first + low + lax.broadcasted_iota(jnp.int32, shape, 0)
    keys = keys.reshape((high - low) // 8, 8, TILE)
    allowed = keys >= starts[None]
    if causal:
        allowed = allowed & (keys <= positions[None])
    bias_ref[low:high] = jnp.where(allowed, 0.0, MASKED).reshape(shape)


def turn_values(v_ref, turned):
    for g in range(turned.shape[0]):
        turned[g, :HD] = v_ref[:, g * HD : (g + 1) * HD].T
        turned[g, HD:] = jnp.ones((ONES, turned.shape[2]), turned.dtype)


def lanes_of(tile, j):
    return slice((tile * GROUP + j) * TILE, (tile * GROUP + j + 1) * TILE)


def weigh(q_ref, k_ref, bias_ref, old_top, tile, low, high, g, emit):
    keys = k_ref[low:high, g * HD : (g + 1) * HD]
    heads = range(g * GROUP, (g + 1) * GROUP)
    queries = jnp.concatenate(
        [q_ref[tile * TILE : (tile + 1) * TILE, h * HD : (h + 1) * HD] for h in heads], axis=0
    )
    all_scores = lax.dot_general(
        keys, queries, (((1,), (1,)), ((), ())), preferred_element_type=jnp.float32
    )
    for j in range(GROUP):
        scores = all_scores[:, j * TILE : (j + 1) * TILE] + bias_ref[low:high]
        scores = scores.reshape((high - low) // 8, 8, TILE)
        highest = jnp.max(jnp.max(scores, axis=0), axis=0, keepdims=True)
        top = jnp.broadcast_to(highest, (8, TILE))
        factor = None
        if old_top is not None:
            old = old_top[g, :, lanes_of(tile, j)]
            top = jnp.maximum(old, top)
            factor = jnp.exp2((old - top) * EXP_SCALE)
        weights = jnp.exp2((scores - top[None]) * EXP_SCALE)
        emit(j, weights.reshape(high - low, TILE).astype(jnp.bfloat16), top, factor)


def mix(values, weights, g, tile, old, emit):
    all_added = jnp.dot(values, weights, preferred_element_type=jnp.float32)
    for j in range(GROUP):
        at = lanes_of(tile, j)
        added = all_added[:, j * TILE : (j + 1) * TILE]
        value, total = added[:HD], added[HD : HD + 8]
        if old is not None:
            acc_ref, sum_ref, factor_ref = old
            factor = factor_ref[g, :, at]
            total = total + sum_ref[g, :, at] * factor
            kept = acc_ref[g, :, at].reshape(HD // 8, 8, TILE) * factor[None]
            value = value + kept.reshape(HD, TILE)
        emit(g, j, value, total)


def keep(state, tile):
    def emit(g, j, value, total):
        for ref, array in zip(state, (value, total)):
            ref[g, :, lanes_of(tile, j)] = array

    return emit


def finish(out_ref, row):
    def emit(g, j, value, total):
        head = g * GROUP + j
        value = value.reshape(HD // 8, 8, TILE) * (1.0 / total)[None]
        value = value.reshape(HD, TILE).astype(out_ref.dtype).T
        out_ref[row : row + TILE, head * HD : (head + 1) * HD] = value

    return emit


def block_of(k_ref, v_ref, row):
    parts = []
    for g in range(k_ref.shape[1] // HD):
        span = slice(g * HD, (g + 1) * HD)
        parts += [k_ref[pl.ds(row, BLK), span], v_ref[pl.ds(row, BLK), span]]
    return jnp.concatenate(parts, axis=1)


def own_slot(slot, me, blocks):
    local = slot - me * blocks
    return jnp.where((local >= 0) & (local < blocks), local, blocks)


def own_kernel(
    pre, lengths_ref, slot_ref, q_ref, k_ref, v_ref, acc_ref, sum_ref, top_ref, *refs
):
    sent_hbm, (turned, bias, sent, counts, sems) = refs[:-5], refs[-5:]
    rows = q_ref.shape[0]
    blocks = rows // BLK
    per_peer = blocks // pre
    me = lax.axis_index("pre")
    first = me * rows
    for owner in range(pre):
        counts[owner] = 0

    def step(b, _):
        owner = slot_ref[me * blocks + b] // blocks
        n = counts[owner]
        counts[owner] = n + 1
        distance = lax.rem(owner - me + pre, pre)
        at = jnp.where(distance > 1, (distance - 2) * per_peer + n, (pre - 2) * per_peer)
        sent[at] = block_of(k_ref, v_ref, pl.multiple_of(b * BLK, BLK))
        return 0

    lax.fori_loop(0, blocks, step, 0, unroll=4)
    stores = [
        pltpu.make_async_copy(sent.at[n * per_peer : (n + 1) * per_peer], ref, sems.at[n])
        for n, ref in enumerate(sent_hbm)
    ]
    for store in stores:
        store.start()
    turn_values(v_ref, turned)
    for tile in range(rows // TILE):
        high = (tile + 1) * TILE
        fill_bias(bias, lengths_ref, first + tile * TILE, first, 0, high, True)
        for g in range(turned.shape[0]):
            all_weights = []

            def emit(j, weights, top, factor):
                all_weights.append(weights)
                top_ref[g, :, lanes_of(tile, j)] = top

            weigh(q_ref, k_ref, bias, None, tile, 0, high, g, emit)
            all_weights = jnp.concatenate(all_weights, axis=1)
            mix(turned[g, :, :high], all_weights, g, tile, None, keep((acc_ref, sum_ref), tile))
    for store in stores:
        store.wait()


def lowest_key(lengths_ref, hop, tile, rows):
    first = lax.axis_index("pre") * rows
    key_first = first - hop * rows
    low = jnp.maximum(start_of(lengths_ref, first + tile * TILE) - key_first, 0)
    return jnp.where(key_first >= 0, jnp.minimum(low, rows), rows)


def where_seen(low, rows, act):
    for at in range(0, rows, TILE):
        pl.when((low >= at) & (low < at + TILE))(functools.partial(act, at))


def scores_kernel(hop, lengths_ref, q_ref, k_ref, old_top, weights_ref, factor_ref, top_ref, bias):
    rows = q_ref.shape[0]
    first = lax.axis_index("pre") * rows
    for tile in range(rows // TILE):

        def act(at):
            fill_bias(
                bias, lengths_ref, first + tile * TILE, first - hop * rows, at, rows, False
            )
            for g in range(weights_ref.shape[1]):

                def emit(j, weights, top, factor):
                    weights_ref[tile, g, at:rows, j * TILE : (j + 1) * TILE] = weights
                    top_ref[g, :, lanes_of(tile, j)] = top
                    factor_ref[g, :, lanes_of(tile, j)] = factor

                weigh(q_ref, k_ref, bias, old_top, tile, at, rows, g, emit)

        where_seen(lowest_key(lengths_ref, hop, tile, rows), rows, act)


def values_kernel(
    hop, first_out, last, lengths_ref, v_ref, weights_ref, factor_ref, acc_in, sum_in, *refs
):
    refs = refs if first_out else refs[1:]
    out_hbm, *state, turned, out_buf, sems = refs
    rows = v_ref.shape[0]
    tiles = rows // TILE
    kv_count = turned.shape[0]
    lows = [lowest_key(lengths_ref, hop, tile, rows) for tile in range(tiles)]
    pl.when(lows[0] < rows)(functools.partial(turn_values, v_ref, turned))
    stores = []
    for tile, low in enumerate(lows):
        end_it = finish(out_buf, tile * TILE)

        def act(at):
            def emit(*result):
                if not last:
                    keep(state, tile)(*result)
                end_it(*result)

            for g in range(kv_count):
                weights = weights_ref[tile, g, at:rows]
                old = (acc_in, sum_in, factor_ref)
                mix(turned[g, :, at:rows], weights, g, tile, old, emit)

        where_seen(low, rows, act)
        span = slice(tile * TILE, (tile + 1) * TILE)
        store = pltpu.make_async_copy(out_buf.at[span], out_hbm.at[span], sems.at[tile])
        stores.append(store)
        if first_out:

            @pl.when(low == rows)
            def _():
                for g in range(kv_count):
                    for j in range(GROUP):
                        end_it(g, j, *(ref[g, :, lanes_of(tile, j)] for ref in (acc_in, sum_in)))

            store.start()
        else:
            pl.when(low < rows)(store.start)
    for low, store in zip(lows, stores):
        if first_out:
            store.wait()
        else:
            pl.when(low < rows)(store.wait)


def place_forwarded(cache, slot_ref, k_ref, v_ref, distance, pre, blocks):
    me = lax.axis_index("pre")
    source = lax.rem(me - distance + pre, pre)

    def step(b, _):
        at = own_slot(slot_ref[source * blocks + b], me, blocks)
        cache[at] = block_of(k_ref, v_ref, pl.multiple_of(b * BLK, BLK))
        return 0

    def run():
        lax.fori_loop(0, blocks, step, 0, unroll=4)

    if distance < 2:
        run()
    else:
        pl.when(me >= distance)(run)


def place_packed(cache, slot_ref, got_ref, distance, forwarded, pre, blocks):
    me = lax.axis_index("pre")
    source = lax.rem(me - distance + pre, pre)
    most = got_ref.shape[0] - 1

    def step(b, n):
        at = own_slot(slot_ref[source * blocks + b], me, blocks)
        cache[at] = got_ref[jnp.minimum(n, most)]
        return n + jnp.where(at < blocks, 1, 0)

    def run():
        lax.fori_loop(0, blocks, step, jnp.int32(0), unroll=4)

    if forwarded:
        pl.when(me < distance)(run)
    else:
        run()


def place_near_kernel(pre, slot_ref, k_ref, v_ref, pk_ref, pv_ref, cache_ref):
    blocks = k_ref.shape[0] // BLK
    place_forwarded(cache_ref, slot_ref, k_ref, v_ref, 0, pre, blocks)
    place_forwarded(cache_ref, slot_ref, pk_ref, pv_ref, 1, pre, blocks)


def place_far_kernel(pre, hops, slot_ref, cache_in, *refs):
    got, chain, (cache_hbm, cache, sem) = refs[: pre - 2], refs[pre - 2 : -3], refs[-3:]
    blocks = cache_hbm.shape[0]
    cache[...] = cache_in[...]
    for distance in range(2, pre):
        n = distance - 2
        if distance <= hops:
            k_ref, v_ref = chain[2 * n], chain[2 * n + 1]
            place_forwarded(cache, slot_ref, k_ref, v_ref, distance, pre, blocks)
        place_packed(cache, slot_ref, got[n], distance, distance <= hops, pre, blocks)
    store = pltpu.make_async_copy(cache.at[0:blocks], cache_hbm, sem)
    store.start()
    store.wait()


def on_device(queries, new_keys, new_values, lengths, block_slot):
    rows, q_width = queries.shape
    kv_width = new_keys.shape[1]
    kv_count = kv_width // HD
    blocks = rows // BLK
    pre = lax.axis_size("pre")
    per_peer = blocks // pre
    hops = pre // 2
    tiles = rows // TILE
    bf16, f32 = jnp.bfloat16, jnp.float32
    shape = jax.ShapeDtypeStruct
    params = pltpu.CompilerParams(vmem_limit_bytes=24 * 2**20)
    own_params = pltpu.CompilerParams(vmem_limit_bytes=44 * 2**20)
    ring = [(i, (i + 1) % pre) for i in range(pre)]
    acc_shape = shape((kv_count, HD, GROUP * rows), f32)
    stat_shape = shape((kv_count, 8, GROUP * rows), f32)
    weights_shape = shape((tiles, kv_count, rows, GROUP * TILE), bf16)
    attended_shape = shape(queries.shape, bf16)
    cache_shape = shape((blocks, BLK, 2 * kv_width), bf16)
    open_cache = shape((blocks + 1, BLK, 2 * kv_width), bf16)
    turned = pltpu.VMEM((kv_count, HD + ONES, rows), bf16)
    bias = pltpu.VMEM((rows, TILE), f32)

    def cost(share, moved):
        pairs = int(rows * rows * share)
        return pl.CostEstimate(
            flops=4 * pairs * q_width,
            bytes_accessed=moved * 2**20,
            transcendentals=pairs * kv_count * GROUP,
        )

    def after(array, *others):
        return lax.optimization_barrier((array, *others))[0]

    k, v = lax.ppermute(new_keys, "pre", ring), lax.ppermute(new_values, "pre", ring)

    packed = shape((per_peer, BLK, 2 * kv_width), bf16)
    acc, total, top, *sent = pl.pallas_call(
        functools.partial(own_kernel, pre),
        out_shape=(acc_shape, stat_shape, stat_shape) + (packed,) * (pre - 2),
        in_specs=[SMEM, SMEM] + [VMEM] * 3,
        out_specs=(VMEM,) * 3 + (HBM,) * (pre - 2),
        scratch_shapes=[
            turned,
            bias,
            pltpu.VMEM(((pre - 2) * per_peer + 1, BLK, 2 * kv_width), bf16),
            pltpu.SMEM((pre,), jnp.int32),
            pltpu.SemaphoreType.DMA((pre - 2,)),
        ],
        cost_estimate=cost(1, 4),
        compiler_params=own_params,
        name="own_attention",
    )(lengths, block_slot, queries, new_keys, new_values)
    got = [
        lax.ppermute(sent[d - 2], "pre", [(i, i + d - pre) for i in range(pre - d, pre)])
        for d in range(2, hops + 1)
    ]

    k = after(k, top)
    chain = [new_keys, new_values]
    attended = None
    for hop in range(1, hops + 1):
        first_out, last = hop == 1, hop == hops
        onward = [(i, i + 1) for i in range(hop, pre - 1)]
        next_k = None if last else lax.ppermute(k, "pre", onward)
        weights, factor, top = pl.pallas_call(
            functools.partial(scores_kernel, hop),
            out_shape=(weights_shape, stat_shape, stat_shape),
            in_specs=[SMEM] + [VMEM] * 3,
            out_specs=(VMEM,) * 3,
            scratch_shapes=[bias],
            cost_estimate=cost(0.5, 3),
            compiler_params=params,
            name="scores",
        )(lengths, queries, k, top)
        v = after(v, factor)
        chain += [k, v]
        next_v = None if last else lax.ppermute(v, "pre", onward)
        attended, *state = pl.pallas_call(
            functools.partial(values_kernel, hop, first_out, last),
            out_shape=(attended_shape,) + (() if last else (acc_shape, stat_shape)),
            in_specs=[SMEM] + [VMEM] * 5 + ([] if first_out else [HBM]),
            out_specs=(HBM,) + (() if last else (VMEM, VMEM)),
            scratch_shapes=[
                turned,
                pltpu.VMEM((rows, q_width), bf16),
                pltpu.SemaphoreType.DMA((tiles,)),
            ],
            input_output_aliases={} if first_out else {6: 0},
            cost_estimate=cost(0.5, 3),
            compiler_params=params,
            name="values",
        )(lengths, v, weights, factor, acc, total, *([] if first_out else [attended]))
        if first_out:
            for d in range(hops + 1, pre):
                pairs = [(i, (i + d) % pre) for i in range(pre)]
                got.append(lax.ppermute(after(sent[d - 2], state[1]), "pre", pairs))
            cache = pl.pallas_call(
                functools.partial(place_near_kernel, pre),
                out_shape=open_cache,
                in_specs=[SMEM] + [VMEM] * 4,
                out_specs=VMEM,
                cost_estimate=cost(0, 2),
                compiler_params=params,
                name="place_near",
            )(block_slot, *chain)
        if not last:
            acc, total = state
            k, v = after(next_k, total), next_v

    rest = got + chain[4:]
    cache = pl.pallas_call(
        functools.partial(place_far_kernel, pre, hops),
        out_shape=cache_shape,
        in_specs=[SMEM] + [VMEM] * (1 + len(rest)),
        out_specs=HBM,
        scratch_shapes=[pltpu.VMEM(open_cache.shape, bf16), pltpu.SemaphoreType.DMA],
        cost_estimate=cost(0, 2),
        compiler_params=params,
        name="place_far",
    )(block_slot, cache, *rest)
    return (attended, cache)


def solution(mesh):
    placed = (
        P(("parts", "pre"), "tp"),
        P(("parts", "pre"), "tp"),
        P(("parts", "pre"), "tp"),
        P("parts"),
        P("parts"),
    )
    return jax.shard_map(
        on_device,
        mesh=mesh,
        in_specs=placed,
        out_specs=(P(("parts", "pre"), "tp"), P(("parts", "pre"), None, "tp")),
        check_vma=False,
    )
```

```python
import functools
import math

import jax
import jax.numpy as jnp
from jax import lax
from jax.experimental import pallas as pl
from jax.experimental.pallas import tpu as pltpu
from jax.sharding import PartitionSpec as P

HD = 128
BLK = 16
GROUP = 4
TILE = 256
ONES = 16
MASKED = -1e30
EXP_SCALE = math.log2(math.e) * HD ** (-0.5)

VMEM = pl.BlockSpec(memory_space=pltpu.VMEM)
SMEM = pl.BlockSpec(memory_space=pltpu.SMEM)
HBM = pl.BlockSpec(memory_space=pltpu.HBM)


def start_of(lengths_ref, position):
    end = jnp.int32(0)
    start = jnp.int32(0)
    for r in range(lengths_ref.shape[0]):
        end = end + lengths_ref[r]
        start = jnp.where(end <= position, end, start)
    return start


def row_starts(lengths_ref, positions):
    end = jnp.int32(0)
    starts = jnp.zeros_like(positions)
    for r in range(lengths_ref.shape[0]):
        end = end + lengths_ref[r]
        starts = jnp.where(positions >= end, end, starts)
    return starts


def fill_bias(bias_ref, lengths_ref, row_first, key_first, low, high, causal):
    shape = (high - low, TILE)
    positions = row_first + lax.broadcasted_iota(jnp.int32, (8, TILE), 1)
    starts = row_starts(lengths_ref, positions)
    keys = key_first + low + lax.broadcasted_iota(jnp.int32, shape, 0)
    keys = keys.reshape((high - low) // 8, 8, TILE)
    allowed = keys >= starts[None]
    if causal:
        allowed = allowed & (keys <= positions[None])
    bias_ref[low:high] = jnp.where(allowed, 0.0, MASKED).reshape(shape)


def turn_values(v_ref, turned):
    for g in range(turned.shape[0]):
        turned[g, :HD] = v_ref[:, g * HD : (g + 1) * HD].T
        turned[g, HD:] = jnp.ones((ONES, turned.shape[2]), turned.dtype)


def lanes_of(tile, j):
    return slice((tile * GROUP + j) * TILE, (tile * GROUP + j + 1) * TILE)


def weigh(q_ref, k_ref, bias_ref, old_top, tile, low, high, g, emit):
    keys = k_ref[low:high, g * HD : (g + 1) * HD]
    heads = range(g * GROUP, (g + 1) * GROUP)
    queries = jnp.concatenate(
        [q_ref[tile * TILE : (tile + 1) * TILE, h * HD : (h + 1) * HD] for h in heads], axis=0
    )
    all_scores = lax.dot_general(
        keys, queries, (((1,), (1,)), ((), ())), preferred_element_type=jnp.float32
    )
    for j in range(GROUP):
        scores = all_scores[:, j * TILE : (j + 1) * TILE] + bias_ref[low:high]
        scores = scores.reshape((high - low) // 8, 8, TILE)
        highest = jnp.max(jnp.max(scores, axis=0), axis=0, keepdims=True)
        top = jnp.broadcast_to(highest, (8, TILE))
        factor = None
        if old_top is not None:
            old = old_top[g, :, lanes_of(tile, j)]
            top = jnp.maximum(old, top)
            factor = jnp.exp2((old - top) * EXP_SCALE)
        weights = jnp.exp2((scores - top[None]) * EXP_SCALE)
        emit(j, weights.reshape(high - low, TILE).astype(jnp.bfloat16), top, factor)


def mix(values, weights, g, tile, old, emit):
    all_added = jnp.dot(values, weights, preferred_element_type=jnp.float32)
    for j in range(GROUP):
        at = lanes_of(tile, j)
        added = all_added[:, j * TILE : (j + 1) * TILE]
        value, total = added[:HD], added[HD : HD + 8]
        if old is not None:
            acc_ref, sum_ref, factor_ref = old
            factor = factor_ref[g, :, at]
            total = total + sum_ref[g, :, at] * factor
            kept = acc_ref[g, :, at].reshape(HD // 8, 8, TILE) * factor[None]
            value = value + kept.reshape(HD, TILE)
        emit(g, j, value, total)


def keep(state, tile):
    def emit(g, j, value, total):
        for ref, array in zip(state, (value, total)):
            ref[g, :, lanes_of(tile, j)] = array

    return emit


def finish(out_ref, row):
    def emit(g, j, value, total):
        head = g * GROUP + j
        value = value.reshape(HD // 8, 8, TILE) * (1.0 / total)[None]
        value = value.reshape(HD, TILE).astype(out_ref.dtype).T
        out_ref[row : row + TILE, head * HD : (head + 1) * HD] = value

    return emit


def block_of(k_ref, v_ref, row):
    parts = []
    for g in range(k_ref.shape[1] // HD):
        span = slice(g * HD, (g + 1) * HD)
        parts += [k_ref[pl.ds(row, BLK), span], v_ref[pl.ds(row, BLK), span]]
    return jnp.concatenate(parts, axis=1)


def own_slot(slot, me, blocks):
    local = slot - me * blocks
    return jnp.where((local >= 0) & (local < blocks), local, blocks)


def own_kernel(
    pre, lengths_ref, slot_ref, q_hbm, k_hbm, v_hbm,
    q_ref, acc_ref, sum_ref, top_ref, cache_ref, *refs,
):
    sent_hbm, (k_ref, v_ref, turned, bias, sent, counts, sems, load_sems) = refs[:-8], refs[-8:]
    loads = [
        pltpu.make_async_copy(src, dst, load_sems.at[n])
        for n, (src, dst) in enumerate(((k_hbm, k_ref), (v_hbm, v_ref), (q_hbm, q_ref)))
    ]
    for load in loads:
        load.start()
    rows = q_ref.shape[0]
    blocks = rows // BLK
    per_peer = blocks // pre
    me = lax.axis_index("pre")
    first = me * rows
    for owner in range(pre):
        counts[owner] = 0
    loads[0].wait()
    loads[1].wait()

    def step(b, _):
        slot = slot_ref[me * blocks + b]
        owner = slot // blocks
        n = counts[owner]
        counts[owner] = n + 1
        distance = lax.rem(owner - me + pre, pre)
        at = jnp.where(distance > 1, (distance - 2) * per_peer + n, (pre - 2) * per_peer)
        block = block_of(k_ref, v_ref, pl.multiple_of(b * BLK, BLK))
        sent[at] = block
        cache_ref[own_slot(slot, me, blocks)] = block
        return 0

    lax.fori_loop(0, blocks, step, 0, unroll=4)
    stores = [
        pltpu.make_async_copy(sent.at[n * per_peer : (n + 1) * per_peer], ref, sems.at[n])
        for n, ref in enumerate(sent_hbm)
    ]
    for store in stores:
        store.start()
    turn_values(v_ref, turned)
    loads[2].wait()
    for tile in range(rows // TILE):
        high = (tile + 1) * TILE
        fill_bias(bias, lengths_ref, first + tile * TILE, first, 0, high, True)
        for g in range(turned.shape[0]):
            all_weights = []

            def emit(j, weights, top, factor):
                all_weights.append(weights)
                top_ref[g, :, lanes_of(tile, j)] = top

            weigh(q_ref, k_ref, bias, None, tile, 0, high, g, emit)
            all_weights = jnp.concatenate(all_weights, axis=1)
            mix(turned[g, :, :high], all_weights, g, tile, None, keep((acc_ref, sum_ref), tile))
    for store in stores:
        store.wait()


def lowest_key(lengths_ref, hop, tile, rows):
    first = lax.axis_index("pre") * rows
    key_first = first - hop * rows
    low = jnp.maximum(start_of(lengths_ref, first + tile * TILE) - key_first, 0)
    return jnp.where(key_first >= 0, jnp.minimum(low, rows), rows)


def where_seen(low, rows, act):
    for at in range(0, rows, TILE):
        pl.when((low >= at) & (low < at + TILE))(functools.partial(act, at))


def scores_kernel(hop, lengths_ref, q_ref, k_ref, old_top, weights_ref, factor_ref, *refs):
    *top_refs, bias = refs
    rows = q_ref.shape[0]
    first = lax.axis_index("pre") * rows
    for tile in range(rows // TILE):

        def act(at):
            fill_bias(
                bias, lengths_ref, first + tile * TILE, first - hop * rows, at, rows, False
            )
            for g in range(weights_ref.shape[1]):

                def emit(j, weights, top, factor):
                    weights_ref[tile, g, at:rows, j * TILE : (j + 1) * TILE] = weights
                    for top_ref in top_refs:
                        top_ref[g, :, lanes_of(tile, j)] = top
                    factor_ref[g, :, lanes_of(tile, j)] = factor

                weigh(q_ref, k_ref, bias, old_top, tile, at, rows, g, emit)

        where_seen(lowest_key(lengths_ref, hop, tile, rows), rows, act)


def values_kernel(
    hop, first_out, last, lengths_ref, v_ref, weights_ref, factor_ref, acc_in, sum_in, *refs
):
    refs = refs if first_out else refs[1:]
    out_hbm, *state, turned, out_buf, sems = refs
    rows = v_ref.shape[0]
    tiles = rows // TILE
    kv_count = turned.shape[0]
    lows = [lowest_key(lengths_ref, hop, tile, rows) for tile in range(tiles)]
    pl.when(lows[0] < rows)(functools.partial(turn_values, v_ref, turned))
    stores = []
    for tile, low in enumerate(lows):
        end_it = finish(out_buf, tile * TILE)

        def act(at):
            def emit(*result):
                if not last:
                    keep(state, tile)(*result)
                end_it(*result)

            for g in range(kv_count):
                weights = weights_ref[tile, g, at:rows]
                old = (acc_in, sum_in, factor_ref)
                mix(turned[g, :, at:rows], weights, g, tile, old, emit)

        where_seen(low, rows, act)
        span = slice(tile * TILE, (tile + 1) * TILE)
        store = pltpu.make_async_copy(out_buf.at[span], out_hbm.at[span], sems.at[tile])
        stores.append(store)
        if first_out:

            @pl.when(low == rows)
            def _():
                for g in range(kv_count):
                    for j in range(GROUP):
                        end_it(g, j, *(ref[g, :, lanes_of(tile, j)] for ref in (acc_in, sum_in)))

            store.start()
        else:
            pl.when(low < rows)(store.start)
    for low, store in zip(lows, stores):
        if first_out:
            store.wait()
        else:
            pl.when(low < rows)(store.wait)


def place_forwarded(cache, slot_ref, k_ref, v_ref, distance, pre, blocks):
    me = lax.axis_index("pre")
    source = lax.rem(me - distance + pre, pre)

    def step(b, _):
        at = own_slot(slot_ref[source * blocks + b], me, blocks)
        cache[at] = block_of(k_ref, v_ref, pl.multiple_of(b * BLK, BLK))
        return 0

    def run():
        lax.fori_loop(0, blocks, step, 0, unroll=4)

    if distance < 2:
        run()
    else:
        pl.when(me >= distance)(run)


def place_packed(cache, slot_ref, got_ref, distance, forwarded, pre, blocks):
    me = lax.axis_index("pre")
    source = lax.rem(me - distance + pre, pre)
    most = got_ref.shape[0] - 1

    def step(b, n):
        at = own_slot(slot_ref[source * blocks + b], me, blocks)
        cache[at] = got_ref[jnp.minimum(n, most)]
        return n + jnp.where(at < blocks, 1, 0)

    def run():
        lax.fori_loop(0, blocks, step, jnp.int32(0), unroll=4)

    if forwarded:
        pl.when(me < distance)(run)
    else:
        run()


def place_near_kernel(pre, slot_ref, cache_in, k_ref, v_ref, cache_ref):
    cache_ref[...] = cache_in[...]
    place_forwarded(cache_ref, slot_ref, k_ref, v_ref, 1, pre, k_ref.shape[0] // BLK)


def place_far_kernel(pre, hops, slot_ref, cache_in, *refs):
    got, chain, (cache_hbm, cache, sem) = refs[: pre - 2], refs[pre - 2 : -3], refs[-3:]
    blocks = cache_hbm.shape[0]
    cache[...] = cache_in[...]
    for distance in range(2, pre):
        n = distance - 2
        if distance <= hops:
            k_ref, v_ref = chain[2 * n], chain[2 * n + 1]
            place_forwarded(cache, slot_ref, k_ref, v_ref, distance, pre, blocks)
        place_packed(cache, slot_ref, got[n], distance, distance <= hops, pre, blocks)
    store = pltpu.make_async_copy(cache.at[0:blocks], cache_hbm, sem)
    store.start()
    store.wait()


def on_device(queries, new_keys, new_values, lengths, block_slot):
    rows, q_width = queries.shape
    kv_width = new_keys.shape[1]
    kv_count = kv_width // HD
    blocks = rows // BLK
    pre = lax.axis_size("pre")
    per_peer = blocks // pre
    hops = pre // 2
    tiles = rows // TILE
    bf16, f32 = jnp.bfloat16, jnp.float32
    shape = jax.ShapeDtypeStruct
    params = pltpu.CompilerParams(vmem_limit_bytes=24 * 2**20)
    own_params = pltpu.CompilerParams(vmem_limit_bytes=44 * 2**20)
    ring = [(i, (i + 1) % pre) for i in range(pre)]
    acc_shape = shape((kv_count, HD, GROUP * rows), f32)
    stat_shape = shape((kv_count, 8, GROUP * rows), f32)
    weights_shape = shape((tiles, kv_count, rows, GROUP * TILE), bf16)
    attended_shape = shape(queries.shape, bf16)
    cache_shape = shape((blocks, BLK, 2 * kv_width), bf16)
    open_cache = shape((blocks + 1, BLK, 2 * kv_width), bf16)
    turned = pltpu.VMEM((kv_count, HD + ONES, rows), bf16)
    bias = pltpu.VMEM((rows, TILE), f32)

    def cost(share, moved):
        pairs = int(rows * rows * share)
        return pl.CostEstimate(
            flops=4 * pairs * q_width,
            bytes_accessed=moved * 2**20,
            transcendentals=pairs * kv_count * GROUP,
        )

    def after(array, *others):
        return lax.optimization_barrier((array, *others))[0]

    k, v = lax.ppermute(new_keys, "pre", ring), lax.ppermute(new_values, "pre", ring)

    packed = shape((per_peer, BLK, 2 * kv_width), bf16)
    in_hbm = (
        pltpu.with_memory_space_constraint(x, pltpu.HBM) for x in (queries, new_keys, new_values)
    )
    q, acc, total, top, cache, *sent = pl.pallas_call(
        functools.partial(own_kernel, pre),
        out_shape=(attended_shape, acc_shape, stat_shape, stat_shape, open_cache)
        + (packed,) * (pre - 2),
        in_specs=[SMEM, SMEM] + [HBM] * 3,
        out_specs=(VMEM,) * 5 + (HBM,) * (pre - 2),
        scratch_shapes=[
            pltpu.VMEM((rows, kv_width), bf16),
            pltpu.VMEM((rows, kv_width), bf16),
            turned,
            bias,
            pltpu.VMEM(((pre - 2) * per_peer + 1, BLK, 2 * kv_width), bf16),
            pltpu.SMEM((pre,), jnp.int32),
            pltpu.SemaphoreType.DMA((pre - 2,)),
            pltpu.SemaphoreType.DMA((3,)),
        ],
        cost_estimate=cost(1, 4),
        compiler_params=own_params,
        name="own_attention",
    )(lengths, block_slot, *in_hbm)
    got = [
        lax.ppermute(sent[d - 2], "pre", [(i, i + d - pre) for i in range(pre - d, pre)])
        for d in range(2, hops + 1)
    ]

    k = after(k, top)
    chain = []
    attended = None
    for hop in range(1, hops + 1):
        first_out, last = hop == 1, hop == hops
        onward = [(i, i + 1) for i in range(hop, pre - 1)]
        next_k = None if last else lax.ppermute(k, "pre", onward)
        weights, factor, *tops = pl.pallas_call(
            functools.partial(scores_kernel, hop),
            out_shape=(weights_shape, stat_shape) + (() if last else (stat_shape,)),
            in_specs=[SMEM] + [VMEM] * 3,
            out_specs=(VMEM,) * (2 if last else 3),
            scratch_shapes=[bias],
            cost_estimate=cost(0.5, 3),
            compiler_params=params,
            name="scores",
        )(lengths, q, k, top)
        v = after(v, factor)
        if first_out and got:
            total, *got = lax.optimization_barrier((total, *got))
        chain += [k, v]
        next_v = None if last else lax.ppermute(v, "pre", onward)
        attended, *state = pl.pallas_call(
            functools.partial(values_kernel, hop, first_out, last),
            out_shape=(attended_shape,) + (() if last else (acc_shape, stat_shape)),
            in_specs=[SMEM] + [VMEM] * 5 + ([] if first_out else [HBM]),
            out_specs=(HBM,) + (() if last else (VMEM, VMEM)),
            scratch_shapes=[
                turned,
                pltpu.VMEM((rows, q_width), bf16),
                pltpu.SemaphoreType.DMA((tiles,)),
            ],
            input_output_aliases={} if first_out else {6: 0},
            cost_estimate=cost(0.5, 3),
            compiler_params=params,
            name="values",
        )(lengths, v, weights, factor, acc, total, *([] if first_out else [attended]))
        if first_out:
            for d in range(hops + 1, pre):
                pairs = [(i, (i + d) % pre) for i in range(pre)]
                got.append(lax.ppermute(after(sent[d - 2], state[1]), "pre", pairs))
            cache = pl.pallas_call(
                functools.partial(place_near_kernel, pre),
                out_shape=open_cache,
                in_specs=[SMEM] + [VMEM] * 3,
                out_specs=VMEM,
                cost_estimate=cost(0, 2),
                compiler_params=params,
                name="place_near",
            )(block_slot, cache, *chain)
        if not last:
            (top,) = tops
            acc, total = state
            k, v = after(next_k, total), next_v

    rest = got + chain[2:]
    cache = pl.pallas_call(
        functools.partial(place_far_kernel, pre, hops),
        out_shape=cache_shape,
        in_specs=[SMEM] + [VMEM] * (1 + len(rest)),
        out_specs=HBM,
        scratch_shapes=[pltpu.VMEM(open_cache.shape, bf16), pltpu.SemaphoreType.DMA],
        cost_estimate=cost(0, 2),
        compiler_params=params,
        name="place_far",
    )(block_slot, cache, *rest)
    return (attended, cache)


def solution(mesh):
    placed = (
        P(("parts", "pre"), "tp"),
        P(("parts", "pre"), "tp"),
        P(("parts", "pre"), "tp"),
        P("parts"),
        P("parts"),
    )
    return jax.shard_map(
        on_device,
        mesh=mesh,
        in_specs=placed,
        out_specs=(P(("parts", "pre"), "tp"), P(("parts", "pre"), None, "tp")),
        check_vma=False,
    )
```

```python
import functools
import math

import jax
import jax.numpy as jnp
from jax import lax
from jax.experimental import pallas as pl
from jax.experimental.pallas import tpu as pltpu
from jax.sharding import PartitionSpec as P

HD = 128
BLK = 16
GROUP = 4
TILE = 256
ONES = 16
MASKED = -1e30
EXP_SCALE = math.log2(math.e) * HD ** (-0.5)

VMEM = pl.BlockSpec(memory_space=pltpu.VMEM)
SMEM = pl.BlockSpec(memory_space=pltpu.SMEM)
HBM = pl.BlockSpec(memory_space=pltpu.HBM)


def start_of(lengths_ref, position):
    end = jnp.int32(0)
    start = jnp.int32(0)
    for r in range(lengths_ref.shape[0]):
        end = end + lengths_ref[r]
        start = jnp.where(end <= position, end, start)
    return start


def row_starts(lengths_ref, positions):
    end = jnp.int32(0)
    starts = jnp.zeros_like(positions)
    for r in range(lengths_ref.shape[0]):
        end = end + lengths_ref[r]
        starts = jnp.where(positions >= end, end, starts)
    return starts


def fill_bias(bias_ref, lengths_ref, row_first, key_first, low, high, causal):
    shape = (high - low, TILE)
    positions = row_first + lax.broadcasted_iota(jnp.int32, (8, TILE), 1)
    starts = row_starts(lengths_ref, positions)
    keys = key_first + low + lax.broadcasted_iota(jnp.int32, shape, 0)
    keys = keys.reshape((high - low) // 8, 8, TILE)
    allowed = keys >= starts[None]
    if causal:
        allowed = allowed & (keys <= positions[None])
    bias_ref[low:high] = jnp.where(allowed, 0.0, MASKED).reshape(shape)


def turn_values(v_ref, turned):
    for g in range(turned.shape[0]):
        turned[g, :HD] = v_ref[:, g * HD : (g + 1) * HD].T
        turned[g, HD:] = jnp.ones((ONES, turned.shape[2]), turned.dtype)


def lanes_of(tile, j):
    return slice((tile * GROUP + j) * TILE, (tile * GROUP + j + 1) * TILE)


def weigh(q_ref, k_ref, bias_ref, old_top, tile, low, high, g, emit):
    keys = k_ref[low:high, g * HD : (g + 1) * HD]
    heads = range(g * GROUP, (g + 1) * GROUP)
    queries = jnp.concatenate(
        [q_ref[tile * TILE : (tile + 1) * TILE, h * HD : (h + 1) * HD] for h in heads], axis=0
    )
    all_scores = lax.dot_general(
        keys, queries, (((1,), (1,)), ((), ())), preferred_element_type=jnp.float32
    )
    for j in range(GROUP):
        scores = all_scores[:, j * TILE : (j + 1) * TILE] + bias_ref[low:high]
        scores = scores.reshape((high - low) // 8, 8, TILE)
        highest = jnp.max(jnp.max(scores, axis=0), axis=0, keepdims=True)
        top = jnp.broadcast_to(highest, (8, TILE))
        factor = None
        if old_top is not None:
            old = old_top[g, :, lanes_of(tile, j)]
            top = jnp.maximum(old, top)
            factor = jnp.exp2((old - top) * EXP_SCALE)
        weights = jnp.exp2((scores - top[None]) * EXP_SCALE)
        emit(j, weights.reshape(high - low, TILE).astype(jnp.bfloat16), top, factor)


def mix(values, weights, g, tile, old, emit):
    all_added = jnp.dot(values, weights, preferred_element_type=jnp.float32)
    for j in range(GROUP):
        at = lanes_of(tile, j)
        added = all_added[:, j * TILE : (j + 1) * TILE]
        value, total = added[:HD], added[HD : HD + 8]
        if old is not None:
            acc_ref, sum_ref, factor_ref = old
            factor = factor_ref[g, :, at]
            total = total + sum_ref[g, :, at] * factor
            kept = acc_ref[g, :, at].reshape(HD // 8, 8, TILE) * factor[None]
            value = value + kept.reshape(HD, TILE)
        emit(g, j, value, total)


def keep(state, tile):
    def emit(g, j, value, total):
        for ref, array in zip(state, (value, total)):
            ref[g, :, lanes_of(tile, j)] = array

    return emit


def finish(out_ref, row):
    def emit(g, j, value, total):
        head = g * GROUP + j
        value = value.reshape(HD // 8, 8, TILE) * (1.0 / total)[None]
        value = value.reshape(HD, TILE).astype(out_ref.dtype).T
        out_ref[row : row + TILE, head * HD : (head + 1) * HD] = value

    return emit


def block_of(k_ref, v_ref, row):
    parts = []
    for g in range(k_ref.shape[1] // HD):
        span = slice(g * HD, (g + 1) * HD)
        parts += [k_ref[pl.ds(row, BLK), span], v_ref[pl.ds(row, BLK), span]]
    return jnp.concatenate(parts, axis=1)


def own_slot(slot, me, blocks):
    local = slot - me * blocks
    return jnp.where((local >= 0) & (local < blocks), local, blocks)


def own_kernel(
    pre, lengths_ref, slot_ref, q_hbm, k_hbm, v_hbm,
    q_ref, acc_ref, sum_ref, top_ref, cache_ref, *refs,
):
    sent_hbm, (k_ref, v_ref, turned, bias, sent, counts, sems, load_sems) = refs[:-8], refs[-8:]
    loads = [
        pltpu.make_async_copy(src, dst, load_sems.at[n])
        for n, (src, dst) in enumerate(((k_hbm, k_ref), (v_hbm, v_ref), (q_hbm, q_ref)))
    ]
    for load in loads:
        load.start()
    rows = q_ref.shape[0]
    blocks = rows // BLK
    per_peer = blocks // pre
    me = lax.axis_index("pre")
    first = me * rows
    for owner in range(pre):
        counts[owner] = 0
    loads[0].wait()
    loads[1].wait()

    def step(b, _):
        slot = slot_ref[me * blocks + b]
        owner = slot // blocks
        n = counts[owner]
        counts[owner] = n + 1
        distance = lax.rem(owner - me + pre, pre)
        at = jnp.where(distance > 1, (distance - 2) * per_peer + n, (pre - 2) * per_peer)
        block = block_of(k_ref, v_ref, pl.multiple_of(b * BLK, BLK))
        sent[at] = block
        cache_ref[own_slot(slot, me, blocks)] = block
        return 0

    lax.fori_loop(0, blocks, step, 0, unroll=8)
    stores = [
        pltpu.make_async_copy(sent.at[n * per_peer : (n + 1) * per_peer], ref, sems.at[n])
        for n, ref in enumerate(sent_hbm)
    ]
    for store in stores:
        store.start()
    turn_values(v_ref, turned)
    loads[2].wait()
    for tile in range(rows // TILE):
        high = (tile + 1) * TILE
        fill_bias(bias, lengths_ref, first + tile * TILE, first, 0, high, True)
        for g in range(turned.shape[0]):
            all_weights = []

            def emit(j, weights, top, factor):
                all_weights.append(weights)
                top_ref[g, :, lanes_of(tile, j)] = top

            weigh(q_ref, k_ref, bias, None, tile, 0, high, g, emit)
            all_weights = jnp.concatenate(all_weights, axis=1)
            mix(turned[g, :, :high], all_weights, g, tile, None, keep((acc_ref, sum_ref), tile))
    for store in stores:
        store.wait()


def lowest_key(lengths_ref, hop, tile, rows):
    first = lax.axis_index("pre") * rows
    key_first = first - hop * rows
    low = jnp.maximum(start_of(lengths_ref, first + tile * TILE) - key_first, 0)
    return jnp.where(key_first >= 0, jnp.minimum(low, rows), rows)


def where_seen(low, rows, act):
    for at in range(0, rows, TILE):
        pl.when((low >= at) & (low < at + TILE))(functools.partial(act, at))


def scores_kernel(hop, lengths_ref, q_ref, k_ref, old_top, weights_ref, factor_ref, *refs):
    *top_refs, bias = refs
    rows = q_ref.shape[0]
    first = lax.axis_index("pre") * rows
    for tile in range(rows // TILE):

        def act(at):
            fill_bias(
                bias, lengths_ref, first + tile * TILE, first - hop * rows, at, rows, False
            )
            for g in range(weights_ref.shape[1]):

                def emit(j, weights, top, factor):
                    weights_ref[tile, g, at:rows, j * TILE : (j + 1) * TILE] = weights
                    for top_ref in top_refs:
                        top_ref[g, :, lanes_of(tile, j)] = top
                    factor_ref[g, :, lanes_of(tile, j)] = factor

                weigh(q_ref, k_ref, bias, old_top, tile, at, rows, g, emit)

        where_seen(lowest_key(lengths_ref, hop, tile, rows), rows, act)


def values_kernel(
    hop, first_out, last, lengths_ref, v_ref, weights_ref, factor_ref, acc_in, sum_in, *refs
):
    refs = refs if first_out else refs[1:]
    out_hbm, *state, turned, out_buf, sems = refs
    rows = v_ref.shape[0]
    tiles = rows // TILE
    kv_count = turned.shape[0]
    lows = [lowest_key(lengths_ref, hop, tile, rows) for tile in range(tiles)]
    pl.when(lows[0] < rows)(functools.partial(turn_values, v_ref, turned))
    stores = []
    for tile, low in enumerate(lows):
        end_it = finish(out_buf, tile * TILE)

        def act(at):
            def emit(*result):
                if not last:
                    keep(state, tile)(*result)
                end_it(*result)

            for g in range(kv_count):
                weights = weights_ref[tile, g, at:rows]
                old = (acc_in, sum_in, factor_ref)
                mix(turned[g, :, at:rows], weights, g, tile, old, emit)

        where_seen(low, rows, act)
        span = slice(tile * TILE, (tile + 1) * TILE)
        store = pltpu.make_async_copy(out_buf.at[span], out_hbm.at[span], sems.at[tile])
        stores.append(store)
        if first_out:

            @pl.when(low == rows)
            def _():
                for g in range(kv_count):
                    for j in range(GROUP):
                        end_it(g, j, *(ref[g, :, lanes_of(tile, j)] for ref in (acc_in, sum_in)))

            store.start()
        else:
            pl.when(low < rows)(store.start)
    for low, store in zip(lows, stores):
        if first_out:
            store.wait()
        else:
            pl.when(low < rows)(store.wait)


def place_forwarded(cache, slot_ref, k_ref, v_ref, distance, pre, blocks):
    me = lax.axis_index("pre")
    source = lax.rem(me - distance + pre, pre)

    def step(b, _):
        at = own_slot(slot_ref[source * blocks + b], me, blocks)
        cache[at] = block_of(k_ref, v_ref, pl.multiple_of(b * BLK, BLK))
        return 0

    def run():
        lax.fori_loop(0, blocks, step, 0, unroll=8)

    if distance < 2:
        run()
    else:
        pl.when(me >= distance - 1)(run)


def place_packed(cache, slot_ref, got_ref, distance, forwarded, pre, blocks):
    me = lax.axis_index("pre")
    source = lax.rem(me - distance + pre, pre)
    most = got_ref.shape[0] - 1

    def step(b, n):
        at = own_slot(slot_ref[source * blocks + b], me, blocks)
        cache[at] = got_ref[jnp.minimum(n, most)]
        return n + jnp.where(at < blocks, 1, 0)

    def run():
        lax.fori_loop(0, blocks, step, jnp.int32(0), unroll=8)

    if forwarded:
        pl.when(me < distance - 1)(run)
    else:
        run()


def place_near_kernel(pre, slot_ref, cache_in, k_ref, v_ref, cache_ref):
    cache_ref[...] = cache_in[...]
    place_forwarded(cache_ref, slot_ref, k_ref, v_ref, 1, pre, k_ref.shape[0] // BLK)


def place_far_kernel(pre, hops, slot_ref, cache_in, *refs):
    got, chain, (cache_hbm, cache, sem) = refs[: pre - 2], refs[pre - 2 : -3], refs[-3:]
    blocks = cache_hbm.shape[0]
    cache[...] = cache_in[...]
    for distance in range(2, pre):
        n = distance - 2
        if distance <= hops:
            k_ref, v_ref = chain[2 * n], chain[2 * n + 1]
            place_forwarded(cache, slot_ref, k_ref, v_ref, distance, pre, blocks)
        place_packed(cache, slot_ref, got[n], distance, distance <= hops, pre, blocks)
    store = pltpu.make_async_copy(cache.at[0:blocks], cache_hbm, sem)
    store.start()
    store.wait()


def on_device(queries, new_keys, new_values, lengths, block_slot):
    rows, q_width = queries.shape
    kv_width = new_keys.shape[1]
    kv_count = kv_width // HD
    blocks = rows // BLK
    pre = lax.axis_size("pre")
    per_peer = blocks // pre
    hops = pre // 2
    tiles = rows // TILE
    bf16, f32 = jnp.bfloat16, jnp.float32
    shape = jax.ShapeDtypeStruct
    params = pltpu.CompilerParams(vmem_limit_bytes=24 * 2**20)
    own_params = pltpu.CompilerParams(vmem_limit_bytes=44 * 2**20)
    ring = [(i, (i + 1) % pre) for i in range(pre)]
    acc_shape = shape((kv_count, HD, GROUP * rows), f32)
    stat_shape = shape((kv_count, 8, GROUP * rows), f32)
    weights_shape = shape((tiles, kv_count, rows, GROUP * TILE), bf16)
    attended_shape = shape(queries.shape, bf16)
    cache_shape = shape((blocks, BLK, 2 * kv_width), bf16)
    open_cache = shape((blocks + 1, BLK, 2 * kv_width), bf16)
    turned = pltpu.VMEM((kv_count, HD + ONES, rows), bf16)
    bias = pltpu.VMEM((rows, TILE), f32)

    def cost(share, moved):
        pairs = int(rows * rows * share)
        return pl.CostEstimate(
            flops=4 * pairs * q_width,
            bytes_accessed=moved * 2**20,
            transcendentals=pairs * kv_count * GROUP,
        )

    def after(array, *others):
        return lax.optimization_barrier((array, *others))[0]

    k, v = lax.ppermute(new_keys, "pre", ring), lax.ppermute(new_values, "pre", ring)

    packed = shape((per_peer, BLK, 2 * kv_width), bf16)
    in_hbm = (
        pltpu.with_memory_space_constraint(x, pltpu.HBM) for x in (queries, new_keys, new_values)
    )
    q, acc, total, top, cache, *sent = pl.pallas_call(
        functools.partial(own_kernel, pre),
        out_shape=(attended_shape, acc_shape, stat_shape, stat_shape, open_cache)
        + (packed,) * (pre - 2),
        in_specs=[SMEM, SMEM] + [HBM] * 3,
        out_specs=(VMEM,) * 5 + (HBM,) * (pre - 2),
        scratch_shapes=[
            pltpu.VMEM((rows, kv_width), bf16),
            pltpu.VMEM((rows, kv_width), bf16),
            turned,
            bias,
            pltpu.VMEM(((pre - 2) * per_peer + 1, BLK, 2 * kv_width), bf16),
            pltpu.SMEM((pre,), jnp.int32),
            pltpu.SemaphoreType.DMA((pre - 2,)),
            pltpu.SemaphoreType.DMA((3,)),
        ],
        cost_estimate=cost(1, 4),
        compiler_params=own_params,
        name="own_attention",
    )(lengths, block_slot, *in_hbm)
    got = [
        lax.ppermute(sent[d - 2], "pre", [((i - d) % pre, i) for i in range(d - 1)])
        for d in range(2, hops + 1)
    ]

    k = after(k, top)
    chain = []
    attended = None
    for hop in range(1, hops + 1):
        first_out, last = hop == 1, hop == hops
        onward = [(i, i + 1) for i in range(hop - 1, pre - 1)]
        next_k = None if last else lax.ppermute(k, "pre", onward)
        weights, factor, *tops = pl.pallas_call(
            functools.partial(scores_kernel, hop),
            out_shape=(weights_shape, stat_shape) + (() if last else (stat_shape,)),
            in_specs=[SMEM] + [VMEM] * 3,
            out_specs=(VMEM,) * (2 if last else 3),
            scratch_shapes=[bias],
            cost_estimate=cost(0.5, 3),
            compiler_params=params,
            name="scores",
        )(lengths, q, k, top)
        v = after(v, factor)
        if last:
            for d in range(hops + 1, pre):
                pairs = [(i, (i + d) % pre) for i in range(pre)]
                got.append(lax.ppermute(after(sent[d - 2], factor), "pre", pairs))
        chain += [k, v]
        next_v = None if last else lax.ppermute(v, "pre", onward)
        attended, *state = pl.pallas_call(
            functools.partial(values_kernel, hop, first_out, last),
            out_shape=(attended_shape,) + (() if last else (acc_shape, stat_shape)),
            in_specs=[SMEM] + [VMEM] * 5 + ([] if first_out else [HBM]),
            out_specs=(HBM,) + (() if last else (VMEM, VMEM)),
            scratch_shapes=[
                turned,
                pltpu.VMEM((rows, q_width), bf16),
                pltpu.SemaphoreType.DMA((tiles,)),
            ],
            input_output_aliases={} if first_out else {6: 0},
            cost_estimate=cost(0.5, 3),
            compiler_params=params,
            name="values",
        )(lengths, v, weights, factor, acc, total, *([] if first_out else [attended]))
        if first_out:
            cache = pl.pallas_call(
                functools.partial(place_near_kernel, pre),
                out_shape=open_cache,
                in_specs=[SMEM] + [VMEM] * 3,
                out_specs=VMEM,
                cost_estimate=cost(0, 2),
                compiler_params=params,
                name="place_near",
            )(block_slot, cache, *chain)
        if not last:
            (top,) = tops
            acc, total = state
            k, v = after(next_k, total), next_v

    rest = got + chain[2:]
    cache = pl.pallas_call(
        functools.partial(place_far_kernel, pre, hops),
        out_shape=cache_shape,
        in_specs=[SMEM] + [VMEM] * (1 + len(rest)),
        out_specs=HBM,
        scratch_shapes=[pltpu.VMEM(open_cache.shape, bf16), pltpu.SemaphoreType.DMA],
        cost_estimate=cost(0, 2),
        compiler_params=params,
        name="place_far",
    )(block_slot, cache, *rest)
    return (attended, cache)


def solution(mesh):
    placed = (
        P(("parts", "pre"), "tp"),
        P(("parts", "pre"), "tp"),
        P(("parts", "pre"), "tp"),
        P("parts"),
        P("parts"),
    )
    return jax.shard_map(
        on_device,
        mesh=mesh,
        in_specs=placed,
        out_specs=(P(("parts", "pre"), "tp"), P(("parts", "pre"), None, "tp")),
        check_vma=False,
    )
```

```python
import functools
import math

import jax
import jax.numpy as jnp
from jax import lax
from jax.experimental import pallas as pl
from jax.experimental.pallas import tpu as pltpu
from jax.sharding import PartitionSpec as P

HD = 128
BLK = 16
GROUP = 4
TILE = 256
ONES = 16
MASKED = -1e30
EXP_SCALE = math.log2(math.e) * HD ** (-0.5)

VMEM = pl.BlockSpec(memory_space=pltpu.VMEM)
SMEM = pl.BlockSpec(memory_space=pltpu.SMEM)
HBM = pl.BlockSpec(memory_space=pltpu.HBM)


def start_of(lengths_ref, position):
    end = jnp.int32(0)
    start = jnp.int32(0)
    for r in range(lengths_ref.shape[0]):
        end = end + lengths_ref[r]
        start = jnp.where(end <= position, end, start)
    return start


def row_starts(lengths_ref, positions):
    end = jnp.int32(0)
    starts = jnp.zeros_like(positions)
    for r in range(lengths_ref.shape[0]):
        end = end + lengths_ref[r]
        starts = jnp.where(positions >= end, end, starts)
    return starts


def fill_bias(bias_ref, lengths_ref, row_first, key_first, low, high, causal):
    shape = (high - low, TILE)
    positions = row_first + lax.broadcasted_iota(jnp.int32, (8, TILE), 1)
    starts = row_starts(lengths_ref, positions)
    keys = key_first + low + lax.broadcasted_iota(jnp.int32, shape, 0)
    keys = keys.reshape((high - low) // 8, 8, TILE)
    allowed = keys >= starts[None]
    if causal:
        allowed = allowed & (keys <= positions[None])
    bias_ref[low:high] = jnp.where(allowed, 0.0, MASKED).reshape(shape)


def turn_values(v_ref, turned):
    for g in range(turned.shape[0]):
        turned[g, :HD] = v_ref[:, g * HD : (g + 1) * HD].T
        turned[g, HD:] = jnp.ones((ONES, turned.shape[2]), turned.dtype)


def lanes_of(tile, j):
    return slice((tile * GROUP + j) * TILE, (tile * GROUP + j + 1) * TILE)


def weigh(q_ref, k_ref, bias_ref, old_top, tile, low, high, g, emit):
    keys = k_ref[low:high, g * HD : (g + 1) * HD]
    heads = range(g * GROUP, (g + 1) * GROUP)
    queries = jnp.concatenate(
        [q_ref[tile * TILE : (tile + 1) * TILE, h * HD : (h + 1) * HD] for h in heads], axis=0
    )
    all_scores = lax.dot_general(
        keys, queries, (((1,), (1,)), ((), ())), preferred_element_type=jnp.float32
    )
    for j in range(GROUP):
        scores = all_scores[:, j * TILE : (j + 1) * TILE] + bias_ref[low:high]
        scores = scores.reshape((high - low) // 8, 8, TILE)
        highest = jnp.max(jnp.max(scores, axis=0), axis=0, keepdims=True)
        top = jnp.broadcast_to(highest, (8, TILE))
        factor = None
        if old_top is not None:
            old = old_top[g, :, lanes_of(tile, j)]
            top = jnp.maximum(old, top)
            factor = jnp.exp2((old - top) * EXP_SCALE)
        weights = jnp.exp2((scores - top[None]) * EXP_SCALE)
        emit(j, weights.reshape(high - low, TILE).astype(jnp.bfloat16), top, factor)


def mix(values, weights, g, tile, old, emit):
    all_added = jnp.dot(values, weights, preferred_element_type=jnp.float32)
    for j in range(GROUP):
        at = lanes_of(tile, j)
        added = all_added[:, j * TILE : (j + 1) * TILE]
        value, total = added[:HD], added[HD : HD + 8]
        if old is not None:
            acc_ref, sum_ref, factor_ref = old
            factor = factor_ref[g, :, at]
            total = total + sum_ref[g, :, at] * factor
            kept = acc_ref[g, :, at].reshape(HD // 8, 8, TILE) * factor[None]
            value = value + kept.reshape(HD, TILE)
        emit(g, j, value, total)


def keep(state, tile):
    def emit(g, j, value, total):
        for ref, array in zip(state, (value, total)):
            ref[g, :, lanes_of(tile, j)] = array

    return emit


def finish(out_ref, row):
    def emit(g, j, value, total):
        head = g * GROUP + j
        value = value.reshape(HD // 8, 8, TILE) * (1.0 / total)[None]
        value = value.reshape(HD, TILE).astype(out_ref.dtype).T
        out_ref[row : row + TILE, head * HD : (head + 1) * HD] = value

    return emit


def block_of(k_ref, v_ref, row):
    parts = []
    for g in range(k_ref.shape[1] // HD):
        span = slice(g * HD, (g + 1) * HD)
        parts += [k_ref[pl.ds(row, BLK), span], v_ref[pl.ds(row, BLK), span]]
    return jnp.concatenate(parts, axis=1)


def own_slot(slot, me, blocks):
    local = slot - me * blocks
    return jnp.where((local >= 0) & (local < blocks), local, blocks)


def own_kernel(
    pre, lengths_ref, slot_ref, q_hbm, k_hbm, v_hbm,
    q_ref, acc_ref, sum_ref, top_ref, cache_ref, *refs,
):
    sent_hbm, (k_ref, v_ref, turned, bias, sent, counts, sems, load_sems) = refs[:-8], refs[-8:]
    loads = [
        pltpu.make_async_copy(src, dst, load_sems.at[n])
        for n, (src, dst) in enumerate(((k_hbm, k_ref), (v_hbm, v_ref), (q_hbm, q_ref)))
    ]
    for load in loads:
        load.start()
    rows = q_ref.shape[0]
    blocks = rows // BLK
    per_peer = blocks // pre
    me = lax.axis_index("pre")
    first = me * rows
    for owner in range(pre):
        counts[owner] = 0
    loads[0].wait()
    loads[1].wait()

    def step(b, _):
        slot = slot_ref[me * blocks + b]
        owner = slot // blocks
        n = counts[owner]
        counts[owner] = n + 1
        distance = lax.rem(owner - me + pre, pre)
        at = jnp.where(distance > 1, (distance - 2) * per_peer + n, (pre - 2) * per_peer)
        block = block_of(k_ref, v_ref, pl.multiple_of(b * BLK, BLK))
        sent[at] = block
        cache_ref[own_slot(slot, me, blocks)] = block
        return 0

    lax.fori_loop(0, blocks, step, 0, unroll=8)
    stores = [
        pltpu.make_async_copy(sent.at[n * per_peer : (n + 1) * per_peer], ref, sems.at[n])
        for n, ref in enumerate(sent_hbm)
    ]
    for store in stores:
        store.start()
    turn_values(v_ref, turned)
    loads[2].wait()
    for tile in range(rows // TILE):
        high = (tile + 1) * TILE
        fill_bias(bias, lengths_ref, first + tile * TILE, first, 0, high, True)
        for g in range(turned.shape[0]):
            all_weights = []

            def emit(j, weights, top, factor):
                all_weights.append(weights)
                top_ref[g, :, lanes_of(tile, j)] = top

            weigh(q_ref, k_ref, bias, None, tile, 0, high, g, emit)
            all_weights = jnp.concatenate(all_weights, axis=1)
            mix(turned[g, :, :high], all_weights, g, tile, None, keep((acc_ref, sum_ref), tile))
    for store in stores:
        store.wait()


def lowest_key(lengths_ref, hop, tile, rows):
    first = lax.axis_index("pre") * rows
    key_first = first - hop * rows
    low = jnp.maximum(start_of(lengths_ref, first + tile * TILE) - key_first, 0)
    return jnp.where(key_first >= 0, jnp.minimum(low, rows), rows)


def where_seen(low, rows, act):
    for at in range(0, rows, TILE):
        pl.when((low >= at) & (low < at + TILE))(functools.partial(act, at))


def scores_kernel(hop, lengths_ref, q_ref, k_ref, old_top, weights_ref, factor_ref, *refs):
    *top_refs, bias = refs
    rows = q_ref.shape[0]
    first = lax.axis_index("pre") * rows
    for tile in range(rows // TILE):

        def act(at):
            fill_bias(
                bias, lengths_ref, first + tile * TILE, first - hop * rows, at, rows, False
            )
            for g in range(weights_ref.shape[1]):

                def emit(j, weights, top, factor):
                    weights_ref[tile, g, at:rows, j * TILE : (j + 1) * TILE] = weights
                    for top_ref in top_refs:
                        top_ref[g, :, lanes_of(tile, j)] = top
                    factor_ref[g, :, lanes_of(tile, j)] = factor

                weigh(q_ref, k_ref, bias, old_top, tile, at, rows, g, emit)

        where_seen(lowest_key(lengths_ref, hop, tile, rows), rows, act)


def place_forwarded(cache, slot_ref, k_ref, v_ref, distance, pre, blocks):
    me = lax.axis_index("pre")
    source = lax.rem(me - distance + pre, pre)

    def step(b, _):
        at = own_slot(slot_ref[source * blocks + b], me, blocks)
        cache[at] = block_of(k_ref, v_ref, pl.multiple_of(b * BLK, BLK))
        return 0

    def run():
        lax.fori_loop(0, blocks, step, 0, unroll=8)

    if distance < 2:
        run()
    else:
        pl.when(me >= distance - 1)(run)


def place_packed(cache, slot_ref, got_ref, distance, pre, blocks):
    me = lax.axis_index("pre")
    source = lax.rem(me - distance + pre, pre)
    most = got_ref.shape[0] - 1

    def step(b, n):
        at = own_slot(slot_ref[source * blocks + b], me, blocks)
        cache[at] = got_ref[jnp.minimum(n, most)]
        return n + jnp.where(at < blocks, 1, 0)

    @pl.when(me < distance - 1)
    def _():
        lax.fori_loop(0, blocks, step, jnp.int32(0), unroll=8)


def list_places(places_ref, slot_ref, hops, pre, blocks):
    me = lax.axis_index("pre")
    per_peer = blocks // pre
    for distance in range(hops + 1, pre):
        source = lax.rem(me - distance + pre, pre)
        base = (distance - hops - 1) * (per_peer + 1)

        def step(b, n):
            at = own_slot(slot_ref[source * blocks + b], me, blocks)
            places_ref[base + n] = at
            return n + jnp.where(at < blocks, 1, 0)

        lax.fori_loop(0, blocks, step, jnp.int32(0), unroll=8)


def values_kernel(
    hop, hops, pre, lengths_ref, slot_ref, v_ref, k_ref, weights_ref, factor_ref,
    acc_in, sum_in, cache_in, *refs,
):
    first_out, last = hop == 1, hop == hops
    refs = list(refs)
    if not first_out:
        got_ref, _ = refs.pop(0), refs.pop(0)
    out_hbm, cache_out = refs.pop(0), refs.pop(0)
    state = () if last else (refs.pop(0), refs.pop(0))
    places_ref = refs.pop(0) if first_out else None
    turned, out_buf, sems, *rest = refs
    rows = v_ref.shape[0]
    blocks = rows // BLK
    tiles = rows // TILE
    kv_count = turned.shape[0]

    cache = rest[0] if last else cache_out
    cache[...] = cache_in[...]
    place_forwarded(cache, slot_ref, k_ref, v_ref, hop, pre, blocks)
    if first_out:
        list_places(places_ref, slot_ref, hops, pre, blocks)
    else:
        place_packed(cache, slot_ref, got_ref, hop, pre, blocks)
    if last:
        cache_store = pltpu.make_async_copy(cache.at[0:blocks], cache_out, sems.at[tiles])
        cache_store.start()

    lows = [lowest_key(lengths_ref, hop, tile, rows) for tile in range(tiles)]
    pl.when(lows[0] < rows)(functools.partial(turn_values, v_ref, turned))
    stores = []
    for tile, low in enumerate(lows):
        end_it = finish(out_buf, tile * TILE)

        def act(at):
            def emit(*result):
                if not last:
                    keep(state, tile)(*result)
                end_it(*result)

            for g in range(kv_count):
                weights = weights_ref[tile, g, at:rows]
                old = (acc_in, sum_in, factor_ref)
                mix(turned[g, :, at:rows], weights, g, tile, old, emit)

        where_seen(low, rows, act)
        span = slice(tile * TILE, (tile + 1) * TILE)
        store = pltpu.make_async_copy(out_buf.at[span], out_hbm.at[span], sems.at[tile])
        stores.append(store)
        if first_out:

            @pl.when(low == rows)
            def _():
                for g in range(kv_count):
                    for j in range(GROUP):
                        end_it(g, j, *(ref[g, :, lanes_of(tile, j)] for ref in (acc_in, sum_in)))

            store.start()
        else:
            pl.when(low < rows)(store.start)
    for low, store in zip(lows, stores):
        if first_out:
            store.wait()
        else:
            pl.when(low < rows)(store.wait)
    if last:
        cache_store.wait()


def place_last_kernel(places_ref, cache_in, *refs):
    *got, cache_hbm, sems = refs
    per_peer = got[0].shape[0]
    copies = []
    for i, got_ref in enumerate(got):
        for n in range(per_peer):
            at = places_ref[i * (per_peer + 1) + n]
            copy = pltpu.make_async_copy(
                got_ref.at[n], cache_hbm.at[at], sems.at[i * per_peer + n]
            )
            copy.start()
            copies.append(copy)
    for copy in copies:
        copy.wait()


def on_device(queries, new_keys, new_values, lengths, block_slot):
    rows, q_width = queries.shape
    kv_width = new_keys.shape[1]
    kv_count = kv_width // HD
    blocks = rows // BLK
    pre = lax.axis_size("pre")
    per_peer = blocks // pre
    hops = pre // 2
    tiles = rows // TILE
    bf16, f32 = jnp.bfloat16, jnp.float32
    shape = jax.ShapeDtypeStruct
    params = pltpu.CompilerParams(vmem_limit_bytes=24 * 2**20)
    own_params = pltpu.CompilerParams(vmem_limit_bytes=44 * 2**20)
    ring = [(i, (i + 1) % pre) for i in range(pre)]
    acc_shape = shape((kv_count, HD, GROUP * rows), f32)
    stat_shape = shape((kv_count, 8, GROUP * rows), f32)
    weights_shape = shape((tiles, kv_count, rows, GROUP * TILE), bf16)
    attended_shape = shape(queries.shape, bf16)
    cache_shape = shape((blocks, BLK, 2 * kv_width), bf16)
    open_cache = shape((blocks + 1, BLK, 2 * kv_width), bf16)
    turned = pltpu.VMEM((kv_count, HD + ONES, rows), bf16)
    bias = pltpu.VMEM((rows, TILE), f32)

    def cost(share, moved):
        pairs = int(rows * rows * share)
        return pl.CostEstimate(
            flops=4 * pairs * q_width,
            bytes_accessed=moved * 2**20,
            transcendentals=pairs * kv_count * GROUP,
        )

    def after(array, *others):
        return lax.optimization_barrier((array, *others))[0]

    k, v = lax.ppermute(new_keys, "pre", ring), lax.ppermute(new_values, "pre", ring)

    packed = shape((per_peer, BLK, 2 * kv_width), bf16)
    in_hbm = (
        pltpu.with_memory_space_constraint(x, pltpu.HBM) for x in (queries, new_keys, new_values)
    )
    q, acc, total, top, cache, *sent = pl.pallas_call(
        functools.partial(own_kernel, pre),
        out_shape=(attended_shape, acc_shape, stat_shape, stat_shape, open_cache)
        + (packed,) * (pre - 2),
        in_specs=[SMEM, SMEM] + [HBM] * 3,
        out_specs=(VMEM,) * 5 + (HBM,) * (pre - 2),
        scratch_shapes=[
            pltpu.VMEM((rows, kv_width), bf16),
            pltpu.VMEM((rows, kv_width), bf16),
            turned,
            bias,
            pltpu.VMEM(((pre - 2) * per_peer + 1, BLK, 2 * kv_width), bf16),
            pltpu.SMEM((pre,), jnp.int32),
            pltpu.SemaphoreType.DMA((pre - 2,)),
            pltpu.SemaphoreType.DMA((3,)),
        ],
        cost_estimate=cost(1, 4),
        compiler_params=own_params,
        name="own_attention",
    )(lengths, block_slot, *in_hbm)
    got = [
        lax.ppermute(sent[d - 2], "pre", [((i - d) % pre, i) for i in range(d - 1)])
        for d in range(2, hops + 1)
    ]

    k = after(k, top)
    attended = None
    for hop in range(1, hops + 1):
        first_out, last = hop == 1, hop == hops
        onward = [(i, i + 1) for i in range(hop - 1, pre - 1)]
        next_k = None if last else lax.ppermute(k, "pre", onward)
        weights, factor, *tops = pl.pallas_call(
            functools.partial(scores_kernel, hop),
            out_shape=(weights_shape, stat_shape) + (() if last else (stat_shape,)),
            in_specs=[SMEM] + [VMEM] * 3,
            out_specs=(VMEM,) * (2 if last else 3),
            scratch_shapes=[bias],
            cost_estimate=cost(0.5, 3),
            compiler_params=params,
            name="scores",
        )(lengths, q, k, top)
        v = after(v, factor)
        if last:
            for d in range(hops + 1, pre):
                pairs = [(i, (i + d) % pre) for i in range(pre)]
                got.append(lax.ppermute(after(sent[d - 2], factor), "pre", pairs))
        next_v = None if last else lax.ppermute(v, "pre", onward)
        places = shape(((pre - 1 - hops) * (per_peer + 1),), jnp.int32)
        carry = () if last else (acc_shape, stat_shape)
        extra = [] if first_out else [got[hop - 2], attended]
        attended, cache, *state = pl.pallas_call(
            functools.partial(values_kernel, hop, hops, pre),
            out_shape=(attended_shape, cache_shape if last else open_cache)
            + carry
            + ((places,) if first_out else ()),
            in_specs=[SMEM, SMEM] + [VMEM] * 7 + ([] if first_out else [VMEM, HBM]),
            out_specs=(HBM, HBM if last else VMEM)
            + (VMEM,) * len(carry)
            + ((SMEM,) if first_out else ()),
            scratch_shapes=[
                turned,
                pltpu.VMEM((rows, q_width), bf16),
                pltpu.SemaphoreType.DMA((tiles + 1,)),
            ]
            + ([pltpu.VMEM(open_cache.shape, bf16)] if last else []),
            input_output_aliases={} if first_out else {10: 0},
            cost_estimate=cost(0.5, 3),
            compiler_params=params,
            name="values",
        )(lengths, block_slot, v, k, weights, factor, acc, total, cache, *extra)
        if first_out:
            far_places = state.pop()
        if not last:
            (top,) = tops
            acc, total = state
            k, v = after(next_k, total), next_v

    cache = pl.pallas_call(
        place_last_kernel,
        out_shape=cache_shape,
        in_specs=[SMEM, HBM] + [VMEM] * (pre - 1 - hops),
        out_specs=HBM,
        scratch_shapes=[pltpu.SemaphoreType.DMA(((pre - 1 - hops) * per_peer,))],
        input_output_aliases={1: 0},
        cost_estimate=cost(0, 1),
        compiler_params=params,
        name="place_last",
    )(far_places, cache, *got[hops - 1 :])
    return (attended, cache)


def solution(mesh):
    placed = (
        P(("parts", "pre"), "tp"),
        P(("parts", "pre"), "tp"),
        P(("parts", "pre"), "tp"),
        P("parts"),
        P("parts"),
    )
    return jax.shard_map(
        on_device,
        mesh=mesh,
        in_specs=placed,
        out_specs=(P(("parts", "pre"), "tp"), P(("parts", "pre"), None, "tp")),
        check_vma=False,
    )
```

```python
import functools
import math

import jax
import jax.numpy as jnp
from jax import lax
from jax.experimental import pallas as pl
from jax.experimental.pallas import tpu as pltpu
from jax.sharding import PartitionSpec as P

HD = 128
BLK = 16
GROUP = 4
TILE = 256
ONES = 16
MASKED = -1e30
EXP_SCALE = math.log2(math.e) * HD ** (-0.5)

VMEM = pl.BlockSpec(memory_space=pltpu.VMEM)
SMEM = pl.BlockSpec(memory_space=pltpu.SMEM)
HBM = pl.BlockSpec(memory_space=pltpu.HBM)


def start_of(lengths_ref, position):
    end = jnp.int32(0)
    start = jnp.int32(0)
    for r in range(lengths_ref.shape[0]):
        end = end + lengths_ref[r]
        start = jnp.where(end <= position, end, start)
    return start


def row_starts(lengths_ref, positions):
    end = jnp.int32(0)
    starts = jnp.zeros_like(positions)
    for r in range(lengths_ref.shape[0]):
        end = end + lengths_ref[r]
        starts = jnp.where(positions >= end, end, starts)
    return starts


def fill_bias(bias_ref, lengths_ref, row_first, key_first, low, high, causal):
    shape = (high - low, TILE)
    positions = row_first + lax.broadcasted_iota(jnp.int32, (8, TILE), 1)
    starts = row_starts(lengths_ref, positions)
    keys = key_first + low + lax.broadcasted_iota(jnp.int32, shape, 0)
    keys = keys.reshape((high - low) // 8, 8, TILE)
    allowed = keys >= starts[None]
    if causal:
        allowed = allowed & (keys <= positions[None])
    bias_ref[low:high] = jnp.where(allowed, 0.0, MASKED).reshape(shape)


def turn_values(v_ref, turned):
    for g in range(turned.shape[0]):
        turned[g, :HD] = v_ref[:, g * HD : (g + 1) * HD].T
        turned[g, HD:] = jnp.ones((ONES, turned.shape[2]), turned.dtype)


def lanes_of(tile, j):
    return slice((tile * GROUP + j) * TILE, (tile * GROUP + j + 1) * TILE)


def weigh(q_ref, k_ref, bias_ref, old_top, tile, low, high, g, emit):
    keys = k_ref[low:high, g * HD : (g + 1) * HD]
    heads = range(g * GROUP, (g + 1) * GROUP)
    queries = jnp.concatenate(
        [q_ref[tile * TILE : (tile + 1) * TILE, h * HD : (h + 1) * HD] for h in heads], axis=0
    )
    all_scores = lax.dot_general(
        keys, queries, (((1,), (1,)), ((), ())), preferred_element_type=jnp.float32
    )
    for j in range(GROUP):
        scores = all_scores[:, j * TILE : (j + 1) * TILE] + bias_ref[low:high]
        scores = scores.reshape((high - low) // 8, 8, TILE)
        highest = jnp.max(jnp.max(scores, axis=0), axis=0, keepdims=True)
        top = jnp.broadcast_to(highest, (8, TILE))
        factor = None
        if old_top is not None:
            old = old_top[g, :, lanes_of(tile, j)]
            top = jnp.maximum(old, top)
            factor = jnp.exp2((old - top) * EXP_SCALE)
        weights = jnp.exp2((scores - top[None]) * EXP_SCALE)
        emit(j, weights.reshape(high - low, TILE).astype(jnp.bfloat16), top, factor)


def mix(values, weights, g, tile, old, emit):
    all_added = jnp.dot(values, weights, preferred_element_type=jnp.float32)
    for j in range(GROUP):
        at = lanes_of(tile, j)
        added = all_added[:, j * TILE : (j + 1) * TILE]
        value, total = added[:HD], added[HD : HD + 8]
        if old is not None:
            acc_ref, sum_ref, factor_ref = old
            factor = factor_ref[g, :, at]
            total = total + sum_ref[g, :, at] * factor
            kept = acc_ref[g, :, at].reshape(HD // 8, 8, TILE) * factor[None]
            value = value + kept.reshape(HD, TILE)
        emit(g, j, value, total)


def keep(state, tile):
    def emit(g, j, value, total):
        for ref, array in zip(state, (value, total)):
            ref[g, :, lanes_of(tile, j)] = array

    return emit


def finish(out_ref, row):
    def emit(g, j, value, total):
        head = g * GROUP + j
        value = value.reshape(HD // 8, 8, TILE) * (1.0 / total)[None]
        value = value.reshape(HD, TILE).astype(out_ref.dtype).T
        out_ref[row : row + TILE, head * HD : (head + 1) * HD] = value

    return emit


def block_of(k_ref, v_ref, row):
    parts = []
    for g in range(k_ref.shape[1] // HD):
        span = slice(g * HD, (g + 1) * HD)
        parts += [k_ref[pl.ds(row, BLK), span], v_ref[pl.ds(row, BLK), span]]
    return jnp.concatenate(parts, axis=1)


def own_slot(slot, me, blocks):
    local = slot - me * blocks
    return jnp.where((local >= 0) & (local < blocks), local, blocks)


def own_kernel(
    pre, hops, lengths_ref, slot_ref, q_hbm, k_hbm, v_hbm,
    q_ref, acc_ref, sum_ref, top_ref, cache_ref, *refs,
):
    sent_hbm, (k_ref, v_ref, turned, bias, sent, counts, sems, load_sems) = refs[:-8], refs[-8:]
    loads = [
        pltpu.make_async_copy(src, dst, load_sems.at[n])
        for n, (src, dst) in enumerate(((k_hbm, k_ref), (v_hbm, v_ref), (q_hbm, q_ref)))
    ]
    for load in loads:
        load.start()
    rows = q_ref.shape[0]
    blocks = rows // BLK
    per_peer = blocks // pre
    me = lax.axis_index("pre")
    first = me * rows
    for owner in range(pre):
        counts[owner] = 0
    loads[0].wait()
    loads[1].wait()

    def step(b, _):
        slot = slot_ref[me * blocks + b]
        owner = slot // blocks
        n = counts[owner]
        counts[owner] = n + 1
        distance = lax.rem(owner - me + pre, pre)
        spare = (pre - 1 - hops) * per_peer
        at = jnp.where(distance > hops, (distance - hops - 1) * per_peer + n, spare)
        block = block_of(k_ref, v_ref, pl.multiple_of(b * BLK, BLK))
        sent[at] = block
        cache_ref[own_slot(slot, me, blocks)] = block
        return 0

    lax.fori_loop(0, blocks, step, 0, unroll=8)
    stores = [
        pltpu.make_async_copy(sent.at[n * per_peer : (n + 1) * per_peer], ref, sems.at[n])
        for n, ref in enumerate(sent_hbm)
    ]
    for store in stores:
        store.start()
    turn_values(v_ref, turned)
    loads[2].wait()
    for tile in range(rows // TILE):
        high = (tile + 1) * TILE
        fill_bias(bias, lengths_ref, first + tile * TILE, first, 0, high, True)
        for g in range(turned.shape[0]):
            all_weights = []

            def emit(j, weights, top, factor):
                all_weights.append(weights)
                top_ref[g, :, lanes_of(tile, j)] = top

            weigh(q_ref, k_ref, bias, None, tile, 0, high, g, emit)
            all_weights = jnp.concatenate(all_weights, axis=1)
            mix(turned[g, :, :high], all_weights, g, tile, None, keep((acc_ref, sum_ref), tile))
    for store in stores:
        store.wait()


def lowest_key(lengths_ref, hop, tile, rows):
    first = lax.axis_index("pre") * rows
    key_first = first - hop * rows
    low = jnp.maximum(start_of(lengths_ref, first + tile * TILE) - key_first, 0)
    return jnp.where(key_first >= 0, jnp.minimum(low, rows), rows)


def where_seen(low, rows, act):
    for at in range(0, rows, TILE):
        pl.when((low >= at) & (low < at + TILE))(functools.partial(act, at))


def scores_kernel(hop, lengths_ref, q_ref, k_ref, old_top, weights_ref, factor_ref, *refs):
    *top_refs, bias = refs
    rows = q_ref.shape[0]
    first = lax.axis_index("pre") * rows
    for tile in range(rows // TILE):

        def act(at):
            fill_bias(
                bias, lengths_ref, first + tile * TILE, first - hop * rows, at, rows, False
            )
            for g in range(weights_ref.shape[1]):

                def emit(j, weights, top, factor):
                    weights_ref[tile, g, at:rows, j * TILE : (j + 1) * TILE] = weights
                    for top_ref in top_refs:
                        top_ref[g, :, lanes_of(tile, j)] = top
                    factor_ref[g, :, lanes_of(tile, j)] = factor

                weigh(q_ref, k_ref, bias, old_top, tile, at, rows, g, emit)

        where_seen(lowest_key(lengths_ref, hop, tile, rows), rows, act)


def place_blocks(cache, slot_ref, k_ref, v_ref, distance, pre, blocks):
    me = lax.axis_index("pre")
    source = lax.rem(me - distance + pre, pre)

    def step(b, _):
        at = own_slot(slot_ref[source * blocks + b], me, blocks)
        cache[at] = block_of(k_ref, v_ref, pl.multiple_of(b * BLK, BLK))
        return 0

    lax.fori_loop(0, blocks, step, 0, unroll=8)


def list_places(places_ref, slot_ref, hops, pre, blocks):
    me = lax.axis_index("pre")
    per_peer = blocks // pre
    for distance in range(hops + 1, pre):
        source = lax.rem(me - distance + pre, pre)
        base = (distance - hops - 1) * (per_peer + 1)

        def step(b, n):
            at = own_slot(slot_ref[source * blocks + b], me, blocks)
            places_ref[base + n] = at
            return n + jnp.where(at < blocks, 1, 0)

        lax.fori_loop(0, blocks, step, jnp.int32(0), unroll=8)


def values_kernel(
    hop, hops, pre, lengths_ref, slot_ref, v_ref, k_ref, weights_ref, factor_ref,
    acc_in, sum_in, cache_in, *refs,
):
    first_out, last = hop == 1, hop == hops
    refs = list(refs)
    if not first_out:
        refs.pop(0)
    out_hbm, cache_out = refs.pop(0), refs.pop(0)
    state = () if last else (refs.pop(0), refs.pop(0))
    places_ref = refs.pop(0) if first_out else None
    turned, out_buf, sems, *rest = refs
    rows = v_ref.shape[0]
    blocks = rows // BLK
    tiles = rows // TILE
    kv_count = turned.shape[0]

    cache = rest[0] if last else cache_out
    cache[...] = cache_in[...]
    place_blocks(cache, slot_ref, k_ref, v_ref, hop, pre, blocks)
    if first_out:
        list_places(places_ref, slot_ref, hops, pre, blocks)
    if last:
        cache_store = pltpu.make_async_copy(cache.at[0:blocks], cache_out, sems.at[tiles])
        cache_store.start()

    lows = [lowest_key(lengths_ref, hop, tile, rows) for tile in range(tiles)]
    pl.when(lows[0] < rows)(functools.partial(turn_values, v_ref, turned))
    stores = []
    for tile, low in enumerate(lows):
        end_it = finish(out_buf, tile * TILE)

        def act(at):
            def emit(*result):
                if not last:
                    keep(state, tile)(*result)
                end_it(*result)

            for g in range(kv_count):
                weights = weights_ref[tile, g, at:rows]
                old = (acc_in, sum_in, factor_ref)
                mix(turned[g, :, at:rows], weights, g, tile, old, emit)

        where_seen(low, rows, act)
        span = slice(tile * TILE, (tile + 1) * TILE)
        store = pltpu.make_async_copy(out_buf.at[span], out_hbm.at[span], sems.at[tile])
        stores.append(store)
        if first_out:

            @pl.when(low == rows)
            def _():
                for g in range(kv_count):
                    for j in range(GROUP):
                        end_it(g, j, *(ref[g, :, lanes_of(tile, j)] for ref in (acc_in, sum_in)))

            store.start()
        else:
            pl.when(low < rows)(store.start)
    for low, store in zip(lows, stores):
        if first_out:
            store.wait()
        else:
            pl.when(low < rows)(store.wait)
    if last:
        cache_store.wait()


def place_last_kernel(places_ref, cache_in, *refs):
    *got, cache_hbm, sems = refs
    per_peer = got[0].shape[0]
    copies = []
    for i, got_ref in enumerate(got):
        for n in range(per_peer):
            at = places_ref[i * (per_peer + 1) + n]
            copy = pltpu.make_async_copy(
                got_ref.at[n], cache_hbm.at[at], sems.at[i * per_peer + n]
            )
            copy.start()
            copies.append(copy)
    for copy in copies:
        copy.wait()


def on_device(queries, new_keys, new_values, lengths, block_slot):
    rows, q_width = queries.shape
    kv_width = new_keys.shape[1]
    kv_count = kv_width // HD
    blocks = rows // BLK
    pre = lax.axis_size("pre")
    per_peer = blocks // pre
    hops = pre // 2
    tiles = rows // TILE
    bf16, f32 = jnp.bfloat16, jnp.float32
    shape = jax.ShapeDtypeStruct
    params = pltpu.CompilerParams(vmem_limit_bytes=24 * 2**20)
    own_params = pltpu.CompilerParams(vmem_limit_bytes=44 * 2**20)
    ring = [(i, (i + 1) % pre) for i in range(pre)]
    acc_shape = shape((kv_count, HD, GROUP * rows), f32)
    stat_shape = shape((kv_count, 8, GROUP * rows), f32)
    weights_shape = shape((tiles, kv_count, rows, GROUP * TILE), bf16)
    attended_shape = shape(queries.shape, bf16)
    cache_shape = shape((blocks, BLK, 2 * kv_width), bf16)
    open_cache = shape((blocks + 1, BLK, 2 * kv_width), bf16)
    turned = pltpu.VMEM((kv_count, HD + ONES, rows), bf16)
    bias = pltpu.VMEM((rows, TILE), f32)

    def cost(share, moved):
        pairs = int(rows * rows * share)
        return pl.CostEstimate(
            flops=4 * pairs * q_width,
            bytes_accessed=moved * 2**20,
            transcendentals=pairs * kv_count * GROUP,
        )

    def after(array, *others):
        return lax.optimization_barrier((array, *others))[0]

    k, v = lax.ppermute(new_keys, "pre", ring), lax.ppermute(new_values, "pre", ring)

    packed = shape((per_peer, BLK, 2 * kv_width), bf16)
    in_hbm = (
        pltpu.with_memory_space_constraint(x, pltpu.HBM) for x in (queries, new_keys, new_values)
    )
    q, acc, total, top, cache, *sent = pl.pallas_call(
        functools.partial(own_kernel, pre, hops),
        out_shape=(attended_shape, acc_shape, stat_shape, stat_shape, open_cache)
        + (packed,) * (pre - 1 - hops),
        in_specs=[SMEM, SMEM] + [HBM] * 3,
        out_specs=(VMEM,) * 5 + (HBM,) * (pre - 1 - hops),
        scratch_shapes=[
            pltpu.VMEM((rows, kv_width), bf16),
            pltpu.VMEM((rows, kv_width), bf16),
            turned,
            bias,
            pltpu.VMEM(((pre - 1 - hops) * per_peer + 1, BLK, 2 * kv_width), bf16),
            pltpu.SMEM((pre,), jnp.int32),
            pltpu.SemaphoreType.DMA((pre - 1 - hops,)),
            pltpu.SemaphoreType.DMA((3,)),
        ],
        cost_estimate=cost(1, 4),
        compiler_params=own_params,
        name="own_attention",
    )(lengths, block_slot, *in_hbm)
    got = []
    k = after(k, top)
    attended = None
    for hop in range(1, hops + 1):
        first_out, last = hop == 1, hop == hops
        next_k = None if last else lax.ppermute(k, "pre", ring)
        weights, factor, *tops = pl.pallas_call(
            functools.partial(scores_kernel, hop),
            out_shape=(weights_shape, stat_shape) + (() if last else (stat_shape,)),
            in_specs=[SMEM] + [VMEM] * 3,
            out_specs=(VMEM,) * (2 if last else 3),
            scratch_shapes=[bias],
            cost_estimate=cost(0.5, 3),
            compiler_params=params,
            name="scores",
        )(lengths, q, k, top)
        v = after(v, factor)
        if last:
            for d in range(hops + 1, pre):
                pairs = [(i, (i + d) % pre) for i in range(pre)]
                got.append(lax.ppermute(after(sent[d - hops - 1], factor), "pre", pairs))
        next_v = None if last else lax.ppermute(v, "pre", ring)
        places = shape(((pre - 1 - hops) * (per_peer + 1),), jnp.int32)
        carry = () if last else (acc_shape, stat_shape)
        extra = [] if first_out else [attended]
        attended, cache, *state = pl.pallas_call(
            functools.partial(values_kernel, hop, hops, pre),
            out_shape=(attended_shape, cache_shape if last else open_cache)
            + carry
            + ((places,) if first_out else ()),
            in_specs=[SMEM, SMEM] + [VMEM] * 7 + ([] if first_out else [HBM]),
            out_specs=(HBM, HBM if last else VMEM)
            + (VMEM,) * len(carry)
            + ((SMEM,) if first_out else ()),
            scratch_shapes=[
                turned,
                pltpu.VMEM((rows, q_width), bf16),
                pltpu.SemaphoreType.DMA((tiles + 1,)),
            ]
            + ([pltpu.VMEM(open_cache.shape, bf16)] if last else []),
            input_output_aliases={} if first_out else {9: 0},
            cost_estimate=cost(0.5, 3),
            compiler_params=params,
            name="values",
        )(lengths, block_slot, v, k, weights, factor, acc, total, cache, *extra)
        if first_out:
            far_places = state.pop()
        if not last:
            (top,) = tops
            acc, total = state
            k, v = after(next_k, total), next_v

    cache = pl.pallas_call(
        place_last_kernel,
        out_shape=cache_shape,
        in_specs=[SMEM, HBM] + [VMEM] * (pre - 1 - hops),
        out_specs=HBM,
        scratch_shapes=[pltpu.SemaphoreType.DMA(((pre - 1 - hops) * per_peer,))],
        input_output_aliases={1: 0},
        cost_estimate=cost(0, 1),
        compiler_params=params,
        name="place_last",
    )(far_places, cache, *got)
    return (attended, cache)


def solution(mesh):
    placed = (
        P(("parts", "pre"), "tp"),
        P(("parts", "pre"), "tp"),
        P(("parts", "pre"), "tp"),
        P("parts"),
        P("parts"),
    )
    return jax.shard_map(
        on_device,
        mesh=mesh,
        in_specs=placed,
        out_specs=(P(("parts", "pre"), "tp"), P(("parts", "pre"), None, "tp")),
        check_vma=False,
    )
```

```python
import functools
import math

import jax
import jax.numpy as jnp
from jax import lax
from jax.experimental import pallas as pl
from jax.experimental.pallas import tpu as pltpu
from jax.sharding import PartitionSpec as P

HD = 128
BLK = 16
GROUP = 4
TILE = 256
ONES = 16
MASKED = -1e30
EXP_SCALE = math.log2(math.e) * HD ** (-0.5)

VMEM = pl.BlockSpec(memory_space=pltpu.VMEM)
SMEM = pl.BlockSpec(memory_space=pltpu.SMEM)
HBM = pl.BlockSpec(memory_space=pltpu.HBM)


def start_of(lengths_ref, position):
    end = jnp.int32(0)
    start = jnp.int32(0)
    for r in range(lengths_ref.shape[0]):
        end = end + lengths_ref[r]
        start = jnp.where(end <= position, end, start)
    return start


def row_starts(lengths_ref, positions):
    end = jnp.int32(0)
    starts = jnp.zeros_like(positions)
    for r in range(lengths_ref.shape[0]):
        end = end + lengths_ref[r]
        starts = jnp.where(positions >= end, end, starts)
    return starts


def fill_bias(bias_ref, lengths_ref, row_first, key_first, low, high, causal):
    shape = (high - low, TILE)
    positions = row_first + lax.broadcasted_iota(jnp.int32, (8, TILE), 1)
    starts = row_starts(lengths_ref, positions)
    keys = key_first + low + lax.broadcasted_iota(jnp.int32, shape, 0)
    keys = keys.reshape((high - low) // 8, 8, TILE)
    allowed = keys >= starts[None]
    if causal:
        allowed = allowed & (keys <= positions[None])
    bias_ref[low:high] = jnp.where(allowed, 0.0, MASKED).reshape(shape)


def turn_values(v_ref, turned):
    for g in range(turned.shape[0]):
        turned[g, :HD] = v_ref[:, g * HD : (g + 1) * HD].T
        turned[g, HD:] = jnp.ones((ONES, turned.shape[2]), turned.dtype)


def lanes_of(tile, j):
    return slice((tile * GROUP + j) * TILE, (tile * GROUP + j + 1) * TILE)


def weigh(q_ref, k_ref, bias_ref, old_top, tile, low, high, g, emit):
    keys = k_ref[low:high, g * HD : (g + 1) * HD]
    heads = range(g * GROUP, (g + 1) * GROUP)
    queries = jnp.concatenate(
        [q_ref[tile * TILE : (tile + 1) * TILE, h * HD : (h + 1) * HD] for h in heads], axis=0
    )
    all_scores = lax.dot_general(
        keys, queries, (((1,), (1,)), ((), ())), preferred_element_type=jnp.float32
    )
    for j in range(GROUP):
        scores = all_scores[:, j * TILE : (j + 1) * TILE] + bias_ref[low:high]
        scores = scores.reshape((high - low) // 8, 8, TILE)
        highest = jnp.max(jnp.max(scores, axis=0), axis=0, keepdims=True)
        top = jnp.broadcast_to(highest, (8, TILE))
        factor = None
        if old_top is not None:
            old = old_top[g, :, lanes_of(tile, j)]
            top = jnp.maximum(old, top)
            factor = jnp.exp2((old - top) * EXP_SCALE)
        weights = jnp.exp2((scores - top[None]) * EXP_SCALE)
        emit(j, weights.reshape(high - low, TILE).astype(jnp.bfloat16), top, factor)


def mix(values, weights, g, tile, old, emit):
    all_added = jnp.dot(values, weights, preferred_element_type=jnp.float32)
    for j in range(GROUP):
        at = lanes_of(tile, j)
        added = all_added[:, j * TILE : (j + 1) * TILE]
        value, total = added[:HD], added[HD : HD + 8]
        if old is not None:
            acc_ref, sum_ref, factor_ref = old
            factor = factor_ref[g, :, at]
            total = total + sum_ref[g, :, at] * factor
            kept = acc_ref[g, :, at].reshape(HD // 8, 8, TILE) * factor[None]
            value = value + kept.reshape(HD, TILE)
        emit(g, j, value, total)


def keep(state, tile):
    def emit(g, j, value, total):
        for ref, array in zip(state, (value, total)):
            ref[g, :, lanes_of(tile, j)] = array

    return emit


def finish(out_ref, row):
    def emit(g, j, value, total):
        head = g * GROUP + j
        value = value.reshape(HD // 8, 8, TILE) * (1.0 / total)[None]
        value = value.reshape(HD, TILE).astype(out_ref.dtype).T
        out_ref[row : row + TILE, head * HD : (head + 1) * HD] = value

    return emit


def block_of(k_ref, v_ref, row):
    parts = []
    for g in range(k_ref.shape[1] // HD):
        span = slice(g * HD, (g + 1) * HD)
        parts += [k_ref[pl.ds(row, BLK), span], v_ref[pl.ds(row, BLK), span]]
    return jnp.concatenate(parts, axis=1)


def own_slot(slot, me, blocks):
    local = slot - me * blocks
    return jnp.where((local >= 0) & (local < blocks), local, blocks)


def own_kernel(
    pre, hops, lengths_ref, slot_ref, q_hbm, k_hbm, v_hbm,
    q_ref, acc_ref, sum_ref, top_ref, cache_ref, *refs,
):
    sent_hbm, (k_ref, v_ref, turned, bias, sent, counts, sems, load_sems) = refs[:-8], refs[-8:]
    loads = [
        pltpu.make_async_copy(src, dst, load_sems.at[n])
        for n, (src, dst) in enumerate(((k_hbm, k_ref), (v_hbm, v_ref), (q_hbm, q_ref)))
    ]
    for load in loads:
        load.start()
    rows = q_ref.shape[0]
    blocks = rows // BLK
    per_peer = blocks // pre
    me = lax.axis_index("pre")
    first = me * rows
    for owner in range(pre):
        counts[owner] = 0
    loads[0].wait()
    loads[1].wait()

    def step(b, _):
        slot = slot_ref[me * blocks + b]
        owner = slot // blocks
        n = counts[owner]
        counts[owner] = n + 1
        distance = lax.rem(owner - me + pre, pre)
        spare = (pre - 1 - hops) * per_peer
        at = jnp.where(distance > hops, (distance - hops - 1) * per_peer + n, spare)
        block = block_of(k_ref, v_ref, pl.multiple_of(b * BLK, BLK))
        sent[at] = block
        cache_ref[own_slot(slot, me, blocks)] = block
        return 0

    lax.fori_loop(0, blocks, step, 0, unroll=8)
    stores = [
        pltpu.make_async_copy(sent.at[n * per_peer : (n + 1) * per_peer], ref, sems.at[n])
        for n, ref in enumerate(sent_hbm)
    ]
    for store in stores:
        store.start()
    turn_values(v_ref, turned)
    loads[2].wait()
    for tile in range(rows // TILE):
        high = (tile + 1) * TILE
        fill_bias(bias, lengths_ref, first + tile * TILE, first, 0, high, True)
        for g in range(turned.shape[0]):
            all_weights = []

            def emit(j, weights, top, factor):
                all_weights.append(weights)
                top_ref[g, :, lanes_of(tile, j)] = top

            weigh(q_ref, k_ref, bias, None, tile, 0, high, g, emit)
            all_weights = jnp.concatenate(all_weights, axis=1)
            mix(turned[g, :, :high], all_weights, g, tile, None, keep((acc_ref, sum_ref), tile))
    for store in stores:
        store.wait()


def lowest_key(lengths_ref, hop, tile, rows):
    first = lax.axis_index("pre") * rows
    key_first = first - hop * rows
    low = jnp.maximum(start_of(lengths_ref, first + tile * TILE) - key_first, 0)
    return jnp.where(key_first >= 0, jnp.minimum(low, rows), rows)


def where_seen(low, rows, act):
    for at in range(0, rows, TILE):
        pl.when((low >= at) & (low < at + TILE))(functools.partial(act, at))


def scores_kernel(hop, lengths_ref, q_ref, k_ref, old_top, weights_ref, factor_ref, *refs):
    *top_refs, bias = refs
    rows = q_ref.shape[0]
    first = lax.axis_index("pre") * rows
    for tile in range(rows // TILE):

        def act(at):
            fill_bias(
                bias, lengths_ref, first + tile * TILE, first - hop * rows, at, rows, False
            )
            for g in range(weights_ref.shape[1]):

                def emit(j, weights, top, factor):
                    weights_ref[tile, g, at:rows, j * TILE : (j + 1) * TILE] = weights
                    for top_ref in top_refs:
                        top_ref[g, :, lanes_of(tile, j)] = top
                    factor_ref[g, :, lanes_of(tile, j)] = factor

                weigh(q_ref, k_ref, bias, old_top, tile, at, rows, g, emit)

        where_seen(lowest_key(lengths_ref, hop, tile, rows), rows, act)


def place_blocks(cache, slot_ref, k_ref, v_ref, distance, pre, blocks):
    me = lax.axis_index("pre")
    source = lax.rem(me - distance + pre, pre)

    def step(b, _):
        at = own_slot(slot_ref[source * blocks + b], me, blocks)
        cache[at] = block_of(k_ref, v_ref, pl.multiple_of(b * BLK, BLK))
        return 0

    lax.fori_loop(0, blocks, step, 0, unroll=8)


def list_places(places_ref, slot_ref, hops, pre, blocks):
    me = lax.axis_index("pre")
    stride = blocks // pre + 1
    for i, distance in enumerate(range(hops, pre)):
        source = lax.rem(me - distance + pre, pre)

        def step(b, n):
            at = own_slot(slot_ref[source * blocks + b], me, blocks)
            places_ref[i * stride + n] = at
            if i == 0:
                places_ref[(pre - hops) * stride + n] = b
            return n + jnp.where(at < blocks, 1, 0)

        lax.fori_loop(0, blocks, step, jnp.int32(0), unroll=8)


def place_listed(cache, places_ref, k_ref, v_ref, got_refs):
    per_peer = got_refs[0].shape[0]
    stride = per_peer + 1
    for n in range(per_peer):
        b = places_ref[(len(got_refs) + 1) * stride + n]
        cache[places_ref[n]] = block_of(k_ref, v_ref, pl.multiple_of(b * BLK, BLK))
        for i, got_ref in enumerate(got_refs):
            cache[places_ref[(i + 1) * stride + n]] = got_ref[n]


def values_kernel(
    hop, hops, pre, lengths_ref, slot_ref, v_ref, k_ref, weights_ref, factor_ref,
    acc_in, sum_in, cache_in, *refs,
):
    first_out, last = hop == 1, hop == hops
    refs = list(refs)
    if not first_out:
        refs.pop(0)
    got_refs = [refs.pop(0) for _ in range(hops + 1, pre)] if last else []
    out_hbm, cache_out = refs.pop(0), refs.pop(0)
    state = () if last else (refs.pop(0), refs.pop(0))
    places_ref = refs.pop(0) if first_out else None
    turned, out_buf, sems, *rest = refs
    rows = v_ref.shape[0]
    blocks = rows // BLK
    tiles = rows // TILE
    kv_count = turned.shape[0]

    cache = rest[0] if last else cache_out
    cache[...] = cache_in[...]
    if last:
        place_listed(cache, slot_ref, k_ref, v_ref, got_refs)
    else:
        place_blocks(cache, slot_ref, k_ref, v_ref, hop, pre, blocks)
    if first_out:
        list_places(places_ref, slot_ref, hops, pre, blocks)
    if last:
        cache_store = pltpu.make_async_copy(cache.at[0:blocks], cache_out, sems.at[tiles])
        cache_store.start()

    lows = [lowest_key(lengths_ref, hop, tile, rows) for tile in range(tiles)]
    pl.when(lows[0] < rows)(functools.partial(turn_values, v_ref, turned))
    stores = []
    for tile, low in enumerate(lows):
        end_it = finish(out_buf, tile * TILE)

        def act(at):
            def emit(*result):
                if not last:
                    keep(state, tile)(*result)
                end_it(*result)

            for g in range(kv_count):
                weights = weights_ref[tile, g, at:rows]
                old = (acc_in, sum_in, factor_ref)
                mix(turned[g, :, at:rows], weights, g, tile, old, emit)

        where_seen(low, rows, act)
        span = slice(tile * TILE, (tile + 1) * TILE)
        store = pltpu.make_async_copy(out_buf.at[span], out_hbm.at[span], sems.at[tile])
        stores.append(store)
        if first_out:

            @pl.when(low == rows)
            def _():
                for g in range(kv_count):
                    for j in range(GROUP):
                        end_it(g, j, *(ref[g, :, lanes_of(tile, j)] for ref in (acc_in, sum_in)))

            store.start()
        else:
            pl.when(low < rows)(store.start)
    for low, store in zip(lows, stores):
        if first_out:
            store.wait()
        else:
            pl.when(low < rows)(store.wait)
    if last:
        cache_store.wait()


def on_device(queries, new_keys, new_values, lengths, block_slot):
    rows, q_width = queries.shape
    kv_width = new_keys.shape[1]
    kv_count = kv_width // HD
    blocks = rows // BLK
    pre = lax.axis_size("pre")
    per_peer = blocks // pre
    hops = pre // 2
    tiles = rows // TILE
    bf16, f32 = jnp.bfloat16, jnp.float32
    shape = jax.ShapeDtypeStruct
    params = pltpu.CompilerParams(vmem_limit_bytes=24 * 2**20)
    own_params = pltpu.CompilerParams(vmem_limit_bytes=44 * 2**20)
    ring = [(i, (i + 1) % pre) for i in range(pre)]
    acc_shape = shape((kv_count, HD, GROUP * rows), f32)
    stat_shape = shape((kv_count, 8, GROUP * rows), f32)
    weights_shape = shape((tiles, kv_count, rows, GROUP * TILE), bf16)
    attended_shape = shape(queries.shape, bf16)
    cache_shape = shape((blocks, BLK, 2 * kv_width), bf16)
    open_cache = shape((blocks + 1, BLK, 2 * kv_width), bf16)
    turned = pltpu.VMEM((kv_count, HD + ONES, rows), bf16)
    bias = pltpu.VMEM((rows, TILE), f32)

    def cost(share, moved):
        pairs = int(rows * rows * share)
        return pl.CostEstimate(
            flops=4 * pairs * q_width,
            bytes_accessed=moved * 2**20,
            transcendentals=pairs * kv_count * GROUP,
        )

    def after(array, *others):
        return lax.optimization_barrier((array, *others))[0]

    k, v = lax.ppermute(new_keys, "pre", ring), lax.ppermute(new_values, "pre", ring)

    packed = shape((per_peer, BLK, 2 * kv_width), bf16)
    in_hbm = (
        pltpu.with_memory_space_constraint(x, pltpu.HBM) for x in (queries, new_keys, new_values)
    )
    q, acc, total, top, cache, *sent = pl.pallas_call(
        functools.partial(own_kernel, pre, hops),
        out_shape=(attended_shape, acc_shape, stat_shape, stat_shape, open_cache)
        + (packed,) * (pre - 1 - hops),
        in_specs=[SMEM, SMEM] + [HBM] * 3,
        out_specs=(VMEM,) * 5 + (HBM,) * (pre - 1 - hops),
        scratch_shapes=[
            pltpu.VMEM((rows, kv_width), bf16),
            pltpu.VMEM((rows, kv_width), bf16),
            turned,
            bias,
            pltpu.VMEM(((pre - 1 - hops) * per_peer + 1, BLK, 2 * kv_width), bf16),
            pltpu.SMEM((pre,), jnp.int32),
            pltpu.SemaphoreType.DMA((pre - 1 - hops,)),
            pltpu.SemaphoreType.DMA((3,)),
        ],
        cost_estimate=cost(1, 4),
        compiler_params=own_params,
        name="own_attention",
    )(lengths, block_slot, *in_hbm)
    got = []
    k = after(k, top)
    attended = None
    for hop in range(1, hops + 1):
        first_out, last = hop == 1, hop == hops
        next_k = None if last else lax.ppermute(k, "pre", ring)
        weights, factor, *tops = pl.pallas_call(
            functools.partial(scores_kernel, hop),
            out_shape=(weights_shape, stat_shape) + (() if last else (stat_shape,)),
            in_specs=[SMEM] + [VMEM] * 3,
            out_specs=(VMEM,) * (2 if last else 3),
            scratch_shapes=[bias],
            cost_estimate=cost(0.5, 3),
            compiler_params=params,
            name="scores",
        )(lengths, q, k, top)
        v = after(v, factor)
        if last:
            for d in range(hops + 1, pre):
                pairs = [(i, (i + d) % pre) for i in range(pre)]
                got.append(lax.ppermute(after(sent[d - hops - 1], factor), "pre", pairs))
        next_v = None if last else lax.ppermute(v, "pre", ring)
        places = shape(((pre - hops + 1) * (per_peer + 1),), jnp.int32)
        carry = () if last else (acc_shape, stat_shape)
        extra = ([] if first_out else [attended]) + (got if last else [])
        attended, cache, *state = pl.pallas_call(
            functools.partial(values_kernel, hop, hops, pre),
            out_shape=(attended_shape, cache_shape if last else open_cache)
            + carry
            + ((places,) if first_out else ()),
            in_specs=[SMEM, SMEM]
            + [VMEM] * 7
            + ([] if first_out else [HBM])
            + ([VMEM] * len(got) if last else []),
            out_specs=(HBM, HBM if last else VMEM)
            + (VMEM,) * len(carry)
            + ((SMEM,) if first_out else ()),
            scratch_shapes=[
                turned,
                pltpu.VMEM((rows, q_width), bf16),
                pltpu.SemaphoreType.DMA((tiles + 1,)),
            ]
            + ([pltpu.VMEM(open_cache.shape, bf16)] if last else []),
            input_output_aliases={} if first_out else {9: 0},
            cost_estimate=cost(0.5, 3),
            compiler_params=params,
            name="values",
        )(lengths, far_places if last else block_slot, v, k, weights, factor, acc, total, cache, *extra)
        if first_out:
            far_places = state.pop()
        if not last:
            (top,) = tops
            acc, total = state
            k, v = after(next_k, total), next_v

    return (attended, cache)


def solution(mesh):
    placed = (
        P(("parts", "pre"), "tp"),
        P(("parts", "pre"), "tp"),
        P(("parts", "pre"), "tp"),
        P("parts"),
        P("parts"),
    )
    return jax.shard_map(
        on_device,
        mesh=mesh,
        in_specs=placed,
        out_specs=(P(("parts", "pre"), "tp"), P(("parts", "pre"), None, "tp")),
        check_vma=False,
    )
```

```python
import functools
import math

import jax
import jax.numpy as jnp
from jax import lax
from jax.experimental import pallas as pl
from jax.experimental.pallas import tpu as pltpu
from jax.sharding import PartitionSpec as P

HD = 128
BLK = 16
GROUP = 4
TILE = 256
ONES = 16
MASKED = -1e30
EXP_SCALE = math.log2(math.e) * HD ** (-0.5)

VMEM = pl.BlockSpec(memory_space=pltpu.VMEM)
SMEM = pl.BlockSpec(memory_space=pltpu.SMEM)
HBM = pl.BlockSpec(memory_space=pltpu.HBM)


def start_of(lengths_ref, position):
    end = jnp.int32(0)
    start = jnp.int32(0)
    for r in range(lengths_ref.shape[0]):
        end = end + lengths_ref[r]
        start = jnp.where(end <= position, end, start)
    return start


def row_starts(lengths_ref, positions):
    end = jnp.int32(0)
    starts = jnp.zeros_like(positions)
    for r in range(lengths_ref.shape[0]):
        end = end + lengths_ref[r]
        starts = jnp.where(positions >= end, end, starts)
    return starts


def fill_bias(bias_ref, lengths_ref, row_first, key_first, low, high, causal):
    shape = (high - low, TILE)
    positions = row_first + lax.broadcasted_iota(jnp.int32, (8, TILE), 1)
    starts = row_starts(lengths_ref, positions)
    keys = key_first + low + lax.broadcasted_iota(jnp.int32, shape, 0)
    keys = keys.reshape((high - low) // 8, 8, TILE)
    allowed = keys >= starts[None]
    if causal:
        allowed = allowed & (keys <= positions[None])
    bias_ref[low:high] = jnp.where(allowed, 0.0, MASKED).reshape(shape)


def turn_values(v_ref, turned):
    for g in range(turned.shape[0]):
        turned[g, :HD] = v_ref[:, g * HD : (g + 1) * HD].T
        turned[g, HD:] = jnp.ones((ONES, turned.shape[2]), turned.dtype)


def lanes_of(tile, j):
    return slice((tile * GROUP + j) * TILE, (tile * GROUP + j + 1) * TILE)


def weigh(q_ref, k_ref, bias_ref, old_top, tile, low, high, g, emit):
    keys = k_ref[low:high, g * HD : (g + 1) * HD]
    heads = range(g * GROUP, (g + 1) * GROUP)
    queries = jnp.concatenate(
        [q_ref[tile * TILE : (tile + 1) * TILE, h * HD : (h + 1) * HD] for h in heads], axis=0
    )
    all_scores = lax.dot_general(
        keys, queries, (((1,), (1,)), ((), ())), preferred_element_type=jnp.float32
    )
    for j in range(GROUP):
        scores = all_scores[:, j * TILE : (j + 1) * TILE] + bias_ref[low:high]
        scores = scores.reshape((high - low) // 8, 8, TILE)
        highest = jnp.max(jnp.max(scores, axis=0), axis=0, keepdims=True)
        top = jnp.broadcast_to(highest, (8, TILE))
        factor = None
        if old_top is not None:
            old = old_top[g, :, lanes_of(tile, j)]
            top = jnp.maximum(old, top)
            factor = jnp.exp2((old - top) * EXP_SCALE)
        weights = jnp.exp2((scores - top[None]) * EXP_SCALE)
        emit(j, weights.reshape(high - low, TILE).astype(jnp.bfloat16), top, factor)


def mix(values, weights, g, tile, old, emit):
    all_added = jnp.dot(values, weights, preferred_element_type=jnp.float32)
    for j in range(GROUP):
        at = lanes_of(tile, j)
        added = all_added[:, j * TILE : (j + 1) * TILE]
        value, total = added[:HD], added[HD : HD + 8]
        if old is not None:
            acc_ref, sum_ref, factor_ref = old
            factor = factor_ref[g, :, at]
            total = total + sum_ref[g, :, at] * factor
            kept = acc_ref[g, :, at].reshape(HD // 8, 8, TILE) * factor[None]
            value = value + kept.reshape(HD, TILE)
        emit(g, j, value, total)


def keep(state, tile):
    def emit(g, j, value, total):
        for ref, array in zip(state, (value, total)):
            ref[g, :, lanes_of(tile, j)] = array

    return emit


def finish(out_ref, row):
    def emit(g, j, value, total):
        head = g * GROUP + j
        value = value.reshape(HD // 8, 8, TILE) * (1.0 / total)[None]
        value = value.reshape(HD, TILE).astype(out_ref.dtype).T
        out_ref[row : row + TILE, head * HD : (head + 1) * HD] = value

    return emit


def block_of(k_ref, v_ref, row):
    parts = []
    for g in range(k_ref.shape[1] // HD):
        span = slice(g * HD, (g + 1) * HD)
        parts += [k_ref[pl.ds(row, BLK), span], v_ref[pl.ds(row, BLK), span]]
    return jnp.concatenate(parts, axis=1)


def own_slot(slot, me, blocks):
    local = slot - me * blocks
    return jnp.where((local >= 0) & (local < blocks), local, blocks)


def own_kernel(
    pre, hops, lengths_ref, slot_ref, q_hbm, k_hbm, v_hbm,
    q_ref, acc_ref, sum_ref, top_ref, cache_ref, *refs,
):
    sent_hbm, (k_ref, v_ref, turned, bias, sent, counts, sems, load_sems) = refs[:-8], refs[-8:]
    loads = [
        pltpu.make_async_copy(src, dst, load_sems.at[n])
        for n, (src, dst) in enumerate(((k_hbm, k_ref), (v_hbm, v_ref), (q_hbm, q_ref)))
    ]
    for load in loads:
        load.start()
    rows = q_ref.shape[0]
    blocks = rows // BLK
    per_peer = blocks // pre
    me = lax.axis_index("pre")
    first = me * rows
    for owner in range(pre):
        counts[owner] = 0
    loads[0].wait()
    loads[1].wait()

    def step(b, _):
        slot = slot_ref[me * blocks + b]
        owner = slot // blocks
        n = counts[owner]
        counts[owner] = n + 1
        distance = lax.rem(owner - me + pre, pre)
        spare = (pre - 1 - hops) * per_peer
        at = jnp.where(distance > hops, (distance - hops - 1) * per_peer + n, spare)
        block = block_of(k_ref, v_ref, pl.multiple_of(b * BLK, BLK))
        sent[at] = block
        cache_ref[own_slot(slot, me, blocks)] = block
        return 0

    lax.fori_loop(0, blocks, step, 0, unroll=8)
    stores = [
        pltpu.make_async_copy(sent.at[n * per_peer : (n + 1) * per_peer], ref, sems.at[n])
        for n, ref in enumerate(sent_hbm)
    ]
    for store in stores:
        store.start()
    turn_values(v_ref, turned)
    loads[2].wait()
    for tile in range(rows // TILE):
        high = (tile + 1) * TILE
        fill_bias(bias, lengths_ref, first + tile * TILE, first, 0, high, True)
        for g in range(turned.shape[0]):
            all_weights = []

            def emit(j, weights, top, factor):
                all_weights.append(weights)
                top_ref[g, :, lanes_of(tile, j)] = top

            weigh(q_ref, k_ref, bias, None, tile, 0, high, g, emit)
            all_weights = jnp.concatenate(all_weights, axis=1)
            mix(turned[g, :, :high], all_weights, g, tile, None, keep((acc_ref, sum_ref), tile))
    for store in stores:
        store.wait()


def lowest_key(lengths_ref, hop, tile, rows):
    first = lax.axis_index("pre") * rows
    key_first = first - hop * rows
    low = jnp.maximum(start_of(lengths_ref, first + tile * TILE) - key_first, 0)
    return jnp.where(key_first >= 0, jnp.minimum(low, rows), rows)


def where_seen(low, rows, act):
    for at in range(0, rows, TILE):
        pl.when((low >= at) & (low < at + TILE))(functools.partial(act, at))


def scores_kernel(hop, lengths_ref, q_ref, k_ref, old_top, weights_ref, factor_ref, *refs):
    *top_refs, bias = refs
    rows = q_ref.shape[0]
    first = lax.axis_index("pre") * rows
    for tile in range(rows // TILE):

        def act(at):
            fill_bias(
                bias, lengths_ref, first + tile * TILE, first - hop * rows, at, rows, False
            )
            for g in range(weights_ref.shape[1]):

                def emit(j, weights, top, factor):
                    weights_ref[tile, g, at:rows, j * TILE : (j + 1) * TILE] = weights
                    for top_ref in top_refs:
                        top_ref[g, :, lanes_of(tile, j)] = top
                    factor_ref[g, :, lanes_of(tile, j)] = factor

                weigh(q_ref, k_ref, bias, old_top, tile, at, rows, g, emit)

        where_seen(lowest_key(lengths_ref, hop, tile, rows), rows, act)


def place_blocks(cache, slot_ref, k_ref, v_ref, distance, pre, blocks):
    me = lax.axis_index("pre")
    source = lax.rem(me - distance + pre, pre)

    def step(b, _):
        at = own_slot(slot_ref[source * blocks + b], me, blocks)
        cache[at] = block_of(k_ref, v_ref, pl.multiple_of(b * BLK, BLK))
        return 0

    lax.fori_loop(0, blocks, step, 0, unroll=8)


def list_places(places_ref, slot_ref, hops, pre, blocks):
    me = lax.axis_index("pre")
    stride = blocks // pre + 1
    for i, distance in enumerate(range(hops, pre)):
        source = lax.rem(me - distance + pre, pre)

        def step(b, n):
            at = own_slot(slot_ref[source * blocks + b], me, blocks)
            places_ref[i * stride + n] = at
            if i == 0:
                places_ref[(pre - hops) * stride + n] = b
            return n + jnp.where(at < blocks, 1, 0)

        lax.fori_loop(0, blocks, step, jnp.int32(0), unroll=8)


def place_listed(cache, places_ref, k_ref, v_ref, got_refs):
    per_peer = got_refs[0].shape[0]
    stride = per_peer + 1
    for n in range(per_peer):
        b = places_ref[(len(got_refs) + 1) * stride + n]
        cache[places_ref[n]] = block_of(k_ref, v_ref, pl.multiple_of(b * BLK, BLK))
        for i, got_ref in enumerate(got_refs):
            cache[places_ref[(i + 1) * stride + n]] = got_ref[n]


def values_kernel(
    hop, hops, pre, lengths_ref, slot_ref, v_ref, k_ref, weights_ref, factor_ref,
    acc_in, sum_in, cache_in, *refs,
):
    first_out, last = hop == 1, hop == hops
    refs = list(refs)
    if not first_out:
        refs.pop(0)
    got_refs = [refs.pop(0) for _ in range(hops + 1, pre)] if last else []
    out_hbm, cache_out = refs.pop(0), refs.pop(0)
    state = () if last else (refs.pop(0), refs.pop(0))
    places_ref = refs.pop(0) if first_out else None
    turned, out_buf, sems, *rest = refs
    rows = v_ref.shape[0]
    blocks = rows // BLK
    tiles = rows // TILE
    kv_count = turned.shape[0]

    cache = rest[0] if last else cache_out
    cache[...] = cache_in[...]
    if last:
        place_listed(cache, slot_ref, k_ref, v_ref, got_refs)
    else:
        place_blocks(cache, slot_ref, k_ref, v_ref, hop, pre, blocks)
    if first_out:
        list_places(places_ref, slot_ref, hops, pre, blocks)
    if last:
        cache_store = pltpu.make_async_copy(cache.at[0:blocks], cache_out, sems.at[tiles])
        cache_store.start()

    lows = [lowest_key(lengths_ref, hop, tile, rows) for tile in range(tiles)]
    pl.when(lows[0] < rows)(functools.partial(turn_values, v_ref, turned))
    stores = []
    for tile, low in enumerate(lows):
        end_it = finish(out_buf, tile * TILE)

        def act(at):
            def emit(*result):
                if not last:
                    keep(state, tile)(*result)
                end_it(*result)

            for g in range(kv_count):
                weights = weights_ref[tile, g, at:rows]
                old = (acc_in, sum_in, factor_ref)
                mix(turned[g, :, at:rows], weights, g, tile, old, emit)

        where_seen(low, rows, act)
        span = slice(tile * TILE, (tile + 1) * TILE)
        store = pltpu.make_async_copy(out_buf.at[span], out_hbm.at[span], sems.at[tile])
        stores.append(store)
        if first_out:

            @pl.when(low == rows)
            def _():
                for g in range(kv_count):
                    for j in range(GROUP):
                        end_it(g, j, *(ref[g, :, lanes_of(tile, j)] for ref in (acc_in, sum_in)))

            store.start()
        else:
            pl.when(low < rows)(store.start)
    for low, store in zip(lows, stores):
        if first_out:
            store.wait()
        else:
            pl.when(low < rows)(store.wait)
    if last:
        cache_store.wait()


def on_device(queries, new_keys, new_values, lengths, block_slot):
    rows, q_width = queries.shape
    kv_width = new_keys.shape[1]
    kv_count = kv_width // HD
    blocks = rows // BLK
    pre = lax.axis_size("pre")
    per_peer = blocks // pre
    hops = pre // 2
    tiles = rows // TILE
    bf16, f32 = jnp.bfloat16, jnp.float32
    shape = jax.ShapeDtypeStruct
    params = pltpu.CompilerParams(vmem_limit_bytes=24 * 2**20)
    own_params = pltpu.CompilerParams(vmem_limit_bytes=44 * 2**20)
    ring = [(i, (i + 1) % pre) for i in range(pre)]
    acc_shape = shape((kv_count, HD, GROUP * rows), f32)
    stat_shape = shape((kv_count, 8, GROUP * rows), f32)
    weights_shape = shape((tiles, kv_count, rows, GROUP * TILE), bf16)
    attended_shape = shape(queries.shape, bf16)
    cache_shape = shape((blocks, BLK, 2 * kv_width), bf16)
    open_cache = shape((blocks + 1, BLK, 2 * kv_width), bf16)
    turned = pltpu.VMEM((kv_count, HD + ONES, rows), bf16)
    bias = pltpu.VMEM((rows, TILE), f32)

    def cost(share, moved):
        pairs = int(rows * rows * share)
        return pl.CostEstimate(
            flops=4 * pairs * q_width,
            bytes_accessed=moved * 2**20,
            transcendentals=pairs * kv_count * GROUP,
        )

    def after(array, *others):
        return lax.optimization_barrier((array, *others))[0]

    k, v = lax.ppermute(new_keys, "pre", ring), lax.ppermute(new_values, "pre", ring)

    packed = shape((per_peer, BLK, 2 * kv_width), bf16)
    in_hbm = (
        pltpu.with_memory_space_constraint(x, pltpu.HBM) for x in (queries, new_keys, new_values)
    )
    q, acc, total, top, cache, *sent = pl.pallas_call(
        functools.partial(own_kernel, pre, hops),
        out_shape=(attended_shape, acc_shape, stat_shape, stat_shape, open_cache)
        + (packed,) * (pre - 1 - hops),
        in_specs=[SMEM, SMEM] + [HBM] * 3,
        out_specs=(VMEM,) * 5 + (HBM,) * (pre - 1 - hops),
        scratch_shapes=[
            pltpu.VMEM((rows, kv_width), bf16),
            pltpu.VMEM((rows, kv_width), bf16),
            turned,
            bias,
            pltpu.VMEM(((pre - 1 - hops) * per_peer + 1, BLK, 2 * kv_width), bf16),
            pltpu.SMEM((pre,), jnp.int32),
            pltpu.SemaphoreType.DMA((pre - 1 - hops,)),
            pltpu.SemaphoreType.DMA((3,)),
        ],
        cost_estimate=cost(1, 4),
        compiler_params=own_params,
        name="own_attention",
    )(lengths, block_slot, *in_hbm)
    got = []
    k = after(k, top)
    attended = None
    for hop in range(1, hops + 1):
        first_out, last = hop == 1, hop == hops
        next_k = None if last else lax.ppermute(k, "pre", ring)
        weights, factor, *tops = pl.pallas_call(
            functools.partial(scores_kernel, hop),
            out_shape=(weights_shape, stat_shape) + (() if last else (stat_shape,)),
            in_specs=[SMEM] + [VMEM] * 3,
            out_specs=(VMEM,) * (2 if last else 3),
            scratch_shapes=[bias],
            cost_estimate=cost(0.5, 3),
            compiler_params=params,
            name="scores",
        )(lengths, q, k, top)
        v = after(v, factor)
        next_v = None if last else lax.ppermute(v, "pre", ring)
        if first_out:
            for d in range(hops + 1, pre):
                pairs = [(i, (i + d) % pre) for i in range(pre)]
                got.append(lax.ppermute(after(sent[d - hops - 1], v), "pre", pairs))
        places = shape(((pre - hops + 1) * (per_peer + 1),), jnp.int32)
        carry = () if last else (acc_shape, stat_shape)
        extra = ([] if first_out else [attended]) + (got if last else [])
        attended, cache, *state = pl.pallas_call(
            functools.partial(values_kernel, hop, hops, pre),
            out_shape=(attended_shape, cache_shape if last else open_cache)
            + carry
            + ((places,) if first_out else ()),
            in_specs=[SMEM, SMEM]
            + [VMEM] * 7
            + ([] if first_out else [HBM])
            + ([VMEM] * len(got) if last else []),
            out_specs=(HBM, HBM if last else VMEM)
            + (VMEM,) * len(carry)
            + ((SMEM,) if first_out else ()),
            scratch_shapes=[
                turned,
                pltpu.VMEM((rows, q_width), bf16),
                pltpu.SemaphoreType.DMA((tiles + 1,)),
            ]
            + ([pltpu.VMEM(open_cache.shape, bf16)] if last else []),
            input_output_aliases={} if first_out else {9: 0},
            cost_estimate=cost(0.5, 3),
            compiler_params=params,
            name="values",
        )(lengths, far_places if last else block_slot, v, k, weights, factor, acc, total, cache, *extra)
        if first_out:
            far_places = state.pop()
        if not last:
            (top,) = tops
            acc, total = state
            k, v = after(next_k, total), next_v

    return (attended, cache)


def solution(mesh):
    placed = (
        P(("parts", "pre"), "tp"),
        P(("parts", "pre"), "tp"),
        P(("parts", "pre"), "tp"),
        P("parts"),
        P("parts"),
    )
    return jax.shard_map(
        on_device,
        mesh=mesh,
        in_specs=placed,
        out_specs=(P(("parts", "pre"), "tp"), P(("parts", "pre"), None, "tp")),
        check_vma=False,
    )
```

```python
import functools
import math

import jax
import jax.numpy as jnp
from jax import lax
from jax.experimental import pallas as pl
from jax.experimental.pallas import tpu as pltpu
from jax.sharding import PartitionSpec as P

HD = 128
BLK = 16
GROUP = 4
TILE = 256
ONES = 16
MASKED = -1e30
EXP_SCALE = math.log2(math.e) * HD ** (-0.5)

VMEM = pl.BlockSpec(memory_space=pltpu.VMEM)
SMEM = pl.BlockSpec(memory_space=pltpu.SMEM)
HBM = pl.BlockSpec(memory_space=pltpu.HBM)


def start_of(lengths_ref, position):
    end = jnp.int32(0)
    start = jnp.int32(0)
    for r in range(lengths_ref.shape[0]):
        end = end + lengths_ref[r]
        start = jnp.where(end <= position, end, start)
    return start


def row_starts(lengths_ref, positions):
    end = jnp.int32(0)
    starts = jnp.zeros_like(positions)
    for r in range(lengths_ref.shape[0]):
        end = end + lengths_ref[r]
        starts = jnp.where(positions >= end, end, starts)
    return starts


def fill_bias(bias_ref, lengths_ref, row_first, key_first, low, high, causal):
    shape = (high - low, TILE)
    positions = row_first + lax.broadcasted_iota(jnp.int32, (8, TILE), 1)
    starts = row_starts(lengths_ref, positions)
    keys = key_first + low + lax.broadcasted_iota(jnp.int32, shape, 0)
    keys = keys.reshape((high - low) // 8, 8, TILE)
    allowed = keys >= starts[None]
    if causal:
        allowed = allowed & (keys <= positions[None])
    bias_ref[low:high] = jnp.where(allowed, 0.0, MASKED).reshape(shape)


def turn_values(v_ref, turned):
    for g in range(turned.shape[0]):
        turned[g, :HD] = v_ref[:, g * HD : (g + 1) * HD].T
        turned[g, HD:] = jnp.ones((ONES, turned.shape[2]), turned.dtype)


def lanes_of(tile, j):
    return slice((tile * GROUP + j) * TILE, (tile * GROUP + j + 1) * TILE)


def weigh(q_ref, k_ref, bias_ref, old_top, tile, low, high, g, emit):
    keys = k_ref[low:high, g * HD : (g + 1) * HD]
    heads = range(g * GROUP, (g + 1) * GROUP)
    queries = jnp.concatenate(
        [q_ref[tile * TILE : (tile + 1) * TILE, h * HD : (h + 1) * HD] for h in heads], axis=0
    )
    all_scores = lax.dot_general(
        keys, queries, (((1,), (1,)), ((), ())), preferred_element_type=jnp.float32
    )
    for j in range(GROUP):
        scores = all_scores[:, j * TILE : (j + 1) * TILE] + bias_ref[low:high]
        scores = scores.reshape((high - low) // 8, 8, TILE)
        highest = jnp.max(jnp.max(scores, axis=0), axis=0, keepdims=True)
        top = jnp.broadcast_to(highest, (8, TILE))
        factor = None
        if old_top is not None:
            old = old_top[g, :, lanes_of(tile, j)]
            top = jnp.maximum(old, top)
            factor = jnp.exp2((old - top) * EXP_SCALE)
        weights = jnp.exp2((scores - top[None]) * EXP_SCALE)
        emit(j, weights.reshape(high - low, TILE).astype(jnp.bfloat16), top, factor)


def mix(values, weights, g, tile, old, emit):
    all_added = jnp.dot(values, weights, preferred_element_type=jnp.float32)
    for j in range(GROUP):
        at = lanes_of(tile, j)
        added = all_added[:, j * TILE : (j + 1) * TILE]
        value, total = added[:HD], added[HD : HD + 8]
        if old is not None:
            acc_ref, sum_ref, factor_ref = old
            factor = factor_ref[g, :, at]
            total = total + sum_ref[g, :, at] * factor
            kept = acc_ref[g, :, at].reshape(HD // 8, 8, TILE) * factor[None]
            value = value + kept.reshape(HD, TILE)
        emit(g, j, value, total)


def keep(state, tile):
    def emit(g, j, value, total):
        for ref, array in zip(state, (value, total)):
            ref[g, :, lanes_of(tile, j)] = array

    return emit


def finish(out_ref, row):
    def emit(g, j, value, total):
        head = g * GROUP + j
        value = value.reshape(HD // 8, 8, TILE) * (1.0 / total)[None]
        value = value.reshape(HD, TILE).astype(out_ref.dtype).T
        out_ref[row : row + TILE, head * HD : (head + 1) * HD] = value

    return emit


def block_of(k_ref, v_ref, row):
    parts = []
    for g in range(k_ref.shape[1] // HD):
        span = slice(g * HD, (g + 1) * HD)
        parts += [k_ref[pl.ds(row, BLK), span], v_ref[pl.ds(row, BLK), span]]
    return jnp.concatenate(parts, axis=1)


def own_slot(slot, me, blocks):
    local = slot - me * blocks
    return jnp.where((local >= 0) & (local < blocks), local, blocks)


def own_kernel(
    pre, lengths_ref, slot_ref, q_hbm, k_hbm, v_hbm,
    q_ref, acc_ref, sum_ref, top_ref, cache_ref, *refs,
):
    sent_hbm, (k_ref, v_ref, turned, bias, sent, counts, sems, load_sems) = refs[:-8], refs[-8:]
    loads = [
        pltpu.make_async_copy(src, dst, load_sems.at[n])
        for n, (src, dst) in enumerate(((k_hbm, k_ref), (v_hbm, v_ref), (q_hbm, q_ref)))
    ]
    for load in loads:
        load.start()
    rows = q_ref.shape[0]
    blocks = rows // BLK
    per_peer = blocks // pre
    me = lax.axis_index("pre")
    first = me * rows
    for owner in range(pre):
        counts[owner] = 0
    loads[0].wait()
    loads[1].wait()

    def step(b, _):
        slot = slot_ref[me * blocks + b]
        owner = slot // blocks
        n = counts[owner]
        counts[owner] = n + 1
        distance = lax.rem(owner - me + pre, pre)
        at = jnp.where(distance > 1, (distance - 2) * per_peer + n, (pre - 2) * per_peer)
        block = block_of(k_ref, v_ref, pl.multiple_of(b * BLK, BLK))
        sent[at] = block
        cache_ref[own_slot(slot, me, blocks)] = block
        return 0

    lax.fori_loop(0, blocks, step, 0, unroll=8)
    stores = [
        pltpu.make_async_copy(sent.at[n * per_peer : (n + 1) * per_peer], ref, sems.at[n])
        for n, ref in enumerate(sent_hbm)
    ]
    for store in stores:
        store.start()
    turn_values(v_ref, turned)
    loads[2].wait()
    for tile in range(rows // TILE):
        high = (tile + 1) * TILE
        fill_bias(bias, lengths_ref, first + tile * TILE, first, 0, high, True)
        for g in range(turned.shape[0]):
            all_weights = []

            def emit(j, weights, top, factor):
                all_weights.append(weights)
                top_ref[g, :, lanes_of(tile, j)] = top

            weigh(q_ref, k_ref, bias, None, tile, 0, high, g, emit)
            all_weights = jnp.concatenate(all_weights, axis=1)
            mix(turned[g, :, :high], all_weights, g, tile, None, keep((acc_ref, sum_ref), tile))
    for store in stores:
        store.wait()


def lowest_key(lengths_ref, hop, tile, rows):
    first = lax.axis_index("pre") * rows
    key_first = first - hop * rows
    low = jnp.maximum(start_of(lengths_ref, first + tile * TILE) - key_first, 0)
    return jnp.where(key_first >= 0, jnp.minimum(low, rows), rows)


def where_seen(low, rows, act):
    for at in range(0, rows, TILE):
        pl.when((low >= at) & (low < at + TILE))(functools.partial(act, at))


def scores_kernel(hop, lengths_ref, q_ref, k_ref, old_top, weights_ref, factor_ref, *refs):
    *top_refs, bias = refs
    rows = q_ref.shape[0]
    first = lax.axis_index("pre") * rows
    for tile in range(rows // TILE):

        def act(at):
            fill_bias(
                bias, lengths_ref, first + tile * TILE, first - hop * rows, at, rows, False
            )
            for g in range(weights_ref.shape[1]):

                def emit(j, weights, top, factor):
                    weights_ref[tile, g, at:rows, j * TILE : (j + 1) * TILE] = weights
                    for top_ref in top_refs:
                        top_ref[g, :, lanes_of(tile, j)] = top
                    factor_ref[g, :, lanes_of(tile, j)] = factor

                weigh(q_ref, k_ref, bias, old_top, tile, at, rows, g, emit)

        where_seen(lowest_key(lengths_ref, hop, tile, rows), rows, act)


def place_blocks(cache, slot_ref, k_ref, v_ref, distance, pre, blocks):
    me = lax.axis_index("pre")
    source = lax.rem(me - distance + pre, pre)

    def step(b, _):
        at = own_slot(slot_ref[source * blocks + b], me, blocks)
        cache[at] = block_of(k_ref, v_ref, pl.multiple_of(b * BLK, BLK))
        return 0

    lax.fori_loop(0, blocks, step, 0, unroll=8)


def list_places(places_ref, slot_ref, hops, pre, blocks):
    me = lax.axis_index("pre")
    stride = blocks // pre + 1
    for distance in range(2, pre):
        source = lax.rem(me - distance + pre, pre)

        def step(b, n):
            at = own_slot(slot_ref[source * blocks + b], me, blocks)
            places_ref[(distance - 2) * stride + n] = at
            if distance == hops:
                places_ref[(pre - 2) * stride + n] = b
            return n + jnp.where(at < blocks, 1, 0)

        lax.fori_loop(0, blocks, step, jnp.int32(0), unroll=8)


def place_listed(cache, places_ref, hops, k_ref, v_ref, got_refs):
    me = lax.axis_index("pre")
    per_peer = got_refs[0].shape[0]
    stride = per_peer + 1

    def packed(distance):
        for n in range(per_peer):
            cache[places_ref[(distance - 2) * stride + n]] = got_refs[distance - 2][n]

    def forwarded():
        for n in range(per_peer):
            b = places_ref[len(got_refs) * stride + n]
            at = places_ref[(hops - 2) * stride + n]
            cache[at] = block_of(k_ref, v_ref, pl.multiple_of(b * BLK, BLK))

    for distance in range(2, len(got_refs) + 2):
        if distance > hops:
            packed(distance)
        else:
            pl.when(me < distance)(functools.partial(packed, distance))
    pl.when(me >= hops)(forwarded)


def values_kernel(
    hop, hops, pre, lengths_ref, slot_ref, v_ref, k_ref, weights_ref, factor_ref,
    acc_in, sum_in, cache_in, *refs,
):
    first_out, last = hop == 1, hop == hops
    refs = list(refs)
    if not first_out:
        refs.pop(0)
    got_refs = [refs.pop(0) for _ in range(2, pre)] if last else []
    out_hbm, cache_out = refs.pop(0), refs.pop(0)
    state = () if last else (refs.pop(0), refs.pop(0))
    places_ref = refs.pop(0) if first_out else None
    turned, out_buf, sems, *rest = refs
    rows = v_ref.shape[0]
    blocks = rows // BLK
    tiles = rows // TILE
    kv_count = turned.shape[0]

    cache = rest[0] if last else cache_out
    cache[...] = cache_in[...]
    if last:
        place_listed(cache, slot_ref, hops, k_ref, v_ref, got_refs)
    elif first_out:
        place_blocks(cache, slot_ref, k_ref, v_ref, hop, pre, blocks)
    else:

        @pl.when(lax.axis_index("pre") >= hop)
        def _():
            place_blocks(cache, slot_ref, k_ref, v_ref, hop, pre, blocks)

    if first_out:
        list_places(places_ref, slot_ref, hops, pre, blocks)
    if last:
        cache_store = pltpu.make_async_copy(cache.at[0:blocks], cache_out, sems.at[tiles])
        cache_store.start()

    lows = [lowest_key(lengths_ref, hop, tile, rows) for tile in range(tiles)]
    pl.when(lows[0] < rows)(functools.partial(turn_values, v_ref, turned))
    stores = []
    for tile, low in enumerate(lows):
        end_it = finish(out_buf, tile * TILE)

        def act(at):
            def emit(*result):
                if not last:
                    keep(state, tile)(*result)
                end_it(*result)

            for g in range(kv_count):
                weights = weights_ref[tile, g, at:rows]
                old = (acc_in, sum_in, factor_ref)
                mix(turned[g, :, at:rows], weights, g, tile, old, emit)

        where_seen(low, rows, act)
        span = slice(tile * TILE, (tile + 1) * TILE)
        store = pltpu.make_async_copy(out_buf.at[span], out_hbm.at[span], sems.at[tile])
        stores.append(store)
        if first_out:

            @pl.when(low == rows)
            def _():
                for g in range(kv_count):
                    for j in range(GROUP):
                        end_it(g, j, *(ref[g, :, lanes_of(tile, j)] for ref in (acc_in, sum_in)))

            store.start()
        else:
            pl.when(low < rows)(store.start)
    for low, store in zip(lows, stores):
        if first_out:
            store.wait()
        else:
            pl.when(low < rows)(store.wait)
    if last:
        cache_store.wait()


def on_device(queries, new_keys, new_values, lengths, block_slot):
    rows, q_width = queries.shape
    kv_width = new_keys.shape[1]
    kv_count = kv_width // HD
    blocks = rows // BLK
    pre = lax.axis_size("pre")
    per_peer = blocks // pre
    hops = pre // 2
    tiles = rows // TILE
    bf16, f32 = jnp.bfloat16, jnp.float32
    shape = jax.ShapeDtypeStruct
    params = pltpu.CompilerParams(vmem_limit_bytes=24 * 2**20)
    own_params = pltpu.CompilerParams(vmem_limit_bytes=44 * 2**20)
    ring = [(i, (i + 1) % pre) for i in range(pre)]
    acc_shape = shape((kv_count, HD, GROUP * rows), f32)
    stat_shape = shape((kv_count, 8, GROUP * rows), f32)
    weights_shape = shape((tiles, kv_count, rows, GROUP * TILE), bf16)
    attended_shape = shape(queries.shape, bf16)
    cache_shape = shape((blocks, BLK, 2 * kv_width), bf16)
    open_cache = shape((blocks + 1, BLK, 2 * kv_width), bf16)
    turned = pltpu.VMEM((kv_count, HD + ONES, rows), bf16)
    bias = pltpu.VMEM((rows, TILE), f32)

    def cost(share, moved):
        pairs = int(rows * rows * share)
        return pl.CostEstimate(
            flops=4 * pairs * q_width,
            bytes_accessed=moved * 2**20,
            transcendentals=pairs * kv_count * GROUP,
        )

    def after(array, *others):
        return lax.optimization_barrier((array, *others))[0]

    k, v = lax.ppermute(new_keys, "pre", ring), lax.ppermute(new_values, "pre", ring)

    packed = shape((per_peer, BLK, 2 * kv_width), bf16)
    in_hbm = (
        pltpu.with_memory_space_constraint(x, pltpu.HBM) for x in (queries, new_keys, new_values)
    )
    q, acc, total, top, cache, *sent = pl.pallas_call(
        functools.partial(own_kernel, pre),
        out_shape=(attended_shape, acc_shape, stat_shape, stat_shape, open_cache)
        + (packed,) * (pre - 2),
        in_specs=[SMEM, SMEM] + [HBM] * 3,
        out_specs=(VMEM,) * 5 + (HBM,) * (pre - 2),
        scratch_shapes=[
            pltpu.VMEM((rows, kv_width), bf16),
            pltpu.VMEM((rows, kv_width), bf16),
            turned,
            bias,
            pltpu.VMEM(((pre - 2) * per_peer + 1, BLK, 2 * kv_width), bf16),
            pltpu.SMEM((pre,), jnp.int32),
            pltpu.SemaphoreType.DMA((pre - 2,)),
            pltpu.SemaphoreType.DMA((3,)),
        ],
        cost_estimate=cost(1, 4),
        compiler_params=own_params,
        name="own_attention",
    )(lengths, block_slot, *in_hbm)
    got = []
    k = after(k, top)
    attended = None
    for hop in range(1, hops + 1):
        first_out, last = hop == 1, hop == hops
        onward = [(i, i + 1) for i in range(hop, pre - 1)]
        next_k = None if last else lax.ppermute(k, "pre", onward)
        weights, factor, *tops = pl.pallas_call(
            functools.partial(scores_kernel, hop),
            out_shape=(weights_shape, stat_shape) + (() if last else (stat_shape,)),
            in_specs=[SMEM] + [VMEM] * 3,
            out_specs=(VMEM,) * (2 if last else 3),
            scratch_shapes=[bias],
            cost_estimate=cost(0.5, 3),
            compiler_params=params,
            name="scores",
        )(lengths, q, k, top)
        v = after(v, factor)
        next_v = None if last else lax.ppermute(v, "pre", onward)
        if first_out:
            for d in reversed(range(2, pre)):
                targets = range(d if d <= hops else pre)
                pairs = [((i - d) % pre, i) for i in targets]
                got.insert(0, lax.ppermute(after(sent[d - 2], v), "pre", pairs))
        places = shape(((pre - 1) * (per_peer + 1),), jnp.int32)
        carry = () if last else (acc_shape, stat_shape)
        extra = ([] if first_out else [attended]) + (got if last else [])
        attended, cache, *state = pl.pallas_call(
            functools.partial(values_kernel, hop, hops, pre),
            out_shape=(attended_shape, cache_shape if last else open_cache)
            + carry
            + ((places,) if first_out else ()),
            in_specs=[SMEM, SMEM]
            + [VMEM] * 7
            + ([] if first_out else [HBM])
            + ([VMEM] * len(got) if last else []),
            out_specs=(HBM, HBM if last else VMEM)
            + (VMEM,) * len(carry)
            + ((SMEM,) if first_out else ()),
            scratch_shapes=[
                turned,
                pltpu.VMEM((rows, q_width), bf16),
                pltpu.SemaphoreType.DMA((tiles + 1,)),
            ]
            + ([pltpu.VMEM(open_cache.shape, bf16)] if last else []),
            input_output_aliases={} if first_out else {9: 0},
            cost_estimate=cost(0.5, 3),
            compiler_params=params,
            name="values",
        )(lengths, far_places if last else block_slot, v, k, weights, factor, acc, total, cache, *extra)
        if first_out:
            far_places = state.pop()
        if not last:
            (top,) = tops
            acc, total = state
            k, v = after(next_k, total), next_v

    return (attended, cache)


def solution(mesh):
    placed = (
        P(("parts", "pre"), "tp"),
        P(("parts", "pre"), "tp"),
        P(("parts", "pre"), "tp"),
        P("parts"),
        P("parts"),
    )
    return jax.shard_map(
        on_device,
        mesh=mesh,
        in_specs=placed,
        out_specs=(P(("parts", "pre"), "tp"), P(("parts", "pre"), None, "tp")),
        check_vma=False,
    )
```

```python
import functools
import math

import jax
import jax.numpy as jnp
from jax import lax
from jax.experimental import pallas as pl
from jax.experimental.pallas import tpu as pltpu
from jax.sharding import PartitionSpec as P

HD = 128
BLK = 16
GROUP = 4
TILE = 256
ONES = 16
MASKED = -1e30
EXP_SCALE = math.log2(math.e) * HD ** (-0.5)

VMEM = pl.BlockSpec(memory_space=pltpu.VMEM)
SMEM = pl.BlockSpec(memory_space=pltpu.SMEM)
HBM = pl.BlockSpec(memory_space=pltpu.HBM)


def start_of(lengths_ref, position):
    end = jnp.int32(0)
    start = jnp.int32(0)
    for r in range(lengths_ref.shape[0]):
        end = end + lengths_ref[r]
        start = jnp.where(end <= position, end, start)
    return start


def row_starts(lengths_ref, positions):
    end = jnp.int32(0)
    starts = jnp.zeros_like(positions)
    for r in range(lengths_ref.shape[0]):
        end = end + lengths_ref[r]
        starts = jnp.where(positions >= end, end, starts)
    return starts


def fill_bias(bias_ref, lengths_ref, row_first, key_first, low, high, causal):
    shape = (high - low, TILE)
    positions = row_first + lax.broadcasted_iota(jnp.int32, (8, TILE), 1)
    starts = row_starts(lengths_ref, positions)
    keys = key_first + low + lax.broadcasted_iota(jnp.int32, shape, 0)
    keys = keys.reshape((high - low) // 8, 8, TILE)
    allowed = keys >= starts[None]
    if causal:
        allowed = allowed & (keys <= positions[None])
    bias_ref[low:high] = jnp.where(allowed, 0.0, MASKED).reshape(shape)


def turn_values(v_ref, turned):
    for g in range(turned.shape[0]):
        turned[g, :HD] = v_ref[:, g * HD : (g + 1) * HD].T
        turned[g, HD:] = jnp.ones((ONES, turned.shape[2]), turned.dtype)


def lanes_of(tile, j):
    return slice((tile * GROUP + j) * TILE, (tile * GROUP + j + 1) * TILE)


def weigh(q_ref, k_ref, bias_ref, old_top, tile, low, high, g, emit):
    keys = k_ref[low:high, g * HD : (g + 1) * HD]
    heads = range(g * GROUP, (g + 1) * GROUP)
    queries = jnp.concatenate(
        [q_ref[tile * TILE : (tile + 1) * TILE, h * HD : (h + 1) * HD] for h in heads], axis=0
    )
    all_scores = lax.dot_general(
        keys, queries, (((1,), (1,)), ((), ())), preferred_element_type=jnp.float32
    )
    for j in range(GROUP):
        scores = all_scores[:, j * TILE : (j + 1) * TILE] + bias_ref[low:high]
        scores = scores.reshape((high - low) // 8, 8, TILE)
        highest = jnp.max(jnp.max(scores, axis=0), axis=0, keepdims=True)
        top = jnp.broadcast_to(highest, (8, TILE))
        factor = None
        if old_top is not None:
            old = old_top[g, :, lanes_of(tile, j)]
            top = jnp.maximum(old, top)
            factor = jnp.exp2((old - top) * EXP_SCALE)
        weights = jnp.exp2((scores - top[None]) * EXP_SCALE)
        emit(j, weights.reshape(high - low, TILE).astype(jnp.bfloat16), top, factor)


def mix(values, weights, g, tile, old, emit):
    all_added = jnp.dot(values, weights, preferred_element_type=jnp.float32)
    for j in range(GROUP):
        at = lanes_of(tile, j)
        added = all_added[:, j * TILE : (j + 1) * TILE]
        value, total = added[:HD], added[HD : HD + 8]
        if old is not None:
            acc_ref, sum_ref, factor_ref = old
            factor = factor_ref[g, :, at]
            total = total + sum_ref[g, :, at] * factor
            kept = acc_ref[g, :, at].reshape(HD // 8, 8, TILE) * factor[None]
            value = value + kept.reshape(HD, TILE)
        emit(g, j, value, total)


def keep(state, tile):
    def emit(g, j, value, total):
        for ref, array in zip(state, (value, total)):
            ref[g, :, lanes_of(tile, j)] = array

    return emit


def finish(out_ref, row):
    def emit(g, j, value, total):
        head = g * GROUP + j
        value = value.reshape(HD // 8, 8, TILE) * (1.0 / total)[None]
        value = value.reshape(HD, TILE).astype(out_ref.dtype).T
        out_ref[row : row + TILE, head * HD : (head + 1) * HD] = value

    return emit


def block_of(k_ref, v_ref, row):
    parts = []
    for g in range(k_ref.shape[1] // HD):
        span = slice(g * HD, (g + 1) * HD)
        parts += [k_ref[pl.ds(row, BLK), span], v_ref[pl.ds(row, BLK), span]]
    return jnp.concatenate(parts, axis=1)


def own_slot(slot, me, blocks):
    local = slot - me * blocks
    return jnp.where((local >= 0) & (local < blocks), local, blocks)


def own_kernel(
    pre, lengths_ref, slot_ref, q_hbm, k_hbm, v_hbm,
    q_ref, acc_ref, sum_ref, top_ref, cache_ref, *refs,
):
    sent_hbm, (k_ref, v_ref, turned, bias, sent, counts, sems, load_sems) = refs[:-8], refs[-8:]
    loads = [
        pltpu.make_async_copy(src, dst, load_sems.at[n])
        for n, (src, dst) in enumerate(((k_hbm, k_ref), (v_hbm, v_ref), (q_hbm, q_ref)))
    ]
    for load in loads:
        load.start()
    rows = q_ref.shape[0]
    blocks = rows // BLK
    per_peer = blocks // pre
    me = lax.axis_index("pre")
    first = me * rows
    for owner in range(pre):
        counts[owner] = 0
    loads[0].wait()
    loads[1].wait()

    def step(b, _):
        slot = slot_ref[me * blocks + b]
        owner = slot // blocks
        n = counts[owner]
        counts[owner] = n + 1
        distance = lax.rem(owner - me + pre, pre)
        at = jnp.where(distance > 1, (distance - 2) * per_peer + n, (pre - 2) * per_peer)
        block = block_of(k_ref, v_ref, pl.multiple_of(b * BLK, BLK))
        sent[at] = block
        cache_ref[own_slot(slot, me, blocks)] = block
        return 0

    lax.fori_loop(0, blocks, step, 0, unroll=8)
    stores = [
        pltpu.make_async_copy(sent.at[n * per_peer : (n + 1) * per_peer], ref, sems.at[n])
        for n, ref in enumerate(sent_hbm)
    ]
    for store in stores:
        store.start()
    turn_values(v_ref, turned)
    loads[2].wait()
    for tile in range(rows // TILE):
        high = (tile + 1) * TILE
        fill_bias(bias, lengths_ref, first + tile * TILE, first, 0, high, True)
        for g in range(turned.shape[0]):
            all_weights = []

            def emit(j, weights, top, factor):
                all_weights.append(weights)
                top_ref[g, :, lanes_of(tile, j)] = top

            weigh(q_ref, k_ref, bias, None, tile, 0, high, g, emit)
            all_weights = jnp.concatenate(all_weights, axis=1)
            mix(turned[g, :, :high], all_weights, g, tile, None, keep((acc_ref, sum_ref), tile))
    for store in stores:
        store.wait()


def lowest_key(lengths_ref, hop, tile, rows):
    first = lax.axis_index("pre") * rows
    key_first = first - hop * rows
    low = jnp.maximum(start_of(lengths_ref, first + tile * TILE) - key_first, 0)
    return jnp.where(key_first >= 0, jnp.minimum(low, rows), rows)


def where_seen(low, rows, act):
    for at in range(0, rows, TILE):
        pl.when((low >= at) & (low < at + TILE))(functools.partial(act, at))


def scores_kernel(hop, lengths_ref, q_ref, k_ref, old_top, weights_ref, factor_ref, *refs):
    *top_refs, bias = refs
    rows = q_ref.shape[0]
    first = lax.axis_index("pre") * rows
    for tile in range(rows // TILE):

        def act(at):
            fill_bias(
                bias, lengths_ref, first + tile * TILE, first - hop * rows, at, rows, False
            )
            for g in range(weights_ref.shape[1]):

                def emit(j, weights, top, factor):
                    weights_ref[tile, g, at:rows, j * TILE : (j + 1) * TILE] = weights
                    for top_ref in top_refs:
                        top_ref[g, :, lanes_of(tile, j)] = top
                    factor_ref[g, :, lanes_of(tile, j)] = factor

                weigh(q_ref, k_ref, bias, old_top, tile, at, rows, g, emit)

        where_seen(lowest_key(lengths_ref, hop, tile, rows), rows, act)


def place_blocks(cache, slot_ref, k_ref, v_ref, distance, pre, blocks):
    me = lax.axis_index("pre")
    source = lax.rem(me - distance + pre, pre)

    def step(b, _):
        at = own_slot(slot_ref[source * blocks + b], me, blocks)
        cache[at] = block_of(k_ref, v_ref, pl.multiple_of(b * BLK, BLK))
        return 0

    lax.fori_loop(0, blocks, step, 0, unroll=8)


def list_places(places_ref, slot_ref, hops, pre, blocks):
    me = lax.axis_index("pre")
    stride = blocks // pre + 1
    for distance in range(2, pre):
        source = lax.rem(me - distance + pre, pre)

        def step(b, n):
            at = own_slot(slot_ref[source * blocks + b], me, blocks)
            places_ref[(distance - 2) * stride + n] = at
            if distance == hops:
                places_ref[(pre - 2) * stride + n] = b
            return n + jnp.where(at < blocks, 1, 0)

        lax.fori_loop(0, blocks, step, jnp.int32(0), unroll=8)


def place_listed(cache, places_ref, hops, k_ref, v_ref, got_refs):
    me = lax.axis_index("pre")
    per_peer = got_refs[0].shape[0]
    stride = per_peer + 1

    def packed(distance):
        for n in range(per_peer):
            cache[places_ref[(distance - 2) * stride + n]] = got_refs[distance - 2][n]

    def forwarded():
        for n in range(per_peer):
            b = places_ref[len(got_refs) * stride + n]
            at = places_ref[(hops - 2) * stride + n]
            cache[at] = block_of(k_ref, v_ref, pl.multiple_of(b * BLK, BLK))

    for distance in range(2, len(got_refs) + 2):
        if distance > hops:
            packed(distance)
        else:
            pl.when(me < distance)(functools.partial(packed, distance))
    pl.when(me >= hops)(forwarded)


def values_kernel(
    hop, hops, pre, lengths_ref, slot_ref, v_ref, k_ref, weights_ref, factor_ref,
    acc_in, sum_in, cache_in, *refs,
):
    first_out, last = hop == 1, hop == hops
    refs = list(refs)
    if not first_out:
        refs.pop(0)
    got_refs = [refs.pop(0) for _ in range(2, pre)][::-1] if last else []
    out_hbm, cache_out = refs.pop(0), refs.pop(0)
    state = () if last else (refs.pop(0), refs.pop(0))
    places_ref = refs.pop(0) if first_out else None
    turned, out_buf, sems, *rest = refs
    rows = v_ref.shape[0]
    blocks = rows // BLK
    tiles = rows // TILE
    kv_count = turned.shape[0]

    cache = rest[0] if last else cache_out
    cache[...] = cache_in[...]
    if last:
        place_listed(cache, slot_ref, hops, k_ref, v_ref, got_refs)
    elif first_out:
        place_blocks(cache, slot_ref, k_ref, v_ref, hop, pre, blocks)
    else:

        @pl.when(lax.axis_index("pre") >= hop)
        def _():
            place_blocks(cache, slot_ref, k_ref, v_ref, hop, pre, blocks)

    if first_out:
        list_places(places_ref, slot_ref, hops, pre, blocks)
    if last:
        cache_store = pltpu.make_async_copy(cache.at[0:blocks], cache_out, sems.at[tiles])
        cache_store.start()

    lows = [lowest_key(lengths_ref, hop, tile, rows) for tile in range(tiles)]
    pl.when(lows[0] < rows)(functools.partial(turn_values, v_ref, turned))
    stores = []
    for tile, low in enumerate(lows):
        end_it = finish(out_buf, tile * TILE)

        def act(at):
            def emit(*result):
                if not last:
                    keep(state, tile)(*result)
                end_it(*result)

            for g in range(kv_count):
                weights = weights_ref[tile, g, at:rows]
                old = (acc_in, sum_in, factor_ref)
                mix(turned[g, :, at:rows], weights, g, tile, old, emit)

        where_seen(low, rows, act)
        span = slice(tile * TILE, (tile + 1) * TILE)
        store = pltpu.make_async_copy(out_buf.at[span], out_hbm.at[span], sems.at[tile])
        stores.append(store)
        if first_out:

            @pl.when(low == rows)
            def _():
                for g in range(kv_count):
                    for j in range(GROUP):
                        end_it(g, j, *(ref[g, :, lanes_of(tile, j)] for ref in (acc_in, sum_in)))

            store.start()
        else:
            pl.when(low < rows)(store.start)
    for low, store in zip(lows, stores):
        if first_out:
            store.wait()
        else:
            pl.when(low < rows)(store.wait)
    if last:
        cache_store.wait()


def on_device(queries, new_keys, new_values, lengths, block_slot):
    rows, q_width = queries.shape
    kv_width = new_keys.shape[1]
    kv_count = kv_width // HD
    blocks = rows // BLK
    pre = lax.axis_size("pre")
    per_peer = blocks // pre
    hops = pre // 2
    tiles = rows // TILE
    bf16, f32 = jnp.bfloat16, jnp.float32
    shape = jax.ShapeDtypeStruct
    params = pltpu.CompilerParams(vmem_limit_bytes=24 * 2**20)
    own_params = pltpu.CompilerParams(vmem_limit_bytes=44 * 2**20)
    ring = [(i, (i + 1) % pre) for i in range(pre)]
    acc_shape = shape((kv_count, HD, GROUP * rows), f32)
    stat_shape = shape((kv_count, 8, GROUP * rows), f32)
    weights_shape = shape((tiles, kv_count, rows, GROUP * TILE), bf16)
    attended_shape = shape(queries.shape, bf16)
    cache_shape = shape((blocks, BLK, 2 * kv_width), bf16)
    open_cache = shape((blocks + 1, BLK, 2 * kv_width), bf16)
    turned = pltpu.VMEM((kv_count, HD + ONES, rows), bf16)
    bias = pltpu.VMEM((rows, TILE), f32)

    def cost(share, moved):
        pairs = int(rows * rows * share)
        return pl.CostEstimate(
            flops=4 * pairs * q_width,
            bytes_accessed=moved * 2**20,
            transcendentals=pairs * kv_count * GROUP,
        )

    def after(array, *others):
        return lax.optimization_barrier((array, *others))[0]

    k, v = lax.ppermute(new_keys, "pre", ring), lax.ppermute(new_values, "pre", ring)

    packed = shape((per_peer, BLK, 2 * kv_width), bf16)
    in_hbm = (
        pltpu.with_memory_space_constraint(x, pltpu.HBM) for x in (queries, new_keys, new_values)
    )
    q, acc, total, top, cache, *sent = pl.pallas_call(
        functools.partial(own_kernel, pre),
        out_shape=(attended_shape, acc_shape, stat_shape, stat_shape, open_cache)
        + (packed,) * (pre - 2),
        in_specs=[SMEM, SMEM] + [HBM] * 3,
        out_specs=(VMEM,) * 5 + (HBM,) * (pre - 2),
        scratch_shapes=[
            pltpu.VMEM((rows, kv_width), bf16),
            pltpu.VMEM((rows, kv_width), bf16),
            turned,
            bias,
            pltpu.VMEM(((pre - 2) * per_peer + 1, BLK, 2 * kv_width), bf16),
            pltpu.SMEM((pre,), jnp.int32),
            pltpu.SemaphoreType.DMA((pre - 2,)),
            pltpu.SemaphoreType.DMA((3,)),
        ],
        cost_estimate=cost(1, 4),
        compiler_params=own_params,
        name="own_attention",
    )(lengths, block_slot, *in_hbm)
    got = []
    k = after(k, top)
    attended = None
    for hop in range(1, hops + 1):
        first_out, last = hop == 1, hop == hops
        onward = [(i, i + 1) for i in range(hop, pre - 1)]
        next_k = None if last else lax.ppermute(k, "pre", onward)
        weights, factor, *tops = pl.pallas_call(
            functools.partial(scores_kernel, hop),
            out_shape=(weights_shape, stat_shape) + (() if last else (stat_shape,)),
            in_specs=[SMEM] + [VMEM] * 3,
            out_specs=(VMEM,) * (2 if last else 3),
            scratch_shapes=[bias],
            cost_estimate=cost(0.5, 3),
            compiler_params=params,
            name="scores",
        )(lengths, q, k, top)
        v = after(v, factor)
        next_v = None if last else lax.ppermute(v, "pre", onward)
        if first_out:
            for d in reversed(range(2, pre)):
                targets = range(d if d <= hops else pre)
                pairs = [((i - d) % pre, i) for i in targets]
                got.insert(0, lax.ppermute(after(sent[d - 2], v), "pre", pairs))
        places = shape(((pre - 1) * (per_peer + 1),), jnp.int32)
        carry = () if last else (acc_shape, stat_shape)
        extra = ([] if first_out else [attended]) + (got[::-1] if last else [])
        attended, cache, *state = pl.pallas_call(
            functools.partial(values_kernel, hop, hops, pre),
            out_shape=(attended_shape, cache_shape if last else open_cache)
            + carry
            + ((places,) if first_out else ()),
            in_specs=[SMEM, SMEM]
            + [VMEM] * 7
            + ([] if first_out else [HBM])
            + ([VMEM] * len(got) if last else []),
            out_specs=(HBM, HBM if last else VMEM)
            + (VMEM,) * len(carry)
            + ((SMEM,) if first_out else ()),
            scratch_shapes=[
                turned,
                pltpu.VMEM((rows, q_width), bf16),
                pltpu.SemaphoreType.DMA((tiles + 1,)),
            ]
            + ([pltpu.VMEM(open_cache.shape, bf16)] if last else []),
            input_output_aliases={} if first_out else {9: 0},
            cost_estimate=cost(0.5, 3),
            compiler_params=params,
            name="values",
        )(lengths, far_places if last else block_slot, v, k, weights, factor, acc, total, cache, *extra)
        if first_out:
            far_places = state.pop()
        if not last:
            (top,) = tops
            acc, total = state
            k, v = after(next_k, total), next_v

    return (attended, cache)


def solution(mesh):
    placed = (
        P(("parts", "pre"), "tp"),
        P(("parts", "pre"), "tp"),
        P(("parts", "pre"), "tp"),
        P("parts"),
        P("parts"),
    )
    return jax.shard_map(
        on_device,
        mesh=mesh,
        in_specs=placed,
        out_specs=(P(("parts", "pre"), "tp"), P(("parts", "pre"), None, "tp")),
        check_vma=False,
    )
```

```python
import functools
import math

import jax
import jax.numpy as jnp
from jax import lax
from jax.experimental import pallas as pl
from jax.experimental.pallas import tpu as pltpu
from jax.sharding import PartitionSpec as P

HD = 128
BLK = 16
GROUP = 4
TILE = 256
ONES = 16
MASKED = -1e30
EXP_SCALE = math.log2(math.e) * HD ** (-0.5)

VMEM = pl.BlockSpec(memory_space=pltpu.VMEM)
SMEM = pl.BlockSpec(memory_space=pltpu.SMEM)
HBM = pl.BlockSpec(memory_space=pltpu.HBM)


def start_of(lengths_ref, position):
    end = jnp.int32(0)
    start = jnp.int32(0)
    for r in range(lengths_ref.shape[0]):
        end = end + lengths_ref[r]
        start = jnp.where(end <= position, end, start)
    return start


def row_starts(lengths_ref, positions):
    end = jnp.int32(0)
    starts = jnp.zeros_like(positions)
    for r in range(lengths_ref.shape[0]):
        end = end + lengths_ref[r]
        starts = jnp.where(positions >= end, end, starts)
    return starts


def fill_bias(bias_ref, lengths_ref, row_first, key_first, low, high, causal):
    shape = (high - low, TILE)
    positions = row_first + lax.broadcasted_iota(jnp.int32, (8, TILE), 1)
    starts = row_starts(lengths_ref, positions)
    keys = key_first + low + lax.broadcasted_iota(jnp.int32, shape, 0)
    keys = keys.reshape((high - low) // 8, 8, TILE)
    allowed = keys >= starts[None]
    if causal:
        allowed = allowed & (keys <= positions[None])
    bias_ref[low:high] = jnp.where(allowed, 0.0, MASKED).reshape(shape)


def turn_values(v_ref, turned):
    for g in range(turned.shape[0]):
        turned[g, :HD] = v_ref[:, g * HD : (g + 1) * HD].T
        turned[g, HD:] = jnp.ones((ONES, turned.shape[2]), turned.dtype)


def lanes_of(tile, j):
    return slice((tile * GROUP + j) * TILE, (tile * GROUP + j + 1) * TILE)


def weigh(q_ref, k_ref, bias_ref, old_top, tile, low, high, g, emit):
    keys = k_ref[low:high, g * HD : (g + 1) * HD]
    heads = range(g * GROUP, (g + 1) * GROUP)
    queries = jnp.concatenate(
        [q_ref[tile * TILE : (tile + 1) * TILE, h * HD : (h + 1) * HD] for h in heads], axis=0
    )
    all_scores = lax.dot_general(
        keys, queries, (((1,), (1,)), ((), ())), preferred_element_type=jnp.float32
    )
    for j in range(GROUP):
        scores = all_scores[:, j * TILE : (j + 1) * TILE] + bias_ref[low:high]
        scores = scores.reshape((high - low) // 8, 8, TILE)
        highest = jnp.max(jnp.max(scores, axis=0), axis=0, keepdims=True)
        top = jnp.broadcast_to(highest, (8, TILE))
        factor = None
        if old_top is not None:
            old = old_top[g, :, lanes_of(tile, j)]
            top = jnp.maximum(old, top)
            factor = jnp.exp2((old - top) * EXP_SCALE)
        weights = jnp.exp2((scores - top[None]) * EXP_SCALE)
        emit(j, weights.reshape(high - low, TILE).astype(jnp.bfloat16), top, factor)


def mix(values, weights, g, tile, old, emit):
    all_added = jnp.dot(values, weights, preferred_element_type=jnp.float32)
    for j in range(GROUP):
        at = lanes_of(tile, j)
        added = all_added[:, j * TILE : (j + 1) * TILE]
        value, total = added[:HD], added[HD : HD + 8]
        if old is not None:
            acc_ref, sum_ref, factor_ref = old
            factor = factor_ref[g, :, at]
            total = total + sum_ref[g, :, at] * factor
            kept = acc_ref[g, :, at].reshape(HD // 8, 8, TILE) * factor[None]
            value = value + kept.reshape(HD, TILE)
        emit(g, j, value, total)


def keep(state, tile):
    def emit(g, j, value, total):
        for ref, array in zip(state, (value, total)):
            ref[g, :, lanes_of(tile, j)] = array

    return emit


def finish(out_ref, row):
    def emit(g, j, value, total):
        head = g * GROUP + j
        value = value.reshape(HD // 8, 8, TILE) * (1.0 / total)[None]
        value = value.reshape(HD, TILE).astype(out_ref.dtype).T
        out_ref[row : row + TILE, head * HD : (head + 1) * HD] = value

    return emit


def block_of(k_ref, v_ref, row):
    parts = []
    for g in range(k_ref.shape[1] // HD):
        span = slice(g * HD, (g + 1) * HD)
        parts += [k_ref[pl.ds(row, BLK), span], v_ref[pl.ds(row, BLK), span]]
    return jnp.concatenate(parts, axis=1)


def own_slot(slot, me, blocks):
    local = slot - me * blocks
    return jnp.where((local >= 0) & (local < blocks), local, blocks)


def list_places(places_ref, slot_ref, hops, pre, blocks):
    me = lax.axis_index("pre")
    stride = blocks // pre + 1
    for distance in range(2, pre):
        source = lax.rem(me - distance + pre, pre)

        def step(b, n):
            at = own_slot(slot_ref[source * blocks + b], me, blocks)
            places_ref[(distance - 2) * stride + n] = at
            if distance <= hops:
                places_ref[(pre - 2 + distance - 2) * stride + n] = b
            return n + jnp.where(at < blocks, 1, 0)

        lax.fori_loop(0, blocks, step, jnp.int32(0), unroll=8)


def own_kernel(
    pre, hops, lengths_ref, slot_ref, q_hbm, k_hbm, v_hbm,
    q_ref, acc_ref, sum_ref, top_ref, cache_ref, places_ref, *refs,
):
    sent_hbm, refs = refs[: pre - 2], refs[pre - 2 :]
    k_ref, v_ref, turned, bias, sent_values, sent, counts, sems, load_sems = refs
    loads = [
        pltpu.make_async_copy(src, dst, load_sems.at[n])
        for n, (src, dst) in enumerate(((k_hbm, k_ref), (v_hbm, v_ref), (q_hbm, q_ref)))
    ]
    for load in loads:
        load.start()
    rows = q_ref.shape[0]
    blocks = rows // BLK
    per_peer = blocks // pre
    me = lax.axis_index("pre")
    first = me * rows
    for owner in range(pre):
        counts[owner] = 0
    list_places(places_ref, slot_ref, hops, pre, blocks)
    loads[0].wait()
    loads[1].wait()

    def step(b, _):
        slot = slot_ref[me * blocks + b]
        owner = slot // blocks
        n = counts[owner]
        counts[owner] = n + 1
        distance = lax.rem(owner - me + pre, pre)
        row = pl.multiple_of(b * BLK, BLK)
        on_ring = (distance > 1) & (distance <= hops)
        at = jnp.where(on_ring, (distance - 2) * per_peer + n, (hops - 1) * per_peer)
        sent_values[at] = v_ref[pl.ds(row, BLK)]
        beyond = (distance - hops - 1) * per_peer + n
        at = jnp.where(distance > hops, beyond, (pre - 1 - hops) * per_peer)
        block = block_of(k_ref, v_ref, row)
        sent[at] = block
        cache_ref[own_slot(slot, me, blocks)] = block
        return 0

    lax.fori_loop(0, blocks, step, 0, unroll=4)
    packed = [sent_values.at[n * per_peer : (n + 1) * per_peer] for n in range(hops - 1)]
    packed += [sent.at[n * per_peer : (n + 1) * per_peer] for n in range(pre - 1 - hops)]
    stores = [
        pltpu.make_async_copy(src, dst, sems.at[n])
        for n, (src, dst) in enumerate(zip(packed, sent_hbm))
    ]
    for store in stores:
        store.start()
    turn_values(v_ref, turned)
    loads[2].wait()
    for tile in range(rows // TILE):
        high = (tile + 1) * TILE
        fill_bias(bias, lengths_ref, first + tile * TILE, first, 0, high, True)
        for g in range(turned.shape[0]):
            all_weights = []

            def emit(j, weights, top, factor):
                all_weights.append(weights)
                top_ref[g, :, lanes_of(tile, j)] = top

            weigh(q_ref, k_ref, bias, None, tile, 0, high, g, emit)
            all_weights = jnp.concatenate(all_weights, axis=1)
            mix(turned[g, :, :high], all_weights, g, tile, None, keep((acc_ref, sum_ref), tile))
    for store in stores:
        store.wait()


def lowest_key(lengths_ref, hop, tile, rows):
    first = lax.axis_index("pre") * rows
    key_first = first - hop * rows
    low = jnp.maximum(start_of(lengths_ref, first + tile * TILE) - key_first, 0)
    return jnp.where(key_first >= 0, jnp.minimum(low, rows), rows)


def where_seen(low, rows, act):
    for at in range(0, rows, TILE):
        pl.when((low >= at) & (low < at + TILE))(functools.partial(act, at))


def scores_kernel(hop, lengths_ref, q_ref, k_ref, old_top, weights_ref, factor_ref, *refs):
    *top_refs, bias = refs
    rows = q_ref.shape[0]
    first = lax.axis_index("pre") * rows
    for tile in range(rows // TILE):

        def act(at):
            fill_bias(
                bias, lengths_ref, first + tile * TILE, first - hop * rows, at, rows, False
            )
            for g in range(weights_ref.shape[1]):

                def emit(j, weights, top, factor):
                    weights_ref[tile, g, at:rows, j * TILE : (j + 1) * TILE] = weights
                    for top_ref in top_refs:
                        top_ref[g, :, lanes_of(tile, j)] = top
                    factor_ref[g, :, lanes_of(tile, j)] = factor

                weigh(q_ref, k_ref, bias, old_top, tile, at, rows, g, emit)

        where_seen(lowest_key(lengths_ref, hop, tile, rows), rows, act)


def place_blocks(cache, slot_ref, k_ref, v_ref, distance, pre, blocks):
    me = lax.axis_index("pre")
    source = lax.rem(me - distance + pre, pre)

    def step(b, _):
        at = own_slot(slot_ref[source * blocks + b], me, blocks)
        cache[at] = block_of(k_ref, v_ref, pl.multiple_of(b * BLK, BLK))
        return 0

    lax.fori_loop(0, blocks, step, 0, unroll=8)


def place_listed(cache, places_ref, hop, pre, k_ref, v_ref, got_ref):
    me = lax.axis_index("pre")
    per_peer = got_ref.shape[0]
    stride = per_peer + 1

    def place(values_at):
        for n in range(per_peer):
            at = places_ref[(hop - 2) * stride + n]
            b = places_ref[(pre - 2 + hop - 2) * stride + n]
            rows = pl.ds(pl.multiple_of(b * BLK, BLK), BLK)
            values = values_at(n, rows)
            parts = []
            for g in range(k_ref.shape[1] // HD):
                span = slice(g * HD, (g + 1) * HD)
                parts += [k_ref[rows, span], values[:, span]]
            cache[at] = jnp.concatenate(parts, axis=1)

    pl.when(me >= hop)(lambda: place(lambda n, rows: v_ref[rows]))
    pl.when(me < hop)(lambda: place(lambda n, rows: got_ref[n]))


def place_packed(cache, places_ref, distance, got_ref):
    per_peer = got_ref.shape[0]
    for n in range(per_peer):
        cache[places_ref[(distance - 2) * (per_peer + 1) + n]] = got_ref[n]


def values_kernel(
    hop, hops, pre, lengths_ref, slot_ref, v_ref, k_ref, weights_ref, factor_ref,
    acc_in, sum_in, cache_in, *refs,
):
    first_out, last = hop == 1, hop == hops
    refs = list(refs)
    if not first_out:
        refs.pop(0)
    got_far = [refs.pop(0) for _ in range(hops + 1, pre)][::-1] if last else []
    got_ref = None if first_out else refs.pop(0)
    out_hbm, cache_out = refs.pop(0), refs.pop(0)
    state = () if last else (refs.pop(0), refs.pop(0))
    turned, out_buf, sems, *rest = refs
    rows = v_ref.shape[0]
    blocks = rows // BLK
    tiles = rows // TILE
    kv_count = turned.shape[0]

    cache = rest[0] if last else cache_out
    cache[...] = cache_in[...]
    if first_out:
        place_blocks(cache, slot_ref, k_ref, v_ref, hop, pre, blocks)
    else:
        place_listed(cache, slot_ref, hop, pre, k_ref, v_ref, got_ref)
    if last:
        for n, far_ref in enumerate(got_far):
            place_packed(cache, slot_ref, hops + 1 + n, far_ref)
        cache_store = pltpu.make_async_copy(cache.at[0:blocks], cache_out, sems.at[tiles])
        cache_store.start()

    lows = [lowest_key(lengths_ref, hop, tile, rows) for tile in range(tiles)]
    pl.when(lows[0] < rows)(functools.partial(turn_values, v_ref, turned))
    stores = []
    for tile, low in enumerate(lows):
        end_it = finish(out_buf, tile * TILE)

        def act(at):
            def emit(*result):
                if not last:
                    keep(state, tile)(*result)
                end_it(*result)

            for g in range(kv_count):
                weights = weights_ref[tile, g, at:rows]
                old = (acc_in, sum_in, factor_ref)
                mix(turned[g, :, at:rows], weights, g, tile, old, emit)

        where_seen(low, rows, act)
        span = slice(tile * TILE, (tile + 1) * TILE)
        store = pltpu.make_async_copy(out_buf.at[span], out_hbm.at[span], sems.at[tile])
        stores.append(store)
        if first_out:

            @pl.when(low == rows)
            def _():
                for g in range(kv_count):
                    for j in range(GROUP):
                        end_it(g, j, *(ref[g, :, lanes_of(tile, j)] for ref in (acc_in, sum_in)))

            store.start()
        else:
            pl.when(low < rows)(store.start)
    for low, store in zip(lows, stores):
        if first_out:
            store.wait()
        else:
            pl.when(low < rows)(store.wait)
    if last:
        cache_store.wait()


def on_device(queries, new_keys, new_values, lengths, block_slot):
    rows, q_width = queries.shape
    kv_width = new_keys.shape[1]
    kv_count = kv_width // HD
    blocks = rows // BLK
    pre = lax.axis_size("pre")
    per_peer = blocks // pre
    hops = pre // 2
    tiles = rows // TILE
    bf16, f32 = jnp.bfloat16, jnp.float32
    shape = jax.ShapeDtypeStruct
    params = pltpu.CompilerParams(vmem_limit_bytes=24 * 2**20)
    own_params = pltpu.CompilerParams(vmem_limit_bytes=44 * 2**20)
    ring = [(i, (i + 1) % pre) for i in range(pre)]
    acc_shape = shape((kv_count, HD, GROUP * rows), f32)
    stat_shape = shape((kv_count, 8, GROUP * rows), f32)
    weights_shape = shape((tiles, kv_count, rows, GROUP * TILE), bf16)
    attended_shape = shape(queries.shape, bf16)
    cache_shape = shape((blocks, BLK, 2 * kv_width), bf16)
    open_cache = shape((blocks + 1, BLK, 2 * kv_width), bf16)
    turned = pltpu.VMEM((kv_count, HD + ONES, rows), bf16)
    bias = pltpu.VMEM((rows, TILE), f32)

    def cost(share, moved):
        pairs = int(rows * rows * share)
        return pl.CostEstimate(
            flops=4 * pairs * q_width,
            bytes_accessed=moved * 2**20,
            transcendentals=pairs * kv_count * GROUP,
        )

    def after(array, *others):
        return lax.optimization_barrier((array, *others))[0]

    k, v = lax.ppermute(new_keys, "pre", ring), lax.ppermute(new_values, "pre", ring)

    packed = (shape((per_peer, BLK, kv_width), bf16),) * (hops - 1)
    packed += (shape((per_peer, BLK, 2 * kv_width), bf16),) * (pre - 1 - hops)
    places = shape(((pre - 2 + hops - 1) * (per_peer + 1),), jnp.int32)
    in_hbm = (
        pltpu.with_memory_space_constraint(x, pltpu.HBM) for x in (queries, new_keys, new_values)
    )
    q, acc, total, top, cache, places, *sent = pl.pallas_call(
        functools.partial(own_kernel, pre, hops),
        out_shape=(attended_shape, acc_shape, stat_shape, stat_shape, open_cache, places)
        + packed,
        in_specs=[SMEM, SMEM] + [HBM] * 3,
        out_specs=(VMEM,) * 5 + (SMEM,) + (HBM,) * (pre - 2),
        scratch_shapes=[
            pltpu.VMEM((rows, kv_width), bf16),
            pltpu.VMEM((rows, kv_width), bf16),
            turned,
            bias,
            pltpu.VMEM(((hops - 1) * per_peer + 1, BLK, kv_width), bf16),
            pltpu.VMEM(((pre - 1 - hops) * per_peer + 1, BLK, 2 * kv_width), bf16),
            pltpu.SMEM((pre,), jnp.int32),
            pltpu.SemaphoreType.DMA((pre - 2,)),
            pltpu.SemaphoreType.DMA((3,)),
        ],
        cost_estimate=cost(1, 4),
        compiler_params=own_params,
        name="own_attention",
    )(lengths, block_slot, *in_hbm)
    got = []
    k = after(k, top)
    attended = None
    for hop in range(1, hops + 1):
        first_out, last = hop == 1, hop == hops
        onward = [(i, i + 1) for i in range(hop, pre - 1)]
        next_k = None if last else lax.ppermute(k, "pre", ring)
        weights, factor, *tops = pl.pallas_call(
            functools.partial(scores_kernel, hop),
            out_shape=(weights_shape, stat_shape) + (() if last else (stat_shape,)),
            in_specs=[SMEM] + [VMEM] * 3,
            out_specs=(VMEM,) * (2 if last else 3),
            scratch_shapes=[bias],
            cost_estimate=cost(0.5, 3),
            compiler_params=params,
            name="scores",
        )(lengths, q, k, top)
        v = after(v, factor)
        next_v = None if last else lax.ppermute(v, "pre", onward)
        if first_out:
            for d in reversed(range(2, pre)):
                targets = range(d if d <= hops else pre)
                pairs = [((i - d) % pre, i) for i in targets]
                got.insert(0, lax.ppermute(after(sent[d - 2], v), "pre", pairs))
        carry = () if last else (acc_shape, stat_shape)
        extra = [] if first_out else [attended]
        extra += got[: hops - 2 : -1] if last else []
        extra += [] if first_out else [got[hop - 2]]
        attended, cache, *state = pl.pallas_call(
            functools.partial(values_kernel, hop, hops, pre),
            out_shape=(attended_shape, cache_shape if last else open_cache)
            + carry,
            in_specs=[SMEM, SMEM]
            + [VMEM] * 7
            + ([] if first_out else [HBM])
            + [VMEM] * (len(extra) - 1),
            out_specs=(HBM, HBM if last else VMEM)
            + (VMEM,) * len(carry),
            scratch_shapes=[
                turned,
                pltpu.VMEM((rows, q_width), bf16),
                pltpu.SemaphoreType.DMA((tiles + 1,)),
            ]
            + ([pltpu.VMEM(open_cache.shape, bf16)] if last else []),
            input_output_aliases={} if first_out else {9: 0},
            cost_estimate=cost(0.5, 3),
            compiler_params=params,
            name="values",
        )(lengths, block_slot if first_out else places, v, k, weights, factor, acc, total, cache, *extra)
        if not last:
            (top,) = tops
            acc, total = state
            k, v = after(next_k, total), next_v

    return (attended, cache)


def solution(mesh):
    placed = (
        P(("parts", "pre"), "tp"),
        P(("parts", "pre"), "tp"),
        P(("parts", "pre"), "tp"),
        P("parts"),
        P("parts"),
    )
    return jax.shard_map(
        on_device,
        mesh=mesh,
        in_specs=placed,
        out_specs=(P(("parts", "pre"), "tp"), P(("parts", "pre"), None, "tp")),
        check_vma=False,
    )
```

```python
import functools
import math

import jax
import jax.numpy as jnp
from jax import lax
from jax.experimental import pallas as pl
from jax.experimental.pallas import tpu as pltpu
from jax.sharding import PartitionSpec as P

HD = 128
BLK = 16
GROUP = 4
TILE = 256
ONES = 16
MASKED = -1e30
EXP_SCALE = math.log2(math.e) * HD ** (-0.5)

VMEM = pl.BlockSpec(memory_space=pltpu.VMEM)
SMEM = pl.BlockSpec(memory_space=pltpu.SMEM)
HBM = pl.BlockSpec(memory_space=pltpu.HBM)


def start_of(lengths_ref, position):
    end = jnp.int32(0)
    start = jnp.int32(0)
    for r in range(lengths_ref.shape[0]):
        end = end + lengths_ref[r]
        start = jnp.where(end <= position, end, start)
    return start


def row_starts(lengths_ref, positions):
    end = jnp.int32(0)
    starts = jnp.zeros_like(positions)
    for r in range(lengths_ref.shape[0]):
        end = end + lengths_ref[r]
        starts = jnp.where(positions >= end, end, starts)
    return starts


def fill_bias(bias_ref, lengths_ref, row_first, key_first, low, high, causal):
    shape = (high - low, TILE)
    positions = row_first + lax.broadcasted_iota(jnp.int32, (8, TILE), 1)
    starts = row_starts(lengths_ref, positions)
    keys = key_first + low + lax.broadcasted_iota(jnp.int32, shape, 0)
    keys = keys.reshape((high - low) // 8, 8, TILE)
    allowed = keys >= starts[None]
    if causal:
        allowed = allowed & (keys <= positions[None])
    bias_ref[low:high] = jnp.where(allowed, 0.0, MASKED).reshape(shape)


def turn_values(v_ref, turned):
    for g in range(turned.shape[0]):
        turned[g, :HD] = v_ref[:, g * HD : (g + 1) * HD].T
        turned[g, HD:] = jnp.ones((ONES, turned.shape[2]), turned.dtype)


def lanes_of(tile, j):
    return slice((tile * GROUP + j) * TILE, (tile * GROUP + j + 1) * TILE)


def weigh(q_ref, k_ref, bias_ref, old_top, tile, low, high, g, emit):
    keys = k_ref[low:high, g * HD : (g + 1) * HD]
    heads = range(g * GROUP, (g + 1) * GROUP)
    queries = jnp.concatenate(
        [q_ref[tile * TILE : (tile + 1) * TILE, h * HD : (h + 1) * HD] for h in heads], axis=0
    )
    all_scores = lax.dot_general(
        keys, queries, (((1,), (1,)), ((), ())), preferred_element_type=jnp.float32
    )
    for j in range(GROUP):
        scores = all_scores[:, j * TILE : (j + 1) * TILE] + bias_ref[low:high]
        scores = scores.reshape((high - low) // 8, 8, TILE)
        highest = jnp.max(jnp.max(scores, axis=0), axis=0, keepdims=True)
        top = jnp.broadcast_to(highest, (8, TILE))
        factor = None
        if old_top is not None:
            old = old_top[g, :, lanes_of(tile, j)]
            top = jnp.maximum(old, top)
            factor = jnp.exp2((old - top) * EXP_SCALE)
        weights = jnp.exp2((scores - top[None]) * EXP_SCALE)
        emit(j, weights.reshape(high - low, TILE).astype(jnp.bfloat16), top, factor)


def mix(values, weights, g, tile, old, emit):
    all_added = jnp.dot(values, weights, preferred_element_type=jnp.float32)
    for j in range(GROUP):
        at = lanes_of(tile, j)
        added = all_added[:, j * TILE : (j + 1) * TILE]
        value, total = added[:HD], added[HD : HD + 8]
        if old is not None:
            acc_ref, sum_ref, factor_ref = old
            factor = factor_ref[g, :, at]
            total = total + sum_ref[g, :, at] * factor
            kept = acc_ref[g, :, at].reshape(HD // 8, 8, TILE) * factor[None]
            value = value + kept.reshape(HD, TILE)
        emit(g, j, value, total)


def keep(state, tile):
    def emit(g, j, value, total):
        for ref, array in zip(state, (value, total)):
            ref[g, :, lanes_of(tile, j)] = array

    return emit


def finish(out_ref, row):
    def emit(g, j, value, total):
        head = g * GROUP + j
        value = value.reshape(HD // 8, 8, TILE) * (1.0 / total)[None]
        value = value.reshape(HD, TILE).astype(out_ref.dtype).T
        out_ref[row : row + TILE, head * HD : (head + 1) * HD] = value

    return emit


def block_of(k_ref, v_ref, row):
    parts = []
    for g in range(k_ref.shape[1] // HD):
        span = slice(g * HD, (g + 1) * HD)
        parts += [k_ref[pl.ds(row, BLK), span], v_ref[pl.ds(row, BLK), span]]
    return jnp.concatenate(parts, axis=1)


def own_slot(slot, me, blocks):
    local = slot - me * blocks
    return jnp.where((local >= 0) & (local < blocks), local, blocks)


def list_places(places_ref, slot_ref, hops, pre, blocks):
    me = lax.axis_index("pre")
    stride = blocks // pre + 1
    for distance in range(2, pre):
        source = lax.rem(me - distance + pre, pre)

        def step(b, n):
            at = own_slot(slot_ref[source * blocks + b], me, blocks)
            places_ref[(distance - 2) * stride + n] = at
            if distance <= hops:
                places_ref[(pre - 2 + distance - 2) * stride + n] = b
            return n + jnp.where(at < blocks, 1, 0)

        lax.fori_loop(0, blocks, step, jnp.int32(0), unroll=8)


def load_kernel(src, dst, sem):
    copy = pltpu.make_async_copy(src, dst, sem)
    copy.start()
    copy.wait()


def own_kernel(
    pre, hops, lengths_ref, slot_ref, q_hbm, k_hbm, v_ref,
    q_ref, acc_ref, sum_ref, top_ref, cache_ref, places_ref, *refs,
):
    sent_hbm, refs = refs[: pre - 2], refs[pre - 2 :]
    k_ref, turned, bias, sent_values, sent, counts, sems, load_sems = refs
    loads = [
        pltpu.make_async_copy(src, dst, load_sems.at[n])
        for n, (src, dst) in enumerate(((k_hbm, k_ref), (q_hbm, q_ref)))
    ]
    for load in loads:
        load.start()
    rows = q_ref.shape[0]
    blocks = rows // BLK
    per_peer = blocks // pre
    me = lax.axis_index("pre")
    first = me * rows
    for owner in range(pre):
        counts[owner] = 0
    list_places(places_ref, slot_ref, hops, pre, blocks)
    loads[0].wait()

    def step(b, _):
        slot = slot_ref[me * blocks + b]
        owner = slot // blocks
        n = counts[owner]
        counts[owner] = n + 1
        distance = lax.rem(owner - me + pre, pre)
        row = pl.multiple_of(b * BLK, BLK)
        on_ring = (distance > 1) & (distance <= hops)
        at = jnp.where(on_ring, (distance - 2) * per_peer + n, (hops - 1) * per_peer)
        sent_values[at] = v_ref[pl.ds(row, BLK)]
        beyond = (distance - hops - 1) * per_peer + n
        at = jnp.where(distance > hops, beyond, (pre - 1 - hops) * per_peer)
        block = block_of(k_ref, v_ref, row)
        sent[at] = block
        cache_ref[own_slot(slot, me, blocks)] = block
        return 0

    lax.fori_loop(0, blocks, step, 0, unroll=4)
    packed = [sent_values.at[n * per_peer : (n + 1) * per_peer] for n in range(hops - 1)]
    packed += [sent.at[n * per_peer : (n + 1) * per_peer] for n in range(pre - 1 - hops)]
    stores = [
        pltpu.make_async_copy(src, dst, sems.at[n])
        for n, (src, dst) in enumerate(zip(packed, sent_hbm))
    ]
    for store in stores:
        store.start()
    turn_values(v_ref, turned)
    loads[1].wait()
    for tile in range(rows // TILE):
        high = (tile + 1) * TILE
        fill_bias(bias, lengths_ref, first + tile * TILE, first, 0, high, True)
        for g in range(turned.shape[0]):
            all_weights = []

            def emit(j, weights, top, factor):
                all_weights.append(weights)
                top_ref[g, :, lanes_of(tile, j)] = top

            weigh(q_ref, k_ref, bias, None, tile, 0, high, g, emit)
            all_weights = jnp.concatenate(all_weights, axis=1)
            mix(turned[g, :, :high], all_weights, g, tile, None, keep((acc_ref, sum_ref), tile))
    for store in stores:
        store.wait()


def lowest_key(lengths_ref, hop, tile, rows):
    first = lax.axis_index("pre") * rows
    key_first = first - hop * rows
    low = jnp.maximum(start_of(lengths_ref, first + tile * TILE) - key_first, 0)
    return jnp.where(key_first >= 0, jnp.minimum(low, rows), rows)


def where_seen(low, rows, act):
    for at in range(0, rows, TILE):
        pl.when((low >= at) & (low < at + TILE))(functools.partial(act, at))


def scores_kernel(hop, lengths_ref, q_ref, k_ref, old_top, weights_ref, factor_ref, *refs):
    *top_refs, bias = refs
    rows = q_ref.shape[0]
    first = lax.axis_index("pre") * rows
    for tile in range(rows // TILE):

        def act(at):
            fill_bias(
                bias, lengths_ref, first + tile * TILE, first - hop * rows, at, rows, False
            )
            for g in range(weights_ref.shape[1]):

                def emit(j, weights, top, factor):
                    weights_ref[tile, g, at:rows, j * TILE : (j + 1) * TILE] = weights
                    for top_ref in top_refs:
                        top_ref[g, :, lanes_of(tile, j)] = top
                    factor_ref[g, :, lanes_of(tile, j)] = factor

                weigh(q_ref, k_ref, bias, old_top, tile, at, rows, g, emit)

        where_seen(lowest_key(lengths_ref, hop, tile, rows), rows, act)


def place_blocks(cache, slot_ref, k_ref, v_ref, distance, pre, blocks):
    me = lax.axis_index("pre")
    source = lax.rem(me - distance + pre, pre)

    def step(b, _):
        at = own_slot(slot_ref[source * blocks + b], me, blocks)
        cache[at] = block_of(k_ref, v_ref, pl.multiple_of(b * BLK, BLK))
        return 0

    lax.fori_loop(0, blocks, step, 0, unroll=8)


def place_listed(cache, places_ref, hop, pre, k_ref, v_ref, got_ref):
    me = lax.axis_index("pre")
    per_peer = got_ref.shape[0]
    stride = per_peer + 1

    def place(values_at):
        for n in range(per_peer):
            at = places_ref[(hop - 2) * stride + n]
            b = places_ref[(pre - 2 + hop - 2) * stride + n]
            rows = pl.ds(pl.multiple_of(b * BLK, BLK), BLK)
            values = values_at(n, rows)
            parts = []
            for g in range(k_ref.shape[1] // HD):
                span = slice(g * HD, (g + 1) * HD)
                parts += [k_ref[rows, span], values[:, span]]
            cache[at] = jnp.concatenate(parts, axis=1)

    pl.when(me >= hop)(lambda: place(lambda n, rows: v_ref[rows]))
    pl.when(me < hop)(lambda: place(lambda n, rows: got_ref[n]))


def place_packed(cache, places_ref, distance, got_ref):
    per_peer = got_ref.shape[0]
    for n in range(per_peer):
        cache[places_ref[(distance - 2) * (per_peer + 1) + n]] = got_ref[n]


def values_kernel(
    hop, hops, pre, lengths_ref, slot_ref, v_ref, k_ref, weights_ref, factor_ref,
    acc_in, sum_in, cache_in, *refs,
):
    first_out, last = hop == 1, hop == hops
    refs = list(refs)
    if not first_out:
        refs.pop(0)
    got_far = [refs.pop(0) for _ in range(hops + 1, pre)][::-1] if last else []
    got_ref = None if first_out else refs.pop(0)
    out_hbm, cache_out = refs.pop(0), refs.pop(0)
    state = () if last else (refs.pop(0), refs.pop(0))
    turned, out_buf, sems, *rest = refs
    rows = v_ref.shape[0]
    blocks = rows // BLK
    tiles = rows // TILE
    kv_count = turned.shape[0]

    cache = rest[0] if last else cache_out
    cache[...] = cache_in[...]
    if first_out:
        place_blocks(cache, slot_ref, k_ref, v_ref, hop, pre, blocks)
    else:
        place_listed(cache, slot_ref, hop, pre, k_ref, v_ref, got_ref)
    if last:
        for n, far_ref in enumerate(got_far):
            place_packed(cache, slot_ref, hops + 1 + n, far_ref)
        cache_store = pltpu.make_async_copy(cache.at[0:blocks], cache_out, sems.at[tiles])
        cache_store.start()

    lows = [lowest_key(lengths_ref, hop, tile, rows) for tile in range(tiles)]
    pl.when(lows[0] < rows)(functools.partial(turn_values, v_ref, turned))
    stores = []
    for tile, low in enumerate(lows):
        end_it = finish(out_buf, tile * TILE)

        def act(at):
            def emit(*result):
                if not last:
                    keep(state, tile)(*result)
                end_it(*result)

            for g in range(kv_count):
                weights = weights_ref[tile, g, at:rows]
                old = (acc_in, sum_in, factor_ref)
                mix(turned[g, :, at:rows], weights, g, tile, old, emit)

        where_seen(low, rows, act)
        span = slice(tile * TILE, (tile + 1) * TILE)
        store = pltpu.make_async_copy(out_buf.at[span], out_hbm.at[span], sems.at[tile])
        stores.append(store)
        if first_out:

            @pl.when(low == rows)
            def _():
                for g in range(kv_count):
                    for j in range(GROUP):
                        end_it(g, j, *(ref[g, :, lanes_of(tile, j)] for ref in (acc_in, sum_in)))

            store.start()
        else:
            pl.when(low < rows)(store.start)
    for low, store in zip(lows, stores):
        if first_out:
            store.wait()
        else:
            pl.when(low < rows)(store.wait)
    if last:
        cache_store.wait()


def on_device(queries, new_keys, new_values, lengths, block_slot):
    rows, q_width = queries.shape
    kv_width = new_keys.shape[1]
    kv_count = kv_width // HD
    blocks = rows // BLK
    pre = lax.axis_size("pre")
    per_peer = blocks // pre
    hops = pre // 2
    tiles = rows // TILE
    bf16, f32 = jnp.bfloat16, jnp.float32
    shape = jax.ShapeDtypeStruct
    params = pltpu.CompilerParams(vmem_limit_bytes=24 * 2**20)
    own_params = pltpu.CompilerParams(vmem_limit_bytes=44 * 2**20)
    ring = [(i, (i + 1) % pre) for i in range(pre)]
    acc_shape = shape((kv_count, HD, GROUP * rows), f32)
    stat_shape = shape((kv_count, 8, GROUP * rows), f32)
    weights_shape = shape((tiles, kv_count, rows, GROUP * TILE), bf16)
    attended_shape = shape(queries.shape, bf16)
    cache_shape = shape((blocks, BLK, 2 * kv_width), bf16)
    open_cache = shape((blocks + 1, BLK, 2 * kv_width), bf16)
    turned = pltpu.VMEM((kv_count, HD + ONES, rows), bf16)
    bias = pltpu.VMEM((rows, TILE), f32)

    def cost(share, moved):
        pairs = int(rows * rows * share)
        return pl.CostEstimate(
            flops=4 * pairs * q_width,
            bytes_accessed=moved * 2**20,
            transcendentals=pairs * kv_count * GROUP,
        )

    def after(array, *others):
        return lax.optimization_barrier((array, *others))[0]

    k = lax.ppermute(new_keys, "pre", ring)
    near_values = pl.pallas_call(
        load_kernel,
        out_shape=shape(new_values.shape, bf16),
        in_specs=[HBM],
        out_specs=VMEM,
        scratch_shapes=[pltpu.SemaphoreType.DMA],
        cost_estimate=cost(0, 1),
        compiler_params=params,
        name="load_values",
    )(pltpu.with_memory_space_constraint(new_values, pltpu.HBM))
    v = lax.ppermute(near_values, "pre", ring)

    packed = (shape((per_peer, BLK, kv_width), bf16),) * (hops - 1)
    packed += (shape((per_peer, BLK, 2 * kv_width), bf16),) * (pre - 1 - hops)
    places = shape(((pre - 2 + hops - 1) * (per_peer + 1),), jnp.int32)
    in_hbm = (pltpu.with_memory_space_constraint(x, pltpu.HBM) for x in (queries, new_keys))
    q, acc, total, top, cache, places, *sent = pl.pallas_call(
        functools.partial(own_kernel, pre, hops),
        out_shape=(attended_shape, acc_shape, stat_shape, stat_shape, open_cache, places)
        + packed,
        in_specs=[SMEM, SMEM, HBM, HBM, VMEM],
        out_specs=(VMEM,) * 5 + (SMEM,) + (HBM,) * (pre - 2),
        scratch_shapes=[
            pltpu.VMEM((rows, kv_width), bf16),
            turned,
            bias,
            pltpu.VMEM(((hops - 1) * per_peer + 1, BLK, kv_width), bf16),
            pltpu.VMEM(((pre - 1 - hops) * per_peer + 1, BLK, 2 * kv_width), bf16),
            pltpu.SMEM((pre,), jnp.int32),
            pltpu.SemaphoreType.DMA((pre - 2,)),
            pltpu.SemaphoreType.DMA((2,)),
        ],
        cost_estimate=cost(1, 4),
        compiler_params=own_params,
        name="own_attention",
    )(lengths, block_slot, *in_hbm, near_values)
    got = []
    k = after(k, top)
    attended = None
    for hop in range(1, hops + 1):
        first_out, last = hop == 1, hop == hops
        onward = [(i, i + 1) for i in range(hop, pre - 1)]
        next_k = None if last else lax.ppermute(k, "pre", ring)
        weights, factor, *tops = pl.pallas_call(
            functools.partial(scores_kernel, hop),
            out_shape=(weights_shape, stat_shape) + (() if last else (stat_shape,)),
            in_specs=[SMEM] + [VMEM] * 3,
            out_specs=(VMEM,) * (2 if last else 3),
            scratch_shapes=[bias],
            cost_estimate=cost(0.5, 3),
            compiler_params=params,
            name="scores",
        )(lengths, q, k, top)
        v = after(v, factor)
        next_v = None if last else lax.ppermute(v, "pre", onward)
        if first_out:
            for d in reversed(range(2, pre)):
                targets = range(d if d <= hops else pre)
                pairs = [((i - d) % pre, i) for i in targets]
                got.insert(0, lax.ppermute(after(sent[d - 2], v), "pre", pairs))
        carry = () if last else (acc_shape, stat_shape)
        extra = [] if first_out else [attended]
        extra += got[: hops - 2 : -1] if last else []
        extra += [] if first_out else [got[hop - 2]]
        attended, cache, *state = pl.pallas_call(
            functools.partial(values_kernel, hop, hops, pre),
            out_shape=(attended_shape, cache_shape if last else open_cache)
            + carry,
            in_specs=[SMEM, SMEM]
            + [VMEM] * 7
            + ([] if first_out else [HBM])
            + [VMEM] * (len(extra) - 1),
            out_specs=(HBM, HBM if last else VMEM)
            + (VMEM,) * len(carry),
            scratch_shapes=[
                turned,
                pltpu.VMEM((rows, q_width), bf16),
                pltpu.SemaphoreType.DMA((tiles + 1,)),
            ]
            + ([pltpu.VMEM(open_cache.shape, bf16)] if last else []),
            input_output_aliases={} if first_out else {9: 0},
            cost_estimate=cost(0.5, 3),
            compiler_params=params,
            name="values",
        )(lengths, block_slot if first_out else places, v, k, weights, factor, acc, total, cache, *extra)
        if not last:
            (top,) = tops
            acc, total = state
            k, v = after(next_k, total), next_v

    return (attended, cache)


def solution(mesh):
    placed = (
        P(("parts", "pre"), "tp"),
        P(("parts", "pre"), "tp"),
        P(("parts", "pre"), "tp"),
        P("parts"),
        P("parts"),
    )
    return jax.shard_map(
        on_device,
        mesh=mesh,
        in_specs=placed,
        out_specs=(P(("parts", "pre"), "tp"), P(("parts", "pre"), None, "tp")),
        check_vma=False,
    )
```

```python
import functools
import math

import jax
import jax.numpy as jnp
from jax import lax
from jax.experimental import pallas as pl
from jax.experimental.pallas import tpu as pltpu
from jax.sharding import PartitionSpec as P

HD = 128
BLK = 16
GROUP = 4
TILE = 256
ONES = 16
MASKED = -1e30
EXP_SCALE = math.log2(math.e) * HD ** (-0.5)

VMEM = pl.BlockSpec(memory_space=pltpu.VMEM)
SMEM = pl.BlockSpec(memory_space=pltpu.SMEM)
HBM = pl.BlockSpec(memory_space=pltpu.HBM)


def start_of(lengths_ref, position):
    end = jnp.int32(0)
    start = jnp.int32(0)
    for r in range(lengths_ref.shape[0]):
        end = end + lengths_ref[r]
        start = jnp.where(end <= position, end, start)
    return start


def row_starts(lengths_ref, positions):
    end = jnp.int32(0)
    starts = jnp.zeros_like(positions)
    for r in range(lengths_ref.shape[0]):
        end = end + lengths_ref[r]
        starts = jnp.where(positions >= end, end, starts)
    return starts


def fill_bias(bias_ref, lengths_ref, row_first, key_first, low, high, causal):
    shape = (high - low, TILE)
    positions = row_first + lax.broadcasted_iota(jnp.int32, (8, TILE), 1)
    starts = row_starts(lengths_ref, positions)
    keys = key_first + low + lax.broadcasted_iota(jnp.int32, shape, 0)
    keys = keys.reshape((high - low) // 8, 8, TILE)
    allowed = keys >= starts[None]
    if causal:
        allowed = allowed & (keys <= positions[None])
    bias_ref[low:high] = jnp.where(allowed, 0.0, MASKED).reshape(shape)


def turn_values(v_ref, turned):
    for g in range(turned.shape[0]):
        turned[g, :HD] = v_ref[:, g * HD : (g + 1) * HD].T
        turned[g, HD:] = jnp.ones((ONES, turned.shape[2]), turned.dtype)


def lanes_of(tile, j):
    return slice((tile * GROUP + j) * TILE, (tile * GROUP + j + 1) * TILE)


def weigh(q_ref, k_ref, bias_ref, old_top, tile, low, high, g, emit):
    keys = k_ref[low:high, g * HD : (g + 1) * HD]
    heads = range(g * GROUP, (g + 1) * GROUP)
    queries = jnp.concatenate(
        [q_ref[tile * TILE : (tile + 1) * TILE, h * HD : (h + 1) * HD] for h in heads], axis=0
    )
    all_scores = lax.dot_general(
        keys, queries, (((1,), (1,)), ((), ())), preferred_element_type=jnp.float32
    )
    for j in range(GROUP):
        scores = all_scores[:, j * TILE : (j + 1) * TILE] + bias_ref[low:high]
        scores = scores.reshape((high - low) // 8, 8, TILE)
        highest = jnp.max(jnp.max(scores, axis=0), axis=0, keepdims=True)
        top = jnp.broadcast_to(highest, (8, TILE))
        factor = None
        if old_top is not None:
            old = old_top[g, :, lanes_of(tile, j)]
            top = jnp.maximum(old, top)
            factor = jnp.exp2((old - top) * EXP_SCALE)
        weights = jnp.exp2((scores - top[None]) * EXP_SCALE)
        emit(j, weights.reshape(high - low, TILE).astype(jnp.bfloat16), top, factor)


def mix(values, weights, g, tile, old, emit):
    all_added = jnp.dot(values, weights, preferred_element_type=jnp.float32)
    for j in range(GROUP):
        at = lanes_of(tile, j)
        added = all_added[:, j * TILE : (j + 1) * TILE]
        value, total = added[:HD], added[HD : HD + 8]
        if old is not None:
            acc_ref, sum_ref, factor_ref = old
            factor = factor_ref[g, :, at]
            total = total + sum_ref[g, :, at] * factor
            kept = acc_ref[g, :, at].reshape(HD // 8, 8, TILE) * factor[None]
            value = value + kept.reshape(HD, TILE)
        emit(g, j, value, total)


def keep(state, tile):
    def emit(g, j, value, total):
        for ref, array in zip(state, (value, total)):
            ref[g, :, lanes_of(tile, j)] = array

    return emit


def finish(out_ref, row):
    def emit(g, j, value, total):
        head = g * GROUP + j
        value = value.reshape(HD // 8, 8, TILE) * (1.0 / total)[None]
        value = value.reshape(HD, TILE).astype(out_ref.dtype).T
        out_ref[row : row + TILE, head * HD : (head + 1) * HD] = value

    return emit


def block_of(k_ref, v_ref, row):
    parts = []
    for g in range(k_ref.shape[1] // HD):
        span = slice(g * HD, (g + 1) * HD)
        parts += [k_ref[pl.ds(row, BLK), span], v_ref[pl.ds(row, BLK), span]]
    return jnp.concatenate(parts, axis=1)


def own_slot(slot, me, blocks):
    local = slot - me * blocks
    return jnp.where((local >= 0) & (local < blocks), local, blocks)


def list_places(places_ref, slot_ref, hops, pre, blocks):
    me = lax.axis_index("pre")
    stride = blocks // pre + 1
    for distance in range(2, pre):
        source = lax.rem(me - distance + pre, pre)

        def step(b, n):
            at = own_slot(slot_ref[source * blocks + b], me, blocks)
            places_ref[(distance - 2) * stride + n] = at
            if distance <= hops:
                places_ref[(pre - 2 + distance - 2) * stride + n] = b
            return n + jnp.where(at < blocks, 1, 0)

        lax.fori_loop(0, blocks, step, jnp.int32(0), unroll=8)


def own_kernel(
    pre, hops, lengths_ref, slot_ref, q_hbm, k_hbm, v_hbm,
    q_ref, acc_ref, sum_ref, top_ref, cache_ref, places_ref, *refs,
):
    sent_hbm, refs = refs[: pre - 2], refs[pre - 2 :]
    k_ref, v_ref, turned, bias, sent_values, sent, counts, sems, load_sems = refs
    loads = [
        pltpu.make_async_copy(src, dst, load_sems.at[n])
        for n, (src, dst) in enumerate(((k_hbm, k_ref), (v_hbm, v_ref), (q_hbm, q_ref)))
    ]
    for load in loads:
        load.start()
    rows = q_ref.shape[0]
    blocks = rows // BLK
    per_peer = blocks // pre
    me = lax.axis_index("pre")
    first = me * rows
    for owner in range(pre):
        counts[owner] = 0
    list_places(places_ref, slot_ref, hops, pre, blocks)
    loads[0].wait()
    loads[1].wait()

    def step(b, _):
        slot = slot_ref[me * blocks + b]
        owner = slot // blocks
        n = counts[owner]
        counts[owner] = n + 1
        distance = lax.rem(owner - me + pre, pre)
        row = pl.multiple_of(b * BLK, BLK)
        on_ring = (distance > 1) & (distance <= hops)
        at = jnp.where(on_ring, (distance - 2) * per_peer + n, (hops - 1) * per_peer)
        sent_values[at] = v_ref[pl.ds(row, BLK)]
        beyond = (distance - hops - 1) * per_peer + n
        at = jnp.where(distance > hops, beyond, (pre - 1 - hops) * per_peer)
        block = block_of(k_ref, v_ref, row)
        sent[at] = block
        cache_ref[own_slot(slot, me, blocks)] = block
        return 0

    lax.fori_loop(0, blocks, step, 0, unroll=4)
    packed = [sent_values.at[n * per_peer : (n + 1) * per_peer] for n in range(hops - 1)]
    packed += [sent.at[n * per_peer : (n + 1) * per_peer] for n in range(pre - 1 - hops)]
    stores = [
        pltpu.make_async_copy(src, dst, sems.at[n])
        for n, (src, dst) in enumerate(zip(packed, sent_hbm))
    ]
    for store in stores:
        store.start()
    turn_values(v_ref, turned)
    loads[2].wait()
    for tile in range(rows // TILE):
        high = (tile + 1) * TILE
        fill_bias(bias, lengths_ref, first + tile * TILE, first, 0, high, True)
        for g in range(turned.shape[0]):
            all_weights = []

            def emit(j, weights, top, factor):
                all_weights.append(weights)
                top_ref[g, :, lanes_of(tile, j)] = top

            weigh(q_ref, k_ref, bias, None, tile, 0, high, g, emit)
            all_weights = jnp.concatenate(all_weights, axis=1)
            mix(turned[g, :, :high], all_weights, g, tile, None, keep((acc_ref, sum_ref), tile))
    for store in stores:
        store.wait()


def lowest_key(lengths_ref, hop, tile, rows):
    first = lax.axis_index("pre") * rows
    key_first = first - hop * rows
    low = jnp.maximum(start_of(lengths_ref, first + tile * TILE) - key_first, 0)
    return jnp.where(key_first >= 0, jnp.minimum(low, rows), rows)


def where_seen(low, rows, act):
    for at in range(0, rows, TILE):
        pl.when((low >= at) & (low < at + TILE))(functools.partial(act, at))


def scores_kernel(hop, lengths_ref, q_ref, k_ref, old_top, weights_ref, factor_ref, *refs):
    *top_refs, bias = refs
    rows = q_ref.shape[0]
    first = lax.axis_index("pre") * rows
    for tile in range(rows // TILE):

        def act(at):
            fill_bias(
                bias, lengths_ref, first + tile * TILE, first - hop * rows, at, rows, False
            )
            for g in range(weights_ref.shape[1]):

                def emit(j, weights, top, factor):
                    weights_ref[tile, g, at:rows, j * TILE : (j + 1) * TILE] = weights
                    for top_ref in top_refs:
                        top_ref[g, :, lanes_of(tile, j)] = top
                    factor_ref[g, :, lanes_of(tile, j)] = factor

                weigh(q_ref, k_ref, bias, old_top, tile, at, rows, g, emit)

        where_seen(lowest_key(lengths_ref, hop, tile, rows), rows, act)


def place_blocks(cache, slot_ref, k_ref, v_ref, distance, pre, blocks):
    me = lax.axis_index("pre")
    source = lax.rem(me - distance + pre, pre)

    def step(b, _):
        at = own_slot(slot_ref[source * blocks + b], me, blocks)
        cache[at] = block_of(k_ref, v_ref, pl.multiple_of(b * BLK, BLK))
        return 0

    lax.fori_loop(0, blocks, step, 0, unroll=8)


def place_listed(cache, places_ref, hop, pre, k_ref, v_ref, got_ref):
    me = lax.axis_index("pre")
    per_peer = got_ref.shape[0]
    stride = per_peer + 1

    def place(values_at):
        for n in range(per_peer):
            at = places_ref[(hop - 2) * stride + n]
            b = places_ref[(pre - 2 + hop - 2) * stride + n]
            rows = pl.ds(pl.multiple_of(b * BLK, BLK), BLK)
            values = values_at(n, rows)
            parts = []
            for g in range(k_ref.shape[1] // HD):
                span = slice(g * HD, (g + 1) * HD)
                parts += [k_ref[rows, span], values[:, span]]
            cache[at] = jnp.concatenate(parts, axis=1)

    pl.when(me >= hop - 1)(lambda: place(lambda n, rows: v_ref[rows]))
    pl.when(me < hop - 1)(lambda: place(lambda n, rows: got_ref[n]))


def place_packed(cache, places_ref, distance, got_ref):
    per_peer = got_ref.shape[0]
    for n in range(per_peer):
        cache[places_ref[(distance - 2) * (per_peer + 1) + n]] = got_ref[n]


def values_kernel(
    hop, hops, pre, lengths_ref, slot_ref, v_ref, k_ref, weights_ref, factor_ref,
    acc_in, sum_in, cache_in, *refs,
):
    first_out, last = hop == 1, hop == hops
    refs = list(refs)
    if not first_out:
        refs.pop(0)
    got_ref = None if first_out else refs.pop(0)
    got_far = [refs.pop(0) for _ in range(hops + 1, pre)] if last else []
    out_hbm, cache_out = refs.pop(0), refs.pop(0)
    state = () if last else (refs.pop(0), refs.pop(0))
    turned, out_buf, sems, *rest = refs
    rows = v_ref.shape[0]
    blocks = rows // BLK
    tiles = rows // TILE
    kv_count = turned.shape[0]

    cache = rest[0] if last else cache_out
    cache[...] = cache_in[...]
    if first_out:
        place_blocks(cache, slot_ref, k_ref, v_ref, hop, pre, blocks)
    else:
        place_listed(cache, slot_ref, hop, pre, k_ref, v_ref, got_ref)
    if last:
        for n, far_ref in enumerate(got_far):
            place_packed(cache, slot_ref, hops + 1 + n, far_ref)
        cache_store = pltpu.make_async_copy(cache.at[0:blocks], cache_out, sems.at[tiles])
        cache_store.start()

    lows = [lowest_key(lengths_ref, hop, tile, rows) for tile in range(tiles)]
    pl.when(lows[0] < rows)(functools.partial(turn_values, v_ref, turned))
    stores = []
    for tile, low in enumerate(lows):
        end_it = finish(out_buf, tile * TILE)

        def act(at):
            def emit(*result):
                if not last:
                    keep(state, tile)(*result)
                end_it(*result)

            for g in range(kv_count):
                weights = weights_ref[tile, g, at:rows]
                old = (acc_in, sum_in, factor_ref)
                mix(turned[g, :, at:rows], weights, g, tile, old, emit)

        where_seen(low, rows, act)
        span = slice(tile * TILE, (tile + 1) * TILE)
        store = pltpu.make_async_copy(out_buf.at[span], out_hbm.at[span], sems.at[tile])
        stores.append(store)
        if first_out:

            @pl.when(low == rows)
            def _():
                for g in range(kv_count):
                    for j in range(GROUP):
                        end_it(g, j, *(ref[g, :, lanes_of(tile, j)] for ref in (acc_in, sum_in)))

            store.start()
        else:
            pl.when(low < rows)(store.start)
    for low, store in zip(lows, stores):
        if first_out:
            store.wait()
        else:
            pl.when(low < rows)(store.wait)
    if last:
        cache_store.wait()


def on_device(queries, new_keys, new_values, lengths, block_slot):
    rows, q_width = queries.shape
    kv_width = new_keys.shape[1]
    kv_count = kv_width // HD
    blocks = rows // BLK
    pre = lax.axis_size("pre")
    per_peer = blocks // pre
    hops = pre // 2
    tiles = rows // TILE
    bf16, f32 = jnp.bfloat16, jnp.float32
    shape = jax.ShapeDtypeStruct
    params = pltpu.CompilerParams(vmem_limit_bytes=24 * 2**20)
    own_params = pltpu.CompilerParams(vmem_limit_bytes=44 * 2**20)
    ring = [(i, (i + 1) % pre) for i in range(pre)]
    acc_shape = shape((kv_count, HD, GROUP * rows), f32)
    stat_shape = shape((kv_count, 8, GROUP * rows), f32)
    weights_shape = shape((tiles, kv_count, rows, GROUP * TILE), bf16)
    attended_shape = shape(queries.shape, bf16)
    cache_shape = shape((blocks, BLK, 2 * kv_width), bf16)
    open_cache = shape((blocks + 1, BLK, 2 * kv_width), bf16)
    turned = pltpu.VMEM((kv_count, HD + ONES, rows), bf16)
    bias = pltpu.VMEM((rows, TILE), f32)

    def cost(share, moved):
        pairs = int(rows * rows * share)
        return pl.CostEstimate(
            flops=4 * pairs * q_width,
            bytes_accessed=moved * 2**20,
            transcendentals=pairs * kv_count * GROUP,
        )

    def after(array, *others):
        return lax.optimization_barrier((array, *others))[0]

    k, v = lax.ppermute(new_keys, "pre", ring), lax.ppermute(new_values, "pre", ring)

    packed = (shape((per_peer, BLK, kv_width), bf16),) * (hops - 1)
    packed += (shape((per_peer, BLK, 2 * kv_width), bf16),) * (pre - 1 - hops)
    places = shape(((pre - 2 + hops - 1) * (per_peer + 1),), jnp.int32)
    in_hbm = (
        pltpu.with_memory_space_constraint(x, pltpu.HBM) for x in (queries, new_keys, new_values)
    )
    q, acc, total, top, cache, places, *sent = pl.pallas_call(
        functools.partial(own_kernel, pre, hops),
        out_shape=(attended_shape, acc_shape, stat_shape, stat_shape, open_cache, places)
        + packed,
        in_specs=[SMEM, SMEM] + [HBM] * 3,
        out_specs=(VMEM,) * 5 + (SMEM,) + (HBM,) * (pre - 2),
        scratch_shapes=[
            pltpu.VMEM((rows, kv_width), bf16),
            pltpu.VMEM((rows, kv_width), bf16),
            turned,
            bias,
            pltpu.VMEM(((hops - 1) * per_peer + 1, BLK, kv_width), bf16),
            pltpu.VMEM(((pre - 1 - hops) * per_peer + 1, BLK, 2 * kv_width), bf16),
            pltpu.SMEM((pre,), jnp.int32),
            pltpu.SemaphoreType.DMA((pre - 2,)),
            pltpu.SemaphoreType.DMA((3,)),
        ],
        cost_estimate=cost(1, 4),
        compiler_params=own_params,
        name="own_attention",
    )(lengths, block_slot, *in_hbm)
    got = []
    k = after(k, top)
    attended = None
    for hop in range(1, hops + 1):
        first_out, last = hop == 1, hop == hops
        onward = [(i, i + 1) for i in range(hop - 1, pre - 1)]
        next_k = None if last else lax.ppermute(k, "pre", ring)
        weights, factor, *tops = pl.pallas_call(
            functools.partial(scores_kernel, hop),
            out_shape=(weights_shape, stat_shape) + (() if last else (stat_shape,)),
            in_specs=[SMEM] + [VMEM] * 3,
            out_specs=(VMEM,) * (2 if last else 3),
            scratch_shapes=[bias],
            cost_estimate=cost(0.5, 3),
            compiler_params=params,
            name="scores",
        )(lengths, q, k, top)
        v = after(v, factor)
        next_v = None if last else lax.ppermute(v, "pre", onward)
        if first_out:
            for d in range(2, pre):
                targets = range(d - 1 if d <= hops else pre)
                pairs = [((i - d) % pre, i) for i in targets]
                got.append(lax.ppermute(after(sent[d - 2], v), "pre", pairs))
        carry = () if last else (acc_shape, stat_shape)
        extra = [] if first_out else [attended]
        extra += [] if first_out else [got[hop - 2]]
        extra += got[hops - 1 :] if last else []
        attended, cache, *state = pl.pallas_call(
            functools.partial(values_kernel, hop, hops, pre),
            out_shape=(attended_shape, cache_shape if last else open_cache)
            + carry,
            in_specs=[SMEM, SMEM]
            + [VMEM] * 7
            + ([] if first_out else [HBM])
            + [VMEM] * (len(extra) - 1),
            out_specs=(HBM, HBM if last else VMEM)
            + (VMEM,) * len(carry),
            scratch_shapes=[
                turned,
                pltpu.VMEM((rows, q_width), bf16),
                pltpu.SemaphoreType.DMA((tiles + 1,)),
            ]
            + ([pltpu.VMEM(open_cache.shape, bf16)] if last else []),
            input_output_aliases={} if first_out else {9: 0},
            cost_estimate=cost(0.5, 3),
            compiler_params=params,
            name="values",
        )(lengths, block_slot if first_out else places, v, k, weights, factor, acc, total, cache, *extra)
        if not last:
            (top,) = tops
            acc, total = state
            k, v = after(next_k, total), next_v

    return (attended, cache)


def solution(mesh):
    placed = (
        P(("parts", "pre"), "tp"),
        P(("parts", "pre"), "tp"),
        P(("parts", "pre"), "tp"),
        P("parts"),
        P("parts"),
    )
    return jax.shard_map(
        on_device,
        mesh=mesh,
        in_specs=placed,
        out_specs=(P(("parts", "pre"), "tp"), P(("parts", "pre"), None, "tp")),
        check_vma=False,
    )
```

```python
import functools
import math

import jax
import jax.numpy as jnp
from jax import lax
from jax.experimental import pallas as pl
from jax.experimental.pallas import tpu as pltpu
from jax.sharding import PartitionSpec as P

HD = 128
BLK = 16
GROUP = 4
TILE = 256
ONES = 16
MASKED = -1e30
EXP_SCALE = math.log2(math.e) * HD ** (-0.5)

VMEM = pl.BlockSpec(memory_space=pltpu.VMEM)
SMEM = pl.BlockSpec(memory_space=pltpu.SMEM)
HBM = pl.BlockSpec(memory_space=pltpu.HBM)


def start_of(lengths_ref, position):
    end = jnp.int32(0)
    start = jnp.int32(0)
    for r in range(lengths_ref.shape[0]):
        end = end + lengths_ref[r]
        start = jnp.where(end <= position, end, start)
    return start


def row_starts(lengths_ref, positions):
    end = jnp.int32(0)
    starts = jnp.zeros_like(positions)
    for r in range(lengths_ref.shape[0]):
        end = end + lengths_ref[r]
        starts = jnp.where(positions >= end, end, starts)
    return starts


def fill_bias(bias_ref, lengths_ref, row_first, key_first, low, high, causal):
    shape = (high - low, TILE)
    positions = row_first + lax.broadcasted_iota(jnp.int32, (8, TILE), 1)
    starts = row_starts(lengths_ref, positions)
    keys = key_first + low + lax.broadcasted_iota(jnp.int32, shape, 0)
    keys = keys.reshape((high - low) // 8, 8, TILE)
    allowed = keys >= starts[None]
    if causal:
        allowed = allowed & (keys <= positions[None])
    bias_ref[low:high] = jnp.where(allowed, 0.0, MASKED).reshape(shape)


def for_groups(count, act):
    def step(g, _):
        act(g)
        return 0

    lax.fori_loop(0, count, step, 0)


def head_lanes(head):
    return pl.ds(pl.multiple_of(head * HD, HD), HD)


def turn_values(v_ref, turned):
    def act(g):
        turned[g, :HD] = v_ref[:, head_lanes(g)].T
        turned[g, HD:] = jnp.ones((ONES, turned.shape[2]), turned.dtype)

    for_groups(turned.shape[0], act)


def lanes_of(tile, j):
    return slice((tile * GROUP + j) * TILE, (tile * GROUP + j + 1) * TILE)


def weigh(q_ref, k_ref, bias_ref, old_top, tile, low, high, g, emit):
    keys = k_ref[low:high, head_lanes(g)]
    span = slice(tile * TILE, (tile + 1) * TILE)
    queries = jnp.concatenate(
        [q_ref[span, head_lanes(g * GROUP + j)] for j in range(GROUP)], axis=0
    )
    all_scores = lax.dot_general(
        keys, queries, (((1,), (1,)), ((), ())), preferred_element_type=jnp.float32
    )
    for j in range(GROUP):
        scores = all_scores[:, j * TILE : (j + 1) * TILE] + bias_ref[low:high]
        scores = scores.reshape((high - low) // 8, 8, TILE)
        highest = jnp.max(jnp.max(scores, axis=0), axis=0, keepdims=True)
        top = jnp.broadcast_to(highest, (8, TILE))
        factor = None
        if old_top is not None:
            old = old_top[g, :, lanes_of(tile, j)]
            top = jnp.maximum(old, top)
            factor = jnp.exp2((old - top) * EXP_SCALE)
        weights = jnp.exp2((scores - top[None]) * EXP_SCALE)
        emit(j, weights.reshape(high - low, TILE).astype(jnp.bfloat16), top, factor)


def mix(values, weights, g, tile, old, emit):
    all_added = jnp.dot(values, weights, preferred_element_type=jnp.float32)
    for j in range(GROUP):
        at = lanes_of(tile, j)
        added = all_added[:, j * TILE : (j + 1) * TILE]
        value, total = added[:HD], added[HD : HD + 8]
        if old is not None:
            acc_ref, sum_ref, factor_ref = old
            factor = factor_ref[g, :, at]
            total = total + sum_ref[g, :, at] * factor
            kept = acc_ref[g, :, at].reshape(HD // 8, 8, TILE) * factor[None]
            value = value + kept.reshape(HD, TILE)
        emit(g, j, value, total)


def keep(state, tile):
    def emit(g, j, value, total):
        for ref, array in zip(state, (value, total)):
            ref[g, :, lanes_of(tile, j)] = array

    return emit


def finish(out_ref, row):
    def emit(g, j, value, total):
        value = value.reshape(HD // 8, 8, TILE) * (1.0 / total)[None]
        value = value.reshape(HD, TILE).astype(out_ref.dtype).T
        out_ref[row : row + TILE, head_lanes(g * GROUP + j)] = value

    return emit


def block_of(k_ref, v_ref, row):
    parts = []
    for g in range(k_ref.shape[1] // HD):
        span = slice(g * HD, (g + 1) * HD)
        parts += [k_ref[pl.ds(row, BLK), span], v_ref[pl.ds(row, BLK), span]]
    return jnp.concatenate(parts, axis=1)


def own_slot(slot, me, blocks):
    local = slot - me * blocks
    return jnp.where((local >= 0) & (local < blocks), local, blocks)


def list_places(places_ref, slot_ref, hops, pre, blocks):
    me = lax.axis_index("pre")
    stride = blocks // pre + 1
    for distance in range(2, pre):
        source = lax.rem(me - distance + pre, pre)

        def step(b, n):
            at = own_slot(slot_ref[source * blocks + b], me, blocks)
            places_ref[(distance - 2) * stride + n] = at
            if distance <= hops:
                places_ref[(pre - 2 + distance - 2) * stride + n] = b
            return n + jnp.where(at < blocks, 1, 0)

        lax.fori_loop(0, blocks, step, jnp.int32(0), unroll=8)


def own_kernel(
    pre, hops, lengths_ref, slot_ref, q_hbm, k_hbm, v_hbm,
    q_ref, acc_ref, sum_ref, top_ref, cache_ref, places_ref, *refs,
):
    sent_hbm, refs = refs[: pre - 2], refs[pre - 2 :]
    k_ref, v_ref, turned, bias, sent_values, sent, counts, sems, load_sems = refs
    loads = [
        pltpu.make_async_copy(src, dst, load_sems.at[n])
        for n, (src, dst) in enumerate(((k_hbm, k_ref), (v_hbm, v_ref), (q_hbm, q_ref)))
    ]
    for load in loads:
        load.start()
    rows = q_ref.shape[0]
    blocks = rows // BLK
    per_peer = blocks // pre
    me = lax.axis_index("pre")
    first = me * rows
    for owner in range(pre):
        counts[owner] = 0
    list_places(places_ref, slot_ref, hops, pre, blocks)
    loads[0].wait()
    loads[1].wait()

    def step(b, _):
        slot = slot_ref[me * blocks + b]
        owner = slot // blocks
        n = counts[owner]
        counts[owner] = n + 1
        distance = lax.rem(owner - me + pre, pre)
        row = pl.multiple_of(b * BLK, BLK)
        on_ring = (distance > 1) & (distance <= hops)
        at = jnp.where(on_ring, (distance - 2) * per_peer + n, (hops - 1) * per_peer)
        sent_values[at] = v_ref[pl.ds(row, BLK)]
        beyond = (distance - hops - 1) * per_peer + n
        at = jnp.where(distance > hops, beyond, (pre - 1 - hops) * per_peer)
        block = block_of(k_ref, v_ref, row)
        sent[at] = block
        cache_ref[own_slot(slot, me, blocks)] = block
        return 0

    lax.fori_loop(0, blocks, step, 0, unroll=4)
    packed = [sent_values.at[n * per_peer : (n + 1) * per_peer] for n in range(hops - 1)]
    packed += [sent.at[n * per_peer : (n + 1) * per_peer] for n in range(pre - 1 - hops)]
    stores = [
        pltpu.make_async_copy(src, dst, sems.at[n])
        for n, (src, dst) in enumerate(zip(packed, sent_hbm))
    ]
    for store in stores:
        store.start()
    turn_values(v_ref, turned)
    loads[2].wait()
    for tile in range(rows // TILE):
        high = (tile + 1) * TILE
        fill_bias(bias, lengths_ref, first + tile * TILE, first, 0, high, True)

        def attend(g):
            all_weights = []

            def emit(j, weights, top, factor):
                all_weights.append(weights)
                top_ref[g, :, lanes_of(tile, j)] = top

            weigh(q_ref, k_ref, bias, None, tile, 0, high, g, emit)
            weights = jnp.concatenate(all_weights, axis=1)
            mix(turned[g, :, :high], weights, g, tile, None, keep((acc_ref, sum_ref), tile))

        for_groups(turned.shape[0], attend)
    for store in stores:
        store.wait()


def lowest_key(lengths_ref, hop, tile, rows):
    first = lax.axis_index("pre") * rows
    key_first = first - hop * rows
    low = jnp.maximum(start_of(lengths_ref, first + tile * TILE) - key_first, 0)
    return jnp.where(key_first >= 0, jnp.minimum(low, rows), rows)


def where_seen(low, rows, act):
    for at in range(0, rows, TILE):
        pl.when((low >= at) & (low < at + TILE))(functools.partial(act, at))


def scores_kernel(hop, lengths_ref, q_ref, k_ref, old_top, weights_ref, factor_ref, *refs):
    *top_refs, bias = refs
    rows = q_ref.shape[0]
    first = lax.axis_index("pre") * rows
    for tile in range(rows // TILE):

        def act(at):
            fill_bias(
                bias, lengths_ref, first + tile * TILE, first - hop * rows, at, rows, False
            )

            def score(g):
                def emit(j, weights, top, factor):
                    weights_ref[tile, g, at:rows, j * TILE : (j + 1) * TILE] = weights
                    for top_ref in top_refs:
                        top_ref[g, :, lanes_of(tile, j)] = top
                    factor_ref[g, :, lanes_of(tile, j)] = factor

                weigh(q_ref, k_ref, bias, old_top, tile, at, rows, g, emit)

            for_groups(weights_ref.shape[1], score)

        where_seen(lowest_key(lengths_ref, hop, tile, rows), rows, act)


def place_blocks(cache, slot_ref, k_ref, v_ref, distance, pre, blocks):
    me = lax.axis_index("pre")
    source = lax.rem(me - distance + pre, pre)

    def step(b, _):
        at = own_slot(slot_ref[source * blocks + b], me, blocks)
        cache[at] = block_of(k_ref, v_ref, pl.multiple_of(b * BLK, BLK))
        return 0

    lax.fori_loop(0, blocks, step, 0, unroll=8)


def place_listed(cache, places_ref, hop, pre, k_ref, v_ref, got_ref):
    me = lax.axis_index("pre")
    per_peer = got_ref.shape[0]
    stride = per_peer + 1

    def place(values_at):
        for n in range(per_peer):
            at = places_ref[(hop - 2) * stride + n]
            b = places_ref[(pre - 2 + hop - 2) * stride + n]
            rows = pl.ds(pl.multiple_of(b * BLK, BLK), BLK)
            values = values_at(n, rows)
            parts = []
            for g in range(k_ref.shape[1] // HD):
                span = slice(g * HD, (g + 1) * HD)
                parts += [k_ref[rows, span], values[:, span]]
            cache[at] = jnp.concatenate(parts, axis=1)

    pl.when(me >= hop - 1)(lambda: place(lambda n, rows: v_ref[rows]))
    pl.when(me < hop - 1)(lambda: place(lambda n, rows: got_ref[n]))


def place_packed(cache, places_ref, distance, got_ref):
    per_peer = got_ref.shape[0]
    for n in range(per_peer):
        cache[places_ref[(distance - 2) * (per_peer + 1) + n]] = got_ref[n]


def values_kernel(
    hop, hops, pre, lengths_ref, slot_ref, v_ref, k_ref, weights_ref, factor_ref,
    acc_in, sum_in, cache_in, *refs,
):
    first_out, last = hop == 1, hop == hops
    refs = list(refs)
    if not first_out:
        refs.pop(0)
    got_ref = None if first_out else refs.pop(0)
    got_far = [refs.pop(0) for _ in range(hops + 1, pre)] if last else []
    out_hbm, cache_out = refs.pop(0), refs.pop(0)
    state = () if last else (refs.pop(0), refs.pop(0))
    turned, out_buf, sems, *rest = refs
    rows = v_ref.shape[0]
    blocks = rows // BLK
    tiles = rows // TILE
    kv_count = turned.shape[0]

    cache = rest[0] if last else cache_out
    cache[...] = cache_in[...]
    if first_out:
        place_blocks(cache, slot_ref, k_ref, v_ref, hop, pre, blocks)
    else:
        place_listed(cache, slot_ref, hop, pre, k_ref, v_ref, got_ref)
    if last:
        for n, far_ref in enumerate(got_far):
            place_packed(cache, slot_ref, hops + 1 + n, far_ref)
        cache_store = pltpu.make_async_copy(cache.at[0:blocks], cache_out, sems.at[tiles])
        cache_store.start()

    lows = [lowest_key(lengths_ref, hop, tile, rows) for tile in range(tiles)]
    pl.when(lows[0] < rows)(functools.partial(turn_values, v_ref, turned))
    stores = []
    for tile, low in enumerate(lows):
        end_it = finish(out_buf, tile * TILE)

        def act(at):
            def emit(*result):
                if not last:
                    keep(state, tile)(*result)
                end_it(*result)

            def add(g):
                weights = weights_ref[tile, g, at:rows]
                old = (acc_in, sum_in, factor_ref)
                mix(turned[g, :, at:rows], weights, g, tile, old, emit)

            for_groups(kv_count, add)

        where_seen(low, rows, act)
        span = slice(tile * TILE, (tile + 1) * TILE)
        store = pltpu.make_async_copy(out_buf.at[span], out_hbm.at[span], sems.at[tile])
        stores.append(store)
        if first_out:

            @pl.when(low == rows)
            def _():
                def end(g):
                    for j in range(GROUP):
                        end_it(g, j, *(ref[g, :, lanes_of(tile, j)] for ref in (acc_in, sum_in)))

                for_groups(kv_count, end)

            store.start()
        else:
            pl.when(low < rows)(store.start)
    for low, store in zip(lows, stores):
        if first_out:
            store.wait()
        else:
            pl.when(low < rows)(store.wait)
    if last:
        cache_store.wait()


def on_device(queries, new_keys, new_values, lengths, block_slot):
    rows, q_width = queries.shape
    kv_width = new_keys.shape[1]
    kv_count = kv_width // HD
    blocks = rows // BLK
    pre = lax.axis_size("pre")
    per_peer = blocks // pre
    hops = pre // 2
    tiles = rows // TILE
    bf16, f32 = jnp.bfloat16, jnp.float32
    shape = jax.ShapeDtypeStruct
    params = pltpu.CompilerParams(vmem_limit_bytes=24 * 2**20)
    own_params = pltpu.CompilerParams(vmem_limit_bytes=44 * 2**20)
    ring = [(i, (i + 1) % pre) for i in range(pre)]
    acc_shape = shape((kv_count, HD, GROUP * rows), f32)
    stat_shape = shape((kv_count, 8, GROUP * rows), f32)
    weights_shape = shape((tiles, kv_count, rows, GROUP * TILE), bf16)
    attended_shape = shape(queries.shape, bf16)
    cache_shape = shape((blocks, BLK, 2 * kv_width), bf16)
    open_cache = shape((blocks + 1, BLK, 2 * kv_width), bf16)
    turned = pltpu.VMEM((kv_count, HD + ONES, rows), bf16)
    bias = pltpu.VMEM((rows, TILE), f32)

    def cost(share, moved):
        pairs = int(rows * rows * share)
        return pl.CostEstimate(
            flops=4 * pairs * q_width,
            bytes_accessed=moved * 2**20,
            transcendentals=pairs * kv_count * GROUP,
        )

    def after(array, *others):
        return lax.optimization_barrier((array, *others))[0]

    k, v = lax.ppermute(new_keys, "pre", ring), lax.ppermute(new_values, "pre", ring)

    packed = (shape((per_peer, BLK, kv_width), bf16),) * (hops - 1)
    packed += (shape((per_peer, BLK, 2 * kv_width), bf16),) * (pre - 1 - hops)
    places = shape(((pre - 2 + hops - 1) * (per_peer + 1),), jnp.int32)
    in_hbm = (
        pltpu.with_memory_space_constraint(x, pltpu.HBM) for x in (queries, new_keys, new_values)
    )
    q, acc, total, top, cache, places, *sent = pl.pallas_call(
        functools.partial(own_kernel, pre, hops),
        out_shape=(attended_shape, acc_shape, stat_shape, stat_shape, open_cache, places)
        + packed,
        in_specs=[SMEM, SMEM] + [HBM] * 3,
        out_specs=(VMEM,) * 5 + (SMEM,) + (HBM,) * (pre - 2),
        scratch_shapes=[
            pltpu.VMEM((rows, kv_width), bf16),
            pltpu.VMEM((rows, kv_width), bf16),
            turned,
            bias,
            pltpu.VMEM(((hops - 1) * per_peer + 1, BLK, kv_width), bf16),
            pltpu.VMEM(((pre - 1 - hops) * per_peer + 1, BLK, 2 * kv_width), bf16),
            pltpu.SMEM((pre,), jnp.int32),
            pltpu.SemaphoreType.DMA((pre - 2,)),
            pltpu.SemaphoreType.DMA((3,)),
        ],
        cost_estimate=cost(1, 4),
        compiler_params=own_params,
        name="own_attention",
    )(lengths, block_slot, *in_hbm)
    got = []
    k = after(k, top)
    attended = None
    for hop in range(1, hops + 1):
        first_out, last = hop == 1, hop == hops
        onward = [(i, i + 1) for i in range(hop - 1, pre - 1)]
        next_k = None if last else lax.ppermute(k, "pre", ring)
        weights, factor, *tops = pl.pallas_call(
            functools.partial(scores_kernel, hop),
            out_shape=(weights_shape, stat_shape) + (() if last else (stat_shape,)),
            in_specs=[SMEM] + [VMEM] * 3,
            out_specs=(VMEM,) * (2 if last else 3),
            scratch_shapes=[bias],
            cost_estimate=cost(0.5, 3),
            compiler_params=params,
            name="scores",
        )(lengths, q, k, top)
        v = after(v, factor)
        next_v = None if last else lax.ppermute(v, "pre", onward)
        if first_out:
            for d in range(2, pre):
                targets = range(d - 1 if d <= hops else pre)
                pairs = [((i - d) % pre, i) for i in targets]
                got.append(lax.ppermute(after(sent[d - 2], v), "pre", pairs))
        carry = () if last else (acc_shape, stat_shape)
        extra = [] if first_out else [attended]
        extra += [] if first_out else [got[hop - 2]]
        extra += got[hops - 1 :] if last else []
        attended, cache, *state = pl.pallas_call(
            functools.partial(values_kernel, hop, hops, pre),
            out_shape=(attended_shape, cache_shape if last else open_cache)
            + carry,
            in_specs=[SMEM, SMEM]
            + [VMEM] * 7
            + ([] if first_out else [HBM])
            + [VMEM] * (len(extra) - 1),
            out_specs=(HBM, HBM if last else VMEM)
            + (VMEM,) * len(carry),
            scratch_shapes=[
                turned,
                pltpu.VMEM((rows, q_width), bf16),
                pltpu.SemaphoreType.DMA((tiles + 1,)),
            ]
            + ([pltpu.VMEM(open_cache.shape, bf16)] if last else []),
            input_output_aliases={} if first_out else {9: 0},
            cost_estimate=cost(0.5, 3),
            compiler_params=params,
            name="values",
        )(lengths, block_slot if first_out else places, v, k, weights, factor, acc, total, cache, *extra)
        if not last:
            (top,) = tops
            acc, total = state
            k, v = after(next_k, total), next_v

    return (attended, cache)


def solution(mesh):
    placed = (
        P(("parts", "pre"), "tp"),
        P(("parts", "pre"), "tp"),
        P(("parts", "pre"), "tp"),
        P("parts"),
        P("parts"),
    )
    return jax.shard_map(
        on_device,
        mesh=mesh,
        in_specs=placed,
        out_specs=(P(("parts", "pre"), "tp"), P(("parts", "pre"), None, "tp")),
        check_vma=False,
    )
```

```python
import functools
import math

import jax
import jax.numpy as jnp
from jax import lax
from jax.experimental import pallas as pl
from jax.experimental.pallas import tpu as pltpu
from jax.sharding import PartitionSpec as P

HD = 128
BLK = 16
GROUP = 4
TILE = 256
CUT = 128
ONES = 16
MASKED = -1e30
EXP_SCALE = math.log2(math.e) * HD ** (-0.5)

VMEM = pl.BlockSpec(memory_space=pltpu.VMEM)
SMEM = pl.BlockSpec(memory_space=pltpu.SMEM)
HBM = pl.BlockSpec(memory_space=pltpu.HBM)


def start_of(lengths_ref, position):
    end = jnp.int32(0)
    start = jnp.int32(0)
    for r in range(lengths_ref.shape[0]):
        end = end + lengths_ref[r]
        start = jnp.where(end <= position, end, start)
    return start


def row_starts(lengths_ref, positions):
    end = jnp.int32(0)
    starts = jnp.zeros_like(positions)
    for r in range(lengths_ref.shape[0]):
        end = end + lengths_ref[r]
        starts = jnp.where(positions >= end, end, starts)
    return starts


def fill_bias(bias_ref, lengths_ref, row_first, key_first, low, high, causal):
    shape = (high - low, TILE)
    positions = row_first + lax.broadcasted_iota(jnp.int32, (8, TILE), 1)
    starts = row_starts(lengths_ref, positions)
    keys = key_first + low + lax.broadcasted_iota(jnp.int32, shape, 0)
    keys = keys.reshape((high - low) // 8, 8, TILE)
    allowed = keys >= starts[None]
    if causal:
        allowed = allowed & (keys <= positions[None])
    bias_ref[low:high] = jnp.where(allowed, 0.0, MASKED).reshape(shape)


def turn_values(v_ref, turned, first=0):
    for g in range(turned.shape[0]):
        turned[g, :HD, first:] = v_ref[first:, g * HD : (g + 1) * HD].T
        turned[g, HD:, first:] = jnp.ones((ONES, turned.shape[2] - first), turned.dtype)


def lanes_of(tile, j):
    return slice((tile * GROUP + j) * TILE, (tile * GROUP + j + 1) * TILE)


def weigh(q_ref, k_ref, bias_ref, old_top, tile, low, high, g, emit):
    keys = k_ref[low:high, g * HD : (g + 1) * HD]
    heads = range(g * GROUP, (g + 1) * GROUP)
    queries = jnp.concatenate(
        [q_ref[tile * TILE : (tile + 1) * TILE, h * HD : (h + 1) * HD] for h in heads], axis=0
    )
    all_scores = lax.dot_general(
        keys, queries, (((1,), (1,)), ((), ())), preferred_element_type=jnp.float32
    )
    for j in range(GROUP):
        scores = all_scores[:, j * TILE : (j + 1) * TILE] + bias_ref[low:high]
        scores = scores.reshape((high - low) // 8, 8, TILE)
        highest = jnp.max(jnp.max(scores, axis=0), axis=0, keepdims=True)
        top = jnp.broadcast_to(highest, (8, TILE))
        factor = None
        if old_top is not None:
            old = old_top[g, :, lanes_of(tile, j)]
            top = jnp.maximum(old, top)
            factor = jnp.exp2((old - top) * EXP_SCALE)
        weights = jnp.exp2((scores - top[None]) * EXP_SCALE)
        emit(j, weights.reshape(high - low, TILE).astype(jnp.bfloat16), top, factor)


def mix(values, weights, g, tile, old, emit):
    all_added = jnp.dot(values, weights, preferred_element_type=jnp.float32)
    for j in range(GROUP):
        at = lanes_of(tile, j)
        added = all_added[:, j * TILE : (j + 1) * TILE]
        value, total = added[:HD], added[HD : HD + 8]
        if old is not None:
            acc_ref, sum_ref, factor_ref = old
            factor = factor_ref[g, :, at]
            total = total + sum_ref[g, :, at] * factor
            kept = acc_ref[g, :, at].reshape(HD // 8, 8, TILE) * factor[None]
            value = value + kept.reshape(HD, TILE)
        emit(g, j, value, total)


def keep(state, tile):
    def emit(g, j, value, total):
        for ref, array in zip(state, (value, total)):
            ref[g, :, lanes_of(tile, j)] = array

    return emit


def finish(out_ref, row):
    def emit(g, j, value, total):
        head = g * GROUP + j
        value = value.reshape(HD // 8, 8, TILE) * (1.0 / total)[None]
        value = value.reshape(HD, TILE).astype(out_ref.dtype).T
        out_ref[row : row + TILE, head * HD : (head + 1) * HD] = value

    return emit


def block_of(k_ref, v_ref, row):
    parts = []
    for g in range(k_ref.shape[1] // HD):
        span = slice(g * HD, (g + 1) * HD)
        parts += [k_ref[pl.ds(row, BLK), span], v_ref[pl.ds(row, BLK), span]]
    return jnp.concatenate(parts, axis=1)


def own_slot(slot, me, blocks):
    local = slot - me * blocks
    return jnp.where((local >= 0) & (local < blocks), local, blocks)


def list_places(places_ref, slot_ref, hops, pre, blocks):
    me = lax.axis_index("pre")
    stride = blocks // pre + 1
    for distance in range(2, pre):
        source = lax.rem(me - distance + pre, pre)

        def step(b, n):
            at = own_slot(slot_ref[source * blocks + b], me, blocks)
            places_ref[(distance - 2) * stride + n] = at
            if distance <= hops:
                places_ref[(pre - 2 + distance - 2) * stride + n] = b
            return n + jnp.where(at < blocks, 1, 0)

        lax.fori_loop(0, blocks, step, jnp.int32(0), unroll=8)


def own_kernel(
    pre, hops, lengths_ref, slot_ref, q_hbm, k_hbm, v_hbm,
    q_ref, acc_ref, sum_ref, top_ref, cache_ref, places_ref, *refs,
):
    sent_hbm, refs = refs[: pre - 2], refs[pre - 2 :]
    k_ref, v_ref, turned, bias, sent_values, sent, counts, sems, load_sems = refs
    loads = [
        pltpu.make_async_copy(src, dst, load_sems.at[n])
        for n, (src, dst) in enumerate(((k_hbm, k_ref), (v_hbm, v_ref), (q_hbm, q_ref)))
    ]
    for load in loads:
        load.start()
    rows = q_ref.shape[0]
    blocks = rows // BLK
    per_peer = blocks // pre
    me = lax.axis_index("pre")
    first = me * rows
    for owner in range(pre):
        counts[owner] = 0
    list_places(places_ref, slot_ref, hops, pre, blocks)
    loads[0].wait()
    loads[1].wait()

    def step(b, _):
        slot = slot_ref[me * blocks + b]
        owner = slot // blocks
        n = counts[owner]
        counts[owner] = n + 1
        distance = lax.rem(owner - me + pre, pre)
        row = pl.multiple_of(b * BLK, BLK)
        on_ring = (distance > 1) & (distance <= hops)
        at = jnp.where(on_ring, (distance - 2) * per_peer + n, (hops - 1) * per_peer)
        sent_values[at] = v_ref[pl.ds(row, BLK)]
        beyond = (distance - hops - 1) * per_peer + n
        at = jnp.where(distance > hops, beyond, (pre - 1 - hops) * per_peer)
        block = block_of(k_ref, v_ref, row)
        sent[at] = block
        cache_ref[own_slot(slot, me, blocks)] = block
        return 0

    lax.fori_loop(0, blocks, step, 0, unroll=4)
    packed = [sent_values.at[n * per_peer : (n + 1) * per_peer] for n in range(hops - 1)]
    packed += [sent.at[n * per_peer : (n + 1) * per_peer] for n in range(pre - 1 - hops)]
    stores = [
        pltpu.make_async_copy(src, dst, sems.at[n])
        for n, (src, dst) in enumerate(zip(packed, sent_hbm))
    ]
    for store in stores:
        store.start()
    turn_values(v_ref, turned)
    loads[2].wait()
    for tile in range(rows // TILE):
        high = (tile + 1) * TILE
        fill_bias(bias, lengths_ref, first + tile * TILE, first, 0, high, True)
        for g in range(turned.shape[0]):
            all_weights = []

            def emit(j, weights, top, factor):
                all_weights.append(weights)
                top_ref[g, :, lanes_of(tile, j)] = top

            weigh(q_ref, k_ref, bias, None, tile, 0, high, g, emit)
            all_weights = jnp.concatenate(all_weights, axis=1)
            mix(turned[g, :, :high], all_weights, g, tile, None, keep((acc_ref, sum_ref), tile))
    for store in stores:
        store.wait()


def lowest_key(lengths_ref, hop, tile, rows):
    first = lax.axis_index("pre") * rows
    key_first = first - hop * rows
    low = jnp.maximum(start_of(lengths_ref, first + tile * TILE) - key_first, 0)
    return jnp.where(key_first >= 0, jnp.minimum(low, rows), rows)


def where_seen(low, rows, act):
    for at in range(0, rows, CUT):
        pl.when((low >= at) & (low < at + CUT))(functools.partial(act, at))


def scores_kernel(hop, lengths_ref, q_ref, k_ref, old_top, weights_ref, factor_ref, *refs):
    *top_refs, bias = refs
    rows = q_ref.shape[0]
    first = lax.axis_index("pre") * rows
    for tile in range(rows // TILE):

        def act(at):
            fill_bias(
                bias, lengths_ref, first + tile * TILE, first - hop * rows, at, rows, False
            )
            for g in range(weights_ref.shape[1]):

                def emit(j, weights, top, factor):
                    weights_ref[tile, g, at:rows, j * TILE : (j + 1) * TILE] = weights
                    for top_ref in top_refs:
                        top_ref[g, :, lanes_of(tile, j)] = top
                    factor_ref[g, :, lanes_of(tile, j)] = factor

                weigh(q_ref, k_ref, bias, old_top, tile, at, rows, g, emit)

        where_seen(lowest_key(lengths_ref, hop, tile, rows), rows, act)


def place_blocks(cache, slot_ref, k_ref, v_ref, distance, pre, blocks):
    me = lax.axis_index("pre")
    source = lax.rem(me - distance + pre, pre)

    def step(b, _):
        at = own_slot(slot_ref[source * blocks + b], me, blocks)
        cache[at] = block_of(k_ref, v_ref, pl.multiple_of(b * BLK, BLK))
        return 0

    lax.fori_loop(0, blocks, step, 0, unroll=8)


def place_listed(cache, places_ref, hop, pre, k_ref, v_ref, got_ref):
    me = lax.axis_index("pre")
    per_peer = got_ref.shape[0]
    stride = per_peer + 1

    def place(values_at):
        for n in range(per_peer):
            at = places_ref[(hop - 2) * stride + n]
            b = places_ref[(pre - 2 + hop - 2) * stride + n]
            rows = pl.ds(pl.multiple_of(b * BLK, BLK), BLK)
            values = values_at(n, rows)
            parts = []
            for g in range(k_ref.shape[1] // HD):
                span = slice(g * HD, (g + 1) * HD)
                parts += [k_ref[rows, span], values[:, span]]
            cache[at] = jnp.concatenate(parts, axis=1)

    pl.when(me >= hop - 1)(lambda: place(lambda n, rows: v_ref[rows]))
    pl.when(me < hop - 1)(lambda: place(lambda n, rows: got_ref[n]))


def place_packed(cache, places_ref, distance, got_ref):
    per_peer = got_ref.shape[0]
    for n in range(per_peer):
        cache[places_ref[(distance - 2) * (per_peer + 1) + n]] = got_ref[n]


def values_kernel(
    hop, hops, pre, lengths_ref, slot_ref, v_ref, k_ref, weights_ref, factor_ref,
    acc_in, sum_in, cache_in, *refs,
):
    first_out, last = hop == 1, hop == hops
    refs = list(refs)
    if not first_out:
        refs.pop(0)
    got_ref = None if first_out else refs.pop(0)
    got_far = [refs.pop(0) for _ in range(hops + 1, pre)] if last else []
    out_hbm, cache_out = refs.pop(0), refs.pop(0)
    state = () if last else (refs.pop(0), refs.pop(0))
    turned, out_buf, sems, *rest = refs
    rows = v_ref.shape[0]
    blocks = rows // BLK
    tiles = rows // TILE
    kv_count = turned.shape[0]

    cache = rest[0] if last else cache_out
    cache[...] = cache_in[...]
    if first_out:
        place_blocks(cache, slot_ref, k_ref, v_ref, hop, pre, blocks)
    else:
        place_listed(cache, slot_ref, hop, pre, k_ref, v_ref, got_ref)
    if last:
        for n, far_ref in enumerate(got_far):
            place_packed(cache, slot_ref, hops + 1 + n, far_ref)
        cache_store = pltpu.make_async_copy(cache.at[0:blocks], cache_out, sems.at[tiles])
        cache_store.start()

    lows = [lowest_key(lengths_ref, hop, tile, rows) for tile in range(tiles)]
    where_seen(lows[0], rows, functools.partial(turn_values, v_ref, turned))
    stores = []
    for tile, low in enumerate(lows):
        end_it = finish(out_buf, tile * TILE)

        def act(at):
            def emit(*result):
                if not last:
                    keep(state, tile)(*result)
                end_it(*result)

            for g in range(kv_count):
                weights = weights_ref[tile, g, at:rows]
                old = (acc_in, sum_in, factor_ref)
                mix(turned[g, :, at:rows], weights, g, tile, old, emit)

        where_seen(low, rows, act)
        span = slice(tile * TILE, (tile + 1) * TILE)
        store = pltpu.make_async_copy(out_buf.at[span], out_hbm.at[span], sems.at[tile])
        stores.append(store)
        if first_out:

            @pl.when(low == rows)
            def _():
                for g in range(kv_count):
                    for j in range(GROUP):
                        end_it(g, j, *(ref[g, :, lanes_of(tile, j)] for ref in (acc_in, sum_in)))

            store.start()
        else:
            pl.when(low < rows)(store.start)
    for low, store in zip(lows, stores):
        if first_out:
            store.wait()
        else:
            pl.when(low < rows)(store.wait)
    if last:
        cache_store.wait()


def on_device(queries, new_keys, new_values, lengths, block_slot):
    rows, q_width = queries.shape
    kv_width = new_keys.shape[1]
    kv_count = kv_width // HD
    blocks = rows // BLK
    pre = lax.axis_size("pre")
    per_peer = blocks // pre
    hops = pre // 2
    tiles = rows // TILE
    bf16, f32 = jnp.bfloat16, jnp.float32
    shape = jax.ShapeDtypeStruct
    params = pltpu.CompilerParams(vmem_limit_bytes=24 * 2**20)
    own_params = pltpu.CompilerParams(vmem_limit_bytes=44 * 2**20)
    ring = [(i, (i + 1) % pre) for i in range(pre)]
    acc_shape = shape((kv_count, HD, GROUP * rows), f32)
    stat_shape = shape((kv_count, 8, GROUP * rows), f32)
    weights_shape = shape((tiles, kv_count, rows, GROUP * TILE), bf16)
    attended_shape = shape(queries.shape, bf16)
    cache_shape = shape((blocks, BLK, 2 * kv_width), bf16)
    open_cache = shape((blocks + 1, BLK, 2 * kv_width), bf16)
    turned = pltpu.VMEM((kv_count, HD + ONES, rows), bf16)
    bias = pltpu.VMEM((rows, TILE), f32)

    def cost(share, moved):
        pairs = int(rows * rows * share)
        return pl.CostEstimate(
            flops=4 * pairs * q_width,
            bytes_accessed=moved * 2**20,
            transcendentals=pairs * kv_count * GROUP,
        )

    def after(array, *others):
        return lax.optimization_barrier((array, *others))[0]

    k, v = lax.ppermute(new_keys, "pre", ring), lax.ppermute(new_values, "pre", ring)

    packed = (shape((per_peer, BLK, kv_width), bf16),) * (hops - 1)
    packed += (shape((per_peer, BLK, 2 * kv_width), bf16),) * (pre - 1 - hops)
    places = shape(((pre - 2 + hops - 1) * (per_peer + 1),), jnp.int32)
    in_hbm = (
        pltpu.with_memory_space_constraint(x, pltpu.HBM) for x in (queries, new_keys, new_values)
    )
    q, acc, total, top, cache, places, *sent = pl.pallas_call(
        functools.partial(own_kernel, pre, hops),
        out_shape=(attended_shape, acc_shape, stat_shape, stat_shape, open_cache, places)
        + packed,
        in_specs=[SMEM, SMEM] + [HBM] * 3,
        out_specs=(VMEM,) * 5 + (SMEM,) + (HBM,) * (pre - 2),
        scratch_shapes=[
            pltpu.VMEM((rows, kv_width), bf16),
            pltpu.VMEM((rows, kv_width), bf16),
            turned,
            bias,
            pltpu.VMEM(((hops - 1) * per_peer + 1, BLK, kv_width), bf16),
            pltpu.VMEM(((pre - 1 - hops) * per_peer + 1, BLK, 2 * kv_width), bf16),
            pltpu.SMEM((pre,), jnp.int32),
            pltpu.SemaphoreType.DMA((pre - 2,)),
            pltpu.SemaphoreType.DMA((3,)),
        ],
        cost_estimate=cost(1, 4),
        compiler_params=own_params,
        name="own_attention",
    )(lengths, block_slot, *in_hbm)
    got = []
    k = after(k, top)
    attended = None
    for hop in range(1, hops + 1):
        first_out, last = hop == 1, hop == hops
        onward = [(i, i + 1) for i in range(hop - 1, pre - 1)]
        next_k = None if last else lax.ppermute(k, "pre", ring)
        weights, factor, *tops = pl.pallas_call(
            functools.partial(scores_kernel, hop),
            out_shape=(weights_shape, stat_shape) + (() if last else (stat_shape,)),
            in_specs=[SMEM] + [VMEM] * 3,
            out_specs=(VMEM,) * (2 if last else 3),
            scratch_shapes=[bias],
            cost_estimate=cost(0.5, 3),
            compiler_params=params,
            name="scores",
        )(lengths, q, k, top)
        v = after(v, factor)
        next_v = None if last else lax.ppermute(v, "pre", onward)
        if first_out:
            for d in range(2, pre):
                targets = range(d - 1 if d <= hops else pre)
                pairs = [((i - d) % pre, i) for i in targets]
                got.append(lax.ppermute(after(sent[d - 2], v), "pre", pairs))
        carry = () if last else (acc_shape, stat_shape)
        extra = [] if first_out else [attended]
        extra += [] if first_out else [got[hop - 2]]
        extra += got[hops - 1 :] if last else []
        attended, cache, *state = pl.pallas_call(
            functools.partial(values_kernel, hop, hops, pre),
            out_shape=(attended_shape, cache_shape if last else open_cache)
            + carry,
            in_specs=[SMEM, SMEM]
            + [VMEM] * 7
            + ([] if first_out else [HBM])
            + [VMEM] * (len(extra) - 1),
            out_specs=(HBM, HBM if last else VMEM)
            + (VMEM,) * len(carry),
            scratch_shapes=[
                turned,
                pltpu.VMEM((rows, q_width), bf16),
                pltpu.SemaphoreType.DMA((tiles + 1,)),
            ]
            + ([pltpu.VMEM(open_cache.shape, bf16)] if last else []),
            input_output_aliases={} if first_out else {9: 0},
            cost_estimate=cost(0.5, 3),
            compiler_params=params,
            name="values",
        )(lengths, block_slot if first_out else places, v, k, weights, factor, acc, total, cache, *extra)
        if not last:
            (top,) = tops
            acc, total = state
            k, v = after(next_k, total), next_v

    return (attended, cache)


def solution(mesh):
    placed = (
        P(("parts", "pre"), "tp"),
        P(("parts", "pre"), "tp"),
        P(("parts", "pre"), "tp"),
        P("parts"),
        P("parts"),
    )
    return jax.shard_map(
        on_device,
        mesh=mesh,
        in_specs=placed,
        out_specs=(P(("parts", "pre"), "tp"), P(("parts", "pre"), None, "tp")),
        check_vma=False,
    )
```

```python
import functools
import math

import jax
import jax.numpy as jnp
from jax import lax
from jax.experimental import pallas as pl
from jax.experimental.pallas import tpu as pltpu
from jax.sharding import PartitionSpec as P

HD = 128
BLK = 16
GROUP = 4
TILE = 256
ONES = 16
MASKED = -1e30
EXP_SCALE = math.log2(math.e) * HD ** (-0.5)

VMEM = pl.BlockSpec(memory_space=pltpu.VMEM)
SMEM = pl.BlockSpec(memory_space=pltpu.SMEM)
HBM = pl.BlockSpec(memory_space=pltpu.HBM)


def start_of(lengths_ref, position):
    end = jnp.int32(0)
    start = jnp.int32(0)
    for r in range(lengths_ref.shape[0]):
        end = end + lengths_ref[r]
        start = jnp.where(end <= position, end, start)
    return start


def row_starts(lengths_ref, positions):
    end = jnp.int32(0)
    starts = jnp.zeros_like(positions)
    for r in range(lengths_ref.shape[0]):
        end = end + lengths_ref[r]
        starts = jnp.where(positions >= end, end, starts)
    return starts


def fill_bias(bias_ref, lengths_ref, row_first, key_first, low, high, causal):
    shape = (high - low, TILE)
    positions = row_first + lax.broadcasted_iota(jnp.int32, (8, TILE), 1)
    starts = row_starts(lengths_ref, positions)
    keys = key_first + low + lax.broadcasted_iota(jnp.int32, shape, 0)
    keys = keys.reshape((high - low) // 8, 8, TILE)
    allowed = keys >= starts[None]
    if causal:
        allowed = allowed & (keys <= positions[None])
    bias_ref[low:high] = jnp.where(allowed, 0.0, MASKED).reshape(shape)


def turn_values(v_ref, turned):
    for g in range(turned.shape[0]):
        turned[g, :HD] = v_ref[:, g * HD : (g + 1) * HD].T
        turned[g, HD:] = jnp.ones((ONES, turned.shape[2]), turned.dtype)


def lanes_of(tile, j):
    return slice((tile * GROUP + j) * TILE, (tile * GROUP + j + 1) * TILE)


def weigh(q_ref, k_ref, bias_ref, old_top, tile, low, high, g, emit):
    keys = k_ref[low:high, g * HD : (g + 1) * HD]
    heads = range(g * GROUP, (g + 1) * GROUP)
    queries = jnp.concatenate(
        [q_ref[tile * TILE : (tile + 1) * TILE, h * HD : (h + 1) * HD] for h in heads], axis=0
    )
    all_scores = lax.dot_general(
        keys, queries, (((1,), (1,)), ((), ())), preferred_element_type=jnp.float32
    )
    for j in range(GROUP):
        scores = all_scores[:, j * TILE : (j + 1) * TILE] + bias_ref[low:high]
        scores = scores.reshape((high - low) // 8, 8, TILE)
        highest = jnp.max(jnp.max(scores, axis=0), axis=0, keepdims=True)
        top = jnp.broadcast_to(highest, (8, TILE))
        factor = None
        if old_top is not None:
            old = old_top[g, :, lanes_of(tile, j)]
            top = jnp.maximum(old, top)
            factor = jnp.exp2((old - top) * EXP_SCALE)
        weights = jnp.exp2((scores - top[None]) * EXP_SCALE)
        emit(j, weights.reshape(high - low, TILE).astype(jnp.bfloat16), top, factor)


def mix(values, weights, g, tile, old, emit):
    all_added = jnp.dot(values, weights, preferred_element_type=jnp.float32)
    for j in range(GROUP):
        at = lanes_of(tile, j)
        added = all_added[:, j * TILE : (j + 1) * TILE]
        value, total = added[:HD], added[HD : HD + 8]
        if old is not None:
            acc_ref, sum_ref, factor_ref = old
            factor = factor_ref[g, :, at]
            total = total + sum_ref[g, :, at] * factor
            kept = acc_ref[g, :, at].reshape(HD // 8, 8, TILE) * factor[None]
            value = value + kept.reshape(HD, TILE)
        emit(g, j, value, total)


def keep(state, tile):
    def emit(g, j, value, total):
        for ref, array in zip(state, (value, total)):
            ref[g, :, lanes_of(tile, j)] = array

    return emit


def finish(out_ref, row):
    def emit(g, j, value, total):
        head = g * GROUP + j
        value = value.reshape(HD // 8, 8, TILE) * (1.0 / total)[None]
        value = value.reshape(HD, TILE).astype(out_ref.dtype).T
        out_ref[row : row + TILE, head * HD : (head + 1) * HD] = value

    return emit


def block_of(k_ref, v_ref, row):
    parts = []
    for g in range(k_ref.shape[1] // HD):
        span = slice(g * HD, (g + 1) * HD)
        parts += [k_ref[pl.ds(row, BLK), span], v_ref[pl.ds(row, BLK), span]]
    return jnp.concatenate(parts, axis=1)


def own_slot(slot, me, blocks):
    local = slot - me * blocks
    return jnp.where((local >= 0) & (local < blocks), local, blocks)


def list_places(places_ref, slot_ref, hops, pre, blocks):
    me = lax.axis_index("pre")
    stride = blocks // pre + 1
    for distance in range(2, pre):
        source = lax.rem(me - distance + pre, pre)

        def step(b, n):
            at = own_slot(slot_ref[source * blocks + b], me, blocks)
            places_ref[(distance - 2) * stride + n] = at
            if distance <= hops:
                places_ref[(pre - 2 + distance - 2) * stride + n] = b
            return n + jnp.where(at < blocks, 1, 0)

        lax.fori_loop(0, blocks, step, jnp.int32(0), unroll=8)


def own_kernel(
    pre, hops, lengths_ref, slot_ref, q_hbm, k_hbm, v_hbm,
    q_ref, acc_ref, sum_ref, top_ref, cache_ref, places_ref, *refs,
):
    sent_hbm, refs = refs[: pre - 2], refs[pre - 2 :]
    k_ref, v_ref, turned, bias, sent, counts, sems, load_sems = refs
    loads = [
        pltpu.make_async_copy(src, dst, load_sems.at[n])
        for n, (src, dst) in enumerate(((k_hbm, k_ref), (v_hbm, v_ref), (q_hbm, q_ref)))
    ]
    for load in loads:
        load.start()
    rows = q_ref.shape[0]
    blocks = rows // BLK
    per_peer = blocks // pre
    me = lax.axis_index("pre")
    first = me * rows
    for owner in range(pre):
        counts[owner] = 0
    list_places(places_ref, slot_ref, hops, pre, blocks)
    loads[0].wait()
    loads[1].wait()

    def step(b, _):
        slot = slot_ref[me * blocks + b]
        owner = slot // blocks
        n = counts[owner]
        counts[owner] = n + 1
        distance = lax.rem(owner - me + pre, pre)
        row = pl.multiple_of(b * BLK, BLK)
        at = jnp.where(distance > 1, (distance - 2) * per_peer + n, (pre - 2) * per_peer)
        block = block_of(k_ref, v_ref, row)
        sent[at] = block
        cache_ref[own_slot(slot, me, blocks)] = block
        return 0

    lax.fori_loop(0, blocks, step, 0, unroll=4)
    stores = [
        pltpu.make_async_copy(sent.at[n * per_peer : (n + 1) * per_peer], dst, sems.at[n])
        for n, dst in enumerate(sent_hbm)
    ]
    for store in stores:
        store.start()
    turn_values(v_ref, turned)
    loads[2].wait()
    for tile in range(rows // TILE):
        high = (tile + 1) * TILE
        fill_bias(bias, lengths_ref, first + tile * TILE, first, 0, high, True)
        for g in range(turned.shape[0]):
            all_weights = []

            def emit(j, weights, top, factor):
                all_weights.append(weights)
                top_ref[g, :, lanes_of(tile, j)] = top

            weigh(q_ref, k_ref, bias, None, tile, 0, high, g, emit)
            all_weights = jnp.concatenate(all_weights, axis=1)
            mix(turned[g, :, :high], all_weights, g, tile, None, keep((acc_ref, sum_ref), tile))
    for store in stores:
        store.wait()


def lowest_key(lengths_ref, hop, tile, rows):
    first = lax.axis_index("pre") * rows
    key_first = first - hop * rows
    low = jnp.maximum(start_of(lengths_ref, first + tile * TILE) - key_first, 0)
    return jnp.where(key_first >= 0, jnp.minimum(low, rows), rows)


def where_seen(low, rows, act):
    for at in range(0, rows, TILE):
        pl.when((low >= at) & (low < at + TILE))(functools.partial(act, at))


def scores_kernel(hop, lengths_ref, q_ref, k_ref, old_top, weights_ref, factor_ref, *refs):
    *top_refs, bias = refs
    rows = q_ref.shape[0]
    first = lax.axis_index("pre") * rows
    for tile in range(rows // TILE):

        def act(at):
            fill_bias(
                bias, lengths_ref, first + tile * TILE, first - hop * rows, at, rows, False
            )
            for g in range(weights_ref.shape[1]):

                def emit(j, weights, top, factor):
                    weights_ref[tile, g, at:rows, j * TILE : (j + 1) * TILE] = weights
                    for top_ref in top_refs:
                        top_ref[g, :, lanes_of(tile, j)] = top
                    factor_ref[g, :, lanes_of(tile, j)] = factor

                weigh(q_ref, k_ref, bias, old_top, tile, at, rows, g, emit)

        where_seen(lowest_key(lengths_ref, hop, tile, rows), rows, act)


def place_blocks(cache, slot_ref, k_ref, v_ref, distance, pre, blocks):
    me = lax.axis_index("pre")
    source = lax.rem(me - distance + pre, pre)

    def step(b, _):
        at = own_slot(slot_ref[source * blocks + b], me, blocks)
        cache[at] = block_of(k_ref, v_ref, pl.multiple_of(b * BLK, BLK))
        return 0

    lax.fori_loop(0, blocks, step, 0, unroll=8)


def place_listed(cache, places_ref, hop, pre, k_ref, v_ref):
    per_peer = (cache.shape[0] - 1) // pre
    stride = per_peer + 1
    for n in range(per_peer):
        b = places_ref[(pre - 2 + hop - 2) * stride + n]
        block = block_of(k_ref, v_ref, pl.multiple_of(b * BLK, BLK))
        cache[places_ref[(hop - 2) * stride + n]] = block


def place_packed(cache, places_ref, distance, got_ref):
    per_peer = got_ref.shape[0]
    for n in range(per_peer):
        cache[places_ref[(distance - 2) * (per_peer + 1) + n]] = got_ref[n]


def values_kernel(
    hop, hops, pre, lengths_ref, slot_ref, v_ref, k_ref, weights_ref, factor_ref,
    acc_in, sum_in, cache_in, *refs,
):
    first_out, last = hop == 1, hop == hops
    refs = list(refs)
    if not first_out:
        refs.pop(0)
    got_ref = None if first_out else refs.pop(0)
    got_far = [refs.pop(0) for _ in range(hops + 1, pre)] if last else []
    out_hbm, cache_out = refs.pop(0), refs.pop(0)
    state = () if last else (refs.pop(0), refs.pop(0))
    turned, out_buf, sems, *rest = refs
    rows = v_ref.shape[0]
    blocks = rows // BLK
    tiles = rows // TILE
    kv_count = turned.shape[0]

    cache = rest[0] if last else cache_out
    cache[...] = cache_in[...]
    if first_out:
        place_blocks(cache, slot_ref, k_ref, v_ref, hop, pre, blocks)
    else:
        me = lax.axis_index("pre")
        pl.when(me >= hop - 1)(
            lambda: place_listed(cache, slot_ref, hop, pre, k_ref, v_ref)
        )
        pl.when(me < hop - 1)(lambda: place_packed(cache, slot_ref, hop, got_ref))
    if last:
        for n, far_ref in enumerate(got_far):
            place_packed(cache, slot_ref, hops + 1 + n, far_ref)
        cache_store = pltpu.make_async_copy(cache.at[0:blocks], cache_out, sems.at[tiles])
        cache_store.start()

    lows = [lowest_key(lengths_ref, hop, tile, rows) for tile in range(tiles)]
    pl.when(lows[0] < rows)(functools.partial(turn_values, v_ref, turned))
    stores = []
    for tile, low in enumerate(lows):
        end_it = finish(out_buf, tile * TILE)

        def act(at):
            def emit(*result):
                if not last:
                    keep(state, tile)(*result)
                end_it(*result)

            for g in range(kv_count):
                weights = weights_ref[tile, g, at:rows]
                old = (acc_in, sum_in, factor_ref)
                mix(turned[g, :, at:rows], weights, g, tile, old, emit)

        where_seen(low, rows, act)
        span = slice(tile * TILE, (tile + 1) * TILE)
        store = pltpu.make_async_copy(out_buf.at[span], out_hbm.at[span], sems.at[tile])
        stores.append(store)
        if first_out:

            @pl.when(low == rows)
            def _():
                for g in range(kv_count):
                    for j in range(GROUP):
                        end_it(g, j, *(ref[g, :, lanes_of(tile, j)] for ref in (acc_in, sum_in)))

            store.start()
        else:
            pl.when(low < rows)(store.start)
    for low, store in zip(lows, stores):
        if first_out:
            store.wait()
        else:
            pl.when(low < rows)(store.wait)
    if last:
        cache_store.wait()


def on_device(queries, new_keys, new_values, lengths, block_slot):
    rows, q_width = queries.shape
    kv_width = new_keys.shape[1]
    kv_count = kv_width // HD
    blocks = rows // BLK
    pre = lax.axis_size("pre")
    per_peer = blocks // pre
    hops = pre // 2
    tiles = rows // TILE
    bf16, f32 = jnp.bfloat16, jnp.float32
    shape = jax.ShapeDtypeStruct
    params = pltpu.CompilerParams(vmem_limit_bytes=24 * 2**20)
    own_params = pltpu.CompilerParams(vmem_limit_bytes=44 * 2**20)
    ring = [(i, (i + 1) % pre) for i in range(pre)]
    acc_shape = shape((kv_count, HD, GROUP * rows), f32)
    stat_shape = shape((kv_count, 8, GROUP * rows), f32)
    weights_shape = shape((tiles, kv_count, rows, GROUP * TILE), bf16)
    attended_shape = shape(queries.shape, bf16)
    cache_shape = shape((blocks, BLK, 2 * kv_width), bf16)
    open_cache = shape((blocks + 1, BLK, 2 * kv_width), bf16)
    turned = pltpu.VMEM((kv_count, HD + ONES, rows), bf16)
    bias = pltpu.VMEM((rows, TILE), f32)

    def cost(share, moved):
        pairs = int(rows * rows * share)
        return pl.CostEstimate(
            flops=4 * pairs * q_width,
            bytes_accessed=moved * 2**20,
            transcendentals=pairs * kv_count * GROUP,
        )

    def after(array, *others):
        return lax.optimization_barrier((array, *others))[0]

    k, v = lax.ppermute(new_keys, "pre", ring), lax.ppermute(new_values, "pre", ring)

    packed = (shape((per_peer, BLK, 2 * kv_width), bf16),) * (pre - 2)
    places = shape(((pre - 2 + hops - 1) * (per_peer + 1),), jnp.int32)
    in_hbm = (
        pltpu.with_memory_space_constraint(x, pltpu.HBM) for x in (queries, new_keys, new_values)
    )
    q, acc, total, top, cache, places, *sent = pl.pallas_call(
        functools.partial(own_kernel, pre, hops),
        out_shape=(attended_shape, acc_shape, stat_shape, stat_shape, open_cache, places)
        + packed,
        in_specs=[SMEM, SMEM] + [HBM] * 3,
        out_specs=(VMEM,) * 5 + (SMEM,) + (HBM,) * (pre - 2),
        scratch_shapes=[
            pltpu.VMEM((rows, kv_width), bf16),
            pltpu.VMEM((rows, kv_width), bf16),
            turned,
            bias,
            pltpu.VMEM(((pre - 2) * per_peer + 1, BLK, 2 * kv_width), bf16),
            pltpu.SMEM((pre,), jnp.int32),
            pltpu.SemaphoreType.DMA((pre - 2,)),
            pltpu.SemaphoreType.DMA((3,)),
        ],
        cost_estimate=cost(1, 4),
        compiler_params=own_params,
        name="own_attention",
    )(lengths, block_slot, *in_hbm)
    got = []
    k = after(k, top)
    attended = None
    for hop in range(1, hops + 1):
        first_out, last = hop == 1, hop == hops
        onward = [(i, i + 1) for i in range(hop - 1, pre - 1)]
        next_k = None if last else lax.ppermute(k, "pre", ring)
        weights, factor, *tops = pl.pallas_call(
            functools.partial(scores_kernel, hop),
            out_shape=(weights_shape, stat_shape) + (() if last else (stat_shape,)),
            in_specs=[SMEM] + [VMEM] * 3,
            out_specs=(VMEM,) * (2 if last else 3),
            scratch_shapes=[bias],
            cost_estimate=cost(0.5, 3),
            compiler_params=params,
            name="scores",
        )(lengths, q, k, top)
        v = after(v, factor)
        next_v = None if last else lax.ppermute(v, "pre", onward)
        if first_out:
            for d in range(2, pre):
                targets = range(d - 1 if d <= hops else pre)
                pairs = [((i - d) % pre, i) for i in targets]
                got.append(lax.ppermute(after(sent[d - 2], v), "pre", pairs))
        carry = () if last else (acc_shape, stat_shape)
        extra = [] if first_out else [attended]
        extra += [] if first_out else [got[hop - 2]]
        extra += got[hops - 1 :] if last else []
        attended, cache, *state = pl.pallas_call(
            functools.partial(values_kernel, hop, hops, pre),
            out_shape=(attended_shape, cache_shape if last else open_cache)
            + carry,
            in_specs=[SMEM, SMEM]
            + [VMEM] * 7
            + ([] if first_out else [HBM])
            + [VMEM] * (len(extra) - 1),
            out_specs=(HBM, HBM if last else VMEM)
            + (VMEM,) * len(carry),
            scratch_shapes=[
                turned,
                pltpu.VMEM((rows, q_width), bf16),
                pltpu.SemaphoreType.DMA((tiles + 1,)),
            ]
            + ([pltpu.VMEM(open_cache.shape, bf16)] if last else []),
            input_output_aliases={} if first_out else {9: 0},
            cost_estimate=cost(0.5, 3),
            compiler_params=params,
            name="values",
        )(lengths, block_slot if first_out else places, v, k, weights, factor, acc, total, cache, *extra)
        if not last:
            (top,) = tops
            acc, total = state
            k, v = after(next_k, total), next_v

    return (attended, cache)


def solution(mesh):
    placed = (
        P(("parts", "pre"), "tp"),
        P(("parts", "pre"), "tp"),
        P(("parts", "pre"), "tp"),
        P("parts"),
        P("parts"),
    )
    return jax.shard_map(
        on_device,
        mesh=mesh,
        in_specs=placed,
        out_specs=(P(("parts", "pre"), "tp"), P(("parts", "pre"), None, "tp")),
        check_vma=False,
    )
```

```python
import functools
import math

import jax
import jax.numpy as jnp
from jax import lax
from jax.experimental import pallas as pl
from jax.experimental.pallas import tpu as pltpu
from jax.sharding import PartitionSpec as P

HD = 128
BLK = 16
GROUP = 4
TILE = 256
ONES = 16
MASKED = -1e30
EXP_SCALE = math.log2(math.e) * HD ** (-0.5)

VMEM = pl.BlockSpec(memory_space=pltpu.VMEM)
SMEM = pl.BlockSpec(memory_space=pltpu.SMEM)
HBM = pl.BlockSpec(memory_space=pltpu.HBM)


def start_of(lengths_ref, position):
    end = jnp.int32(0)
    start = jnp.int32(0)
    for r in range(lengths_ref.shape[0]):
        end = end + lengths_ref[r]
        start = jnp.where(end <= position, end, start)
    return start


def row_starts(lengths_ref, positions):
    end = jnp.int32(0)
    starts = jnp.zeros_like(positions)
    for r in range(lengths_ref.shape[0]):
        end = end + lengths_ref[r]
        starts = jnp.where(positions >= end, end, starts)
    return starts


def fill_bias(bias_ref, lengths_ref, row_first, key_first, low, high, causal):
    shape = (high - low, TILE)
    positions = row_first + lax.broadcasted_iota(jnp.int32, (8, TILE), 1)
    starts = row_starts(lengths_ref, positions)
    keys = key_first + low + lax.broadcasted_iota(jnp.int32, shape, 0)
    keys = keys.reshape((high - low) // 8, 8, TILE)
    allowed = keys >= starts[None]
    if causal:
        allowed = allowed & (keys <= positions[None])
    bias_ref[low:high] = jnp.where(allowed, 0.0, MASKED).reshape(shape)


def turn_values(v_ref, turned):
    for g in range(turned.shape[0]):
        turned[g, :HD] = v_ref[:, g * HD : (g + 1) * HD].T
        turned[g, HD:] = jnp.ones((ONES, turned.shape[2]), turned.dtype)


def lanes_of(tile, j):
    return slice((tile * GROUP + j) * TILE, (tile * GROUP + j + 1) * TILE)


def weigh(q_ref, k_ref, bias_ref, old_top, tile, low, high, g, emit):
    keys = k_ref[low:high, g * HD : (g + 1) * HD]
    heads = range(g * GROUP, (g + 1) * GROUP)
    queries = jnp.concatenate(
        [q_ref[tile * TILE : (tile + 1) * TILE, h * HD : (h + 1) * HD] for h in heads], axis=0
    )
    all_scores = lax.dot_general(
        keys, queries, (((1,), (1,)), ((), ())), preferred_element_type=jnp.float32
    )
    for j in range(GROUP):
        scores = all_scores[:, j * TILE : (j + 1) * TILE] + bias_ref[low:high]
        scores = scores.reshape((high - low) // 8, 8, TILE)
        highest = jnp.max(jnp.max(scores, axis=0), axis=0, keepdims=True)
        top = jnp.broadcast_to(highest, (8, TILE))
        factor = None
        if old_top is not None:
            old = old_top[g, :, lanes_of(tile, j)]
            top = jnp.maximum(old, top)
            factor = jnp.exp2((old - top) * EXP_SCALE)
        weights = jnp.exp2((scores - top[None]) * EXP_SCALE)
        emit(j, weights.reshape(high - low, TILE).astype(jnp.bfloat16), top, factor)


def mix(values, weights, g, tile, old, emit):
    all_added = jnp.dot(values, weights, preferred_element_type=jnp.float32)
    for j in range(GROUP):
        at = lanes_of(tile, j)
        added = all_added[:, j * TILE : (j + 1) * TILE]
        value, total = added[:HD], added[HD : HD + 8]
        if old is not None:
            acc_ref, sum_ref, factor_ref = old
            factor = factor_ref[g, :, at]
            total = total + sum_ref[g, :, at] * factor
            kept = acc_ref[g, :, at].reshape(HD // 8, 8, TILE) * factor[None]
            value = value + kept.reshape(HD, TILE)
        emit(g, j, value, total)


def keep(state, tile):
    def emit(g, j, value, total):
        for ref, array in zip(state, (value, total)):
            ref[g, :, lanes_of(tile, j)] = array

    return emit


def finish(out_ref, row):
    def emit(g, j, value, total):
        head = g * GROUP + j
        value = value.reshape(HD // 8, 8, TILE) * (1.0 / total)[None]
        value = value.reshape(HD, TILE).astype(out_ref.dtype).T
        out_ref[row : row + TILE, head * HD : (head + 1) * HD] = value

    return emit


def block_of(k_ref, v_ref, row):
    parts = []
    for g in range(k_ref.shape[1] // HD):
        span = slice(g * HD, (g + 1) * HD)
        parts += [k_ref[pl.ds(row, BLK), span], v_ref[pl.ds(row, BLK), span]]
    return jnp.concatenate(parts, axis=1)


def own_slot(slot, me, blocks):
    local = slot - me * blocks
    return jnp.where((local >= 0) & (local < blocks), local, blocks)


def list_places(places_ref, slot_ref, hops, pre, blocks):
    me = lax.axis_index("pre")
    stride = blocks // pre + 1
    for distance in range(2, pre):
        source = lax.rem(me - distance + pre, pre)

        def step(b, n):
            at = own_slot(slot_ref[source * blocks + b], me, blocks)
            places_ref[(distance - 2) * stride + n] = at
            if distance <= hops:
                places_ref[(pre - 2 + distance - 2) * stride + n] = b
            return n + jnp.where(at < blocks, 1, 0)

        lax.fori_loop(0, blocks, step, jnp.int32(0), unroll=8)


def own_kernel(
    pre, hops, lengths_ref, slot_ref, q_hbm, k_hbm, v_hbm,
    q_ref, acc_ref, sum_ref, top_ref, cache_ref, places_ref, *refs,
):
    sent_hbm, refs = refs[: pre - 2], refs[pre - 2 :]
    k_ref, v_ref, turned, bias, sent_values, sent, counts, sems, load_sems = refs
    loads = [
        pltpu.make_async_copy(src, dst, load_sems.at[n])
        for n, (src, dst) in enumerate(((k_hbm, k_ref), (v_hbm, v_ref), (q_hbm, q_ref)))
    ]
    for load in loads:
        load.start()
    rows = q_ref.shape[0]
    blocks = rows // BLK
    per_peer = blocks // pre
    me = lax.axis_index("pre")
    first = me * rows
    for owner in range(pre):
        counts[owner] = 0
    list_places(places_ref, slot_ref, hops, pre, blocks)
    loads[0].wait()
    loads[1].wait()

    def step(b, _):
        slot = slot_ref[me * blocks + b]
        owner = slot // blocks
        n = counts[owner]
        counts[owner] = n + 1
        distance = lax.rem(owner - me + pre, pre)
        row = pl.multiple_of(b * BLK, BLK)
        on_ring = (distance > 1) & (distance <= hops)
        at = jnp.where(on_ring, (distance - 2) * per_peer + n, (hops - 1) * per_peer)
        sent_values[at] = v_ref[pl.ds(row, BLK)]
        beyond = (distance - hops - 1) * per_peer + n
        at = jnp.where(distance > hops, beyond, (pre - 1 - hops) * per_peer)
        block = block_of(k_ref, v_ref, row)
        sent[at] = block
        cache_ref[own_slot(slot, me, blocks)] = block
        return 0

    lax.fori_loop(0, blocks, step, 0, unroll=4)
    packed = [sent_values.at[n * per_peer : (n + 1) * per_peer] for n in range(hops - 1)]
    packed += [sent.at[n * per_peer : (n + 1) * per_peer] for n in range(pre - 1 - hops)]
    stores = [
        pltpu.make_async_copy(src, dst, sems.at[n])
        for n, (src, dst) in enumerate(zip(packed, sent_hbm))
    ]
    for store in stores:
        store.start()
    turn_values(v_ref, turned)
    loads[2].wait()
    for tile in range(rows // TILE):
        high = (tile + 1) * TILE
        fill_bias(bias, lengths_ref, first + tile * TILE, first, 0, high, True)
        for g in range(turned.shape[0]):
            all_weights = []

            def emit(j, weights, top, factor):
                all_weights.append(weights)
                top_ref[g, :, lanes_of(tile, j)] = top

            weigh(q_ref, k_ref, bias, None, tile, 0, high, g, emit)
            all_weights = jnp.concatenate(all_weights, axis=1)
            mix(turned[g, :, :high], all_weights, g, tile, None, keep((acc_ref, sum_ref), tile))
    for store in stores:
        store.wait()


def lowest_key(lengths_ref, hop, tile, rows):
    first = lax.axis_index("pre") * rows
    key_first = first - hop * rows
    low = jnp.maximum(start_of(lengths_ref, first + tile * TILE) - key_first, 0)
    return jnp.where(key_first >= 0, jnp.minimum(low, rows), rows)


def where_seen(low, rows, act):
    for at in range(0, rows, TILE):
        pl.when((low >= at) & (low < at + TILE))(functools.partial(act, at))


def scores_kernel(hop, lengths_ref, q_ref, k_ref, old_top, weights_ref, factor_ref, *refs):
    *top_refs, bias = refs
    rows = q_ref.shape[0]
    first = lax.axis_index("pre") * rows
    for tile in range(rows // TILE):

        def act(at):
            fill_bias(
                bias, lengths_ref, first + tile * TILE, first - hop * rows, at, rows, False
            )
            for g in range(weights_ref.shape[1]):

                def emit(j, weights, top, factor):
                    weights_ref[tile, g, at:rows, j * TILE : (j + 1) * TILE] = weights
                    for top_ref in top_refs:
                        top_ref[g, :, lanes_of(tile, j)] = top
                    factor_ref[g, :, lanes_of(tile, j)] = factor

                weigh(q_ref, k_ref, bias, old_top, tile, at, rows, g, emit)

        where_seen(lowest_key(lengths_ref, hop, tile, rows), rows, act)


def place_blocks(cache, slot_ref, k_ref, v_ref, distance, pre, blocks):
    me = lax.axis_index("pre")
    source = lax.rem(me - distance + pre, pre)

    def step(b, _):
        at = own_slot(slot_ref[source * blocks + b], me, blocks)
        cache[at] = block_of(k_ref, v_ref, pl.multiple_of(b * BLK, BLK))
        return 0

    lax.fori_loop(0, blocks, step, 0, unroll=8)


def stage_listed(staged, places_ref, hop, pre, k_ref, v_ref, got_ref):
    me = lax.axis_index("pre")
    per_peer = got_ref.shape[0]
    stride = per_peer + 1

    def stage(values_at):
        for n in range(per_peer):
            b = places_ref[(pre - 2 + hop - 2) * stride + n]
            rows = pl.ds(pl.multiple_of(b * BLK, BLK), BLK)
            values = values_at(n, rows)
            parts = []
            for g in range(k_ref.shape[1] // HD):
                span = slice(g * HD, (g + 1) * HD)
                parts += [k_ref[rows, span], values[:, span]]
            staged[n] = jnp.concatenate(parts, axis=1)

    pl.when(me >= hop - 1)(lambda: stage(lambda n, rows: v_ref[rows]))
    pl.when(me < hop - 1)(lambda: stage(lambda n, rows: got_ref[n]))


def place_from(blocks_ref, cache_hbm, places_ref, distance, sems, first):
    per_peer = blocks_ref.shape[0]
    copies = []
    for n in range(per_peer):
        at = places_ref[(distance - 2) * (per_peer + 1) + n]
        copies.append(
            pltpu.make_async_copy(blocks_ref.at[n], cache_hbm.at[at], sems.at[first + n])
        )
        copies[-1].start()
    return copies


def values_kernel(
    hop, hops, pre, lengths_ref, slot_ref, v_ref, k_ref, weights_ref, factor_ref,
    acc_in, sum_in, cache_in, *refs,
):
    first_out, last = hop == 1, hop == hops
    refs = list(refs)
    if not first_out:
        refs.pop(0)
        cache_in = None
    got_ref = None if first_out else refs.pop(0)
    got_far = [refs.pop(0) for _ in range(hops + 1, pre)] if last else []
    out_hbm, cache_out = refs.pop(0), refs.pop(0)
    state = () if last else (refs.pop(0), refs.pop(0))
    turned, out_buf, sems, blocks_buf = refs
    rows = v_ref.shape[0]
    blocks = rows // BLK
    tiles = rows // TILE
    kv_count = turned.shape[0]

    if first_out:
        blocks_buf[...] = cache_in[...]
        place_blocks(blocks_buf, slot_ref, k_ref, v_ref, hop, pre, blocks)
        copies = [
            pltpu.make_async_copy(blocks_buf.at[0:blocks], cache_out, sems.at[tiles])
        ]
        copies[0].start()
    else:
        per_peer = blocks // pre
        stage_listed(blocks_buf, slot_ref, hop, pre, k_ref, v_ref, got_ref)
        copies = place_from(blocks_buf, cache_out, slot_ref, hop, sems, tiles)
        for n, far_ref in enumerate(got_far):
            at = tiles + (n + 1) * per_peer
            copies += place_from(far_ref, cache_out, slot_ref, hops + 1 + n, sems, at)

    lows = [lowest_key(lengths_ref, hop, tile, rows) for tile in range(tiles)]
    pl.when(lows[0] < rows)(functools.partial(turn_values, v_ref, turned))
    stores = []
    for tile, low in enumerate(lows):
        end_it = finish(out_buf, tile * TILE)

        def act(at):
            def emit(*result):
                if not last:
                    keep(state, tile)(*result)
                end_it(*result)

            for g in range(kv_count):
                weights = weights_ref[tile, g, at:rows]
                old = (acc_in, sum_in, factor_ref)
                mix(turned[g, :, at:rows], weights, g, tile, old, emit)

        where_seen(low, rows, act)
        span = slice(tile * TILE, (tile + 1) * TILE)
        store = pltpu.make_async_copy(out_buf.at[span], out_hbm.at[span], sems.at[tile])
        stores.append(store)
        if first_out:

            @pl.when(low == rows)
            def _():
                for g in range(kv_count):
                    for j in range(GROUP):
                        end_it(g, j, *(ref[g, :, lanes_of(tile, j)] for ref in (acc_in, sum_in)))

            store.start()
        else:
            pl.when(low < rows)(store.start)
    for low, store in zip(lows, stores):
        if first_out:
            store.wait()
        else:
            pl.when(low < rows)(store.wait)
    for copy in copies:
        copy.wait()


def on_device(queries, new_keys, new_values, lengths, block_slot):
    rows, q_width = queries.shape
    kv_width = new_keys.shape[1]
    kv_count = kv_width // HD
    blocks = rows // BLK
    pre = lax.axis_size("pre")
    per_peer = blocks // pre
    hops = pre // 2
    tiles = rows // TILE
    bf16, f32 = jnp.bfloat16, jnp.float32
    shape = jax.ShapeDtypeStruct
    params = pltpu.CompilerParams(vmem_limit_bytes=24 * 2**20)
    own_params = pltpu.CompilerParams(vmem_limit_bytes=44 * 2**20)
    ring = [(i, (i + 1) % pre) for i in range(pre)]
    acc_shape = shape((kv_count, HD, GROUP * rows), f32)
    stat_shape = shape((kv_count, 8, GROUP * rows), f32)
    weights_shape = shape((tiles, kv_count, rows, GROUP * TILE), bf16)
    attended_shape = shape(queries.shape, bf16)
    cache_shape = shape((blocks, BLK, 2 * kv_width), bf16)
    open_cache = shape((blocks + 1, BLK, 2 * kv_width), bf16)
    turned = pltpu.VMEM((kv_count, HD + ONES, rows), bf16)
    bias = pltpu.VMEM((rows, TILE), f32)

    def cost(share, moved):
        pairs = int(rows * rows * share)
        return pl.CostEstimate(
            flops=4 * pairs * q_width,
            bytes_accessed=moved * 2**20,
            transcendentals=pairs * kv_count * GROUP,
        )

    def after(array, *others):
        return lax.optimization_barrier((array, *others))[0]

    k, v = lax.ppermute(new_keys, "pre", ring), lax.ppermute(new_values, "pre", ring)

    packed = (shape((per_peer, BLK, kv_width), bf16),) * (hops - 1)
    packed += (shape((per_peer, BLK, 2 * kv_width), bf16),) * (pre - 1 - hops)
    places = shape(((pre - 2 + hops - 1) * (per_peer + 1),), jnp.int32)
    in_hbm = (
        pltpu.with_memory_space_constraint(x, pltpu.HBM) for x in (queries, new_keys, new_values)
    )
    q, acc, total, top, cache, places, *sent = pl.pallas_call(
        functools.partial(own_kernel, pre, hops),
        out_shape=(attended_shape, acc_shape, stat_shape, stat_shape, open_cache, places)
        + packed,
        in_specs=[SMEM, SMEM] + [HBM] * 3,
        out_specs=(VMEM,) * 5 + (SMEM,) + (HBM,) * (pre - 2),
        scratch_shapes=[
            pltpu.VMEM((rows, kv_width), bf16),
            pltpu.VMEM((rows, kv_width), bf16),
            turned,
            bias,
            pltpu.VMEM(((hops - 1) * per_peer + 1, BLK, kv_width), bf16),
            pltpu.VMEM(((pre - 1 - hops) * per_peer + 1, BLK, 2 * kv_width), bf16),
            pltpu.SMEM((pre,), jnp.int32),
            pltpu.SemaphoreType.DMA((pre - 2,)),
            pltpu.SemaphoreType.DMA((3,)),
        ],
        cost_estimate=cost(1, 4),
        compiler_params=own_params,
        name="own_attention",
    )(lengths, block_slot, *in_hbm)
    got = []
    k = after(k, top)
    attended = None
    for hop in range(1, hops + 1):
        first_out, last = hop == 1, hop == hops
        onward = [(i, i + 1) for i in range(hop - 1, pre - 1)]
        next_k = None if last else lax.ppermute(k, "pre", ring)
        weights, factor, *tops = pl.pallas_call(
            functools.partial(scores_kernel, hop),
            out_shape=(weights_shape, stat_shape) + (() if last else (stat_shape,)),
            in_specs=[SMEM] + [VMEM] * 3,
            out_specs=(VMEM,) * (2 if last else 3),
            scratch_shapes=[bias],
            cost_estimate=cost(0.5, 3),
            compiler_params=params,
            name="scores",
        )(lengths, q, k, top)
        v = after(v, factor)
        next_v = None if last else lax.ppermute(v, "pre", onward)
        if first_out:
            for d in range(2, pre):
                targets = range(d - 1 if d <= hops else pre)
                pairs = [((i - d) % pre, i) for i in targets]
                got.append(lax.ppermute(after(sent[d - 2], v), "pre", pairs))
        carry = () if last else (acc_shape, stat_shape)
        extra = [] if first_out else [attended]
        extra += [] if first_out else [got[hop - 2]]
        extra += got[hops - 1 :] if last else []
        attended, cache, *state = pl.pallas_call(
            functools.partial(values_kernel, hop, hops, pre),
            out_shape=(attended_shape, cache_shape) + carry,
            in_specs=[SMEM, SMEM]
            + [VMEM] * 6
            + [VMEM if first_out else HBM]
            + ([] if first_out else [HBM])
            + [VMEM] * (len(extra) - 1),
            out_specs=(HBM, HBM) + (VMEM,) * len(carry),
            scratch_shapes=[
                turned,
                pltpu.VMEM((rows, q_width), bf16),
                pltpu.SemaphoreType.DMA((tiles + blocks,)),
                pltpu.VMEM(open_cache.shape if first_out else packed[-1].shape, bf16),
            ],
            input_output_aliases={} if first_out else {8: 1, 9: 0},
            cost_estimate=cost(0.5, 3),
            compiler_params=params,
            name="values",
        )(lengths, block_slot if first_out else places, v, k, weights, factor, acc, total, cache, *extra)
        if not last:
            (top,) = tops
            acc, total = state
            k, v = after(next_k, total), next_v

    return (attended, cache)


def solution(mesh):
    placed = (
        P(("parts", "pre"), "tp"),
        P(("parts", "pre"), "tp"),
        P(("parts", "pre"), "tp"),
        P("parts"),
        P("parts"),
    )
    return jax.shard_map(
        on_device,
        mesh=mesh,
        in_specs=placed,
        out_specs=(P(("parts", "pre"), "tp"), P(("parts", "pre"), None, "tp")),
        check_vma=False,
    )
```

```python
import functools
import math

import jax
import jax.numpy as jnp
from jax import lax
from jax.experimental import pallas as pl
from jax.experimental.pallas import tpu as pltpu
from jax.sharding import PartitionSpec as P

HD = 128
BLK = 16
GROUP = 4
TILE = 256
ONES = 16
MASKED = -1e30
EXP_SCALE = math.log2(math.e) * HD ** (-0.5)

VMEM = pl.BlockSpec(memory_space=pltpu.VMEM)
SMEM = pl.BlockSpec(memory_space=pltpu.SMEM)
HBM = pl.BlockSpec(memory_space=pltpu.HBM)


def start_of(lengths_ref, position):
    end = jnp.int32(0)
    start = jnp.int32(0)
    for r in range(lengths_ref.shape[0]):
        end = end + lengths_ref[r]
        start = jnp.where(end <= position, end, start)
    return start


def row_starts(lengths_ref, positions):
    end = jnp.int32(0)
    starts = jnp.zeros_like(positions)
    for r in range(lengths_ref.shape[0]):
        end = end + lengths_ref[r]
        starts = jnp.where(positions >= end, end, starts)
    return starts


def fill_bias(bias_ref, lengths_ref, row_first, key_first, low, high, causal):
    shape = (high - low, TILE)
    positions = row_first + lax.broadcasted_iota(jnp.int32, (8, TILE), 1)
    starts = row_starts(lengths_ref, positions)
    keys = key_first + low + lax.broadcasted_iota(jnp.int32, shape, 0)
    keys = keys.reshape((high - low) // 8, 8, TILE)
    allowed = keys >= starts[None]
    if causal:
        allowed = allowed & (keys <= positions[None])
    bias_ref[low:high] = jnp.where(allowed, 0.0, MASKED).reshape(shape)


def turn_values(v_ref, turned):
    for g in range(turned.shape[0]):
        turned[g, :HD] = v_ref[:, g * HD : (g + 1) * HD].T
        turned[g, HD:] = jnp.ones((ONES, turned.shape[2]), turned.dtype)


def lanes_of(tile, j):
    return slice((tile * GROUP + j) * TILE, (tile * GROUP + j + 1) * TILE)


def weigh(q_ref, k_ref, bias_ref, old_top, tile, low, high, g, emit):
    keys = k_ref[low:high, g * HD : (g + 1) * HD]
    heads = range(g * GROUP, (g + 1) * GROUP)
    queries = jnp.concatenate(
        [q_ref[tile * TILE : (tile + 1) * TILE, h * HD : (h + 1) * HD] for h in heads], axis=0
    )
    all_scores = lax.dot_general(
        keys, queries, (((1,), (1,)), ((), ())), preferred_element_type=jnp.float32
    )
    for j in range(GROUP):
        scores = all_scores[:, j * TILE : (j + 1) * TILE] + bias_ref[low:high]
        scores = scores.reshape((high - low) // 8, 8, TILE)
        highest = jnp.max(jnp.max(scores, axis=0), axis=0, keepdims=True)
        top = jnp.broadcast_to(highest, (8, TILE))
        factor = None
        if old_top is not None:
            old = old_top[g, :, lanes_of(tile, j)]
            top = jnp.maximum(old, top)
            factor = jnp.exp2((old - top) * EXP_SCALE)
        weights = jnp.exp2((scores - top[None]) * EXP_SCALE)
        emit(j, weights.reshape(high - low, TILE).astype(jnp.bfloat16), top, factor)


def mix(values, weights, g, tile, old, emit):
    all_added = jnp.dot(values, weights, preferred_element_type=jnp.float32)
    for j in range(GROUP):
        at = lanes_of(tile, j)
        added = all_added[:, j * TILE : (j + 1) * TILE]
        value, total = added[:HD], added[HD : HD + 8]
        if old is not None:
            acc_ref, sum_ref, factor_ref = old
            factor = factor_ref[g, :, at]
            total = total + sum_ref[g, :, at] * factor
            kept = acc_ref[g, :, at].reshape(HD // 8, 8, TILE) * factor[None]
            value = value + kept.reshape(HD, TILE)
        emit(g, j, value, total)


def keep(state, tile):
    def emit(g, j, value, total):
        for ref, array in zip(state, (value, total)):
            ref[g, :, lanes_of(tile, j)] = array

    return emit


def finish(out_ref, row):
    def emit(g, j, value, total):
        head = g * GROUP + j
        value = value.reshape(HD // 8, 8, TILE) * (1.0 / total)[None]
        value = value.reshape(HD, TILE).astype(out_ref.dtype).T
        out_ref[row : row + TILE, head * HD : (head + 1) * HD] = value

    return emit


def block_of(k_ref, v_ref, row):
    parts = []
    for g in range(k_ref.shape[1] // HD):
        span = slice(g * HD, (g + 1) * HD)
        parts += [k_ref[pl.ds(row, BLK), span], v_ref[pl.ds(row, BLK), span]]
    return jnp.concatenate(parts, axis=1)


def own_slot(slot, me, blocks):
    local = slot - me * blocks
    return jnp.where((local >= 0) & (local < blocks), local, blocks)


def list_places(places_ref, slot_ref, hops, pre, blocks):
    me = lax.axis_index("pre")
    stride = blocks // pre + 1
    for distance in range(2, pre):
        source = lax.rem(me - distance + pre, pre)

        def step(b, n):
            at = own_slot(slot_ref[source * blocks + b], me, blocks)
            places_ref[(distance - 2) * stride + n] = at
            if distance <= hops:
                places_ref[(pre - 2 + distance - 2) * stride + n] = b
            return n + jnp.where(at < blocks, 1, 0)

        lax.fori_loop(0, blocks, step, jnp.int32(0), unroll=8)


def own_kernel(
    pre, hops, lengths_ref, slot_ref, q_hbm, k_hbm, v_hbm,
    q_ref, acc_ref, sum_ref, top_ref, cache_ref, places_ref, *refs,
):
    sent_hbm, refs = refs[: pre - 2], refs[pre - 2 :]
    k_ref, v_ref, turned, bias, sent_values, sent, counts, sems, load_sems = refs
    loads = [
        pltpu.make_async_copy(src, dst, load_sems.at[n])
        for n, (src, dst) in enumerate(((k_hbm, k_ref), (v_hbm, v_ref), (q_hbm, q_ref)))
    ]
    for load in loads:
        load.start()
    rows = q_ref.shape[0]
    blocks = rows // BLK
    per_peer = blocks // pre
    me = lax.axis_index("pre")
    first = me * rows
    for owner in range(pre):
        counts[owner] = 0
    list_places(places_ref, slot_ref, hops, pre, blocks)
    loads[0].wait()
    loads[1].wait()

    def step(b, _):
        slot = slot_ref[me * blocks + b]
        owner = slot // blocks
        n = counts[owner]
        counts[owner] = n + 1
        distance = lax.rem(owner - me + pre, pre)
        row = pl.multiple_of(b * BLK, BLK)
        on_ring = (distance > 1) & (distance <= hops)
        at = jnp.where(on_ring, (distance - 2) * per_peer + n, (hops - 1) * per_peer)
        sent_values[at] = v_ref[pl.ds(row, BLK)]
        beyond = (distance - hops - 1) * per_peer + n
        at = jnp.where(distance > hops, beyond, (pre - 1 - hops) * per_peer)
        block = block_of(k_ref, v_ref, row)
        sent[at] = block
        cache_ref[own_slot(slot, me, blocks)] = block
        return 0

    lax.fori_loop(0, blocks, step, 0, unroll=4)
    packed = [sent_values.at[n * per_peer : (n + 1) * per_peer] for n in range(hops - 1)]
    packed += [sent.at[n * per_peer : (n + 1) * per_peer] for n in range(pre - 1 - hops)]
    stores = [
        pltpu.make_async_copy(src, dst, sems.at[n])
        for n, (src, dst) in enumerate(zip(packed, sent_hbm))
    ]
    for store in stores:
        store.start()
    turn_values(v_ref, turned)
    loads[2].wait()
    for tile in range(rows // TILE):
        high = (tile + 1) * TILE
        fill_bias(bias.at[tile], lengths_ref, first + tile * TILE, first, 0, high, True)
        for g in range(turned.shape[0]):
            all_weights = []

            def emit(j, weights, top, factor):
                all_weights.append(weights)
                top_ref[g, :, lanes_of(tile, j)] = top

            weigh(q_ref, k_ref, bias.at[tile], None, tile, 0, high, g, emit)
            all_weights = jnp.concatenate(all_weights, axis=1)
            mix(turned[g, :, :high], all_weights, g, tile, None, keep((acc_ref, sum_ref), tile))
    for store in stores:
        store.wait()


def lowest_key(lengths_ref, hop, tile, rows):
    first = lax.axis_index("pre") * rows
    key_first = first - hop * rows
    low = jnp.maximum(start_of(lengths_ref, first + tile * TILE) - key_first, 0)
    return jnp.where(key_first >= 0, jnp.minimum(low, rows), rows)


def where_seen(lows, rows, act):
    for at in range(0, rows, TILE):
        for count in range(1, len(lows) + 1):
            seen = (lows[0] >= at) & (lows[0] < at + TILE) & (lows[count - 1] < rows)
            if count < len(lows):
                seen = seen & (lows[count] == rows)
            pl.when(seen)(functools.partial(act, at, count))


def scores_kernel(hop, lengths_ref, q_ref, k_ref, old_top, weights_ref, factor_ref, *refs):
    *top_refs, bias = refs
    rows = q_ref.shape[0]
    first = lax.axis_index("pre") * rows

    def act(at, count):
        for tile in range(count):
            row_first = first + tile * TILE
            fill_bias(
                bias.at[tile], lengths_ref, row_first, first - hop * rows, at, rows, False
            )
        for tile in range(count):
            for g in range(weights_ref.shape[1]):

                def emit(j, weights, top, factor):
                    weights_ref[tile, g, at:rows, j * TILE : (j + 1) * TILE] = weights
                    for top_ref in top_refs:
                        top_ref[g, :, lanes_of(tile, j)] = top
                    factor_ref[g, :, lanes_of(tile, j)] = factor

                weigh(q_ref, k_ref, bias.at[tile], old_top, tile, at, rows, g, emit)

    where_seen(
        [lowest_key(lengths_ref, hop, tile, rows) for tile in range(rows // TILE)], rows, act
    )


def place_blocks(cache, slot_ref, k_ref, v_ref, distance, pre, blocks):
    me = lax.axis_index("pre")
    source = lax.rem(me - distance + pre, pre)

    def step(b, _):
        at = own_slot(slot_ref[source * blocks + b], me, blocks)
        cache[at] = block_of(k_ref, v_ref, pl.multiple_of(b * BLK, BLK))
        return 0

    lax.fori_loop(0, blocks, step, 0, unroll=8)


def place_listed(cache, places_ref, hop, pre, k_ref, v_ref, got_ref):
    me = lax.axis_index("pre")
    per_peer = got_ref.shape[0]
    stride = per_peer + 1

    def place(values_at):
        for n in range(per_peer):
            at = places_ref[(hop - 2) * stride + n]
            b = places_ref[(pre - 2 + hop - 2) * stride + n]
            rows = pl.ds(pl.multiple_of(b * BLK, BLK), BLK)
            values = values_at(n, rows)
            parts = []
            for g in range(k_ref.shape[1] // HD):
                span = slice(g * HD, (g + 1) * HD)
                parts += [k_ref[rows, span], values[:, span]]
            cache[at] = jnp.concatenate(parts, axis=1)

    pl.when(me >= hop - 1)(lambda: place(lambda n, rows: v_ref[rows]))
    pl.when(me < hop - 1)(lambda: place(lambda n, rows: got_ref[n]))


def place_packed(cache, places_ref, distance, got_ref):
    per_peer = got_ref.shape[0]
    for n in range(per_peer):
        cache[places_ref[(distance - 2) * (per_peer + 1) + n]] = got_ref[n]


def values_kernel(
    hop, hops, pre, lengths_ref, slot_ref, v_ref, k_ref, weights_ref, factor_ref,
    acc_in, sum_in, cache_in, *refs,
):
    first_out, last = hop == 1, hop == hops
    refs = list(refs)
    if not first_out:
        refs.pop(0)
    got_ref = None if first_out else refs.pop(0)
    got_far = [refs.pop(0) for _ in range(hops + 1, pre)] if last else []
    out_hbm, cache_out = refs.pop(0), refs.pop(0)
    state = () if last else (refs.pop(0), refs.pop(0))
    turned, out_buf, sems, *rest = refs
    rows = v_ref.shape[0]
    blocks = rows // BLK
    tiles = rows // TILE
    kv_count = turned.shape[0]

    cache = rest[0] if last else cache_out
    cache[...] = cache_in[...]
    if first_out:
        place_blocks(cache, slot_ref, k_ref, v_ref, hop, pre, blocks)
    else:
        place_listed(cache, slot_ref, hop, pre, k_ref, v_ref, got_ref)
    if last:
        for n, far_ref in enumerate(got_far):
            place_packed(cache, slot_ref, hops + 1 + n, far_ref)
        cache_store = pltpu.make_async_copy(cache.at[0:blocks], cache_out, sems.at[tiles])
        cache_store.start()

    lows = [lowest_key(lengths_ref, hop, tile, rows) for tile in range(tiles)]
    pl.when(lows[0] < rows)(functools.partial(turn_values, v_ref, turned))
    ends = [finish(out_buf, tile * TILE) for tile in range(tiles)]

    def act(at, count):
        for tile in range(count):

            def emit(*result):
                if not last:
                    keep(state, tile)(*result)
                ends[tile](*result)

            for g in range(kv_count):
                weights = weights_ref[tile, g, at:rows]
                old = (acc_in, sum_in, factor_ref)
                mix(turned[g, :, at:rows], weights, g, tile, old, emit)

    where_seen(lows, rows, act)
    stores = []
    for tile, low in enumerate(lows):
        span = slice(tile * TILE, (tile + 1) * TILE)
        store = pltpu.make_async_copy(out_buf.at[span], out_hbm.at[span], sems.at[tile])
        stores.append(store)
        if first_out:

            @pl.when(low == rows)
            def _():
                for g in range(kv_count):
                    for j in range(GROUP):
                        at = lanes_of(tile, j)
                        ends[tile](g, j, acc_in[g, :, at], sum_in[g, :, at])

            store.start()
        else:
            pl.when(low < rows)(store.start)
    for low, store in zip(lows, stores):
        if first_out:
            store.wait()
        else:
            pl.when(low < rows)(store.wait)
    if last:
        cache_store.wait()


def on_device(queries, new_keys, new_values, lengths, block_slot):
    rows, q_width = queries.shape
    kv_width = new_keys.shape[1]
    kv_count = kv_width // HD
    blocks = rows // BLK
    pre = lax.axis_size("pre")
    per_peer = blocks // pre
    hops = pre // 2
    tiles = rows // TILE
    bf16, f32 = jnp.bfloat16, jnp.float32
    shape = jax.ShapeDtypeStruct
    params = pltpu.CompilerParams(vmem_limit_bytes=24 * 2**20)
    own_params = pltpu.CompilerParams(vmem_limit_bytes=44 * 2**20)
    ring = [(i, (i + 1) % pre) for i in range(pre)]
    acc_shape = shape((kv_count, HD, GROUP * rows), f32)
    stat_shape = shape((kv_count, 8, GROUP * rows), f32)
    weights_shape = shape((tiles, kv_count, rows, GROUP * TILE), bf16)
    attended_shape = shape(queries.shape, bf16)
    cache_shape = shape((blocks, BLK, 2 * kv_width), bf16)
    open_cache = shape((blocks + 1, BLK, 2 * kv_width), bf16)
    turned = pltpu.VMEM((kv_count, HD + ONES, rows), bf16)
    bias = pltpu.VMEM((tiles, rows, TILE), f32)

    def cost(share, moved):
        pairs = int(rows * rows * share)
        return pl.CostEstimate(
            flops=4 * pairs * q_width,
            bytes_accessed=moved * 2**20,
            transcendentals=pairs * kv_count * GROUP,
        )

    def after(array, *others):
        return lax.optimization_barrier((array, *others))[0]

    k, v = lax.ppermute(new_keys, "pre", ring), lax.ppermute(new_values, "pre", ring)

    packed = (shape((per_peer, BLK, kv_width), bf16),) * (hops - 1)
    packed += (shape((per_peer, BLK, 2 * kv_width), bf16),) * (pre - 1 - hops)
    places = shape(((pre - 2 + hops - 1) * (per_peer + 1),), jnp.int32)
    in_hbm = (
        pltpu.with_memory_space_constraint(x, pltpu.HBM) for x in (queries, new_keys, new_values)
    )
    q, acc, total, top, cache, places, *sent = pl.pallas_call(
        functools.partial(own_kernel, pre, hops),
        out_shape=(attended_shape, acc_shape, stat_shape, stat_shape, open_cache, places)
        + packed,
        in_specs=[SMEM, SMEM] + [HBM] * 3,
        out_specs=(VMEM,) * 5 + (SMEM,) + (HBM,) * (pre - 2),
        scratch_shapes=[
            pltpu.VMEM((rows, kv_width), bf16),
            pltpu.VMEM((rows, kv_width), bf16),
            turned,
            bias,
            pltpu.VMEM(((hops - 1) * per_peer + 1, BLK, kv_width), bf16),
            pltpu.VMEM(((pre - 1 - hops) * per_peer + 1, BLK, 2 * kv_width), bf16),
            pltpu.SMEM((pre,), jnp.int32),
            pltpu.SemaphoreType.DMA((pre - 2,)),
            pltpu.SemaphoreType.DMA((3,)),
        ],
        cost_estimate=cost(1, 4),
        compiler_params=own_params,
        name="own_attention",
    )(lengths, block_slot, *in_hbm)
    got = []
    k = after(k, top)
    attended = None
    for hop in range(1, hops + 1):
        first_out, last = hop == 1, hop == hops
        onward = [(i, i + 1) for i in range(hop - 1, pre - 1)]
        next_k = None if last else lax.ppermute(k, "pre", ring)
        weights, factor, *tops = pl.pallas_call(
            functools.partial(scores_kernel, hop),
            out_shape=(weights_shape, stat_shape) + (() if last else (stat_shape,)),
            in_specs=[SMEM] + [VMEM] * 3,
            out_specs=(VMEM,) * (2 if last else 3),
            scratch_shapes=[bias],
            cost_estimate=cost(0.5, 3),
            compiler_params=params,
            name="scores",
        )(lengths, q, k, top)
        v = after(v, factor)
        next_v = None if last else lax.ppermute(v, "pre", onward)
        if first_out:
            for d in range(2, pre):
                targets = range(d - 1 if d <= hops else pre)
                pairs = [((i - d) % pre, i) for i in targets]
                got.append(lax.ppermute(after(sent[d - 2], v), "pre", pairs))
        carry = () if last else (acc_shape, stat_shape)
        extra = [] if first_out else [attended]
        extra += [] if first_out else [got[hop - 2]]
        extra += got[hops - 1 :] if last else []
        attended, cache, *state = pl.pallas_call(
            functools.partial(values_kernel, hop, hops, pre),
            out_shape=(attended_shape, cache_shape if last else open_cache)
            + carry,
            in_specs=[SMEM, SMEM]
            + [VMEM] * 7
            + ([] if first_out else [HBM])
            + [VMEM] * (len(extra) - 1),
            out_specs=(HBM, HBM if last else VMEM)
            + (VMEM,) * len(carry),
            scratch_shapes=[
                turned,
                pltpu.VMEM((rows, q_width), bf16),
                pltpu.SemaphoreType.DMA((tiles + 1,)),
            ]
            + ([pltpu.VMEM(open_cache.shape, bf16)] if last else []),
            input_output_aliases={} if first_out else {9: 0},
            cost_estimate=cost(0.5, 3),
            compiler_params=params,
            name="values",
        )(lengths, block_slot if first_out else places, v, k, weights, factor, acc, total, cache, *extra)
        if not last:
            (top,) = tops
            acc, total = state
            k, v = after(next_k, total), next_v

    return (attended, cache)


def solution(mesh):
    placed = (
        P(("parts", "pre"), "tp"),
        P(("parts", "pre"), "tp"),
        P(("parts", "pre"), "tp"),
        P("parts"),
        P("parts"),
    )
    return jax.shard_map(
        on_device,
        mesh=mesh,
        in_specs=placed,
        out_specs=(P(("parts", "pre"), "tp"), P(("parts", "pre"), None, "tp")),
        check_vma=False,
    )
```

```python
import functools
import math

import jax
import jax.numpy as jnp
from jax import lax
from jax.experimental import pallas as pl
from jax.experimental.pallas import tpu as pltpu
from jax.sharding import PartitionSpec as P

HD = 128
BLK = 16
GROUP = 4
TILE = 256
ONES = 16
MASKED = -1e30
EXP_SCALE = math.log2(math.e) * HD ** (-0.5)

VMEM = pl.BlockSpec(memory_space=pltpu.VMEM)
SMEM = pl.BlockSpec(memory_space=pltpu.SMEM)
HBM = pl.BlockSpec(memory_space=pltpu.HBM)


def start_of(lengths_ref, position):
    end = jnp.int32(0)
    start = jnp.int32(0)
    for r in range(lengths_ref.shape[0]):
        end = end + lengths_ref[r]
        start = jnp.where(end <= position, end, start)
    return start


def row_starts(lengths_ref, positions):
    end = jnp.int32(0)
    starts = jnp.zeros_like(positions)
    for r in range(lengths_ref.shape[0]):
        end = end + lengths_ref[r]
        starts = jnp.where(positions >= end, end, starts)
    return starts


def fill_bias(bias_ref, lengths_ref, row_first, key_first, low, high, causal):
    shape = (high - low, TILE)
    positions = row_first + lax.broadcasted_iota(jnp.int32, (8, TILE), 1)
    starts = row_starts(lengths_ref, positions)
    keys = key_first + low + lax.broadcasted_iota(jnp.int32, shape, 0)
    keys = keys.reshape((high - low) // 8, 8, TILE)
    allowed = keys >= starts[None]
    if causal:
        allowed = allowed & (keys <= positions[None])
    bias_ref[low:high] = jnp.where(allowed, 0.0, MASKED).reshape(shape)


def turn_values(v_ref, turned):
    for g in range(turned.shape[0]):
        turned[g, :HD] = v_ref[:, g * HD : (g + 1) * HD].T
        turned[g, HD:] = jnp.ones((ONES, turned.shape[2]), turned.dtype)


def lanes_of(tile, j):
    return slice((tile * GROUP + j) * TILE, (tile * GROUP + j + 1) * TILE)


def weigh(q_ref, k_ref, bias_ref, old_top, tile, low, high, g, emit):
    keys = k_ref[low:high, g * HD : (g + 1) * HD]
    heads = range(g * GROUP, (g + 1) * GROUP)
    queries = jnp.concatenate(
        [q_ref[tile * TILE : (tile + 1) * TILE, h * HD : (h + 1) * HD] for h in heads], axis=0
    )
    all_scores = lax.dot_general(
        keys, queries, (((1,), (1,)), ((), ())), preferred_element_type=jnp.float32
    )
    for j in range(GROUP):
        scores = all_scores[:, j * TILE : (j + 1) * TILE] + bias_ref[low:high]
        scores = scores.reshape((high - low) // 8, 8, TILE)
        highest = jnp.max(jnp.max(scores, axis=0), axis=0, keepdims=True)
        top = jnp.broadcast_to(highest, (8, TILE))
        factor = None
        if old_top is not None:
            old = old_top[g, :, lanes_of(tile, j)]
            top = jnp.maximum(old, top)
            factor = jnp.exp2((old - top) * EXP_SCALE)
        weights = jnp.exp2((scores - top[None]) * EXP_SCALE)
        emit(j, weights.reshape(high - low, TILE).astype(jnp.bfloat16), top, factor)


def mix(values, weights, g, tile, old, emit):
    all_added = jnp.dot(values, weights, preferred_element_type=jnp.float32)
    for j in range(GROUP):
        at = lanes_of(tile, j)
        added = all_added[:, j * TILE : (j + 1) * TILE]
        value, total = added[:HD], added[HD : HD + 8]
        if old is not None:
            acc_ref, sum_ref, factor_ref = old
            factor = factor_ref[g, :, at]
            total = total + sum_ref[g, :, at] * factor
            kept = acc_ref[g, :, at].reshape(HD // 8, 8, TILE) * factor[None]
            value = value + kept.reshape(HD, TILE)
        emit(g, j, value, total)


def keep(state, tile):
    def emit(g, j, value, total):
        for ref, array in zip(state, (value, total)):
            ref[g, :, lanes_of(tile, j)] = array

    return emit


def finish(out_ref, row):
    parts = []

    def emit(g, j, value, total):
        value = value.reshape(HD // 8, 8, TILE) * (1.0 / total)[None]
        parts.append(value.reshape(HD, TILE).astype(out_ref.dtype))
        if j == GROUP - 1:
            stacked = jnp.concatenate(parts, axis=0)
            parts.clear()
            rows = lax.broadcasted_iota(jnp.int32, (TILE, TILE), 0)
            lanes = lax.broadcasted_iota(jnp.int32, (TILE, TILE), 1)
            identity = jnp.where(rows == lanes, 1.0, 0.0).astype(out_ref.dtype)
            turned = lax.dot_general(
                identity, stacked, (((1,), (1,)), ((), ())), preferred_element_type=jnp.float32
            )
            span = slice(g * GROUP * HD, (g + 1) * GROUP * HD)
            out_ref[row : row + TILE, span] = turned.astype(out_ref.dtype)

    return emit


def block_of(k_ref, v_ref, row):
    parts = []
    for g in range(k_ref.shape[1] // HD):
        span = slice(g * HD, (g + 1) * HD)
        parts += [k_ref[pl.ds(row, BLK), span], v_ref[pl.ds(row, BLK), span]]
    return jnp.concatenate(parts, axis=1)


def own_slot(slot, me, blocks):
    local = slot - me * blocks
    return jnp.where((local >= 0) & (local < blocks), local, blocks)


def list_places(places_ref, slot_ref, hops, pre, blocks):
    me = lax.axis_index("pre")
    stride = blocks // pre + 1
    for distance in range(2, pre):
        source = lax.rem(me - distance + pre, pre)

        def step(b, n):
            at = own_slot(slot_ref[source * blocks + b], me, blocks)
            places_ref[(distance - 2) * stride + n] = at
            if distance <= hops:
                places_ref[(pre - 2 + distance - 2) * stride + n] = b
            return n + jnp.where(at < blocks, 1, 0)

        lax.fori_loop(0, blocks, step, jnp.int32(0), unroll=8)


def own_kernel(
    pre, hops, lengths_ref, slot_ref, q_hbm, k_hbm, v_hbm,
    q_ref, acc_ref, sum_ref, top_ref, cache_ref, places_ref, *refs,
):
    sent_hbm, refs = refs[: pre - 2], refs[pre - 2 :]
    k_ref, v_ref, turned, bias, sent_values, sent, counts, sems, load_sems = refs
    loads = [
        pltpu.make_async_copy(src, dst, load_sems.at[n])
        for n, (src, dst) in enumerate(((k_hbm, k_ref), (v_hbm, v_ref), (q_hbm, q_ref)))
    ]
    for load in loads:
        load.start()
    rows = q_ref.shape[0]
    blocks = rows // BLK
    per_peer = blocks // pre
    me = lax.axis_index("pre")
    first = me * rows
    for owner in range(pre):
        counts[owner] = 0
    list_places(places_ref, slot_ref, hops, pre, blocks)
    loads[0].wait()
    loads[1].wait()

    def step(b, _):
        slot = slot_ref[me * blocks + b]
        owner = slot // blocks
        n = counts[owner]
        counts[owner] = n + 1
        distance = lax.rem(owner - me + pre, pre)
        row = pl.multiple_of(b * BLK, BLK)
        on_ring = (distance > 1) & (distance <= hops)
        at = jnp.where(on_ring, (distance - 2) * per_peer + n, (hops - 1) * per_peer)
        sent_values[at] = v_ref[pl.ds(row, BLK)]
        beyond = (distance - hops - 1) * per_peer + n
        at = jnp.where(distance > hops, beyond, (pre - 1 - hops) * per_peer)
        block = block_of(k_ref, v_ref, row)
        sent[at] = block
        cache_ref[own_slot(slot, me, blocks)] = block
        return 0

    lax.fori_loop(0, blocks, step, 0, unroll=4)
    packed = [sent_values.at[n * per_peer : (n + 1) * per_peer] for n in range(hops - 1)]
    packed += [sent.at[n * per_peer : (n + 1) * per_peer] for n in range(pre - 1 - hops)]
    stores = [
        pltpu.make_async_copy(src, dst, sems.at[n])
        for n, (src, dst) in enumerate(zip(packed, sent_hbm))
    ]
    for store in stores:
        store.start()
    turn_values(v_ref, turned)
    loads[2].wait()
    for tile in range(rows // TILE):
        high = (tile + 1) * TILE
        fill_bias(bias, lengths_ref, first + tile * TILE, first, 0, high, True)
        for g in range(turned.shape[0]):
            all_weights = []

            def emit(j, weights, top, factor):
                all_weights.append(weights)
                top_ref[g, :, lanes_of(tile, j)] = top

            weigh(q_ref, k_ref, bias, None, tile, 0, high, g, emit)
            all_weights = jnp.concatenate(all_weights, axis=1)
            mix(turned[g, :, :high], all_weights, g, tile, None, keep((acc_ref, sum_ref), tile))
    for store in stores:
        store.wait()


def lowest_key(lengths_ref, hop, tile, rows):
    first = lax.axis_index("pre") * rows
    key_first = first - hop * rows
    low = jnp.maximum(start_of(lengths_ref, first + tile * TILE) - key_first, 0)
    return jnp.where(key_first >= 0, jnp.minimum(low, rows), rows)


def where_seen(low, rows, act):
    for at in range(0, rows, TILE):
        pl.when((low >= at) & (low < at + TILE))(functools.partial(act, at))


def scores_kernel(hop, lengths_ref, q_ref, k_ref, old_top, weights_ref, factor_ref, *refs):
    *top_refs, bias = refs
    rows = q_ref.shape[0]
    first = lax.axis_index("pre") * rows
    for tile in range(rows // TILE):

        def act(at):
            fill_bias(
                bias, lengths_ref, first + tile * TILE, first - hop * rows, at, rows, False
            )
            for g in range(weights_ref.shape[1]):

                def emit(j, weights, top, factor):
                    weights_ref[tile, g, at:rows, j * TILE : (j + 1) * TILE] = weights
                    for top_ref in top_refs:
                        top_ref[g, :, lanes_of(tile, j)] = top
                    factor_ref[g, :, lanes_of(tile, j)] = factor

                weigh(q_ref, k_ref, bias, old_top, tile, at, rows, g, emit)

        where_seen(lowest_key(lengths_ref, hop, tile, rows), rows, act)


def place_blocks(cache, slot_ref, k_ref, v_ref, distance, pre, blocks):
    me = lax.axis_index("pre")
    source = lax.rem(me - distance + pre, pre)

    def step(b, _):
        at = own_slot(slot_ref[source * blocks + b], me, blocks)
        cache[at] = block_of(k_ref, v_ref, pl.multiple_of(b * BLK, BLK))
        return 0

    lax.fori_loop(0, blocks, step, 0, unroll=8)


def place_listed(cache, places_ref, hop, pre, k_ref, v_ref, got_ref):
    me = lax.axis_index("pre")
    per_peer = got_ref.shape[0]
    stride = per_peer + 1

    def place(values_at):
        for n in range(per_peer):
            at = places_ref[(hop - 2) * stride + n]
            b = places_ref[(pre - 2 + hop - 2) * stride + n]
            rows = pl.ds(pl.multiple_of(b * BLK, BLK), BLK)
            values = values_at(n, rows)
            parts = []
            for g in range(k_ref.shape[1] // HD):
                span = slice(g * HD, (g + 1) * HD)
                parts += [k_ref[rows, span], values[:, span]]
            cache[at] = jnp.concatenate(parts, axis=1)

    pl.when(me >= hop - 1)(lambda: place(lambda n, rows: v_ref[rows]))
    pl.when(me < hop - 1)(lambda: place(lambda n, rows: got_ref[n]))


def place_packed(cache, places_ref, distance, got_ref):
    per_peer = got_ref.shape[0]
    for n in range(per_peer):
        cache[places_ref[(distance - 2) * (per_peer + 1) + n]] = got_ref[n]


def values_kernel(
    hop, hops, pre, lengths_ref, slot_ref, v_ref, k_ref, weights_ref, factor_ref,
    acc_in, sum_in, cache_in, *refs,
):
    first_out, last = hop == 1, hop == hops
    refs = list(refs)
    if not first_out:
        refs.pop(0)
    got_ref = None if first_out else refs.pop(0)
    got_far = [refs.pop(0) for _ in range(hops + 1, pre)] if last else []
    out_hbm, cache_out = refs.pop(0), refs.pop(0)
    state = () if last else (refs.pop(0), refs.pop(0))
    turned, out_buf, sems, *rest = refs
    rows = v_ref.shape[0]
    blocks = rows // BLK
    tiles = rows // TILE
    kv_count = turned.shape[0]

    cache = rest[0] if last else cache_out
    cache[...] = cache_in[...]
    if first_out:
        place_blocks(cache, slot_ref, k_ref, v_ref, hop, pre, blocks)
    else:
        place_listed(cache, slot_ref, hop, pre, k_ref, v_ref, got_ref)
    if last:
        for n, far_ref in enumerate(got_far):
            place_packed(cache, slot_ref, hops + 1 + n, far_ref)
        cache_store = pltpu.make_async_copy(cache.at[0:blocks], cache_out, sems.at[tiles])
        cache_store.start()

    lows = [lowest_key(lengths_ref, hop, tile, rows) for tile in range(tiles)]
    pl.when(lows[0] < rows)(functools.partial(turn_values, v_ref, turned))
    stores = []
    for tile, low in enumerate(lows):
        end_it = finish(out_buf, tile * TILE)

        def act(at):
            def emit(*result):
                if not last:
                    keep(state, tile)(*result)
                end_it(*result)

            for g in range(kv_count):
                weights = weights_ref[tile, g, at:rows]
                old = (acc_in, sum_in, factor_ref)
                mix(turned[g, :, at:rows], weights, g, tile, old, emit)

        where_seen(low, rows, act)
        span = slice(tile * TILE, (tile + 1) * TILE)
        store = pltpu.make_async_copy(out_buf.at[span], out_hbm.at[span], sems.at[tile])
        stores.append(store)
        if first_out:

            @pl.when(low == rows)
            def _():
                for g in range(kv_count):
                    for j in range(GROUP):
                        end_it(g, j, *(ref[g, :, lanes_of(tile, j)] for ref in (acc_in, sum_in)))

            store.start()
        else:
            pl.when(low < rows)(store.start)
    for low, store in zip(lows, stores):
        if first_out:
            store.wait()
        else:
            pl.when(low < rows)(store.wait)
    if last:
        cache_store.wait()


def on_device(queries, new_keys, new_values, lengths, block_slot):
    rows, q_width = queries.shape
    kv_width = new_keys.shape[1]
    kv_count = kv_width // HD
    blocks = rows // BLK
    pre = lax.axis_size("pre")
    per_peer = blocks // pre
    hops = pre // 2
    tiles = rows // TILE
    bf16, f32 = jnp.bfloat16, jnp.float32
    shape = jax.ShapeDtypeStruct
    params = pltpu.CompilerParams(vmem_limit_bytes=24 * 2**20)
    own_params = pltpu.CompilerParams(vmem_limit_bytes=44 * 2**20)
    ring = [(i, (i + 1) % pre) for i in range(pre)]
    acc_shape = shape((kv_count, HD, GROUP * rows), f32)
    stat_shape = shape((kv_count, 8, GROUP * rows), f32)
    weights_shape = shape((tiles, kv_count, rows, GROUP * TILE), bf16)
    attended_shape = shape(queries.shape, bf16)
    cache_shape = shape((blocks, BLK, 2 * kv_width), bf16)
    open_cache = shape((blocks + 1, BLK, 2 * kv_width), bf16)
    turned = pltpu.VMEM((kv_count, HD + ONES, rows), bf16)
    bias = pltpu.VMEM((rows, TILE), f32)

    def cost(share, moved):
        pairs = int(rows * rows * share)
        return pl.CostEstimate(
            flops=4 * pairs * q_width,
            bytes_accessed=moved * 2**20,
            transcendentals=pairs * kv_count * GROUP,
        )

    def after(array, *others):
        return lax.optimization_barrier((array, *others))[0]

    k, v = lax.ppermute(new_keys, "pre", ring), lax.ppermute(new_values, "pre", ring)

    packed = (shape((per_peer, BLK, kv_width), bf16),) * (hops - 1)
    packed += (shape((per_peer, BLK, 2 * kv_width), bf16),) * (pre - 1 - hops)
    places = shape(((pre - 2 + hops - 1) * (per_peer + 1),), jnp.int32)
    in_hbm = (
        pltpu.with_memory_space_constraint(x, pltpu.HBM) for x in (queries, new_keys, new_values)
    )
    q, acc, total, top, cache, places, *sent = pl.pallas_call(
        functools.partial(own_kernel, pre, hops),
        out_shape=(attended_shape, acc_shape, stat_shape, stat_shape, open_cache, places)
        + packed,
        in_specs=[SMEM, SMEM] + [HBM] * 3,
        out_specs=(VMEM,) * 5 + (SMEM,) + (HBM,) * (pre - 2),
        scratch_shapes=[
            pltpu.VMEM((rows, kv_width), bf16),
            pltpu.VMEM((rows, kv_width), bf16),
            turned,
            bias,
            pltpu.VMEM(((hops - 1) * per_peer + 1, BLK, kv_width), bf16),
            pltpu.VMEM(((pre - 1 - hops) * per_peer + 1, BLK, 2 * kv_width), bf16),
            pltpu.SMEM((pre,), jnp.int32),
            pltpu.SemaphoreType.DMA((pre - 2,)),
            pltpu.SemaphoreType.DMA((3,)),
        ],
        cost_estimate=cost(1, 4),
        compiler_params=own_params,
        name="own_attention",
    )(lengths, block_slot, *in_hbm)
    got = []
    k = after(k, top)
    attended = None
    for hop in range(1, hops + 1):
        first_out, last = hop == 1, hop == hops
        onward = [(i, i + 1) for i in range(hop - 1, pre - 1)]
        next_k = None if last else lax.ppermute(k, "pre", ring)
        weights, factor, *tops = pl.pallas_call(
            functools.partial(scores_kernel, hop),
            out_shape=(weights_shape, stat_shape) + (() if last else (stat_shape,)),
            in_specs=[SMEM] + [VMEM] * 3,
            out_specs=(VMEM,) * (2 if last else 3),
            scratch_shapes=[bias],
            cost_estimate=cost(0.5, 3),
            compiler_params=params,
            name="scores",
        )(lengths, q, k, top)
        v = after(v, factor)
        next_v = None if last else lax.ppermute(v, "pre", onward)
        if first_out:
            for d in range(2, pre):
                targets = range(d - 1 if d <= hops else pre)
                pairs = [((i - d) % pre, i) for i in targets]
                got.append(lax.ppermute(after(sent[d - 2], v), "pre", pairs))
        carry = () if last else (acc_shape, stat_shape)
        extra = [] if first_out else [attended]
        extra += [] if first_out else [got[hop - 2]]
        extra += got[hops - 1 :] if last else []
        attended, cache, *state = pl.pallas_call(
            functools.partial(values_kernel, hop, hops, pre),
            out_shape=(attended_shape, cache_shape if last else open_cache)
            + carry,
            in_specs=[SMEM, SMEM]
            + [VMEM] * 7
            + ([] if first_out else [HBM])
            + [VMEM] * (len(extra) - 1),
            out_specs=(HBM, HBM if last else VMEM)
            + (VMEM,) * len(carry),
            scratch_shapes=[
                turned,
                pltpu.VMEM((rows, q_width), bf16),
                pltpu.SemaphoreType.DMA((tiles + 1,)),
            ]
            + ([pltpu.VMEM(open_cache.shape, bf16)] if last else []),
            input_output_aliases={} if first_out else {9: 0},
            cost_estimate=cost(0.5, 3),
            compiler_params=params,
            name="values",
        )(lengths, block_slot if first_out else places, v, k, weights, factor, acc, total, cache, *extra)
        if not last:
            (top,) = tops
            acc, total = state
            k, v = after(next_k, total), next_v

    return (attended, cache)


def solution(mesh):
    placed = (
        P(("parts", "pre"), "tp"),
        P(("parts", "pre"), "tp"),
        P(("parts", "pre"), "tp"),
        P("parts"),
        P("parts"),
    )
    return jax.shard_map(
        on_device,
        mesh=mesh,
        in_specs=placed,
        out_specs=(P(("parts", "pre"), "tp"), P(("parts", "pre"), None, "tp")),
        check_vma=False,
    )
```

```python
import functools
import math

import jax
import jax.numpy as jnp
from jax import lax
from jax.experimental import pallas as pl
from jax.experimental.pallas import tpu as pltpu
from jax.sharding import PartitionSpec as P

HD = 128
BLK = 16
GROUP = 4
TILE = 256
MASKED = -1e30
EXP_SCALE = math.log2(math.e) * HD ** (-0.5)

VMEM = pl.BlockSpec(memory_space=pltpu.VMEM)
SMEM = pl.BlockSpec(memory_space=pltpu.SMEM)
HBM = pl.BlockSpec(memory_space=pltpu.HBM)


def start_of(lengths_ref, position):
    end = jnp.int32(0)
    start = jnp.int32(0)
    for r in range(lengths_ref.shape[0]):
        end = end + lengths_ref[r]
        start = jnp.where(end <= position, end, start)
    return start


def row_starts(lengths_ref, positions):
    end = jnp.int32(0)
    starts = jnp.zeros_like(positions)
    for r in range(lengths_ref.shape[0]):
        end = end + lengths_ref[r]
        starts = jnp.where(positions >= end, end, starts)
    return starts


def fill_bias(bias_ref, lengths_ref, row_first, key_first, low, high, causal):
    shape = (high - low, TILE)
    positions = row_first + lax.broadcasted_iota(jnp.int32, (8, TILE), 1)
    starts = row_starts(lengths_ref, positions)
    keys = key_first + low + lax.broadcasted_iota(jnp.int32, shape, 0)
    keys = keys.reshape((high - low) // 8, 8, TILE)
    allowed = keys >= starts[None]
    if causal:
        allowed = allowed & (keys <= positions[None])
    bias_ref[low:high] = jnp.where(allowed, 0.0, MASKED).reshape(shape)


def turn_values(v_ref, turned):
    for g in range(turned.shape[0]):
        turned[g] = v_ref[:, g * HD : (g + 1) * HD].T


def lanes_of(tile, j):
    return slice((tile * GROUP + j) * TILE, (tile * GROUP + j + 1) * TILE)


def weigh(q_ref, k_ref, bias_ref, old_top, tile, low, high, g, emit):
    keys = k_ref[low:high, g * HD : (g + 1) * HD]
    heads = range(g * GROUP, (g + 1) * GROUP)
    queries = jnp.concatenate(
        [q_ref[tile * TILE : (tile + 1) * TILE, h * HD : (h + 1) * HD] for h in heads], axis=0
    )
    all_scores = lax.dot_general(
        keys, queries, (((1,), (1,)), ((), ())), preferred_element_type=jnp.float32
    )
    for j in range(GROUP):
        scores = all_scores[:, j * TILE : (j + 1) * TILE] + bias_ref[low:high]
        scores = scores.reshape((high - low) // 8, 8, TILE)
        highest = jnp.max(jnp.max(scores, axis=0), axis=0, keepdims=True)
        top = jnp.broadcast_to(highest, (8, TILE))
        factor = None
        if old_top is not None:
            old = old_top[g, :, lanes_of(tile, j)]
            top = jnp.maximum(old, top)
            factor = jnp.exp2((old - top) * EXP_SCALE)
        weights = jnp.exp2((scores - top[None]) * EXP_SCALE)
        total = jnp.sum(weights, axis=0)
        emit(j, weights.reshape(high - low, TILE).astype(jnp.bfloat16), top, factor, total)


def mix(values, weights, g, tile, old, emit):
    all_added = jnp.dot(values, weights, preferred_element_type=jnp.float32)
    for j in range(GROUP):
        at = lanes_of(tile, j)
        value = all_added[:, j * TILE : (j + 1) * TILE]
        if old is not None:
            acc_ref, factor_ref = old
            factor = factor_ref[g, :, at]
            kept = acc_ref[g, :, at].reshape(HD // 8, 8, TILE) * factor[None]
            value = value + kept.reshape(HD, TILE)
        emit(g, j, value)


def keep(acc_ref, tile):
    def emit(g, j, value):
        acc_ref[g, :, lanes_of(tile, j)] = value

    return emit


def finish(out_ref, row):
    def emit(g, j, value, totals):
        head = g * GROUP + j
        total = jnp.broadcast_to(jnp.sum(totals, axis=0, keepdims=True), totals.shape)
        value = value.reshape(HD // 8, 8, TILE) * (1.0 / total)[None]
        value = value.reshape(HD, TILE).astype(out_ref.dtype).T
        out_ref[row : row + TILE, head * HD : (head + 1) * HD] = value

    return emit


def block_of(k_ref, v_ref, row):
    parts = []
    for g in range(k_ref.shape[1] // HD):
        span = slice(g * HD, (g + 1) * HD)
        parts += [k_ref[pl.ds(row, BLK), span], v_ref[pl.ds(row, BLK), span]]
    return jnp.concatenate(parts, axis=1)


def own_slot(slot, me, blocks):
    local = slot - me * blocks
    return jnp.where((local >= 0) & (local < blocks), local, blocks)


def list_places(places_ref, slot_ref, hops, pre, blocks):
    me = lax.axis_index("pre")
    stride = blocks // pre + 1
    for distance in range(2, pre):
        source = lax.rem(me - distance + pre, pre)

        def step(b, n):
            at = own_slot(slot_ref[source * blocks + b], me, blocks)
            places_ref[(distance - 2) * stride + n] = at
            if distance <= hops:
                places_ref[(pre - 2 + distance - 2) * stride + n] = b
            return n + jnp.where(at < blocks, 1, 0)

        lax.fori_loop(0, blocks, step, jnp.int32(0), unroll=8)


def own_kernel(
    pre, hops, lengths_ref, slot_ref, q_hbm, k_hbm, v_hbm,
    q_ref, acc_ref, sum_ref, top_ref, cache_ref, places_ref, *refs,
):
    sent_hbm, refs = refs[: pre - 2], refs[pre - 2 :]
    k_ref, v_ref, turned, bias, sent_values, sent, counts, sems, load_sems = refs
    loads = [
        pltpu.make_async_copy(src, dst, load_sems.at[n])
        for n, (src, dst) in enumerate(((k_hbm, k_ref), (v_hbm, v_ref), (q_hbm, q_ref)))
    ]
    for load in loads:
        load.start()
    rows = q_ref.shape[0]
    blocks = rows // BLK
    per_peer = blocks // pre
    me = lax.axis_index("pre")
    first = me * rows
    for owner in range(pre):
        counts[owner] = 0
    list_places(places_ref, slot_ref, hops, pre, blocks)
    loads[0].wait()
    loads[1].wait()

    def step(b, _):
        slot = slot_ref[me * blocks + b]
        owner = slot // blocks
        n = counts[owner]
        counts[owner] = n + 1
        distance = lax.rem(owner - me + pre, pre)
        row = pl.multiple_of(b * BLK, BLK)
        on_ring = (distance > 1) & (distance <= hops)
        at = jnp.where(on_ring, (distance - 2) * per_peer + n, (hops - 1) * per_peer)
        sent_values[at] = v_ref[pl.ds(row, BLK)]
        beyond = (distance - hops - 1) * per_peer + n
        at = jnp.where(distance > hops, beyond, (pre - 1 - hops) * per_peer)
        block = block_of(k_ref, v_ref, row)
        sent[at] = block
        cache_ref[own_slot(slot, me, blocks)] = block
        return 0

    lax.fori_loop(0, blocks, step, 0, unroll=4)
    packed = [sent_values.at[n * per_peer : (n + 1) * per_peer] for n in range(hops - 1)]
    packed += [sent.at[n * per_peer : (n + 1) * per_peer] for n in range(pre - 1 - hops)]
    stores = [
        pltpu.make_async_copy(src, dst, sems.at[n])
        for n, (src, dst) in enumerate(zip(packed, sent_hbm))
    ]
    for store in stores:
        store.start()
    turn_values(v_ref, turned)
    loads[2].wait()
    for tile in range(rows // TILE):
        high = (tile + 1) * TILE
        fill_bias(bias, lengths_ref, first + tile * TILE, first, 0, high, True)
        for g in range(turned.shape[0]):
            all_weights = []

            def emit(j, weights, top, factor, total):
                all_weights.append(weights)
                top_ref[g, :, lanes_of(tile, j)] = top
                sum_ref[g, :, lanes_of(tile, j)] = total

            weigh(q_ref, k_ref, bias, None, tile, 0, high, g, emit)
            all_weights = jnp.concatenate(all_weights, axis=1)
            mix(turned[g, :, :high], all_weights, g, tile, None, keep(acc_ref, tile))
    for store in stores:
        store.wait()


def lowest_key(lengths_ref, hop, tile, rows):
    first = lax.axis_index("pre") * rows
    key_first = first - hop * rows
    low = jnp.maximum(start_of(lengths_ref, first + tile * TILE) - key_first, 0)
    return jnp.where(key_first >= 0, jnp.minimum(low, rows), rows)


def where_seen(low, rows, act):
    for at in range(0, rows, TILE):
        pl.when((low >= at) & (low < at + TILE))(functools.partial(act, at))


def scores_kernel(hop, lengths_ref, q_ref, k_ref, old_top, old_sum, weights_ref, factor_ref, sum_ref, *refs):
    *top_refs, bias = refs
    rows = q_ref.shape[0]
    first = lax.axis_index("pre") * rows
    for tile in range(rows // TILE):

        def act(at):
            fill_bias(
                bias, lengths_ref, first + tile * TILE, first - hop * rows, at, rows, False
            )
            for g in range(weights_ref.shape[1]):

                def emit(j, weights, top, factor, total):
                    lanes = lanes_of(tile, j)
                    sum_ref[g, :, lanes] = old_sum[g, :, lanes] * factor + total
                    weights_ref[tile, g, at:rows, j * TILE : (j + 1) * TILE] = weights
                    for top_ref in top_refs:
                        top_ref[g, :, lanes_of(tile, j)] = top
                    factor_ref[g, :, lanes_of(tile, j)] = factor

                weigh(q_ref, k_ref, bias, old_top, tile, at, rows, g, emit)

        where_seen(lowest_key(lengths_ref, hop, tile, rows), rows, act)


def place_blocks(cache, slot_ref, k_ref, v_ref, distance, pre, blocks):
    me = lax.axis_index("pre")
    source = lax.rem(me - distance + pre, pre)

    def step(b, _):
        at = own_slot(slot_ref[source * blocks + b], me, blocks)
        cache[at] = block_of(k_ref, v_ref, pl.multiple_of(b * BLK, BLK))
        return 0

    lax.fori_loop(0, blocks, step, 0, unroll=8)


def place_listed(cache, places_ref, hop, pre, k_ref, v_ref, got_ref):
    me = lax.axis_index("pre")
    per_peer = got_ref.shape[0]
    stride = per_peer + 1

    def place(values_at):
        for n in range(per_peer):
            at = places_ref[(hop - 2) * stride + n]
            b = places_ref[(pre - 2 + hop - 2) * stride + n]
            rows = pl.ds(pl.multiple_of(b * BLK, BLK), BLK)
            values = values_at(n, rows)
            parts = []
            for g in range(k_ref.shape[1] // HD):
                span = slice(g * HD, (g + 1) * HD)
                parts += [k_ref[rows, span], values[:, span]]
            cache[at] = jnp.concatenate(parts, axis=1)

    pl.when(me >= hop - 1)(lambda: place(lambda n, rows: v_ref[rows]))
    pl.when(me < hop - 1)(lambda: place(lambda n, rows: got_ref[n]))


def place_packed(cache, places_ref, distance, got_ref):
    per_peer = got_ref.shape[0]
    for n in range(per_peer):
        cache[places_ref[(distance - 2) * (per_peer + 1) + n]] = got_ref[n]


def values_kernel(
    hop, hops, pre, lengths_ref, slot_ref, v_ref, k_ref, weights_ref, factor_ref,
    acc_in, sum_in, old_sum, cache_in, *refs,
):
    first_out, last = hop == 1, hop == hops
    refs = list(refs)
    if not first_out:
        refs.pop(0)
    got_ref = None if first_out else refs.pop(0)
    got_far = [refs.pop(0) for _ in range(hops + 1, pre)] if last else []
    out_hbm, cache_out = refs.pop(0), refs.pop(0)
    acc_ref = None if last else refs.pop(0)
    turned, out_buf, sems, *rest = refs
    rows = v_ref.shape[0]
    blocks = rows // BLK
    tiles = rows // TILE
    kv_count = turned.shape[0]

    cache = rest[0] if last else cache_out
    cache[...] = cache_in[...]
    if first_out:
        place_blocks(cache, slot_ref, k_ref, v_ref, hop, pre, blocks)
    else:
        place_listed(cache, slot_ref, hop, pre, k_ref, v_ref, got_ref)
    if last:
        for n, far_ref in enumerate(got_far):
            place_packed(cache, slot_ref, hops + 1 + n, far_ref)
        cache_store = pltpu.make_async_copy(cache.at[0:blocks], cache_out, sems.at[tiles])
        cache_store.start()

    lows = [lowest_key(lengths_ref, hop, tile, rows) for tile in range(tiles)]
    pl.when(lows[0] < rows)(functools.partial(turn_values, v_ref, turned))
    stores = []
    for tile, low in enumerate(lows):
        end_it = finish(out_buf, tile * TILE)

        def act(at):
            def emit(g, j, value):
                if not last:
                    keep(acc_ref, tile)(g, j, value)
                end_it(g, j, value, sum_in[g, :, lanes_of(tile, j)])

            for g in range(kv_count):
                weights = weights_ref[tile, g, at:rows]
                old = (acc_in, factor_ref)
                mix(turned[g, :, at:rows], weights, g, tile, old, emit)

        where_seen(low, rows, act)
        span = slice(tile * TILE, (tile + 1) * TILE)
        store = pltpu.make_async_copy(out_buf.at[span], out_hbm.at[span], sems.at[tile])
        stores.append(store)
        if first_out:

            @pl.when(low == rows)
            def _():
                for g in range(kv_count):
                    for j in range(GROUP):
                        end_it(g, j, *(ref[g, :, lanes_of(tile, j)] for ref in (acc_in, old_sum)))

            store.start()
        else:
            pl.when(low < rows)(store.start)
    for low, store in zip(lows, stores):
        if first_out:
            store.wait()
        else:
            pl.when(low < rows)(store.wait)
    if last:
        cache_store.wait()


def on_device(queries, new_keys, new_values, lengths, block_slot):
    rows, q_width = queries.shape
    kv_width = new_keys.shape[1]
    kv_count = kv_width // HD
    blocks = rows // BLK
    pre = lax.axis_size("pre")
    per_peer = blocks // pre
    hops = pre // 2
    tiles = rows // TILE
    bf16, f32 = jnp.bfloat16, jnp.float32
    shape = jax.ShapeDtypeStruct
    params = pltpu.CompilerParams(vmem_limit_bytes=24 * 2**20)
    own_params = pltpu.CompilerParams(vmem_limit_bytes=44 * 2**20)
    ring = [(i, (i + 1) % pre) for i in range(pre)]
    acc_shape = shape((kv_count, HD, GROUP * rows), f32)
    stat_shape = shape((kv_count, 8, GROUP * rows), f32)
    weights_shape = shape((tiles, kv_count, rows, GROUP * TILE), bf16)
    attended_shape = shape(queries.shape, bf16)
    cache_shape = shape((blocks, BLK, 2 * kv_width), bf16)
    open_cache = shape((blocks + 1, BLK, 2 * kv_width), bf16)
    turned = pltpu.VMEM((kv_count, HD, rows), bf16)
    bias = pltpu.VMEM((rows, TILE), f32)

    def cost(share, moved):
        pairs = int(rows * rows * share)
        return pl.CostEstimate(
            flops=4 * pairs * q_width,
            bytes_accessed=moved * 2**20,
            transcendentals=pairs * kv_count * GROUP,
        )

    def after(array, *others):
        return lax.optimization_barrier((array, *others))[0]

    k, v = lax.ppermute(new_keys, "pre", ring), lax.ppermute(new_values, "pre", ring)

    packed = (shape((per_peer, BLK, kv_width), bf16),) * (hops - 1)
    packed += (shape((per_peer, BLK, 2 * kv_width), bf16),) * (pre - 1 - hops)
    places = shape(((pre - 2 + hops - 1) * (per_peer + 1),), jnp.int32)
    in_hbm = (
        pltpu.with_memory_space_constraint(x, pltpu.HBM) for x in (queries, new_keys, new_values)
    )
    q, acc, total, top, cache, places, *sent = pl.pallas_call(
        functools.partial(own_kernel, pre, hops),
        out_shape=(attended_shape, acc_shape, stat_shape, stat_shape, open_cache, places)
        + packed,
        in_specs=[SMEM, SMEM] + [HBM] * 3,
        out_specs=(VMEM,) * 5 + (SMEM,) + (HBM,) * (pre - 2),
        scratch_shapes=[
            pltpu.VMEM((rows, kv_width), bf16),
            pltpu.VMEM((rows, kv_width), bf16),
            turned,
            bias,
            pltpu.VMEM(((hops - 1) * per_peer + 1, BLK, kv_width), bf16),
            pltpu.VMEM(((pre - 1 - hops) * per_peer + 1, BLK, 2 * kv_width), bf16),
            pltpu.SMEM((pre,), jnp.int32),
            pltpu.SemaphoreType.DMA((pre - 2,)),
            pltpu.SemaphoreType.DMA((3,)),
        ],
        cost_estimate=cost(1, 4),
        compiler_params=own_params,
        name="own_attention",
    )(lengths, block_slot, *in_hbm)
    got = []
    k = after(k, top)
    attended = None
    for hop in range(1, hops + 1):
        first_out, last = hop == 1, hop == hops
        onward = [(i, i + 1) for i in range(hop - 1, pre - 1)]
        next_k = None if last else lax.ppermute(k, "pre", ring)
        weights, factor, new_total, *tops = pl.pallas_call(
            functools.partial(scores_kernel, hop),
            out_shape=(weights_shape, stat_shape, stat_shape) + (() if last else (stat_shape,)),
            in_specs=[SMEM] + [VMEM] * 4,
            out_specs=(VMEM,) * (3 if last else 4),
            scratch_shapes=[bias],
            cost_estimate=cost(0.5, 3),
            compiler_params=params,
            name="scores",
        )(lengths, q, k, top, total)
        v = after(v, factor)
        next_v = None if last else lax.ppermute(v, "pre", onward)
        if first_out:
            for d in range(2, pre):
                targets = range(d - 1 if d <= hops else pre)
                pairs = [((i - d) % pre, i) for i in targets]
                got.append(lax.ppermute(after(sent[d - 2], v), "pre", pairs))
        carry = () if last else (acc_shape,)
        extra = [] if first_out else [attended]
        extra += [] if first_out else [got[hop - 2]]
        extra += got[hops - 1 :] if last else []
        attended, cache, *state = pl.pallas_call(
            functools.partial(values_kernel, hop, hops, pre),
            out_shape=(attended_shape, cache_shape if last else open_cache)
            + carry,
            in_specs=[SMEM, SMEM]
            + [VMEM] * 8
            + ([] if first_out else [HBM])
            + [VMEM] * (len(extra) - 1),
            out_specs=(HBM, HBM if last else VMEM)
            + (VMEM,) * len(carry),
            scratch_shapes=[
                turned,
                pltpu.VMEM((rows, q_width), bf16),
                pltpu.SemaphoreType.DMA((tiles + 1,)),
            ]
            + ([pltpu.VMEM(open_cache.shape, bf16)] if last else []),
            input_output_aliases={} if first_out else {10: 0},
            cost_estimate=cost(0.5, 3),
            compiler_params=params,
            name="values",
        )(lengths, block_slot if first_out else places, v, k, weights, factor, acc, new_total, total, cache, *extra)
        if not last:
            (top,) = tops
            (acc,) = state
            total = new_total
            k, v = after(next_k, total), next_v

    return (attended, cache)


def solution(mesh):
    placed = (
        P(("parts", "pre"), "tp"),
        P(("parts", "pre"), "tp"),
        P(("parts", "pre"), "tp"),
        P("parts"),
        P("parts"),
    )
    return jax.shard_map(
        on_device,
        mesh=mesh,
        in_specs=placed,
        out_specs=(P(("parts", "pre"), "tp"), P(("parts", "pre"), None, "tp")),
        check_vma=False,
    )
```

```python
import functools
import math

import jax
import jax.numpy as jnp
from jax import lax
from jax.experimental import pallas as pl
from jax.experimental.pallas import tpu as pltpu
from jax.sharding import PartitionSpec as P

HD = 128
BLK = 16
GROUP = 4
TILE = 256
MASKED = -1e30
EXP_SCALE = math.log2(math.e) * HD ** (-0.5)

VMEM = pl.BlockSpec(memory_space=pltpu.VMEM)
SMEM = pl.BlockSpec(memory_space=pltpu.SMEM)
HBM = pl.BlockSpec(memory_space=pltpu.HBM)


def start_of(lengths_ref, position):
    end = jnp.int32(0)
    start = jnp.int32(0)
    for r in range(lengths_ref.shape[0]):
        end = end + lengths_ref[r]
        start = jnp.where(end <= position, end, start)
    return start


def row_starts(lengths_ref, positions):
    end = jnp.int32(0)
    starts = jnp.zeros_like(positions)
    for r in range(lengths_ref.shape[0]):
        end = end + lengths_ref[r]
        starts = jnp.where(positions >= end, end, starts)
    return starts


def fill_bias(bias_ref, lengths_ref, row_first, key_first, low, high, causal):
    shape = (high - low, TILE)
    positions = row_first + lax.broadcasted_iota(jnp.int32, (8, TILE), 1)
    starts = row_starts(lengths_ref, positions)
    keys = key_first + low + lax.broadcasted_iota(jnp.int32, shape, 0)
    keys = keys.reshape((high - low) // 8, 8, TILE)
    allowed = keys >= starts[None]
    if causal:
        allowed = allowed & (keys <= positions[None])
    bias_ref[low:high] = jnp.where(allowed, 0.0, MASKED).reshape(shape)


def turn_values(v_ref, turned):
    for g in range(turned.shape[0]):
        turned[g] = v_ref[:, g * HD : (g + 1) * HD].T


def lanes_of(tile, j):
    return slice((tile * GROUP + j) * TILE, (tile * GROUP + j + 1) * TILE)


def weigh(q_ref, k_ref, bias_ref, old_top, tile, low, high, g, emit):
    keys = k_ref[low:high, g * HD : (g + 1) * HD]
    heads = range(g * GROUP, (g + 1) * GROUP)
    queries = jnp.concatenate(
        [q_ref[tile * TILE : (tile + 1) * TILE, h * HD : (h + 1) * HD] for h in heads], axis=0
    )
    all_scores = lax.dot_general(
        keys, queries, (((1,), (1,)), ((), ())), preferred_element_type=jnp.float32
    )
    for j in range(GROUP):
        scores = all_scores[:, j * TILE : (j + 1) * TILE] + bias_ref[low:high]
        scores = scores.reshape((high - low) // 8, 8, TILE)
        highest = jnp.max(jnp.max(scores, axis=0), axis=0, keepdims=True)
        top = jnp.broadcast_to(highest, (8, TILE))
        factor = None
        if old_top is not None:
            old = old_top[g, :, lanes_of(tile, j)]
            top = jnp.maximum(old, top)
            factor = jnp.exp2((old - top) * EXP_SCALE)
        weights = jnp.exp2((scores - top[None]) * EXP_SCALE)
        total = jnp.sum(weights, axis=0)
        emit(j, weights.reshape(high - low, TILE).astype(jnp.bfloat16), top, factor, total)


def mix(values, weights, g, tile, old, emit):
    all_added = jnp.dot(values, weights, preferred_element_type=jnp.float32)
    for j in range(GROUP):
        at = lanes_of(tile, j)
        value = all_added[:, j * TILE : (j + 1) * TILE]
        if old is not None:
            acc_ref, factor_ref = old
            factor = factor_ref[g, :, at]
            kept = acc_ref[g, :, at].reshape(HD // 8, 8, TILE) * factor[None]
            value = value + kept.reshape(HD, TILE)
        emit(g, j, value)


def keep(acc_ref, tile):
    def emit(g, j, value):
        acc_ref[g, :, lanes_of(tile, j)] = value

    return emit


def finish(out_ref, row):
    def emit(g, j, value, totals):
        head = g * GROUP + j
        total = jnp.broadcast_to(jnp.sum(totals, axis=0, keepdims=True), totals.shape)
        value = value.reshape(HD // 8, 8, TILE) * (1.0 / total)[None]
        value = value.reshape(HD, TILE).astype(out_ref.dtype).T
        out_ref[row : row + TILE, head * HD : (head + 1) * HD] = value

    return emit


def block_of(k_ref, v_ref, row):
    parts = []
    for g in range(k_ref.shape[1] // HD):
        span = slice(g * HD, (g + 1) * HD)
        parts += [k_ref[pl.ds(row, BLK), span], v_ref[pl.ds(row, BLK), span]]
    return jnp.concatenate(parts, axis=1)


def own_slot(slot, me, blocks):
    local = slot - me * blocks
    return jnp.where((local >= 0) & (local < blocks), local, blocks)


def list_places(places_ref, slot_ref, hops, pre, blocks):
    me = lax.axis_index("pre")
    stride = blocks // pre + 1
    for distance in range(2, pre):
        source = lax.rem(me - distance + pre, pre)

        def step(b, n):
            at = own_slot(slot_ref[source * blocks + b], me, blocks)
            places_ref[(distance - 2) * stride + n] = at
            if distance <= hops:
                places_ref[(pre - 2 + distance - 2) * stride + n] = b
            return n + jnp.where(at < blocks, 1, 0)

        lax.fori_loop(0, blocks, step, jnp.int32(0), unroll=8)


def own_kernel(
    pre, hops, lengths_ref, slot_ref, q_hbm, k_hbm, v_hbm,
    q_ref, acc_ref, sum_ref, top_ref, cache_ref, places_ref, *refs,
):
    sent_hbm, refs = refs[: pre - 2], refs[pre - 2 :]
    k_ref, v_ref, turned, bias, sent_values, sent, counts, sems, load_sems = refs
    loads = [
        pltpu.make_async_copy(src, dst, load_sems.at[n])
        for n, (src, dst) in enumerate(((k_hbm, k_ref), (v_hbm, v_ref), (q_hbm, q_ref)))
    ]
    for load in loads:
        load.start()
    rows = q_ref.shape[0]
    blocks = rows // BLK
    per_peer = blocks // pre
    me = lax.axis_index("pre")
    first = me * rows
    for owner in range(pre):
        counts[owner] = 0
    list_places(places_ref, slot_ref, hops, pre, blocks)
    loads[0].wait()
    loads[1].wait()

    def step(b, _):
        slot = slot_ref[me * blocks + b]
        owner = slot // blocks
        n = counts[owner]
        counts[owner] = n + 1
        distance = lax.rem(owner - me + pre, pre)
        row = pl.multiple_of(b * BLK, BLK)
        on_ring = (distance > 1) & (distance <= hops)
        at = jnp.where(on_ring, (distance - 2) * per_peer + n, (hops - 1) * per_peer)
        sent_values[at] = v_ref[pl.ds(row, BLK)]
        beyond = (distance - hops - 1) * per_peer + n
        at = jnp.where(distance > hops, beyond, (pre - 1 - hops) * per_peer)
        block = block_of(k_ref, v_ref, row)
        sent[at] = block
        cache_ref[own_slot(slot, me, blocks)] = block
        return 0

    lax.fori_loop(0, blocks, step, 0, unroll=4)
    packed = [sent_values.at[n * per_peer : (n + 1) * per_peer] for n in range(hops - 1)]
    packed += [sent.at[n * per_peer : (n + 1) * per_peer] for n in range(pre - 1 - hops)]
    stores = [
        pltpu.make_async_copy(src, dst, sems.at[n])
        for n, (src, dst) in enumerate(zip(packed, sent_hbm))
    ]
    for store in stores:
        store.start()
    turn_values(v_ref, turned)
    loads[2].wait()
    for tile in range(rows // TILE):
        high = (tile + 1) * TILE
        fill_bias(bias, lengths_ref, first + tile * TILE, first, 0, high, True)
        for g in range(turned.shape[0]):
            all_weights = []

            def emit(j, weights, top, factor, total):
                all_weights.append(weights)
                top_ref[g, :, lanes_of(tile, j)] = top
                sum_ref[g, :, lanes_of(tile, j)] = total

            weigh(q_ref, k_ref, bias, None, tile, 0, high, g, emit)
            all_weights = jnp.concatenate(all_weights, axis=1)
            mix(turned[g, :, :high], all_weights, g, tile, None, keep(acc_ref, tile))
    for store in stores:
        store.wait()


def lowest_key(lengths_ref, hop, tile, rows):
    first = lax.axis_index("pre") * rows
    key_first = first - hop * rows
    low = jnp.maximum(start_of(lengths_ref, first + tile * TILE) - key_first, 0)
    return jnp.where(key_first >= 0, jnp.minimum(low, rows), rows)


def where_seen(low, rows, act):
    for at in range(0, rows, TILE):
        pl.when((low >= at) & (low < at + TILE))(functools.partial(act, at))


def scores_kernel(hop, lengths_ref, q_ref, k_ref, old_top, old_sum, weights_ref, factor_ref, sum_ref, *refs):
    *top_refs, bias = refs
    rows = q_ref.shape[0]
    first = lax.axis_index("pre") * rows
    for tile in range(rows // TILE):

        def act(at):
            fill_bias(
                bias, lengths_ref, first + tile * TILE, first - hop * rows, at, rows, False
            )
            for g in range(weights_ref.shape[1]):

                def emit(j, weights, top, factor, total):
                    lanes = lanes_of(tile, j)
                    sum_ref[g, :, lanes] = old_sum[g, :, lanes] * factor + total
                    weights_ref[tile, g, at:rows, j * TILE : (j + 1) * TILE] = weights
                    for top_ref in top_refs:
                        top_ref[g, :, lanes_of(tile, j)] = top
                    factor_ref[g, :, lanes_of(tile, j)] = factor

                weigh(q_ref, k_ref, bias, old_top, tile, at, rows, g, emit)

        where_seen(lowest_key(lengths_ref, hop, tile, rows), rows, act)


def place_blocks(cache, slot_ref, k_ref, v_ref, distance, pre, blocks):
    me = lax.axis_index("pre")
    source = lax.rem(me - distance + pre, pre)

    def step(b, _):
        at = own_slot(slot_ref[source * blocks + b], me, blocks)
        cache[at] = block_of(k_ref, v_ref, pl.multiple_of(b * BLK, BLK))
        return 0

    lax.fori_loop(0, blocks, step, 0, unroll=8)


def place_listed(cache, places_ref, hop, pre, k_ref, v_ref, got_ref):
    me = lax.axis_index("pre")
    per_peer = got_ref.shape[0]
    stride = per_peer + 1

    def place(values_at):
        for n in range(per_peer):
            at = places_ref[(hop - 2) * stride + n]
            b = places_ref[(pre - 2 + hop - 2) * stride + n]
            rows = pl.ds(pl.multiple_of(b * BLK, BLK), BLK)
            values = values_at(n, rows)
            parts = []
            for g in range(k_ref.shape[1] // HD):
                span = slice(g * HD, (g + 1) * HD)
                parts += [k_ref[rows, span], values[:, span]]
            cache[at] = jnp.concatenate(parts, axis=1)

    pl.when(me >= hop - 1)(lambda: place(lambda n, rows: v_ref[rows]))
    pl.when(me < hop - 1)(lambda: place(lambda n, rows: got_ref[n]))


def place_packed(cache, places_ref, distance, got_ref):
    per_peer = got_ref.shape[0]
    for n in range(per_peer):
        cache[places_ref[(distance - 2) * (per_peer + 1) + n]] = got_ref[n]


def values_kernel(
    hop, hops, pre, lengths_ref, slot_ref, v_ref, k_ref, weights_ref, factor_ref,
    acc_in, sum_in, old_sum, cache_in, *refs,
):
    first_out, last = hop == 1, hop == hops
    refs = list(refs)
    if not first_out:
        refs.pop(0)
    got_ref = None if first_out else refs.pop(0)
    got_far = [refs.pop(0) for _ in range(hops + 1, pre)] if last else []
    out_hbm, cache_out = refs.pop(0), refs.pop(0)
    acc_ref = None if last else refs.pop(0)
    turned, out_buf, sems, *rest = refs
    rows = v_ref.shape[0]
    blocks = rows // BLK
    tiles = rows // TILE
    kv_count = turned.shape[0]

    lows = [lowest_key(lengths_ref, hop, tile, rows) for tile in range(tiles)]
    pl.when(lows[0] < rows)(functools.partial(turn_values, v_ref, turned))
    stores = []
    for tile, low in enumerate(lows):
        end_it = finish(out_buf, tile * TILE)

        def act(at):
            def emit(g, j, value):
                if not last:
                    keep(acc_ref, tile)(g, j, value)
                end_it(g, j, value, sum_in[g, :, lanes_of(tile, j)])

            for g in range(kv_count):
                weights = weights_ref[tile, g, at:rows]
                old = (acc_in, factor_ref)
                mix(turned[g, :, at:rows], weights, g, tile, old, emit)

        where_seen(low, rows, act)
        span = slice(tile * TILE, (tile + 1) * TILE)
        store = pltpu.make_async_copy(out_buf.at[span], out_hbm.at[span], sems.at[tile])
        stores.append(store)
        if first_out:

            @pl.when(low == rows)
            def _():
                for g in range(kv_count):
                    for j in range(GROUP):
                        end_it(g, j, *(ref[g, :, lanes_of(tile, j)] for ref in (acc_in, old_sum)))

            store.start()
        else:
            pl.when(low < rows)(store.start)
    cache = rest[0] if last else cache_out
    cache[...] = cache_in[...]
    if first_out:
        place_blocks(cache, slot_ref, k_ref, v_ref, hop, pre, blocks)
    else:
        place_listed(cache, slot_ref, hop, pre, k_ref, v_ref, got_ref)
    if last:
        for n, far_ref in enumerate(got_far):
            place_packed(cache, slot_ref, hops + 1 + n, far_ref)
        cache_store = pltpu.make_async_copy(cache.at[0:blocks], cache_out, sems.at[tiles])
        cache_store.start()

    for low, store in zip(lows, stores):
        if first_out:
            store.wait()
        else:
            pl.when(low < rows)(store.wait)
    if last:
        cache_store.wait()


def on_device(queries, new_keys, new_values, lengths, block_slot):
    rows, q_width = queries.shape
    kv_width = new_keys.shape[1]
    kv_count = kv_width // HD
    blocks = rows // BLK
    pre = lax.axis_size("pre")
    per_peer = blocks // pre
    hops = pre // 2
    tiles = rows // TILE
    bf16, f32 = jnp.bfloat16, jnp.float32
    shape = jax.ShapeDtypeStruct
    params = pltpu.CompilerParams(vmem_limit_bytes=24 * 2**20)
    own_params = pltpu.CompilerParams(vmem_limit_bytes=44 * 2**20)
    ring = [(i, (i + 1) % pre) for i in range(pre)]
    acc_shape = shape((kv_count, HD, GROUP * rows), f32)
    stat_shape = shape((kv_count, 8, GROUP * rows), f32)
    weights_shape = shape((tiles, kv_count, rows, GROUP * TILE), bf16)
    attended_shape = shape(queries.shape, bf16)
    cache_shape = shape((blocks, BLK, 2 * kv_width), bf16)
    open_cache = shape((blocks + 1, BLK, 2 * kv_width), bf16)
    turned = pltpu.VMEM((kv_count, HD, rows), bf16)
    bias = pltpu.VMEM((rows, TILE), f32)

    def cost(share, moved):
        pairs = int(rows * rows * share)
        return pl.CostEstimate(
            flops=4 * pairs * q_width,
            bytes_accessed=moved * 2**20,
            transcendentals=pairs * kv_count * GROUP,
        )

    def after(array, *others):
        return lax.optimization_barrier((array, *others))[0]

    k, v = lax.ppermute(new_keys, "pre", ring), lax.ppermute(new_values, "pre", ring)

    packed = (shape((per_peer, BLK, kv_width), bf16),) * (hops - 1)
    packed += (shape((per_peer, BLK, 2 * kv_width), bf16),) * (pre - 1 - hops)
    places = shape(((pre - 2 + hops - 1) * (per_peer + 1),), jnp.int32)
    in_hbm = (
        pltpu.with_memory_space_constraint(x, pltpu.HBM) for x in (queries, new_keys, new_values)
    )
    q, acc, total, top, cache, places, *sent = pl.pallas_call(
        functools.partial(own_kernel, pre, hops),
        out_shape=(attended_shape, acc_shape, stat_shape, stat_shape, open_cache, places)
        + packed,
        in_specs=[SMEM, SMEM] + [HBM] * 3,
        out_specs=(VMEM,) * 5 + (SMEM,) + (HBM,) * (pre - 2),
        scratch_shapes=[
            pltpu.VMEM((rows, kv_width), bf16),
            pltpu.VMEM((rows, kv_width), bf16),
            turned,
            bias,
            pltpu.VMEM(((hops - 1) * per_peer + 1, BLK, kv_width), bf16),
            pltpu.VMEM(((pre - 1 - hops) * per_peer + 1, BLK, 2 * kv_width), bf16),
            pltpu.SMEM((pre,), jnp.int32),
            pltpu.SemaphoreType.DMA((pre - 2,)),
            pltpu.SemaphoreType.DMA((3,)),
        ],
        cost_estimate=cost(1, 4),
        compiler_params=own_params,
        name="own_attention",
    )(lengths, block_slot, *in_hbm)
    got = []
    k = after(k, top)
    attended = None
    for hop in range(1, hops + 1):
        first_out, last = hop == 1, hop == hops
        onward = [(i, i + 1) for i in range(hop - 1, pre - 1)]
        next_k = None if last else lax.ppermute(k, "pre", ring)
        weights, factor, new_total, *tops = pl.pallas_call(
            functools.partial(scores_kernel, hop),
            out_shape=(weights_shape, stat_shape, stat_shape) + (() if last else (stat_shape,)),
            in_specs=[SMEM] + [VMEM] * 4,
            out_specs=(VMEM,) * (3 if last else 4),
            scratch_shapes=[bias],
            cost_estimate=cost(0.5, 3),
            compiler_params=params,
            name="scores",
        )(lengths, q, k, top, total)
        v = after(v, factor)
        next_v = None if last else lax.ppermute(v, "pre", onward)
        if first_out:
            for d in range(2, pre):
                targets = range(d - 1 if d <= hops else pre)
                pairs = [((i - d) % pre, i) for i in targets]
                got.append(lax.ppermute(after(sent[d - 2], v), "pre", pairs))
        carry = () if last else (acc_shape,)
        extra = [] if first_out else [attended]
        extra += [] if first_out else [got[hop - 2]]
        extra += got[hops - 1 :] if last else []
        attended, cache, *state = pl.pallas_call(
            functools.partial(values_kernel, hop, hops, pre),
            out_shape=(attended_shape, cache_shape if last else open_cache)
            + carry,
            in_specs=[SMEM, SMEM]
            + [VMEM] * 8
            + ([] if first_out else [HBM])
            + [VMEM] * (len(extra) - 1),
            out_specs=(HBM, HBM if last else VMEM)
            + (VMEM,) * len(carry),
            scratch_shapes=[
                turned,
                pltpu.VMEM((rows, q_width), bf16),
                pltpu.SemaphoreType.DMA((tiles + 1,)),
            ]
            + ([pltpu.VMEM(open_cache.shape, bf16)] if last else []),
            input_output_aliases={} if first_out else {10: 0},
            cost_estimate=cost(0.5, 3),
            compiler_params=params,
            name="values",
        )(lengths, block_slot if first_out else places, v, k, weights, factor, acc, new_total, total, cache, *extra)
        if not last:
            (top,) = tops
            (acc,) = state
            total = new_total
            k, v = after(next_k, total), next_v

    return (attended, cache)


def solution(mesh):
    placed = (
        P(("parts", "pre"), "tp"),
        P(("parts", "pre"), "tp"),
        P(("parts", "pre"), "tp"),
        P("parts"),
        P("parts"),
    )
    return jax.shard_map(
        on_device,
        mesh=mesh,
        in_specs=placed,
        out_specs=(P(("parts", "pre"), "tp"), P(("parts", "pre"), None, "tp")),
        check_vma=False,
    )
```
